32 devices in a mesh: seq: 8 (over z, y), tp: 4 (over x, core).
Axes of the slice: x: 2, y: 2, z: 4, core: 2. Of those that a mesh axis runs over, the one named last changes fastest.
Arguments:
- normed: bfloat16 [4, 8192, 1024], P(None, 'seq'), may hold values from -6 to 6
- grad_out: bfloat16 [4, 8192, 1024], P(None, 'seq'), may hold values from -16 to 16
- value_weight: bfloat16 [1024, 1024], P(None, 'tp'), may hold values from -0.1875 to 0.1875
- gate_weight: bfloat16 [1024, 1024], P(None, 'tp'), may hold values from -0.1875 to 0.1875
- depth_taps: float32 [9, 1024], P(None, 'tp'), may hold values from -2 to 2
- norm_gain: float32 [1024], P('tp'), may hold values from 0.1 to 1.9
- norm_shift: float32 [1024], P('tp'), may hold values from -1 to 1
- out_weight: bfloat16 [1024, 1024], P(None, 'tp'), may hold values from -0.1875 to 0.1875
- lengths: int32 [4], replicated, may hold values from 2048 to 8192, as said below
Outputs:
- grad_in: bfloat16 [4, 1024, 8192], P(None, ('seq', 'tp'))
- grad_w_value: float32 [1024, 1024], P('seq', 'tp')
- grad_w_gate: float32 [1024, 1024], P('seq', 'tp')
- grad_w_out: float32 [1024, 1024], P('seq', 'tp')
- grad_taps: float32 [9, 1024], P(None, 'tp')
- grad_gain: float32 [1024], P('tp')
- grad_shift: float32 [1024], P('tp')
The draws below stay inside these ranges and needn't reach their ends.
Inputs may be any that keep to these rules, and one draw needn't show every extreme that they name: `lengths`: frames of each recording that are valid; some recording is valid to its last frame.
All inputs are finite; a program needn't handle non-finite values.
Results may differ from the reference program's by a relative error of at most 0.01.
Values may be sent and summed in bfloat16 or wider, within the bound.
No kernel may reach another device: no remote copies, remote signals or barrier semaphores. Data moves between devices by JAX's collectives and lax.ppermute only.
A program may use at most 128 MiB of HBM per device.

```python
import math
import jax
import jax.numpy as jnp
from jax import lax

D = 1024
C = 1024
KERNEL = 9
RECS = 4
L = 8192
N_TP = 4


def draw_grad_out(key, part):
    first, second = jax.random.split(jax.random.fold_in(key, 11), 2)
    base = jnp.clip(jax.random.normal(first, (RECS, L, D), jnp.float32), -6.0, 6.0)
    log_scale = jax.random.uniform(second, (RECS, L, 1), jnp.float32, 0.0, math.log(10.0))
    values = 0.1 * base * jnp.exp(log_scale)
    return jnp.clip(values, -16.0, 16.0).astype(jnp.bfloat16)


def draw_lengths(key, part):
    first, second = jax.random.split(jax.random.fold_in(key, 5))
    drawn = jax.random.randint(first, (RECS,), L // 4, L + 1)
    whole_one = jax.random.randint(second, (), 0, RECS)
    return jnp.where(jnp.arange(RECS) == whole_one, L, drawn).astype(jnp.int32)


def steps_of(own_key, extent, shards, least, top_value):
    level, own = 1.0, jax.random.fold_in(own_key, 6)
    for position, parts in shards:
        draws = jnp.exp(jax.random.uniform(jax.random.fold_in(own, position), (parts,), jnp.float32, least / len(shards), top_value / len(shards)))
        level = level * jnp.repeat(draws, extent[position] // parts).reshape([-1 if axis == position else 1 for axis in range(len(extent))])
    return level


def normal_values(key, shape, deviation, limit, pieces=(), held_as=jnp.bfloat16):
    loudness = steps_of(key, shape, pieces, -0.22, 0.18) if pieces else 1.0
    result = jax.random.normal(key, shape, jnp.float32) * deviation * loudness
    return jnp.minimum(jnp.maximum(result, -limit), limit).astype(held_as)


def setup_inputs(seed: int = 0) -> dict:
    key_list = jax.random.split(jax.random.key(seed), 10)
    return {
        "normed": normal_values(key_list[0], (RECS, L, D), 1.0, 6.0, ((1, 8),)),
        "grad_out": draw_grad_out(jax.random.fold_in(key_list[9], 71), 0),
        "value_weight": normal_values(key_list[2], (D, C), D ** -0.5, 0.1875, ((1, 4),)),
        "gate_weight": normal_values(key_list[3], (D, C), D ** -0.5, 0.1875, ((1, 4),)),
        "depth_taps": normal_values(key_list[4], (KERNEL, C), KERNEL ** -0.5, 2.0, ((1, 4),), jnp.float32),
        "norm_gain": jnp.clip(1.0 + 0.18 * jax.random.normal(key_list[5], (C,), jnp.float32), 0.1, 1.9),
        "norm_shift": jnp.clip(jax.random.uniform(key_list[6], (C,), jnp.float32, -1.0, 1.0) * steps_of(key_list[6], (C,), ((0, 4),), -0.4, 0.0), -1.0, 1.0),
        "out_weight": normal_values(key_list[7], (D, C), C ** -0.5, 0.1875, ((1, 4),)),
        "lengths": draw_lengths(jax.random.fold_in(key_list[9], 71), 0),
    }


epsilon = 1e-05

def reference(normed, grad_out, value_weight, gate_weight, depth_taps, norm_gain, norm_shift, out_weight, lengths):
    frames_all = RECS * L
    margin = (KERNEL - 1) // 2
    positions = jnp.arange(L, dtype=jnp.int32)
    valid_mask = (positions[None, :] < lengths[:, None]).astype(jnp.float32)[:, :, None]
    frame_count = jnp.sum(lengths).astype(jnp.float32)
    rows_in = normed.reshape(frames_all, D)
    value_lin = jnp.dot(rows_in, value_weight, preferred_element_type=jnp.float32).reshape(RECS, L, C)
    gate_lin = jnp.dot(rows_in, gate_weight, preferred_element_type=jnp.float32).reshape(RECS, L, C)
    gate_sig = jax.nn.sigmoid(gate_lin)
    gated_units = valid_mask * value_lin * gate_sig
    gated_pad = jnp.pad(gated_units, ((0, 0), (margin, margin), (0, 0)))
    conv_out = jnp.zeros((RECS, L, C), jnp.float32)
    for tap_index in range(KERNEL):
        conv_out = conv_out + depth_taps[tap_index] * gated_pad[:, tap_index:tap_index + L]
    channel_sum = lax.optimization_barrier(jnp.sum(valid_mask * conv_out, axis=(0, 1)))
    channel_sq = lax.optimization_barrier(jnp.sum(valid_mask * conv_out * conv_out, axis=(0, 1)))
    centre = channel_sum / frame_count
    spread = channel_sq / frame_count - centre * centre
    inv_std = lax.rsqrt(spread + epsilon)
    unit_conv = (conv_out - centre) * inv_std
    normalized = unit_conv * norm_gain + norm_shift
    norm_sig = jax.nn.sigmoid(normalized)
    swished = (valid_mask * normalized * norm_sig).astype(jnp.bfloat16)
    grads_flat = grad_out.reshape(frames_all, D)
    swish_grad = jnp.dot(grads_flat, out_weight, preferred_element_type=jnp.float32).reshape(RECS, L, C)
    grad_w_out = lax.dot_general(grads_flat, swished.reshape(frames_all, C), (((0,), (0,)), ((), ())), preferred_element_type=jnp.float32)
    grad_norm = swish_grad * valid_mask * norm_sig * (1.0 + normalized * (1.0 - norm_sig))
    grad_shift = lax.optimization_barrier(jnp.sum(grad_norm, axis=(0, 1)))
    grad_gain = lax.optimization_barrier(jnp.sum(grad_norm * unit_conv, axis=(0, 1)))
    grad_conv = valid_mask * norm_gain * inv_std * (grad_norm - grad_shift / frame_count - unit_conv * grad_gain / frame_count)
    tap_list = []
    for tap_index in range(KERNEL):
        tap_list.append(lax.optimization_barrier(jnp.sum(grad_conv * gated_pad[:, tap_index:tap_index + L], axis=(0, 1))))
    grad_taps = jnp.stack(tap_list)
    conv_pad = jnp.pad(grad_conv, ((0, 0), (margin, margin), (0, 0)))
    grad_gated = jnp.zeros((RECS, L, C), jnp.float32)
    for tap_index in range(KERNEL):
        first_row = 2 * margin - tap_index
        grad_gated = grad_gated + depth_taps[tap_index] * conv_pad[:, first_row:first_row + L]
    grad_gated = valid_mask * grad_gated
    grad_value = (grad_gated * gate_sig).astype(jnp.bfloat16).reshape(frames_all, C)
    grad_gate = (grad_gated * value_lin * gate_sig * (1.0 - gate_sig)).astype(jnp.bfloat16).reshape(frames_all, C)
    grad_w_value = lax.dot_general(rows_in, grad_value, (((0,), (0,)), ((), ())), preferred_element_type=jnp.float32)
    grad_w_gate = lax.dot_general(rows_in, grad_gate, (((0,), (0,)), ((), ())), preferred_element_type=jnp.float32)
    group_width = C // N_TP

    def add_group(running, group_index):
        first_col = (group_index * group_width).astype(jnp.int32)
        value_part = lax.dynamic_slice_in_dim(grad_value, first_col, group_width, 1)
        gate_part = lax.dynamic_slice_in_dim(grad_gate, first_col, group_width, 1)
        value_cols = lax.dynamic_slice_in_dim(value_weight, first_col, group_width, 1)
        gate_cols = lax.dynamic_slice_in_dim(gate_weight, first_col, group_width, 1)
        partial_value = lax.dot_general(value_part, value_cols, (((1,), (1,)), ((), ())), preferred_element_type=jnp.float32)
        partial_value = partial_value + lax.dot_general(gate_part, gate_cols, (((1,), (1,)), ((), ())), preferred_element_type=jnp.float32)
        rounded = lax.optimization_barrier(partial_value.astype(jnp.bfloat16))
        return (running + rounded.astype(jnp.float32), None)
    groups = jnp.arange(N_TP, dtype=jnp.int32)
    grad_normed, _ = lax.scan(add_group, jnp.zeros((frames_all, D), jnp.float32), groups)
    grad_rows = (grads_flat.astype(jnp.float32) + grad_normed).astype(jnp.bfloat16).reshape(RECS, L, D)
    grad_in = jnp.transpose(grad_rows, (0, 2, 1))
    return (grad_in, grad_w_value, grad_w_gate, grad_w_out, grad_taps, grad_gain, grad_shift)
```

```python
import functools

import jax
import jax.numpy as jnp
from jax import lax
from jax.experimental import pallas as pl
from jax.experimental.pallas import tpu as pltpu
from jax.sharding import PartitionSpec as P

EPSILON = 1e-05
EDGE = 8
LANES = 128
F32 = jnp.float32
BF16 = jnp.bfloat16


def sigmoid(x):
    return 0.5 * jnp.tanh(0.5 * x) + 0.5


def dot(a, b):
    return jnp.dot(a, b, preferred_element_type=F32)


def dot_nt(a, b):
    return lax.dot_general(a, b, (((1,), (1,)), ((), ())), preferred_element_type=F32)


def dot_tn(a, b):
    return lax.dot_general(a, b, (((0,), (0,)), ((), ())), preferred_element_type=F32)


def rows_of(count, first):
    return first + lax.broadcasted_iota(jnp.int32, (count, 1), 0)


def fold_rows(x):
    return jnp.sum(x.reshape(x.shape[0] // 8, 8, x.shape[1]), axis=0)


def block_rows(total, most):
    return max(b for b in range(8, most + 1, 8) if total % b == 0)


def whole(shape):
    return pl.BlockSpec(shape, lambda *i: (0,) * len(shape))


def per_record(shape):
    return pl.BlockSpec((1,) + shape, lambda r: (r,) + (0,) * len(shape))


def smem():
    return pl.BlockSpec(memory_space=pltpu.SMEM)


def call(kernel, name, grid, in_specs, out_specs, out_shape, scratch, flops, moved, aliases=None):
    return pl.pallas_call(
        kernel,
        name=name,
        grid=grid,
        in_specs=in_specs,
        out_specs=out_specs,
        out_shape=out_shape,
        scratch_shapes=scratch,
        input_output_aliases=aliases or {},
        cost_estimate=pl.CostEstimate(flops=int(flops), bytes_accessed=int(moved), transcendentals=0),
        compiler_params=pltpu.CompilerParams(vmem_limit_bytes=40 * 1024 * 1024),
    )


def pick_kernel(sel, grads, out):
    out[0] = dot_nt(sel[...], grads[0]).astype(BF16)


def gate_kernel(meta, x, halo, wv, wg, taps, vl_o, sg_o, conv_o, st_o, gp):
    r = pl.program_id(0)
    hi = meta[0, r]
    lo = meta[1, r]
    frames = x.shape[1]
    width = wv.shape[1]
    halves = width // LANES

    def put(row, value):
        for h in range(halves):
            gp[h, pl.ds(row, value.shape[0]), :] = value[:, h * LANES : (h + 1) * LANES]

    edge_v = dot(halo[0], wv[...])
    edge_g = dot(halo[0], wg[...])
    row = rows_of(2 * EDGE, 0)
    pos = jnp.where(row < EDGE, row - EDGE, row - EDGE + frames)
    edge = jnp.where((pos >= lo) & (pos < hi), edge_v * sigmoid(edge_g), 0.0)
    zero = jnp.zeros((EDGE, width), F32)
    put(0, zero)
    put(EDGE, edge[:EDGE])
    put(2 * EDGE + frames, edge[EDGE:])
    put(3 * EDGE + frames, zero)
    step = block_rows(frames, 256)

    def project(i, carry):
        base = pl.multiple_of(i * step, step)
        xb = x[0, pl.ds(base, step), :]
        v = dot(xb, wv[...])
        s = sigmoid(dot(xb, wg[...]))
        vl_o[0, pl.ds(base, step), :] = v
        sg_o[0, pl.ds(base, step), :] = s
        put(2 * EDGE + base, jnp.where(rows_of(step, base) < hi, v * s, 0.0))
        return carry

    lax.fori_loop(0, frames // step, project, 0)
    span = frames + 2 * EDGE
    cb = block_rows(span, 104)
    kernel = taps.shape[0]
    margin = (kernel - 1) // 2
    for h in range(halves):
        cols = slice(h * LANES, (h + 1) * LANES)

        def convolve(i, carry):
            s1, s2 = carry
            base = pl.multiple_of(i * cb, 8)
            acc = jnp.zeros((cb, LANES), F32)
            for k in range(kernel):
                acc = acc + taps[k : k + 1, cols] * gp[h, pl.ds(base + EDGE - margin + k, cb), :]
            conv_o[0, pl.ds(base, cb), cols] = acc
            pos = rows_of(cb, base - EDGE)
            kept = jnp.where((pos >= 0) & (pos < jnp.minimum(hi, frames)), acc, 0.0)
            return s1 + fold_rows(kept), s2 + fold_rows(kept * kept)

        none = jnp.zeros((8, LANES), F32)
        s1, s2 = lax.fori_loop(0, span // cb, convolve, (none, none))
        st_o[0, 0:1, cols] = jnp.sum(s1, axis=0, keepdims=True)
        st_o[0, 1:2, cols] = jnp.sum(s2, axis=0, keepdims=True)


def swish_kernel(grads, halo, wo, sw_o):
    frames = grads.shape[1]
    edge = dot(halo[0], wo[...])
    sw_o[0, :EDGE, :] = edge[:EDGE]
    sw_o[0, EDGE + frames :, :] = edge[EDGE:]
    step = block_rows(frames, 256)

    def body(i, carry):
        base = pl.multiple_of(i * step, step)
        sw_o[0, pl.ds(base + EDGE, step), :] = dot(grads[0, pl.ds(base, step), :], wo[...])
        return carry

    lax.fori_loop(0, frames // step, body, 0)


def norm_kernel(meta, conv, sw, vec, swished_o, gn_o, st_o):
    r = pl.program_id(0)
    hi = meta[0, r]
    lo = meta[1, r]
    frames = swished_o.shape[1]
    centre, inv, gain, shift = (vec[i : i + 1, :] for i in range(4))

    def part(row, count):
        unit = (conv[0, pl.ds(row, count), :] - centre) * inv
        normalized = unit * gain + shift
        s = sigmoid(normalized)
        pos = rows_of(count, row - EDGE)
        keep = (pos >= lo) & (pos < hi)
        swished = jnp.where(keep, normalized * s, 0.0)
        gn = jnp.where(keep, sw[0, pl.ds(row, count), :] * (s + normalized * s * (1.0 - s)), 0.0)
        gn_o[0, pl.ds(row, count), :] = gn
        return unit, swished, gn

    part(0, EDGE)
    part(frames + EDGE, EDGE)
    step = block_rows(frames, 64)

    def body(i, carry):
        s1, s2 = carry
        base = pl.multiple_of(i * step, step)
        unit, swished, gn = part(base + EDGE, step)
        swished_o[0, pl.ds(base, step), :] = swished.astype(BF16)
        return s1 + fold_rows(gn), s2 + fold_rows(gn * unit)

    none = jnp.zeros((8, conv.shape[2]), F32)
    s1, s2 = lax.fori_loop(0, frames // step, body, (none, none))
    st_o[0, 0:1, :] = jnp.sum(s1, axis=0, keepdims=True)
    st_o[0, 1:2, :] = jnp.sum(s2, axis=0, keepdims=True)


def outer_kernel(left, right, out, acc):
    r = pl.program_id(0)
    add = dot_tn(left[0], right[0])

    @pl.when(r == 0)
    def _():
        acc[...] = add

    @pl.when(r > 0)
    def _():
        acc[...] += add

    @pl.when(r == pl.num_programs(0) - 1)
    def _():
        width = out.shape[2]
        for s in range(out.shape[0]):
            out[s] = acc[:, s * width : (s + 1) * width].astype(BF16)


def back_kernel(record, meta, gn, conv, vl, sg, vec, taps, out, taps_o, gc):
    hi = meta[0, record]
    lo = meta[1, record]
    frames, width = vl.shape[1:]
    halves = width // LANES
    span = frames + 2 * EDGE
    kernel = taps.shape[0]
    margin = (kernel - 1) // 2
    cb = block_rows(span, 104)
    step = block_rows(frames, 64)
    for h in range(halves):
        cols = slice(h * LANES, (h + 1) * LANES)
        centre, scale, offset, slope = (vec[i : i + 1, cols] for i in range(4))

        def conv_grad(i, carry):
            base = pl.multiple_of(i * cb, 8)
            pos = rows_of(cb, base - EDGE)
            mean = offset + (conv[0, pl.ds(base, cb), cols] - centre) * slope
            gc[h, pl.ds(base, cb), :] = scale * gn[0, pl.ds(base, cb), cols] - jnp.where(
                (pos >= lo) & (pos < hi), mean, 0.0
            )
            return carry

        lax.fori_loop(0, span // cb, conv_grad, 0)

        def body(i, sums):
            base = pl.multiple_of(i * step, step)
            v = vl[0, pl.ds(base, step), cols]
            s = sg[0, pl.ds(base, step), cols]
            keep = rows_of(step, base) < hi
            vs = v * s
            gated = jnp.where(keep, vs, 0.0)
            total = jnp.zeros((step, LANES), F32)
            new = []
            for k in range(kernel):
                window = gc[h, pl.ds(base + EDGE + margin - k, step), :]
                total = total + taps[k : k + 1, cols] * window
                new.append(sums[k] + fold_rows(window * gated))
            total = jnp.where(keep, total, 0.0)
            out[pl.ds(base, step), cols] = (total * s).astype(BF16)
            out[pl.ds(base, step), width + h * LANES : width + (h + 1) * LANES] = (
                total * vs * (1.0 - s)
            ).astype(BF16)
            return tuple(new)

        none = jnp.zeros((8, LANES), F32)
        sums = lax.fori_loop(0, frames // step, body, (none,) * kernel)
        for k in range(kernel):
            taps_o[k : k + 1, cols] = jnp.sum(sums[k], axis=0, keepdims=True)


def partial_kernel(own, sibling, w_own, w_sibling, picked, mine, *others):
    for d in range(w_own.shape[0]):
        total = dot_nt(w_own[d], own[...]) + dot_nt(w_sibling[d], sibling[...])
        if d == 0:
            mine[...] = total + picked[0].astype(F32)
        else:
            others[d - 1][...] = total.astype(BF16)


def weights_kernel(x, *refs):
    count = x.shape[0]
    lefts, out, acc = refs[:-2], refs[-2], refs[-1]
    r = pl.program_id(0)
    for i, left in enumerate(lefts):

        @pl.when(r == i)
        def _(i=i, left=left):
            add = dot_tn(left[...], x[0])
            if i == 0:
                acc[...] = add
            else:
                acc[...] += add

    @pl.when(r == pl.num_programs(0) - 1)
    def _():
        width = out.shape[2]
        for s in range(out.shape[0]):
            out[s] = acc[:, s * width : (s + 1) * width].astype(BF16)


def place_kernel(moved, *refs):
    out = refs[-1]
    frames = moved.shape[2]
    for s in range(moved.shape[0]):
        out[0, :, s * frames : (s + 1) * frames] = moved[s]


def everyone(part, axis):
    count = lax.axis_size(axis)
    copies = jnp.broadcast_to(part[None], (count,) + part.shape)
    return jnp.sum(lax.all_to_all(copies, axis, 0, 0, tiled=True), axis=0)


def per_device(
    normed,
    grad_out,
    value_weight,
    gate_weight,
    depth_taps,
    norm_gain,
    norm_shift,
    out_weight,
    lengths,
):
    recs, frames, model = normed.shape
    kernel = depth_taps.shape[0]
    width = value_weight.shape[1]
    seqs = lax.axis_size("seq")
    tps = lax.axis_size("tp")
    chips = tps // 2
    piece = model // (seqs * tps)
    rows = seqs * piece
    shard = model // seqs
    span = frames + 2 * EDGE
    seq_at = lax.axis_index("seq")
    tp_at = lax.axis_index("tp")
    chip_at, core_at = tp_at // 2, tp_at % 2
    count = jnp.sum(lengths).astype(F32)
    first = (seq_at * frames).astype(jnp.int32)
    meta = jnp.stack([lengths - first, jnp.full((recs,), 0, jnp.int32) - first])
    halves = width // LANES
    sds = jax.ShapeDtypeStruct

    low_edge = jnp.concatenate([normed[:, -EDGE:], grad_out[:, -EDGE:]], axis=2)
    high_edge = jnp.concatenate([normed[:, :EDGE], grad_out[:, :EDGE]], axis=2)
    up = [(i, i + 1) for i in range(seqs - 1)]
    down = [(j, i) for i, j in up]
    halo = jnp.concatenate(
        [lax.ppermute(low_edge, "seq", up), lax.ppermute(high_edge, "seq", down)], axis=1
    )
    halo_x, halo_g = halo[:, :, :model], halo[:, :, model:]

    both = jnp.concatenate([value_weight, gate_weight], axis=1).reshape(seqs, tps, piece, 2 * width)

    def chosen(core):
        picks = [
            lax.dynamic_index_in_dim(both, ((chip_at + d) % chips) * 2 + core, 1, keepdims=False)
            for d in range(chips)
        ]
        return jnp.stack(picks).reshape(chips, rows, 2 * width)

    swap = [(i, i ^ 1) for i in range(tps)]
    w_own = chosen(core_at)
    w_sibling = lax.ppermute(chosen(1 - core_at), "tp", swap)

    channel = (
        jnp.arange(seqs, dtype=jnp.int32)[:, None] * (tps * piece)
        + tp_at * piece
        + jnp.arange(piece, dtype=jnp.int32)[None, :]
    ).reshape(rows, 1)
    select = (channel == jnp.arange(model, dtype=jnp.int32)[None, :]).astype(BF16)
    array_bytes = recs * frames * width * 4
    input_bytes = recs * frames * model * 2
    matmul = 2 * recs * frames * model * width

    picked = call(
        pick_kernel,
        "pick",
        (recs,),
        [whole((rows, model)), per_record((frames, model))],
        per_record((rows, frames)),
        sds((recs, rows, frames), BF16),
        [],
        matmul,
        input_bytes,
    )(select, grad_out)

    vl, sg, conv, stats = call(
        gate_kernel,
        "gate_conv",
        (recs,),
        [
            smem(),
            per_record((frames, model)),
            per_record((2 * EDGE, model)),
            whole((model, width)),
            whole((model, width)),
            whole((kernel, width)),
        ],
        [
            per_record((frames, width)),
            per_record((frames, width)),
            per_record((span, width)),
            per_record((2, width)),
        ],
        [
            sds((recs, frames, width), F32),
            sds((recs, frames, width), F32),
            sds((recs, span, width), F32),
            sds((recs, 2, width), F32),
        ],
        [pltpu.VMEM((halves, frames + 4 * EDGE, LANES), F32)],
        2 * matmul,
        input_bytes + 3 * array_bytes,
    )(meta, normed, halo_x, value_weight, gate_weight, depth_taps)
    channel_sum, channel_sq = everyone(jnp.sum(stats, axis=0), "seq")

    sw = call(
        swish_kernel,
        "swish_grad",
        (recs,),
        [per_record((frames, model)), per_record((2 * EDGE, model)), whole((model, width))],
        per_record((span, width)),
        sds((recs, span, width), F32),
        [],
        matmul,
        input_bytes + array_bytes,
    )(grad_out, halo_g, out_weight)

    centre = channel_sum / count
    spread = channel_sq / count - centre * centre
    inv_std = lax.rsqrt(spread + EPSILON)
    swished, gn, sums = call(
        norm_kernel,
        "norm_swish",
        (recs,),
        [smem(), per_record((span, width)), per_record((span, width)), whole((4, width))],
        [per_record((frames, width)), per_record((span, width)), per_record((2, width))],
        [
            sds((recs, frames, width), BF16),
            sds((recs, span, width), F32),
            sds((recs, 2, width), F32),
        ],
        [],
        20 * recs * frames * width,
        3 * array_bytes,
    )(meta, conv, sw, jnp.stack([centre, inv_std, norm_gain, norm_shift]))
    grad_shift, grad_gain = everyone(jnp.sum(sums, axis=0), "seq")

    w_out_parts = call(
        outer_kernel,
        "outer_w_out",
        (recs,),
        [per_record((frames, width)), per_record((frames, model))],
        whole((seqs, width, shard)),
        sds((seqs, width, shard), BF16),
        [pltpu.VMEM((width, model), F32)],
        matmul,
        input_bytes,
    )(swished, grad_out)

    scale = norm_gain * inv_std
    vec = jnp.stack(
        [centre, scale, scale * grad_shift / count, scale * inv_std * grad_gain / count]
    )
    grads, tap_parts = [], []
    for r in range(recs):

        def at(shape, r=r):
            return pl.BlockSpec((1,) + shape, lambda i: (r,) + (0,) * len(shape))

        both_grads, tap_part = call(
            functools.partial(back_kernel, r),
            "back_conv",
            (1,),
            [
                smem(),
                at((span, width)),
                at((span, width)),
                at((frames, width)),
                at((frames, width)),
                whole((4, width)),
                whole((kernel, width)),
            ],
            [whole((frames, 2 * width)), whole((kernel, width))],
            [sds((frames, 2 * width), BF16), sds((kernel, width), F32)],
            [pltpu.VMEM((halves, span, LANES), F32)],
            60 * frames * width,
            4 * array_bytes // recs,
        )(meta, gn, conv, vl, sg, vec, depth_taps)
        grads.append(both_grads)
        tap_parts.append(tap_part)

    grad_in = None
    moved_parts = []
    for r in range(recs):

        def at(shape, r=r):
            return pl.BlockSpec((1,) + shape, lambda i: (r,) + (0,) * len(shape))

        sibling = lax.ppermute(grads[r], "tp", swap)
        parts = call(
            partial_kernel,
            "partial_in",
            (1,),
            [
                whole((frames, 2 * width)),
                whole((frames, 2 * width)),
                whole((chips, rows, 2 * width)),
                whole((chips, rows, 2 * width)),
                at((rows, frames)),
            ],
            [whole((rows, frames))] * chips,
            [sds((rows, frames), F32)] + [sds((rows, frames), BF16)] * (chips - 1),
            [],
            2 * matmul // recs,
            8 * frames * width + 6 * rows * frames,
        )(grads[r], sibling, w_own, w_sibling, picked)
        total = parts[0]
        for d in range(1, chips):
            send = [(i, ((i // 2 + d) % chips) * 2 + i % 2) for i in range(tps)]
            total = total + lax.ppermute(parts[d], "tp", send).astype(F32)
        own = total.astype(BF16).reshape(seqs, piece, frames)
        moved_parts.append(lax.all_to_all(own, "seq", 0, 0, tiled=True))

    w_in_parts = call(
        weights_kernel,
        "outer_w_in",
        (recs,),
        [per_record((frames, model))] + [whole((frames, 2 * width))] * recs,
        whole((seqs, 2 * width, shard)),
        sds((seqs, 2 * width, shard), BF16),
        [pltpu.VMEM((2 * width, model), F32)],
        2 * matmul,
        input_bytes + 4 * recs * frames * width,
    )(normed, *grads)

    for r in range(recs):
        place = call(
            place_kernel,
            "place",
            (1,),
            [whole((seqs, piece, frames))] + ([] if r == 0 else [pl.BlockSpec(memory_space=pl.ANY)]),
            pl.BlockSpec((1, piece, seqs * frames), lambda i, r=r: (r, 0, 0)),
            sds((recs, piece, seqs * frames), BF16),
            [],
            0,
            4 * piece * seqs * frames,
            None if r == 0 else {1: 0},
        )
        grad_in = place(moved_parts[r]) if r == 0 else place(moved_parts[r], grad_in)

    def owned(parts):
        got = lax.all_to_all(parts, "seq", 0, 0, tiled=True)
        return jnp.sum(got.astype(F32), axis=0).T

    grad_w_out = owned(w_out_parts)
    w_in = owned(w_in_parts)
    grad_taps = everyone(sum(tap_parts), "seq")
    return (
        grad_in,
        w_in[:, :width],
        w_in[:, width:],
        grad_w_out,
        grad_taps,
        grad_gain,
        grad_shift,
    )


def solution(mesh):
    placed = (
        P(None, "seq", None),
        P(None, "seq", None),
        P(None, "tp"),
        P(None, "tp"),
        P(None, "tp"),
        P("tp"),
        P("tp"),
        P(None, "tp"),
        P(),
    )
    return jax.shard_map(
        per_device,
        mesh=mesh,
        in_specs=placed,
        out_specs=(
            P(None, ("seq", "tp"), None),
            P("seq", "tp"),
            P("seq", "tp"),
            P("seq", "tp"),
            P(None, "tp"),
            P("tp"),
            P("tp"),
        ),
        check_vma=False,
    )
```

```python
import functools

import jax
import jax.numpy as jnp
from jax import lax
from jax.experimental import pallas as pl
from jax.experimental.pallas import tpu as pltpu
from jax.sharding import PartitionSpec as P

EPSILON = 1e-05
EDGE = 8
LANES = 128
F32 = jnp.float32
BF16 = jnp.bfloat16


def sigmoid(x):
    return 0.5 * jnp.tanh(0.5 * x) + 0.5


def dot(a, b):
    return jnp.dot(a, b, preferred_element_type=F32)


def dot_nt(a, b):
    return lax.dot_general(a, b, (((1,), (1,)), ((), ())), preferred_element_type=F32)


def dot_tn(a, b):
    return lax.dot_general(a, b, (((0,), (0,)), ((), ())), preferred_element_type=F32)


def rows_of(count, first):
    return first + lax.broadcasted_iota(jnp.int32, (count, 1), 0)


def fold_rows(x):
    return jnp.sum(x.reshape(x.shape[0] // 8, 8, x.shape[1]), axis=0)


def block_rows(total, most):
    return max(b for b in range(8, most + 1, 8) if total % b == 0)


def whole(shape):
    return pl.BlockSpec(shape, lambda *i: (0,) * len(shape))


def per_record(shape):
    return pl.BlockSpec((1,) + shape, lambda r: (r,) + (0,) * len(shape))


def smem():
    return pl.BlockSpec(memory_space=pltpu.SMEM)


def anywhere():
    return pl.BlockSpec(memory_space=pl.ANY)


def after(x, *earlier):
    return lax.optimization_barrier((x,) + earlier)[0]


def spread_sums(out, sums):
    for s in range(out.shape[0]):
        out[s] = sums


def call(kernel, name, grid, in_specs, out_specs, out_shape, scratch, flops, moved, aliases=None):
    return pl.pallas_call(
        kernel,
        name=name,
        grid=grid,
        in_specs=in_specs,
        out_specs=out_specs,
        out_shape=out_shape,
        scratch_shapes=scratch,
        input_output_aliases=aliases or {},
        cost_estimate=pl.CostEstimate(flops=int(flops), bytes_accessed=int(moved), transcendentals=0),
        compiler_params=pltpu.CompilerParams(vmem_limit_bytes=60 * 1024 * 1024),
    )


def pick_kernel(sel, grads, out):
    out[0] = dot_nt(sel[...], grads[0]).astype(BF16)


def gate_kernel(meta, x, halo, wv, wg, taps, vl_o, sg_o, conv_o, st_o, gp, st):
    r = pl.program_id(0)
    hi = meta[0, r]
    lo = meta[1, r]
    frames = x.shape[1]
    width = wv.shape[1]
    halves = width // LANES

    def put(row, value):
        for h in range(halves):
            gp[h, pl.ds(row, value.shape[0]), :] = value[:, h * LANES : (h + 1) * LANES]

    edge_v = dot(halo[0], wv[...])
    edge_g = dot(halo[0], wg[...])
    row = rows_of(2 * EDGE, 0)
    pos = jnp.where(row < EDGE, row - EDGE, row - EDGE + frames)
    edge = jnp.where((pos >= lo) & (pos < hi), edge_v * sigmoid(edge_g), 0.0)
    zero = jnp.zeros((EDGE, width), F32)
    put(0, zero)
    put(EDGE, edge[:EDGE])
    put(2 * EDGE + frames, edge[EDGE:])
    put(3 * EDGE + frames, zero)
    step = block_rows(frames, 256)

    def project(i, carry):
        base = pl.multiple_of(i * step, step)
        xb = x[0, pl.ds(base, step), :]
        v = dot(xb, wv[...])
        s = sigmoid(dot(xb, wg[...]))
        vl_o[0, pl.ds(base, step), :] = v
        sg_o[0, pl.ds(base, step), :] = s
        put(2 * EDGE + base, jnp.where(rows_of(step, base) < hi, v * s, 0.0))
        return carry

    lax.fori_loop(0, frames // step, project, 0)
    span = frames + 2 * EDGE
    cb = block_rows(span, 104)
    kernel = taps.shape[0]
    margin = (kernel - 1) // 2
    for h in range(halves):
        cols = slice(h * LANES, (h + 1) * LANES)

        def convolve(i, carry):
            s1, s2 = carry
            base = pl.multiple_of(i * cb, 8)
            acc = jnp.zeros((cb, LANES), F32)
            for k in range(kernel):
                acc = acc + taps[k : k + 1, cols] * gp[h, pl.ds(base + EDGE - margin + k, cb), :]
            conv_o[0, pl.ds(base, cb), cols] = acc
            pos = rows_of(cb, base - EDGE)
            kept = jnp.where((pos >= 0) & (pos < jnp.minimum(hi, frames)), acc, 0.0)
            return s1 + fold_rows(kept), s2 + fold_rows(kept * kept)

        none = jnp.zeros((8, LANES), F32)
        s1, s2 = lax.fori_loop(0, span // cb, convolve, (none, none))
        add = jnp.concatenate(
            [jnp.sum(s1, axis=0, keepdims=True), jnp.sum(s2, axis=0, keepdims=True)], axis=0
        )
        st[:, cols] = jnp.where(r == 0, 0.0, st[:, cols]) + add

    @pl.when(r == pl.num_programs(0) - 1)
    def _():
        spread_sums(st_o, st[...])


def batch_norm(stats, count):
    sums = jnp.sum(stats[...], axis=0)
    centre = sums[0:1] / count
    spread = sums[1:2] / count - centre * centre
    return centre, lax.rsqrt(spread + EPSILON)


def norm_kernel(
    meta, count, stats, affine, grads, halo, wo, conv, swished_o, gn_o, st_o, st, ping, pong
):
    r = pl.program_id(0)
    hi = meta[0, r]
    lo = meta[1, r]
    frames = grads.shape[1]
    centre, inv = batch_norm(stats, count[0, 0])
    gain, shift = affine[0:1, :], affine[1:2, :]

    def part(row, swish_grad):
        size = swish_grad.shape[0]
        unit = (conv[0, pl.ds(row, size), :] - centre) * inv
        normalized = unit * gain + shift
        s = sigmoid(normalized)
        pos = rows_of(size, row - EDGE)
        keep = (pos >= lo) & (pos < hi)
        swished = jnp.where(keep, normalized * s, 0.0)
        gn = jnp.where(keep, swish_grad, 0.0) * (s + normalized * (s - s * s))
        gn_o[0, pl.ds(row, size), :] = gn
        return unit, swished, gn

    edge = dot(halo[0], wo[...])
    part(0, edge[:EDGE])
    part(frames + EDGE, edge[EDGE:])
    step = block_rows(frames, 256)
    small = block_rows(step, 32)
    s1 = jnp.zeros((8, conv.shape[2]), F32)
    s2 = s1
    held = (ping, pong)
    ping[...] = dot(grads[0, :step, :], wo[...])
    for i in range(frames // step):
        now = held[i % 2]
        if (i + 1) * step < frames:
            held[(i + 1) % 2][...] = dot(grads[0, (i + 1) * step : (i + 2) * step, :], wo[...])
        for j in range(step // small):
            base = i * step + j * small
            unit, swished, gn = part(base + EDGE, now[j * small : (j + 1) * small, :])
            swished_o[0, base : base + small, :] = swished.astype(BF16)
            s1 = s1 + fold_rows(gn)
            s2 = s2 + fold_rows(gn * unit)
    add = jnp.concatenate(
        [jnp.sum(s1, axis=0, keepdims=True), jnp.sum(s2, axis=0, keepdims=True)], axis=0
    )
    st[...] = jnp.where(r == 0, 0.0, st[...]) + add

    @pl.when(r == pl.num_programs(0) - 1)
    def _():
        spread_sums(st_o, st[...])


def back_kernel(
    record, meta, count, stats, sums, gain, gn, conv, vl, sg, taps, out, taps_o, gc, acc
):
    i = pl.program_id(0)
    hi = meta[0, record]
    lo = meta[1, record]
    frames, width = vl.shape[1:]
    halves = width // LANES
    span = frames + 2 * EDGE
    kernel = taps.shape[0]
    margin = (kernel - 1) // 2
    cb = block_rows(span, 144)
    step = block_rows(frames, 64)
    total_frames = count[0, 0]
    centre, inv = batch_norm(stats, total_frames)
    grad_sums = jnp.sum(sums[...], axis=0)
    scale = gain[...] * inv
    offset = scale * grad_sums[0:1] / total_frames
    slope = scale * inv * grad_sums[1:2] / total_frames
    first = i * frames

    @pl.when(i == 0)
    def _():
        acc[...] = jnp.zeros_like(acc)

    for h in range(halves):
        cols = slice(h * LANES, (h + 1) * LANES)
        for base in range(0, span, cb):
            pos = rows_of(cb, first + (base - EDGE))
            mean = offset[:, cols] + (conv[0, base : base + cb, cols] - centre[:, cols]) * slope[:, cols]
            gc[h, base : base + cb, :] = scale[:, cols] * gn[0, base : base + cb, cols] - jnp.where(
                (pos >= lo) & (pos < hi), mean, 0.0
            )
        sums_k = [acc[h, k] for k in range(kernel)]
        for base in range(0, frames, step):
            v = vl[0, base : base + step, cols]
            s = sg[0, base : base + step, cols]
            keep = rows_of(step, first + base) < hi
            vs = v * s
            gated = jnp.where(keep, vs, 0.0)
            total = jnp.zeros((step, LANES), F32)
            for k in range(kernel):
                window = gc[h, base + EDGE + margin - k : base + EDGE + margin - k + step, :]
                total = total + taps[k : k + 1, cols] * window
                sums_k[k] = sums_k[k] + fold_rows(window * gated)
            total = jnp.where(keep, total, 0.0)
            out[base : base + step, cols] = (total * s).astype(BF16)
            out[base : base + step, width + h * LANES : width + (h + 1) * LANES] = (
                total * (vs - vs * s)
            ).astype(BF16)
        for k in range(kernel):
            acc[h, k] = sums_k[k]

    @pl.when(i == pl.num_programs(0) - 1)
    def _():
        taps_o[...] = jnp.zeros_like(taps_o)
        for h in range(halves):
            for k in range(kernel):
                taps_o[k : k + 1, h * LANES : (h + 1) * LANES] = jnp.sum(
                    acc[h, k], axis=0, keepdims=True
                )


def partial_kernel(own, sibling, w_own, w_sibling, picked, mine, *others):
    for d in range(w_own.shape[0]):
        total = dot_nt(w_own[d], own[...]) + dot_nt(w_sibling[d], sibling[...])
        if d == 0:
            mine[...] = total + picked[0].astype(F32)
        else:
            others[d - 1][...] = total.astype(BF16)


def outer_kernel(records, parity, x, grads, swished, *refs):
    lefts, taps = refs[:records], refs[records : 2 * records]
    keep, send, acc = refs[2 * records :]
    width = swished.shape[2]
    shard = keep.shape[2]
    r = pl.program_id(0)

    def add(rows, value, first):
        acc[rows, :] = value if first else acc[rows, :] + value

    for i, left in enumerate(lefts):

        @pl.when(r == i)
        def _(i=i, left=left):
            add(slice(0, 2 * width), dot_tn(left[...], x[0]), i == 0)
            add(slice(2 * width, 3 * width), dot_tn(swished[0], grads[0]), i == 0)

    @pl.when(r == records - 1)
    def _():
        tap_sums = taps[0][...]
        for part in taps[1:]:
            tap_sums = tap_sums + part[...]

        def write(place, odd):
            for j in range(place.shape[0]):
                at = (2 * j + odd) * shard
                place[j, : 3 * width, :] = acc[:, at : at + shard].astype(BF16)
                for q in range(width // shard):
                    row = 3 * width + 16 * q
                    place[j, row : row + 16, :] = tap_sums[:, q * shard : (q + 1) * shard].astype(
                        BF16
                    )

        @pl.when(parity[0, 0] == 0)
        def _():
            write(keep, 0)
            write(send, 1)

        @pl.when(parity[0, 0] != 0)
        def _():
            write(keep, 1)
            write(send, 0)


def finish_kernel(kernel, got, value, gate, out, taps):
    width = value.shape[1]
    shard = value.shape[0]

    def total(row, size):
        sums = got[0, row : row + size, :].astype(F32)
        for j in range(1, got.shape[0]):
            sums = sums + got[j, row : row + size, :].astype(F32)
        return sums

    for i, place in enumerate((value, gate, out)):
        place[...] = total(i * width, width).T
    for q in range(width // shard):
        taps[:, q * shard : (q + 1) * shard] = total(3 * width + 16 * q, 16)[:kernel]


def place_kernel(*refs):
    parts, out, sem = refs[:-2], refs[-2], refs[-1]
    frames = parts[0].shape[2]
    copies = [
        pltpu.make_async_copy(
            part.at[s], out.at[r, :, pl.ds(s * frames, frames)], sem.at[r, s]
        )
        for r, part in enumerate(parts)
        for s in range(part.shape[0])
    ]
    for copy in copies:
        copy.start()
    for copy in copies:
        copy.wait()


def exchange(copies, axis):
    return lax.all_to_all(copies, axis, 0, 0, tiled=True)


def per_device(
    normed,
    grad_out,
    value_weight,
    gate_weight,
    depth_taps,
    norm_gain,
    norm_shift,
    out_weight,
    lengths,
):
    recs, frames, model = normed.shape
    kernel = depth_taps.shape[0]
    width = value_weight.shape[1]
    seqs = lax.axis_size("seq")
    tps = lax.axis_size("tp")
    chips = tps // 2
    piece = model // (seqs * tps)
    rows = seqs * piece
    shard = model // seqs
    span = frames + 2 * EDGE
    seq_at = lax.axis_index("seq")
    tp_at = lax.axis_index("tp")
    chip_at, core_at = tp_at // 2, tp_at % 2
    count = jnp.sum(lengths).astype(F32)
    first = (seq_at * frames).astype(jnp.int32)
    meta = jnp.stack([lengths - first, jnp.full((recs,), 0, jnp.int32) - first])
    halves = width // LANES
    counts = count.reshape(1, 1)
    parity = (seq_at % 2).astype(jnp.int32).reshape(1, 1)
    sds = jax.ShapeDtypeStruct

    low_edge = jnp.concatenate([normed[:, -EDGE:], grad_out[:, -EDGE:]], axis=2)
    high_edge = jnp.concatenate([normed[:, :EDGE], grad_out[:, :EDGE]], axis=2)
    up = [(i, i + 1) for i in range(seqs - 1)]
    down = [(j, i) for i, j in up]
    halo = jnp.concatenate(
        [lax.ppermute(low_edge, "seq", up), lax.ppermute(high_edge, "seq", down)], axis=1
    )
    halo_x, halo_g = halo[:, :, :model], halo[:, :, model:]

    both = jnp.concatenate([value_weight, gate_weight], axis=1).reshape(seqs, tps, piece, 2 * width)

    def chosen(core):
        picks = [
            lax.dynamic_index_in_dim(both, ((chip_at + d) % chips) * 2 + core, 1, keepdims=False)
            for d in range(chips)
        ]
        return jnp.stack(picks).reshape(chips, rows, 2 * width)

    swap = [(i, i ^ 1) for i in range(tps)]
    w_own = chosen(core_at)
    w_sibling = lax.ppermute(chosen(1 - core_at), "tp", swap)

    channel = (
        jnp.arange(seqs, dtype=jnp.int32)[:, None] * (tps * piece)
        + tp_at * piece
        + jnp.arange(piece, dtype=jnp.int32)[None, :]
    ).reshape(rows, 1)
    select = (channel == jnp.arange(model, dtype=jnp.int32)[None, :]).astype(BF16)
    array_bytes = recs * frames * width * 4
    input_bytes = recs * frames * model * 2
    matmul = 2 * recs * frames * model * width

    picked = call(
        pick_kernel,
        "pick",
        (recs,),
        [whole((rows, model)), per_record((frames, model))],
        per_record((rows, frames)),
        sds((recs, rows, frames), BF16),
        [],
        matmul,
        input_bytes,
    )(select, grad_out)

    vl, sg, conv, stats = call(
        gate_kernel,
        "gate_conv",
        (recs,),
        [
            smem(),
            per_record((frames, model)),
            per_record((2 * EDGE, model)),
            whole((model, width)),
            whole((model, width)),
            whole((kernel, width)),
        ],
        [
            per_record((frames, width)),
            per_record((frames, width)),
            per_record((span, width)),
            whole((seqs, 2, width)),
        ],
        [
            sds((recs, frames, width), F32),
            sds((recs, frames, width), F32),
            sds((recs, span, width), F32),
            sds((seqs, 2, width), F32),
        ],
        [pltpu.VMEM((halves, frames + 4 * EDGE, LANES), F32), pltpu.VMEM((2, width), F32)],
        2 * matmul,
        input_bytes + 3 * array_bytes,
    )(meta, normed, after(halo_x, picked), value_weight, gate_weight, depth_taps)
    stats = exchange(stats, "seq")

    chunk = block_rows(frames, 256)
    swished, gn, sums = call(
        norm_kernel,
        "swish_norm",
        (recs,),
        [
            smem(),
            smem(),
            whole((seqs, 2, width)),
            whole((2, width)),
            per_record((frames, model)),
            per_record((2 * EDGE, model)),
            whole((model, width)),
            per_record((span, width)),
        ],
        [per_record((frames, width)), per_record((span, width)), whole((seqs, 2, width))],
        [
            sds((recs, frames, width), BF16),
            sds((recs, span, width), F32),
            sds((seqs, 2, width), F32),
        ],
        [
            pltpu.VMEM((2, width), F32),
            pltpu.VMEM((chunk, width), F32),
            pltpu.VMEM((chunk, width), F32),
        ],
        matmul,
        input_bytes + 3 * array_bytes,
    )(meta, counts, stats, jnp.stack([norm_gain, norm_shift]), grad_out, halo_g, out_weight, conv)
    sums = exchange(sums, "seq")
    grad_shift, grad_gain = jnp.sum(sums, axis=0)

    def back(r, marker):
        def window(i):
            return (r, pl.multiple_of(i * chunk, chunk), 0)

        return call(
            functools.partial(back_kernel, r),
            "back_conv",
            (frames // chunk,),
            [
                smem(),
                smem(),
                whole((seqs, 2, width)),
                whole((seqs, 2, width)),
                whole((1, width)),
                pl.BlockSpec((pl.Element(1), pl.Element(chunk + 2 * EDGE), pl.Element(width)), window),
                pl.BlockSpec((pl.Element(1), pl.Element(chunk + 2 * EDGE), pl.Element(width)), window),
                pl.BlockSpec((1, chunk, width), lambda i: (r, i, 0)),
                pl.BlockSpec((1, chunk, width), lambda i: (r, i, 0)),
                whole((kernel, width)),
            ],
            [pl.BlockSpec((chunk, 2 * width), lambda i: (i, 0)), whole((16, width))],
            [sds((frames, 2 * width), BF16), sds((16, width), F32)],
            [
                pltpu.VMEM((halves, chunk + 2 * EDGE, LANES), F32),
                pltpu.VMEM((halves, kernel, 8, LANES), F32),
            ],
            60 * frames * width,
            4 * array_bytes // recs,
        )(meta, counts, stats, sums, norm_gain[None], gn, conv, vl, sg, after(depth_taps, *marker))

    def partials(r, mine):
        sibling = lax.ppermute(mine, "tp", swap)
        return call(
            partial_kernel,
            "partial_in",
            (frames // chunk,),
            [
                pl.BlockSpec((chunk, 2 * width), lambda i: (i, 0)),
                pl.BlockSpec((chunk, 2 * width), lambda i: (i, 0)),
                whole((chips, rows, 2 * width)),
                whole((chips, rows, 2 * width)),
                pl.BlockSpec((1, rows, chunk), lambda i: (r, 0, i)),
            ],
            [pl.BlockSpec((rows, chunk), lambda i: (0, i))] * chips,
            [sds((rows, frames), F32)] + [sds((rows, frames), BF16)] * (chips - 1),
            [],
            2 * matmul // recs,
            8 * frames * width + 6 * rows * frames,
        )(mine, sibling, w_own, w_sibling, picked)

    grads, tap_parts, parts = [], [], []
    for r in range(recs):
        mine, tap_part = back(r, parts[r - 2] if r > 1 else ())
        grads.append(mine)
        tap_parts.append(tap_part)
        if r > 0:
            parts.append(partials(r - 1, grads[r - 1]))
    parts.append(partials(recs - 1, grads[recs - 1]))

    moved = []
    for r in range(recs):
        total = parts[r][0]
        for d in range(1, chips):
            send = [(i, ((i // 2 + d) % chips) * 2 + i % 2) for i in range(tps)]
            total = total + lax.ppermute(parts[r][d], "tp", send).astype(F32)
        own = total.astype(BF16).reshape(seqs, piece, frames)
        moved.append(exchange(own, "seq"))

    slots = 3 * width + 16 * (width // shard)
    half = sds((seqs // 2, slots, shard), BF16)
    keep, send = call(
        functools.partial(outer_kernel, recs),
        "outer",
        (recs,),
        [smem(), per_record((frames, model)), per_record((frames, model)), per_record((frames, width))]
        + [whole((frames, 2 * width))] * recs
        + [whole((16, width))] * recs,
        [whole(half.shape)] * 2,
        [half] * 2,
        [pltpu.VMEM((3 * width, model), F32)],
        3 * matmul,
        2 * input_bytes + 6 * recs * frames * width,
    )(parity, after(normed, *parts[-1]), grad_out, swished, *grads, *tap_parts)
    pairs = [(i, i ^ 1) for i in range(seqs)]
    paired = (keep.astype(F32) + lax.ppermute(send, "seq", pairs).astype(F32)).astype(BF16)
    same = [[i for i in range(seqs) if i % 2 == odd] for odd in range(2)]
    got = lax.all_to_all(paired, "seq", 0, 0, axis_index_groups=same, tiled=True)
    w_value, w_gate, w_out, grad_taps = call(
        functools.partial(finish_kernel, kernel),
        "finish",
        (1,),
        [whole(half.shape)],
        [whole((shard, width))] * 3 + [whole((kernel, width))],
        [sds((shard, width), F32)] * 3 + [sds((kernel, width), F32)],
        [],
        0,
        8 * seqs * slots * shard,
    )(got)
    grad_in = call(
        place_kernel,
        "place",
        (1,),
        [anywhere()] * recs,
        anywhere(),
        sds((recs, piece, seqs * frames), BF16),
        [pltpu.SemaphoreType.DMA((recs, seqs))],
        0,
        4 * recs * piece * seqs * frames,
    )(*moved)
    return (grad_in, w_value, w_gate, w_out, grad_taps, grad_gain, grad_shift)


def solution(mesh):
    placed = (
        P(None, "seq", None),
        P(None, "seq", None),
        P(None, "tp"),
        P(None, "tp"),
        P(None, "tp"),
        P("tp"),
        P("tp"),
        P(None, "tp"),
        P(),
    )
    return jax.shard_map(
        per_device,
        mesh=mesh,
        in_specs=placed,
        out_specs=(
            P(None, ("seq", "tp"), None),
            P("seq", "tp"),
            P("seq", "tp"),
            P("seq", "tp"),
            P(None, "tp"),
            P("tp"),
            P("tp"),
        ),
        check_vma=False,
    )
```

```python
import functools

import jax
import jax.numpy as jnp
from jax import lax
from jax.experimental import pallas as pl
from jax.experimental.pallas import tpu as pltpu
from jax.sharding import PartitionSpec as P

EPSILON = 1e-05
EDGE = 8
LANES = 128
F32 = jnp.float32
BF16 = jnp.bfloat16


def sigmoid(x):
    return 0.5 * jnp.tanh(0.5 * x) + 0.5


def dot(a, b):
    return jnp.dot(a, b, preferred_element_type=F32)


def dot_nt(a, b):
    return lax.dot_general(a, b, (((1,), (1,)), ((), ())), preferred_element_type=F32)


def dot_tn(a, b):
    return lax.dot_general(a, b, (((0,), (0,)), ((), ())), preferred_element_type=F32)


def rows_of(count, first):
    return first + lax.broadcasted_iota(jnp.int32, (count, 1), 0)


def fold_rows(x):
    return jnp.sum(x.reshape(x.shape[0] // 8, 8, x.shape[1]), axis=0)


def block_rows(total, most):
    return max(b for b in range(8, most + 1, 8) if total % b == 0)


def whole(shape):
    return pl.BlockSpec(shape, lambda *i: (0,) * len(shape))


def per_record(shape):
    return pl.BlockSpec((1,) + shape, lambda r: (r,) + (0,) * len(shape))


def smem():
    return pl.BlockSpec(memory_space=pltpu.SMEM)


def anywhere():
    return pl.BlockSpec(memory_space=pl.ANY)


def after(x, *earlier):
    return lax.optimization_barrier((x,) + earlier)[0]


def spread_sums(out, sums):
    for s in range(out.shape[0]):
        out[s] = sums


def call(
    kernel, name, grid, in_specs, out_specs, out_shape, scratch, flops, moved, aliases=None, vmem=60
):
    return pl.pallas_call(
        kernel,
        name=name,
        grid=grid,
        in_specs=in_specs,
        out_specs=out_specs,
        out_shape=out_shape,
        scratch_shapes=scratch,
        input_output_aliases=aliases or {},
        cost_estimate=pl.CostEstimate(flops=int(flops), bytes_accessed=int(moved), transcendentals=0),
        compiler_params=pltpu.CompilerParams(vmem_limit_bytes=vmem * 1024 * 1024),
    )


def gate_kernel(meta, x, halo, wv, wg, taps, vl_o, sg_o, conv_o, st_o, gp, st):
    r = pl.program_id(0)
    hi = meta[0, r]
    lo = meta[1, r]
    frames = x.shape[1]
    width = wv.shape[1]
    halves = width // LANES

    def put(row, value):
        for h in range(halves):
            gp[h, pl.ds(row, value.shape[0]), :] = value[:, h * LANES : (h + 1) * LANES]

    edge_v = dot(halo[0], wv[...])
    edge_g = dot(halo[0], wg[...])
    row = rows_of(2 * EDGE, 0)
    pos = jnp.where(row < EDGE, row - EDGE, row - EDGE + frames)
    edge = jnp.where((pos >= lo) & (pos < hi), edge_v * sigmoid(edge_g), 0.0)
    zero = jnp.zeros((EDGE, width), F32)
    put(0, zero)
    put(EDGE, edge[:EDGE])
    put(2 * EDGE + frames, edge[EDGE:])
    put(3 * EDGE + frames, zero)
    step = block_rows(frames, 512)
    small = block_rows(step, 64)
    for base in range(0, frames, step):
        xb = x[0, base : base + step, :]
        vl_o[0, base : base + step, :] = dot(xb, wv[...])
        sg_o[0, base : base + step, :] = dot(xb, wg[...])

    def gating(i, carry):
        base = pl.multiple_of(i * small, small)
        v = vl_o[0, pl.ds(base, small), :]
        s = sigmoid(sg_o[0, pl.ds(base, small), :])
        sg_o[0, pl.ds(base, small), :] = s
        put(2 * EDGE + base, jnp.where(rows_of(small, base) < hi, v * s, 0.0))
        return carry

    lax.fori_loop(0, frames // small, gating, 0)
    span = frames + 2 * EDGE
    cb = block_rows(span, 104)
    kernel = taps.shape[0]
    margin = (kernel - 1) // 2
    for h in range(halves):
        cols = slice(h * LANES, (h + 1) * LANES)

        def convolve(i, carry):
            s1, s2 = carry
            base = pl.multiple_of(i * cb, 8)
            acc = jnp.zeros((cb, LANES), F32)
            for k in range(kernel):
                acc = acc + taps[k : k + 1, cols] * gp[h, pl.ds(base + EDGE - margin + k, cb), :]
            conv_o[0, pl.ds(base, cb), cols] = acc
            pos = rows_of(cb, base - EDGE)
            kept = jnp.where((pos >= 0) & (pos < jnp.minimum(hi, frames)), acc, 0.0)
            return s1 + fold_rows(kept), s2 + fold_rows(kept * kept)

        none = jnp.zeros((8, LANES), F32)
        s1, s2 = lax.fori_loop(0, span // cb, convolve, (none, none))
        add = jnp.concatenate(
            [jnp.sum(s1, axis=0, keepdims=True), jnp.sum(s2, axis=0, keepdims=True)], axis=0
        )
        st[:, cols] = jnp.where(r == 0, 0.0, st[:, cols]) + add

    @pl.when(r == pl.num_programs(0) - 1)
    def _():
        spread_sums(st_o, st[...])


def batch_norm(stats, count):
    sums = jnp.sum(stats[...], axis=0)
    centre = sums[0:1] / count
    spread = sums[1:2] / count - centre * centre
    return centre, lax.rsqrt(spread + EPSILON)


def norm_kernel(
    meta, count, stats, affine, select, grads, halo, wo, conv,
    swished_o, gn_o, picked_o, st_o, st, ping, pong
):
    r = pl.program_id(0)
    hi = meta[0, r]
    lo = meta[1, r]
    frames = grads.shape[1]
    centre, inv = batch_norm(stats, count[0, 0])
    gain, shift = affine[0:1, :], affine[1:2, :]

    def part(row, swish_grad):
        size = swish_grad.shape[0]
        unit = (conv[0, pl.ds(row, size), :] - centre) * inv
        normalized = unit * gain + shift
        s = sigmoid(normalized)
        pos = rows_of(size, row - EDGE)
        keep = (pos >= lo) & (pos < hi)
        swished = jnp.where(keep, normalized * s, 0.0)
        gn = jnp.where(keep, swish_grad, 0.0) * (s + normalized * (s - s * s))
        gn_o[0, pl.ds(row, size), :] = gn
        return unit, swished, gn

    edge = dot(halo[0], wo[...])
    part(0, edge[:EDGE])
    part(frames + EDGE, edge[EDGE:])
    step = block_rows(frames, 512)
    small = block_rows(step, 32)
    s1 = jnp.zeros((8, conv.shape[2]), F32)
    s2 = s1
    held = (ping, pong)
    ping[...] = dot(grads[0, :step, :], wo[...])
    for i in range(frames // step):
        now = held[i % 2]
        if (i + 1) * step < frames:
            held[(i + 1) % 2][...] = dot(grads[0, (i + 1) * step : (i + 2) * step, :], wo[...])
        picked_o[0, :, i * step : (i + 1) * step] = dot_nt(
            select[...], grads[0, i * step : (i + 1) * step, :]
        ).astype(BF16)
        for j in range(step // small):
            base = i * step + j * small
            unit, swished, gn = part(base + EDGE, now[j * small : (j + 1) * small, :])
            swished_o[0, base : base + small, :] = swished.astype(BF16)
            s1 = s1 + fold_rows(gn)
            s2 = s2 + fold_rows(gn * unit)
    add = jnp.concatenate(
        [jnp.sum(s1, axis=0, keepdims=True), jnp.sum(s2, axis=0, keepdims=True)], axis=0
    )
    st[...] = jnp.where(r == 0, 0.0, st[...]) + add

    @pl.when(r == pl.num_programs(0) - 1)
    def _():
        spread_sums(st_o, st[...])


def back_kernel(
    record, meta, count, stats, sums, gain, gn, conv, vl, sg, taps, out, taps_o, gc, acc
):
    i = pl.program_id(0)
    hi = meta[0, record]
    lo = meta[1, record]
    frames, width = vl.shape[1:]
    halves = width // LANES
    span = frames + 2 * EDGE
    kernel = taps.shape[0]
    margin = (kernel - 1) // 2
    cb = block_rows(span, 144)
    step = block_rows(frames, 64)
    total_frames = count[0, 0]
    centre, inv = batch_norm(stats, total_frames)
    grad_sums = jnp.sum(sums[...], axis=0)
    scale = gain[...] * inv
    offset = scale * grad_sums[0:1] / total_frames
    slope = scale * inv * grad_sums[1:2] / total_frames
    first = i * frames

    @pl.when(i == 0)
    def _():
        acc[...] = jnp.zeros_like(acc)

    for h in range(halves):
        cols = slice(h * LANES, (h + 1) * LANES)
        for base in range(0, span, cb):
            pos = rows_of(cb, first + (base - EDGE))
            mean = offset[:, cols] + (conv[0, base : base + cb, cols] - centre[:, cols]) * slope[:, cols]
            gc[h, base : base + cb, :] = scale[:, cols] * gn[0, base : base + cb, cols] - jnp.where(
                (pos >= lo) & (pos < hi), mean, 0.0
            )
        sums_k = [acc[h, k] for k in range(kernel)]
        for base in range(0, frames, step):
            v = vl[0, base : base + step, cols]
            s = sg[0, base : base + step, cols]
            keep = rows_of(step, first + base) < hi
            vs = v * s
            gated = jnp.where(keep, vs, 0.0)
            total = jnp.zeros((step, LANES), F32)
            for k in range(kernel):
                window = gc[h, base + EDGE + margin - k : base + EDGE + margin - k + step, :]
                total = total + taps[k : k + 1, cols] * window
                sums_k[k] = sums_k[k] + fold_rows(window * gated)
            total = jnp.where(keep, total, 0.0)
            out[base : base + step, cols] = (total * s).astype(BF16)
            out[base : base + step, width + h * LANES : width + (h + 1) * LANES] = (
                total * (vs - vs * s)
            ).astype(BF16)
        for k in range(kernel):
            acc[h, k] = sums_k[k]

    @pl.when(i == pl.num_programs(0) - 1)
    def _():
        taps_o[...] = jnp.zeros_like(taps_o)
        for h in range(halves):
            for k in range(kernel):
                taps_o[k : k + 1, h * LANES : (h + 1) * LANES] = jnp.sum(
                    acc[h, k], axis=0, keepdims=True
                )


def partial_kernel(own, sibling, w_own, w_sibling, picked, mine, *others):
    total = dot_nt(w_own[...], own[...]) + dot_nt(w_sibling[...], sibling[...])
    rows = picked.shape[1]
    mine[...] = total[:rows] + picked[0].astype(F32)
    for d, other in enumerate(others):
        other[...] = total[(d + 1) * rows : (d + 2) * rows].astype(BF16)


def first_outer_kernel(grads, swished, out):
    r = pl.program_id(0)
    add = dot_tn(swished[0], grads[0])

    @pl.when(r == 0)
    def _():
        out[...] = add

    @pl.when(r > 0)
    def _():
        out[...] += add


def outer_kernel(records, parity, x, w_out, *refs):
    lefts, taps = refs[:records], refs[records : 2 * records]
    keep, send, acc = refs[2 * records :]
    width = w_out.shape[0]
    shard = keep.shape[2]
    r = pl.program_id(0)
    for i, left in enumerate(lefts):

        @pl.when(r == i)
        def _(i=i, left=left):
            add = dot_tn(left[...], x[0])
            if i == 0:
                acc[...] = add
            else:
                acc[...] += add

    @pl.when(r == records - 1)
    def _():
        tap_sums = taps[0][...]
        for part in taps[1:]:
            tap_sums = tap_sums + part[...]

        def write(place, odd):
            for j in range(place.shape[0]):
                at = (2 * j + odd) * shard
                place[j, : 2 * width, :] = acc[:, at : at + shard].astype(BF16)
                place[j, 2 * width : 3 * width, :] = w_out[:, at : at + shard].astype(BF16)
                for q in range(width // shard):
                    row = 3 * width + 16 * q
                    place[j, row : row + 16, :] = tap_sums[:, q * shard : (q + 1) * shard].astype(
                        BF16
                    )

        @pl.when(parity[0, 0] == 0)
        def _():
            write(keep, 0)
            write(send, 1)

        @pl.when(parity[0, 0] != 0)
        def _():
            write(keep, 1)
            write(send, 0)


def finish_kernel(kernel, got, value, gate, out, taps):
    width = value.shape[1]
    shard = value.shape[0]

    def total(row, size):
        sums = got[0, row : row + size, :].astype(F32)
        for j in range(1, got.shape[0]):
            sums = sums + got[j, row : row + size, :].astype(F32)
        return sums

    for i, place in enumerate((value, gate, out)):
        place[...] = total(i * width, width).T
    for q in range(width // shard):
        taps[:, q * shard : (q + 1) * shard] = total(3 * width + 16 * q, 16)[:kernel]


def place_kernel(moved, *refs):
    out = refs[-1]
    frames = moved.shape[2]
    for s in range(moved.shape[0]):
        out[0, :, s * frames : (s + 1) * frames] = moved[s]


def exchange(copies, axis):
    return lax.all_to_all(copies, axis, 0, 0, tiled=True)


def per_device(
    normed,
    grad_out,
    value_weight,
    gate_weight,
    depth_taps,
    norm_gain,
    norm_shift,
    out_weight,
    lengths,
):
    recs, frames, model = normed.shape
    kernel = depth_taps.shape[0]
    width = value_weight.shape[1]
    seqs = lax.axis_size("seq")
    tps = lax.axis_size("tp")
    chips = tps // 2
    piece = model // (seqs * tps)
    rows = seqs * piece
    shard = model // seqs
    span = frames + 2 * EDGE
    seq_at = lax.axis_index("seq")
    tp_at = lax.axis_index("tp")
    chip_at, core_at = tp_at // 2, tp_at % 2
    count = jnp.sum(lengths).astype(F32)
    first = (seq_at * frames).astype(jnp.int32)
    meta = jnp.stack([lengths - first, jnp.full((recs,), 0, jnp.int32) - first])
    halves = width // LANES
    counts = count.reshape(1, 1)
    parity = (seq_at % 2).astype(jnp.int32).reshape(1, 1)
    sds = jax.ShapeDtypeStruct

    low_edge = jnp.concatenate([normed[:, -EDGE:], grad_out[:, -EDGE:]], axis=2)
    high_edge = jnp.concatenate([normed[:, :EDGE], grad_out[:, :EDGE]], axis=2)
    up = [(i, i + 1) for i in range(seqs - 1)]
    down = [(j, i) for i, j in up]
    halo = jnp.concatenate(
        [lax.ppermute(low_edge, "seq", up), lax.ppermute(high_edge, "seq", down)], axis=1
    )
    halo_x, halo_g = halo[:, :, :model], halo[:, :, model:]

    both = jnp.concatenate([value_weight, gate_weight], axis=1).reshape(seqs, tps, piece, 2 * width)

    def chosen(core):
        picks = [
            lax.dynamic_index_in_dim(both, ((chip_at + d) % chips) * 2 + core, 1, keepdims=False)
            for d in range(chips)
        ]
        return jnp.stack(picks).reshape(chips * rows, 2 * width)

    swap = [(i, i ^ 1) for i in range(tps)]
    w_own = chosen(core_at)
    w_sibling = lax.ppermute(chosen(1 - core_at), "tp", swap)

    channel = (
        jnp.arange(seqs, dtype=jnp.int32)[:, None] * (tps * piece)
        + tp_at * piece
        + jnp.arange(piece, dtype=jnp.int32)[None, :]
    ).reshape(rows, 1)
    select = (channel == jnp.arange(model, dtype=jnp.int32)[None, :]).astype(BF16)
    array_bytes = recs * frames * width * 4
    input_bytes = recs * frames * model * 2
    matmul = 2 * recs * frames * model * width

    vl, sg, conv, stats = call(
        gate_kernel,
        "gate_conv",
        (recs,),
        [
            smem(),
            per_record((frames, model)),
            per_record((2 * EDGE, model)),
            whole((model, width)),
            whole((model, width)),
            whole((kernel, width)),
        ],
        [
            per_record((frames, width)),
            per_record((frames, width)),
            per_record((span, width)),
            whole((1, 2, width)),
        ],
        [
            sds((recs, frames, width), F32),
            sds((recs, frames, width), F32),
            sds((recs, span, width), F32),
            sds((1, 2, width), F32),
        ],
        [pltpu.VMEM((halves, frames + 4 * EDGE, LANES), F32), pltpu.VMEM((2, width), F32)],
        2 * matmul,
        input_bytes + 3 * array_bytes,
    )(meta, normed, halo_x, value_weight, gate_weight, depth_taps)
    stats = lax.all_gather(stats, "seq", axis=0, tiled=True)

    chunk = block_rows(frames, 256)
    half_rows = block_rows(frames, 512)
    swished, gn, picked, sums = call(
        norm_kernel,
        "swish_norm",
        (recs,),
        [
            smem(),
            smem(),
            whole((seqs, 2, width)),
            whole((2, width)),
            whole((rows, model)),
            per_record((frames, model)),
            per_record((2 * EDGE, model)),
            whole((model, width)),
            per_record((span, width)),
        ],
        [
            per_record((frames, width)),
            per_record((span, width)),
            per_record((rows, frames)),
            whole((seqs, 2, width)),
        ],
        [
            sds((recs, frames, width), BF16),
            sds((recs, span, width), F32),
            sds((recs, rows, frames), BF16),
            sds((seqs, 2, width), F32),
        ],
        [
            pltpu.VMEM((2, width), F32),
            pltpu.VMEM((block_rows(frames, 512), width), F32),
            pltpu.VMEM((block_rows(frames, 512), width), F32),
        ],
        2 * matmul,
        input_bytes + 3 * array_bytes,
    )(
        meta,
        counts,
        stats,
        jnp.stack([norm_gain, norm_shift]),
        select,
        grad_out,
        halo_g,
        out_weight,
        conv,
    )
    w_out = call(
        first_outer_kernel,
        "outer_w_out",
        (recs,),
        [per_record((frames, model)), per_record((frames, width))],
        whole((width, model)),
        sds((width, model), F32),
        [],
        matmul,
        input_bytes,
    )(grad_out, swished)
    sums = exchange(sums, "seq")
    grad_shift, grad_gain = jnp.sum(sums, axis=0)

    def back(r, marker):
        def window(i):
            return (r, pl.multiple_of(i * chunk, chunk), 0)

        return call(
            functools.partial(back_kernel, r),
            "back_conv",
            (frames // chunk,),
            [
                smem(),
                smem(),
                whole((seqs, 2, width)),
                whole((seqs, 2, width)),
                whole((1, width)),
                pl.BlockSpec((pl.Element(1), pl.Element(chunk + 2 * EDGE), pl.Element(width)), window),
                pl.BlockSpec((pl.Element(1), pl.Element(chunk + 2 * EDGE), pl.Element(width)), window),
                pl.BlockSpec((1, chunk, width), lambda i: (r, i, 0)),
                pl.BlockSpec((1, chunk, width), lambda i: (r, i, 0)),
                whole((kernel, width)),
            ],
            [pl.BlockSpec((chunk, 2 * width), lambda i: (i, 0)), whole((16, width))],
            [sds((frames, 2 * width), BF16), sds((16, width), F32)],
            [
                pltpu.VMEM((halves, chunk + 2 * EDGE, LANES), F32),
                pltpu.VMEM((halves, kernel, 8, LANES), F32),
            ],
            60 * frames * width,
            4 * array_bytes // recs,
        )(meta, counts, stats, sums, norm_gain[None], gn, conv, vl, sg, after(depth_taps, *marker))

    def partials(r, mine):
        sibling = lax.ppermute(mine, "tp", swap)
        return call(
            partial_kernel,
            "partial_in",
            (frames // half_rows,),
            [
                pl.BlockSpec((half_rows, 2 * width), lambda i: (i, 0)),
                pl.BlockSpec((half_rows, 2 * width), lambda i: (i, 0)),
                whole((chips * rows, 2 * width)),
                whole((chips * rows, 2 * width)),
                pl.BlockSpec((1, rows, half_rows), lambda i: (r, 0, i)),
            ],
            [pl.BlockSpec((rows, half_rows), lambda i: (0, i))] * chips,
            [sds((rows, frames), F32)] + [sds((rows, frames), BF16)] * (chips - 1),
            [],
            2 * matmul // recs,
            8 * frames * width + 6 * rows * frames,
            vmem=20,
        )(mine, sibling, w_own, w_sibling, picked)

    grads, tap_parts, parts, moved = [], [], [], []

    def deliver(r, *earlier):
        total = after(parts[r][0], *earlier)
        for d in range(1, chips):
            send = [(i, ((i // 2 + d) % chips) * 2 + i % 2) for i in range(tps)]
            total = total + lax.ppermute(parts[r][d], "tp", send).astype(F32)
        own = total.astype(BF16).reshape(seqs, piece, frames)
        moved.append(exchange(own, "seq"))
        return own

    for r in range(recs):
        mine, tap_part = back(r, parts[r - 2] if r > 1 else ())
        grads.append(mine)
        tap_parts.append(tap_part)
        if r > 0:
            parts.append(partials(r - 1, grads[r - 1]))
    owns = [deliver(0, *parts[recs - 2])]
    parts.append(partials(recs - 1, after(grads[recs - 1], owns[0])))
    owns.append(deliver(1, *parts[recs - 1]))

    slots = 3 * width + 16 * (width // shard)
    half = sds((seqs // 2, slots, shard), BF16)
    keep, send = call(
        functools.partial(outer_kernel, recs),
        "outer_w_in",
        (recs,),
        [smem(), per_record((frames, model)), whole((width, model))]
        + [whole((frames, 2 * width))] * recs
        + [whole((16, width))] * recs,
        [whole(half.shape)] * 2,
        [half] * 2,
        [pltpu.VMEM((2 * width, model), F32)],
        2 * matmul,
        input_bytes + 4 * recs * frames * width,
    )(parity, after(normed, owns[1]), w_out, *grads, *tap_parts)
    pairs = [(i, i ^ 1) for i in range(seqs)]
    others = lax.ppermute(send, "seq", pairs)
    for r in range(2, recs):
        owns.append(deliver(r, keep, owns[-1]))
    paired = (after(keep, owns[-2]).astype(F32) + others.astype(F32)).astype(BF16)
    same = [[i for i in range(seqs) if i % 2 == odd] for odd in range(2)]
    got = lax.all_to_all(
        after(paired, owns[-1]), "seq", 0, 0, axis_index_groups=same, tiled=True
    )
    w_value, w_gate, w_out, grad_taps = call(
        functools.partial(finish_kernel, kernel),
        "finish",
        (1,),
        [whole(half.shape)],
        [whole((shard, width))] * 3 + [whole((kernel, width))],
        [sds((shard, width), F32)] * 3 + [sds((kernel, width), F32)],
        [],
        0,
        8 * seqs * slots * shard,
        vmem=20,
    )(got)
    grad_in = ()
    for r in range(recs):
        grad_in = (
            call(
                place_kernel,
                "place",
                (1,),
                [whole((seqs, piece, frames))] + [anywhere()] * len(grad_in),
                pl.BlockSpec((1, piece, seqs * frames), lambda i, r=r: (r, 0, 0)),
                sds((recs, piece, seqs * frames), BF16),
                [],
                0,
                4 * piece * seqs * frames,
                {1: 0} if grad_in else None,
                vmem=20,
            )(moved[r], *grad_in),
        )
    (grad_in,) = grad_in
    return (grad_in, w_value, w_gate, w_out, grad_taps, grad_gain, grad_shift)


def solution(mesh):
    placed = (
        P(None, "seq", None),
        P(None, "seq", None),
        P(None, "tp"),
        P(None, "tp"),
        P(None, "tp"),
        P("tp"),
        P("tp"),
        P(None, "tp"),
        P(),
    )
    return jax.shard_map(
        per_device,
        mesh=mesh,
        in_specs=placed,
        out_specs=(
            P(None, ("seq", "tp"), None),
            P("seq", "tp"),
            P("seq", "tp"),
            P("seq", "tp"),
            P(None, "tp"),
            P("tp"),
            P("tp"),
        ),
        check_vma=False,
    )
```

```python
import functools

import jax
import jax.numpy as jnp
from jax import lax
from jax.experimental import pallas as pl
from jax.experimental.pallas import tpu as pltpu
from jax.sharding import PartitionSpec as P

EPSILON = 1e-05
EDGE = 8
LANES = 128
F32 = jnp.float32
BF16 = jnp.bfloat16


def sigmoid(x):
    return 0.5 * jnp.tanh(0.5 * x) + 0.5


def dot(a, b):
    return jnp.dot(a, b, preferred_element_type=F32)


def dot_nt(a, b):
    return lax.dot_general(a, b, (((1,), (1,)), ((), ())), preferred_element_type=F32)


def dot_tn(a, b):
    return lax.dot_general(a, b, (((0,), (0,)), ((), ())), preferred_element_type=F32)


def rows_of(count, first):
    return first + lax.broadcasted_iota(jnp.int32, (count, 1), 0)


def fold_rows(x):
    return jnp.sum(x.reshape(x.shape[0] // 8, 8, x.shape[1]), axis=0)


def block_rows(total, most):
    return max(b for b in range(8, most + 1, 8) if total % b == 0)


def whole(shape):
    return pl.BlockSpec(shape, lambda *i: (0,) * len(shape))


def per_record(shape):
    return pl.BlockSpec((1,) + shape, lambda r: (r,) + (0,) * len(shape))


def smem():
    return pl.BlockSpec(memory_space=pltpu.SMEM)


def anywhere():
    return pl.BlockSpec(memory_space=pl.ANY)


def after(x, *earlier):
    return lax.optimization_barrier((x,) + earlier)[0]


def spread_sums(out, sums):
    for s in range(out.shape[0]):
        out[s] = sums


def call(
    kernel, name, grid, in_specs, out_specs, out_shape, scratch, flops, moved, aliases=None, vmem=60
):
    return pl.pallas_call(
        kernel,
        name=name,
        grid=grid,
        in_specs=in_specs,
        out_specs=out_specs,
        out_shape=out_shape,
        scratch_shapes=scratch,
        input_output_aliases=aliases or {},
        cost_estimate=pl.CostEstimate(flops=int(flops), bytes_accessed=int(moved), transcendentals=0),
        compiler_params=pltpu.CompilerParams(vmem_limit_bytes=vmem * 1024 * 1024),
    )


def gate_kernel(meta, x, halo, wv, wg, taps, vl_o, sg_o, conv_o, st_o, gp, st):
    r = pl.program_id(0)
    hi = meta[0, r]
    lo = meta[1, r]
    frames = x.shape[1]
    width = wv.shape[1]
    halves = width // LANES

    def put(row, value):
        for h in range(halves):
            gp[h, pl.ds(row, value.shape[0]), :] = value[:, h * LANES : (h + 1) * LANES]

    edge_v = dot(halo[0], wv[...])
    edge_g = dot(halo[0], wg[...])
    row = rows_of(2 * EDGE, 0)
    pos = jnp.where(row < EDGE, row - EDGE, row - EDGE + frames)
    edge = jnp.where((pos >= lo) & (pos < hi), edge_v * sigmoid(edge_g), 0.0)
    zero = jnp.zeros((EDGE, width), F32)
    put(0, zero)
    put(EDGE, edge[:EDGE])
    put(2 * EDGE + frames, edge[EDGE:])
    put(3 * EDGE + frames, zero)
    step = block_rows(frames, 512)
    small = block_rows(step, 64)
    for base in range(0, frames, step):
        xb = x[0, base : base + step, :]
        vl_o[0, base : base + step, :] = dot(xb, wv[...])
        sg_o[0, base : base + step, :] = dot(xb, wg[...])

    def gating(i, carry):
        base = pl.multiple_of(i * small, small)
        v = vl_o[0, pl.ds(base, small), :]
        s = sigmoid(sg_o[0, pl.ds(base, small), :])
        sg_o[0, pl.ds(base, small), :] = s
        put(2 * EDGE + base, jnp.where(rows_of(small, base) < hi, v * s, 0.0))
        return carry

    lax.fori_loop(0, frames // small, gating, 0)
    span = frames + 2 * EDGE
    cb = block_rows(span, 104)
    kernel = taps.shape[0]
    margin = (kernel - 1) // 2
    for h in range(halves):
        cols = slice(h * LANES, (h + 1) * LANES)

        def convolve(i, carry):
            s1, s2 = carry
            base = pl.multiple_of(i * cb, 8)
            acc = jnp.zeros((cb, LANES), F32)
            for k in range(kernel):
                acc = acc + taps[k : k + 1, cols] * gp[h, pl.ds(base + EDGE - margin + k, cb), :]
            conv_o[0, pl.ds(base, cb), cols] = acc
            pos = rows_of(cb, base - EDGE)
            kept = jnp.where((pos >= 0) & (pos < jnp.minimum(hi, frames)), acc, 0.0)
            return s1 + fold_rows(kept), s2 + fold_rows(kept * kept)

        none = jnp.zeros((8, LANES), F32)
        s1, s2 = lax.fori_loop(0, span // cb, convolve, (none, none))
        add = jnp.concatenate(
            [jnp.sum(s1, axis=0, keepdims=True), jnp.sum(s2, axis=0, keepdims=True)], axis=0
        )
        st[:, cols] = jnp.where(r == 0, 0.0, st[:, cols]) + add

    @pl.when(r == pl.num_programs(0) - 1)
    def _():
        spread_sums(st_o, st[...])


def batch_norm(stats, count):
    sums = jnp.sum(stats[...], axis=0)
    centre = sums[0:1] / count
    spread = sums[1:2] / count - centre * centre
    return centre, lax.rsqrt(spread + EPSILON)


def norm_kernel(
    meta, count, stats, affine, select, grads, halo, wo, conv,
    swished_o, gn_o, picked_o, st_o, st, ping, pong
):
    r = pl.program_id(0)
    hi = meta[0, r]
    lo = meta[1, r]
    frames = grads.shape[1]
    centre, inv = batch_norm(stats, count[0, 0])
    gain, shift = affine[0:1, :], affine[1:2, :]

    def part(row, swish_grad):
        size = swish_grad.shape[0]
        unit = (conv[0, pl.ds(row, size), :] - centre) * inv
        normalized = unit * gain + shift
        s = sigmoid(normalized)
        pos = rows_of(size, row - EDGE)
        keep = (pos >= lo) & (pos < hi)
        swished = jnp.where(keep, normalized * s, 0.0)
        gn = jnp.where(keep, swish_grad, 0.0) * (s + normalized * (s - s * s))
        gn_o[0, pl.ds(row, size), :] = gn
        return unit, swished, gn

    edge = dot(halo[0], wo[...])
    part(0, edge[:EDGE])
    part(frames + EDGE, edge[EDGE:])
    step = block_rows(frames, 512)
    small = block_rows(step, 32)
    s1 = jnp.zeros((8, conv.shape[2]), F32)
    s2 = s1
    held = (ping, pong)
    ping[...] = dot(grads[0, :step, :], wo[...])
    for i in range(frames // step):
        now = held[i % 2]
        if (i + 1) * step < frames:
            held[(i + 1) % 2][...] = dot(grads[0, (i + 1) * step : (i + 2) * step, :], wo[...])
        picked_o[0, :, i * step : (i + 1) * step] = dot_nt(
            select[...], grads[0, i * step : (i + 1) * step, :]
        ).astype(BF16)
        for j in range(step // small):
            base = i * step + j * small
            unit, swished, gn = part(base + EDGE, now[j * small : (j + 1) * small, :])
            swished_o[0, base : base + small, :] = swished.astype(BF16)
            s1 = s1 + fold_rows(gn)
            s2 = s2 + fold_rows(gn * unit)
    add = jnp.concatenate(
        [jnp.sum(s1, axis=0, keepdims=True), jnp.sum(s2, axis=0, keepdims=True)], axis=0
    )
    st[...] = jnp.where(r == 0, 0.0, st[...]) + add

    @pl.when(r == pl.num_programs(0) - 1)
    def _():
        spread_sums(st_o, st[...])


def back_kernel(
    record, meta, count, stats, sums, gain, gn, conv, vl, sg, taps, out, taps_o, gc, acc
):
    i = pl.program_id(0)
    hi = meta[0, record]
    lo = meta[1, record]
    frames, width = vl.shape[1:]
    halves = width // LANES
    span = frames + 2 * EDGE
    kernel = taps.shape[0]
    margin = (kernel - 1) // 2
    cb = block_rows(span, 144)
    step = block_rows(frames, 64)
    total_frames = count[0, 0]
    centre, inv = batch_norm(stats, total_frames)
    grad_sums = jnp.sum(sums[...], axis=0)
    scale = gain[...] * inv
    offset = scale * grad_sums[0:1] / total_frames
    slope = scale * inv * grad_sums[1:2] / total_frames
    first = i * frames

    @pl.when(i == 0)
    def _():
        acc[...] = jnp.zeros_like(acc)

    for h in range(halves):
        cols = slice(h * LANES, (h + 1) * LANES)
        for base in range(0, span, cb):
            pos = rows_of(cb, first + (base - EDGE))
            mean = offset[:, cols] + (conv[0, base : base + cb, cols] - centre[:, cols]) * slope[:, cols]
            gc[h, base : base + cb, :] = scale[:, cols] * gn[0, base : base + cb, cols] - jnp.where(
                (pos >= lo) & (pos < hi), mean, 0.0
            )
        sums_k = [acc[h, k] for k in range(kernel)]
        for base in range(0, frames, step):
            v = vl[0, base : base + step, cols]
            s = sg[0, base : base + step, cols]
            keep = rows_of(step, first + base) < hi
            vs = v * s
            gated = jnp.where(keep, vs, 0.0)
            total = jnp.zeros((step, LANES), F32)
            for k in range(kernel):
                window = gc[h, base + EDGE + margin - k : base + EDGE + margin - k + step, :]
                total = total + taps[k : k + 1, cols] * window
                sums_k[k] = sums_k[k] + fold_rows(window * gated)
            total = jnp.where(keep, total, 0.0)
            out[base : base + step, cols] = (total * s).astype(BF16)
            out[base : base + step, width + h * LANES : width + (h + 1) * LANES] = (
                total * (vs - vs * s)
            ).astype(BF16)
        for k in range(kernel):
            acc[h, k] = sums_k[k]

    @pl.when(i == pl.num_programs(0) - 1)
    def _():
        taps_o[...] = jnp.zeros_like(taps_o)
        for h in range(halves):
            for k in range(kernel):
                taps_o[k : k + 1, h * LANES : (h + 1) * LANES] = jnp.sum(
                    acc[h, k], axis=0, keepdims=True
                )


def partial_kernel(own, sibling, w_own, w_sibling, picked, mine, *others):
    total = dot_nt(w_own[...], own[...]) + dot_nt(w_sibling[...], sibling[...])
    rows = picked.shape[1]
    mine[...] = total[:rows] + picked[0].astype(F32)
    for d, other in enumerate(others):
        other[...] = total[(d + 1) * rows : (d + 2) * rows].astype(BF16)


def first_outer_kernel(grads, swished, out):
    r = pl.program_id(0)
    add = dot_tn(swished[0], grads[0])

    @pl.when(r == 0)
    def _():
        out[...] = add

    @pl.when(r > 0)
    def _():
        out[...] += add


def outer_kernel(records, parity, x, w_out, *refs):
    lefts, taps = refs[:records], refs[records : 2 * records]
    keep, send, acc = refs[2 * records :]
    width = w_out.shape[0]
    shard = keep.shape[2]
    r = pl.program_id(0)
    for i, left in enumerate(lefts):

        @pl.when(r == i)
        def _(i=i, left=left):
            add = dot_tn(left[...], x[0])
            if i == 0:
                acc[...] = add
            else:
                acc[...] += add

    @pl.when(r == records - 1)
    def _():
        tap_sums = taps[0][...]
        for part in taps[1:]:
            tap_sums = tap_sums + part[...]

        def write(place, odd):
            for j in range(place.shape[0]):
                at = (2 * j + odd) * shard
                place[j, : 2 * width, :] = acc[:, at : at + shard].astype(BF16)
                place[j, 2 * width : 3 * width, :] = w_out[:, at : at + shard].astype(BF16)
                for q in range(width // shard):
                    row = 3 * width + 16 * q
                    place[j, row : row + 16, :] = tap_sums[:, q * shard : (q + 1) * shard].astype(
                        BF16
                    )

        @pl.when(parity[0, 0] == 0)
        def _():
            write(keep, 0)
            write(send, 1)

        @pl.when(parity[0, 0] != 0)
        def _():
            write(keep, 1)
            write(send, 0)


def finish_kernel(kernel, got, value, gate, out, taps):
    width = value.shape[1]
    shard = value.shape[0]

    def total(row, size):
        sums = got[0, row : row + size, :].astype(F32)
        for j in range(1, got.shape[0]):
            sums = sums + got[j, row : row + size, :].astype(F32)
        return sums

    for i, place in enumerate((value, gate, out)):
        place[...] = total(i * width, width).T
    for q in range(width // shard):
        taps[:, q * shard : (q + 1) * shard] = total(3 * width + 16 * q, 16)[:kernel]


def place_kernel(moved, *refs):
    out = refs[-1]
    frames = moved.shape[2]
    for s in range(moved.shape[0]):
        out[0, :, s * frames : (s + 1) * frames] = moved[s]


def exchange(copies, axis):
    return lax.all_to_all(copies, axis, 0, 0, tiled=True)


def per_device(
    normed,
    grad_out,
    value_weight,
    gate_weight,
    depth_taps,
    norm_gain,
    norm_shift,
    out_weight,
    lengths,
):
    recs, frames, model = normed.shape
    kernel = depth_taps.shape[0]
    width = value_weight.shape[1]
    seqs = lax.axis_size("seq")
    tps = lax.axis_size("tp")
    chips = tps // 2
    piece = model // (seqs * tps)
    rows = seqs * piece
    shard = model // seqs
    span = frames + 2 * EDGE
    seq_at = lax.axis_index("seq")
    tp_at = lax.axis_index("tp")
    chip_at, core_at = tp_at // 2, tp_at % 2
    count = jnp.sum(lengths).astype(F32)
    first = (seq_at * frames).astype(jnp.int32)
    meta = jnp.stack([lengths - first, jnp.full((recs,), 0, jnp.int32) - first])
    halves = width // LANES
    counts = count.reshape(1, 1)
    parity = (seq_at % 2).astype(jnp.int32).reshape(1, 1)
    sds = jax.ShapeDtypeStruct

    low_edge = jnp.concatenate([normed[:, -EDGE:], grad_out[:, -EDGE:]], axis=2)
    high_edge = jnp.concatenate([normed[:, :EDGE], grad_out[:, :EDGE]], axis=2)
    up = [(i, i + 1) for i in range(seqs - 1)]
    down = [(j, i) for i, j in up]
    halo = jnp.concatenate(
        [lax.ppermute(low_edge, "seq", up), lax.ppermute(high_edge, "seq", down)], axis=1
    )
    halo_x, halo_g = halo[:, :, :model], halo[:, :, model:]

    both = jnp.concatenate([value_weight, gate_weight], axis=1).reshape(seqs, tps, piece, 2 * width)

    def chosen(core):
        picks = [
            lax.dynamic_index_in_dim(both, ((chip_at + d) % chips) * 2 + core, 1, keepdims=False)
            for d in range(chips)
        ]
        return jnp.stack(picks).reshape(chips * rows, 2 * width)

    swap = [(i, i ^ 1) for i in range(tps)]
    w_own = chosen(core_at)
    w_sibling = lax.ppermute(chosen(1 - core_at), "tp", swap)

    channel = (
        jnp.arange(seqs, dtype=jnp.int32)[:, None] * (tps * piece)
        + tp_at * piece
        + jnp.arange(piece, dtype=jnp.int32)[None, :]
    ).reshape(rows, 1)
    select = (channel == jnp.arange(model, dtype=jnp.int32)[None, :]).astype(BF16)
    array_bytes = recs * frames * width * 4
    input_bytes = recs * frames * model * 2
    matmul = 2 * recs * frames * model * width

    vl, sg, conv, stats = call(
        gate_kernel,
        "gate_conv",
        (recs,),
        [
            smem(),
            per_record((frames, model)),
            per_record((2 * EDGE, model)),
            whole((model, width)),
            whole((model, width)),
            whole((kernel, width)),
        ],
        [
            per_record((frames, width)),
            per_record((frames, width)),
            per_record((span, width)),
            whole((seqs, 2, width)),
        ],
        [
            sds((recs, frames, width), F32),
            sds((recs, frames, width), F32),
            sds((recs, span, width), F32),
            sds((seqs, 2, width), F32),
        ],
        [pltpu.VMEM((halves, frames + 4 * EDGE, LANES), F32), pltpu.VMEM((2, width), F32)],
        2 * matmul,
        input_bytes + 3 * array_bytes,
    )(meta, normed, halo_x, value_weight, gate_weight, depth_taps)
    stats = exchange(stats, "seq")

    chunk = block_rows(frames, 256)
    half_rows = block_rows(frames, 512)
    swished, gn, picked, sums = call(
        norm_kernel,
        "swish_norm",
        (recs,),
        [
            smem(),
            smem(),
            whole((seqs, 2, width)),
            whole((2, width)),
            whole((rows, model)),
            per_record((frames, model)),
            per_record((2 * EDGE, model)),
            whole((model, width)),
            per_record((span, width)),
        ],
        [
            per_record((frames, width)),
            per_record((span, width)),
            per_record((rows, frames)),
            whole((seqs, 2, width)),
        ],
        [
            sds((recs, frames, width), BF16),
            sds((recs, span, width), F32),
            sds((recs, rows, frames), BF16),
            sds((seqs, 2, width), F32),
        ],
        [
            pltpu.VMEM((2, width), F32),
            pltpu.VMEM((block_rows(frames, 512), width), F32),
            pltpu.VMEM((block_rows(frames, 512), width), F32),
        ],
        2 * matmul,
        input_bytes + 3 * array_bytes,
    )(
        meta,
        counts,
        stats,
        jnp.stack([norm_gain, norm_shift]),
        select,
        grad_out,
        halo_g,
        out_weight,
        conv,
    )
    w_out = call(
        first_outer_kernel,
        "outer_w_out",
        (recs,),
        [per_record((frames, model)), per_record((frames, width))],
        whole((width, model)),
        sds((width, model), F32),
        [],
        matmul,
        input_bytes,
    )(grad_out, swished)
    sums = exchange(sums, "seq")
    grad_shift, grad_gain = jnp.sum(sums, axis=0)

    def back(r, marker):
        def window(i):
            return (r, pl.multiple_of(i * chunk, chunk), 0)

        return call(
            functools.partial(back_kernel, r),
            "back_conv",
            (frames // chunk,),
            [
                smem(),
                smem(),
                whole((seqs, 2, width)),
                whole((seqs, 2, width)),
                whole((1, width)),
                pl.BlockSpec((pl.Element(1), pl.Element(chunk + 2 * EDGE), pl.Element(width)), window),
                pl.BlockSpec((pl.Element(1), pl.Element(chunk + 2 * EDGE), pl.Element(width)), window),
                pl.BlockSpec((1, chunk, width), lambda i: (r, i, 0)),
                pl.BlockSpec((1, chunk, width), lambda i: (r, i, 0)),
                whole((kernel, width)),
            ],
            [pl.BlockSpec((chunk, 2 * width), lambda i: (i, 0)), whole((16, width))],
            [sds((frames, 2 * width), BF16), sds((16, width), F32)],
            [
                pltpu.VMEM((halves, chunk + 2 * EDGE, LANES), F32),
                pltpu.VMEM((halves, kernel, 8, LANES), F32),
            ],
            0,
            1024,
        )(meta, counts, stats, sums, norm_gain[None], gn, conv, vl, sg, after(depth_taps, w_out, *marker))

    def partials(r, mine):
        sibling = lax.ppermute(mine, "tp", swap)
        return call(
            partial_kernel,
            "partial_in",
            (frames // half_rows,),
            [
                pl.BlockSpec((half_rows, 2 * width), lambda i: (i, 0)),
                pl.BlockSpec((half_rows, 2 * width), lambda i: (i, 0)),
                whole((chips * rows, 2 * width)),
                whole((chips * rows, 2 * width)),
                pl.BlockSpec((1, rows, half_rows), lambda i: (r, 0, i)),
            ],
            [pl.BlockSpec((rows, half_rows), lambda i: (0, i))] * chips,
            [sds((rows, frames), F32)] + [sds((rows, frames), BF16)] * (chips - 1),
            [],
            0,
            1024,
            vmem=20,
        )(mine, sibling, w_own, w_sibling, picked)

    grads, tap_parts, parts, moved = [], [], [], []

    def deliver(r, *earlier):
        total = after(parts[r][0], *earlier)
        for d in range(1, chips):
            send = [(i, ((i // 2 + d) % chips) * 2 + i % 2) for i in range(tps)]
            total = total + lax.ppermute(parts[r][d], "tp", send).astype(F32)
        own = total.astype(BF16).reshape(seqs, piece, frames)
        moved.append(exchange(own, "seq"))
        return own

    for r in range(recs):
        mine, tap_part = back(r, parts[r - 2] if r > 1 else ())
        grads.append(mine)
        tap_parts.append(tap_part)
        if r > 0:
            parts.append(partials(r - 1, grads[r - 1]))
    owns = [deliver(0, *parts[recs - 2])]
    parts.append(partials(recs - 1, after(grads[recs - 1], owns[0])))
    owns.append(deliver(1, *parts[recs - 1]))

    slots = 3 * width + 16 * (width // shard)
    half = sds((seqs // 2, slots, shard), BF16)
    keep, send = call(
        functools.partial(outer_kernel, recs),
        "outer_w_in",
        (recs,),
        [smem(), per_record((frames, model)), whole((width, model))]
        + [whole((frames, 2 * width))] * recs
        + [whole((16, width))] * recs,
        [whole(half.shape)] * 2,
        [half] * 2,
        [pltpu.VMEM((2 * width, model), F32)],
        0,
        1024,
    )(parity, after(normed, owns[1]), w_out, *grads, *tap_parts)
    pairs = [(i, i ^ 1) for i in range(seqs)]
    others = lax.ppermute(send, "seq", pairs)
    for r in range(2, recs):
        owns.append(deliver(r, keep, owns[-1]))
    paired = (after(keep, owns[-2]).astype(F32) + others.astype(F32)).astype(BF16)
    same = [[i for i in range(seqs) if i % 2 == odd] for odd in range(2)]
    got = lax.all_to_all(
        after(paired, owns[-1]), "seq", 0, 0, axis_index_groups=same, tiled=True
    )
    w_value, w_gate, w_out, grad_taps = call(
        functools.partial(finish_kernel, kernel),
        "finish",
        (1,),
        [whole(half.shape)],
        [whole((shard, width))] * 3 + [whole((kernel, width))],
        [sds((shard, width), F32)] * 3 + [sds((kernel, width), F32)],
        [],
        0,
        8 * seqs * slots * shard,
        vmem=20,
    )(got)
    grad_in = ()
    for r in range(recs):
        grad_in = (
            call(
                place_kernel,
                "place",
                (1,),
                [whole((seqs, piece, frames))] + [anywhere()] * len(grad_in),
                pl.BlockSpec((1, piece, seqs * frames), lambda i, r=r: (r, 0, 0)),
                sds((recs, piece, seqs * frames), BF16),
                [],
                0,
                4 * piece * seqs * frames,
                {1: 0} if grad_in else None,
                vmem=20,
            )(moved[r], *grad_in),
        )
    (grad_in,) = grad_in
    return (grad_in, w_value, w_gate, w_out, grad_taps, grad_gain, grad_shift)


def solution(mesh):
    placed = (
        P(None, "seq", None),
        P(None, "seq", None),
        P(None, "tp"),
        P(None, "tp"),
        P(None, "tp"),
        P("tp"),
        P("tp"),
        P(None, "tp"),
        P(),
    )
    return jax.shard_map(
        per_device,
        mesh=mesh,
        in_specs=placed,
        out_specs=(
            P(None, ("seq", "tp"), None),
            P("seq", "tp"),
            P("seq", "tp"),
            P("seq", "tp"),
            P(None, "tp"),
            P("tp"),
            P("tp"),
        ),
        check_vma=False,
    )
```

```python
import functools

import jax
import jax.numpy as jnp
from jax import lax
from jax.experimental import pallas as pl
from jax.experimental.pallas import tpu as pltpu
from jax.sharding import PartitionSpec as P

EPSILON = 1e-05
EDGE = 8
LANES = 128
F32 = jnp.float32
BF16 = jnp.bfloat16


def sigmoid(x):
    return 0.5 * jnp.tanh(0.5 * x) + 0.5


def dot(a, b):
    return jnp.dot(a, b, preferred_element_type=F32)


def dot_nt(a, b):
    return lax.dot_general(a, b, (((1,), (1,)), ((), ())), preferred_element_type=F32)


def dot_tn(a, b):
    return lax.dot_general(a, b, (((0,), (0,)), ((), ())), preferred_element_type=F32)


def rows_of(count, first):
    return first + lax.broadcasted_iota(jnp.int32, (count, 1), 0)


def fold_rows(x):
    return jnp.sum(x.reshape(x.shape[0] // 8, 8, x.shape[1]), axis=0)


def block_rows(total, most):
    return max(b for b in range(8, most + 1, 8) if total % b == 0)


def whole(shape):
    return pl.BlockSpec(shape, lambda *i: (0,) * len(shape))


def per_record(shape):
    return pl.BlockSpec((1,) + shape, lambda r: (r,) + (0,) * len(shape))


def smem():
    return pl.BlockSpec(memory_space=pltpu.SMEM)


def anywhere():
    return pl.BlockSpec(memory_space=pl.ANY)


def after(x, *earlier):
    return lax.optimization_barrier((x,) + earlier)[0]


def spread_sums(out, sums):
    for s in range(out.shape[0]):
        out[s] = sums


def call(
    kernel, name, grid, in_specs, out_specs, out_shape, scratch, flops, moved, aliases=None, vmem=60
):
    return pl.pallas_call(
        kernel,
        name=name,
        grid=grid,
        in_specs=in_specs,
        out_specs=out_specs,
        out_shape=out_shape,
        scratch_shapes=scratch,
        input_output_aliases=aliases or {},
        cost_estimate=pl.CostEstimate(flops=int(flops), bytes_accessed=int(moved), transcendentals=0),
        compiler_params=pltpu.CompilerParams(vmem_limit_bytes=vmem * 1024 * 1024),
    )


def gate_kernel(meta, x, halo, wv, wg, taps, vl_o, sg_o, conv_o, st_o, gp, st):
    r = pl.program_id(0)
    hi = meta[0, r]
    lo = meta[1, r]
    frames = x.shape[1]
    width = wv.shape[1]
    halves = width // LANES

    def put(row, value):
        for h in range(halves):
            gp[h, pl.ds(row, value.shape[0]), :] = value[:, h * LANES : (h + 1) * LANES]

    edge_v = dot(halo[0], wv[...])
    edge_g = dot(halo[0], wg[...])
    row = rows_of(2 * EDGE, 0)
    pos = jnp.where(row < EDGE, row - EDGE, row - EDGE + frames)
    edge = jnp.where((pos >= lo) & (pos < hi), edge_v * sigmoid(edge_g), 0.0)
    zero = jnp.zeros((EDGE, width), F32)
    put(0, zero)
    put(EDGE, edge[:EDGE])
    put(2 * EDGE + frames, edge[EDGE:])
    put(3 * EDGE + frames, zero)
    step = block_rows(frames, 512)
    small = block_rows(step, 64)
    for base in range(0, frames, step):
        xb = x[0, base : base + step, :]
        vl_o[0, base : base + step, :] = dot(xb, wv[...])
        sg_o[0, base : base + step, :] = dot(xb, wg[...])

    def gating(i, carry):
        base = pl.multiple_of(i * small, small)
        v = vl_o[0, pl.ds(base, small), :]
        s = sigmoid(sg_o[0, pl.ds(base, small), :])
        sg_o[0, pl.ds(base, small), :] = s
        put(2 * EDGE + base, jnp.where(rows_of(small, base) < hi, v * s, 0.0))
        return carry

    lax.fori_loop(0, frames // small, gating, 0)
    span = frames + 2 * EDGE
    cb = block_rows(span, 104)
    kernel = taps.shape[0]
    margin = (kernel - 1) // 2
    for h in range(halves):
        cols = slice(h * LANES, (h + 1) * LANES)

        def convolve(i, carry):
            s1, s2 = carry
            base = pl.multiple_of(i * cb, 8)
            acc = jnp.zeros((cb, LANES), F32)
            for k in range(kernel):
                acc = acc + taps[k : k + 1, cols] * gp[h, pl.ds(base + EDGE - margin + k, cb), :]
            conv_o[0, pl.ds(base, cb), cols] = acc
            pos = rows_of(cb, base - EDGE)
            kept = jnp.where((pos >= 0) & (pos < jnp.minimum(hi, frames)), acc, 0.0)
            return s1 + fold_rows(kept), s2 + fold_rows(kept * kept)

        none = jnp.zeros((8, LANES), F32)
        s1, s2 = lax.fori_loop(0, span // cb, convolve, (none, none))
        add = jnp.concatenate(
            [jnp.sum(s1, axis=0, keepdims=True), jnp.sum(s2, axis=0, keepdims=True)], axis=0
        )
        st[:, cols] = jnp.where(r == 0, 0.0, st[:, cols]) + add

    @pl.when(r == pl.num_programs(0) - 1)
    def _():
        spread_sums(st_o, st[...])


def batch_norm(stats, count):
    sums = jnp.sum(stats[...], axis=0)
    centre = sums[0:1] / count
    spread = sums[1:2] / count - centre * centre
    return centre, lax.rsqrt(spread + EPSILON)


def norm_kernel(
    meta, count, stats, affine, select, grads, halo, wo, conv,
    swished_o, gn_o, picked_o, st_o, st, ping, pong
):
    r = pl.program_id(0)
    hi = meta[0, r]
    lo = meta[1, r]
    frames = grads.shape[1]
    centre, inv = batch_norm(stats, count[0, 0])
    gain, shift = affine[0:1, :], affine[1:2, :]

    def part(row, swish_grad):
        size = swish_grad.shape[0]
        unit = (conv[0, pl.ds(row, size), :] - centre) * inv
        normalized = unit * gain + shift
        s = sigmoid(normalized)
        pos = rows_of(size, row - EDGE)
        keep = (pos >= lo) & (pos < hi)
        swished = jnp.where(keep, normalized * s, 0.0)
        gn = jnp.where(keep, swish_grad, 0.0) * (s + normalized * (s - s * s))
        gn_o[0, pl.ds(row, size), :] = gn
        return unit, swished, gn

    edge = dot(halo[0], wo[...])
    part(0, edge[:EDGE])
    part(frames + EDGE, edge[EDGE:])
    step = block_rows(frames, 512)
    small = block_rows(step, 32)
    s1 = jnp.zeros((8, conv.shape[2]), F32)
    s2 = s1
    held = (ping, pong)
    ping[...] = dot(grads[0, :step, :], wo[...])
    for i in range(frames // step):
        now = held[i % 2]
        if (i + 1) * step < frames:
            held[(i + 1) % 2][...] = dot(grads[0, (i + 1) * step : (i + 2) * step, :], wo[...])
        picked_o[0, :, i * step : (i + 1) * step] = dot_nt(
            select[...], grads[0, i * step : (i + 1) * step, :]
        ).astype(BF16)
        for j in range(step // small):
            base = i * step + j * small
            unit, swished, gn = part(base + EDGE, now[j * small : (j + 1) * small, :])
            swished_o[0, base : base + small, :] = swished.astype(BF16)
            s1 = s1 + fold_rows(gn)
            s2 = s2 + fold_rows(gn * unit)
    add = jnp.concatenate(
        [jnp.sum(s1, axis=0, keepdims=True), jnp.sum(s2, axis=0, keepdims=True)], axis=0
    )
    st[...] = jnp.where(r == 0, 0.0, st[...]) + add

    @pl.when(r == pl.num_programs(0) - 1)
    def _():
        spread_sums(st_o, st[...])


def back_kernel(
    record, blocks, meta, count, stats, sums, gain, gn, conv, vl, sg, taps, out, taps_o, gc, acc
):
    i = pl.program_id(0)
    frames, width = vl.shape[1:]
    hi = meta[0, record + i // blocks]
    lo = meta[1, record + i // blocks]
    halves = width // LANES
    span = frames + 2 * EDGE
    kernel = taps.shape[0]
    margin = (kernel - 1) // 2
    cb = block_rows(span, 144)
    step = block_rows(frames, 64)
    total_frames = count[0, 0]
    centre, inv = batch_norm(stats, total_frames)
    grad_sums = jnp.sum(sums[...], axis=0)
    scale = gain[...] * inv
    offset = scale * grad_sums[0:1] / total_frames
    slope = scale * inv * grad_sums[1:2] / total_frames
    first = i % blocks * frames

    @pl.when(i == 0)
    def _():
        acc[...] = jnp.zeros_like(acc)

    for h in range(halves):
        cols = slice(h * LANES, (h + 1) * LANES)
        for base in range(0, span, cb):
            pos = rows_of(cb, first + (base - EDGE))
            mean = offset[:, cols] + (conv[0, base : base + cb, cols] - centre[:, cols]) * slope[:, cols]
            gc[h, base : base + cb, :] = scale[:, cols] * gn[0, base : base + cb, cols] - jnp.where(
                (pos >= lo) & (pos < hi), mean, 0.0
            )
        sums_k = [acc[h, k] for k in range(kernel)]
        for base in range(0, frames, step):
            v = vl[0, base : base + step, cols]
            s = sg[0, base : base + step, cols]
            keep = rows_of(step, first + base) < hi
            vs = v * s
            gated = jnp.where(keep, vs, 0.0)
            total = jnp.zeros((step, LANES), F32)
            for k in range(kernel):
                window = gc[h, base + EDGE + margin - k : base + EDGE + margin - k + step, :]
                total = total + taps[k : k + 1, cols] * window
                sums_k[k] = sums_k[k] + fold_rows(window * gated)
            total = jnp.where(keep, total, 0.0)
            out[base : base + step, cols] = (total * s).astype(BF16)
            out[base : base + step, width + h * LANES : width + (h + 1) * LANES] = (
                total * (vs - vs * s)
            ).astype(BF16)
        for k in range(kernel):
            acc[h, k] = sums_k[k]

    @pl.when(i == pl.num_programs(0) - 1)
    def _():
        taps_o[...] = jnp.zeros_like(taps_o)
        for h in range(halves):
            for k in range(kernel):
                taps_o[k : k + 1, h * LANES : (h + 1) * LANES] = jnp.sum(
                    acc[h, k], axis=0, keepdims=True
                )


def partial_kernel(own, sibling, w_own, w_sibling, picked, mine, *others):
    total = dot_nt(w_own[...], own[...]) + dot_nt(w_sibling[...], sibling[...])
    rows = picked.shape[1]
    seqs, _, piece, frames = mine.shape
    mine[...] = (
        (total[:rows] + picked[0].astype(F32)).astype(BF16).reshape(seqs, 1, piece, frames)
    )
    for d, other in enumerate(others):
        other[...] = (
            total[(d + 1) * rows : (d + 2) * rows].astype(BF16).reshape(seqs, 1, piece, frames)
        )


def first_outer_kernel(grads, swished, out):
    r = pl.program_id(0)
    add = dot_tn(swished[0], grads[0])

    @pl.when(r == 0)
    def _():
        out[...] = add

    @pl.when(r > 0)
    def _():
        out[...] += add


def outer_kernel(groups, parity, x, w_out, *refs):
    lefts, taps = refs[: len(groups)], refs[len(groups) : 2 * len(groups)]
    keep, send, acc = refs[2 * len(groups) :]
    records = groups[-1][0] + groups[-1][1]
    width = w_out.shape[0]
    shard = keep.shape[2]
    r = pl.program_id(0)
    for (first, size), left in zip(groups, lefts):

        @pl.when((r >= first) & (r < first + size))
        def _(left=left):
            add = dot_tn(left[...], x[0])
            acc[...] = add + jnp.where(r == 0, 0.0, acc[...])

    @pl.when(r == records - 1)
    def _():
        tap_sums = taps[0][...]
        for part in taps[1:]:
            tap_sums = tap_sums + part[...]

        def write(place, odd):
            for j in range(place.shape[0]):
                at = (2 * j + odd) * shard
                place[j, : 2 * width, :] = acc[:, at : at + shard].astype(BF16)
                place[j, 2 * width : 3 * width, :] = w_out[:, at : at + shard].astype(BF16)
                for q in range(width // shard):
                    row = 3 * width + 16 * q
                    place[j, row : row + 16, :] = tap_sums[:, q * shard : (q + 1) * shard].astype(
                        BF16
                    )

        @pl.when(parity[0, 0] == 0)
        def _():
            write(keep, 0)
            write(send, 1)

        @pl.when(parity[0, 0] != 0)
        def _():
            write(keep, 1)
            write(send, 0)


def finish_kernel(kernel, got, value, gate, out, taps):
    width = value.shape[1]
    shard = value.shape[0]

    def total(row, size):
        sums = got[0, row : row + size, :].astype(F32)
        for j in range(1, got.shape[0]):
            sums = sums + got[j, row : row + size, :].astype(F32)
        return sums

    for i, place in enumerate((value, gate, out)):
        place[...] = total(i * width, width).T
    for q in range(width // shard):
        taps[:, q * shard : (q + 1) * shard] = total(3 * width + 16 * q, 16)[:kernel]


def place_kernel(moved, *refs):
    out = refs[-1]
    frames = moved.shape[3]
    for s in range(moved.shape[0]):
        out[0, :, s * frames : (s + 1) * frames] = moved[s, 0]


def exchange(copies, axis):
    return lax.all_to_all(copies, axis, 0, 0, tiled=True)


def per_device(
    normed,
    grad_out,
    value_weight,
    gate_weight,
    depth_taps,
    norm_gain,
    norm_shift,
    out_weight,
    lengths,
):
    recs, frames, model = normed.shape
    kernel = depth_taps.shape[0]
    width = value_weight.shape[1]
    seqs = lax.axis_size("seq")
    tps = lax.axis_size("tp")
    chips = tps // 2
    piece = model // (seqs * tps)
    rows = seqs * piece
    shard = model // seqs
    span = frames + 2 * EDGE
    seq_at = lax.axis_index("seq")
    tp_at = lax.axis_index("tp")
    chip_at, core_at = tp_at // 2, tp_at % 2
    count = jnp.sum(lengths).astype(F32)
    first = (seq_at * frames).astype(jnp.int32)
    meta = jnp.stack([lengths - first, jnp.full((recs,), 0, jnp.int32) - first])
    halves = width // LANES
    counts = count.reshape(1, 1)
    parity = (seq_at % 2).astype(jnp.int32).reshape(1, 1)
    sds = jax.ShapeDtypeStruct

    low_edge = jnp.concatenate([normed[:, -EDGE:], grad_out[:, -EDGE:]], axis=2)
    high_edge = jnp.concatenate([normed[:, :EDGE], grad_out[:, :EDGE]], axis=2)
    up = [(i, i + 1) for i in range(seqs - 1)]
    down = [(j, i) for i, j in up]
    halo = jnp.concatenate(
        [lax.ppermute(low_edge, "seq", up), lax.ppermute(high_edge, "seq", down)], axis=1
    )
    halo_x, halo_g = halo[:, :, :model], halo[:, :, model:]

    both = jnp.concatenate([value_weight, gate_weight], axis=1).reshape(seqs, tps, piece, 2 * width)

    def chosen(core):
        picks = [
            lax.dynamic_index_in_dim(both, ((chip_at + d) % chips) * 2 + core, 1, keepdims=False)
            for d in range(chips)
        ]
        return jnp.stack(picks).reshape(chips * rows, 2 * width)

    swap = [(i, i ^ 1) for i in range(tps)]
    w_own = chosen(core_at)
    w_sibling = lax.ppermute(chosen(1 - core_at), "tp", swap)

    channel = (
        jnp.arange(seqs, dtype=jnp.int32)[:, None] * (tps * piece)
        + tp_at * piece
        + jnp.arange(piece, dtype=jnp.int32)[None, :]
    ).reshape(rows, 1)
    select = (channel == jnp.arange(model, dtype=jnp.int32)[None, :]).astype(BF16)
    array_bytes = recs * frames * width * 4
    input_bytes = recs * frames * model * 2
    matmul = 2 * recs * frames * model * width

    vl, sg, conv, stats = call(
        gate_kernel,
        "gate_conv",
        (recs,),
        [
            smem(),
            per_record((frames, model)),
            per_record((2 * EDGE, model)),
            whole((model, width)),
            whole((model, width)),
            whole((kernel, width)),
        ],
        [
            per_record((frames, width)),
            per_record((frames, width)),
            per_record((span, width)),
            whole((seqs, 2, width)),
        ],
        [
            sds((recs, frames, width), F32),
            sds((recs, frames, width), F32),
            sds((recs, span, width), F32),
            sds((seqs, 2, width), F32),
        ],
        [pltpu.VMEM((halves, frames + 4 * EDGE, LANES), F32), pltpu.VMEM((2, width), F32)],
        2 * matmul,
        input_bytes + 3 * array_bytes,
    )(meta, normed, halo_x, value_weight, gate_weight, depth_taps)
    stats = exchange(stats, "seq")

    chunk = block_rows(frames, 256)
    half_rows = block_rows(frames, 512)
    swished, gn, picked, sums = call(
        norm_kernel,
        "swish_norm",
        (recs,),
        [
            smem(),
            smem(),
            whole((seqs, 2, width)),
            whole((2, width)),
            whole((rows, model)),
            per_record((frames, model)),
            per_record((2 * EDGE, model)),
            whole((model, width)),
            per_record((span, width)),
        ],
        [
            per_record((frames, width)),
            per_record((span, width)),
            per_record((rows, frames)),
            whole((seqs, 2, width)),
        ],
        [
            sds((recs, frames, width), BF16),
            sds((recs, span, width), F32),
            sds((recs, rows, frames), BF16),
            sds((seqs, 2, width), F32),
        ],
        [
            pltpu.VMEM((2, width), F32),
            pltpu.VMEM((block_rows(frames, 512), width), F32),
            pltpu.VMEM((block_rows(frames, 512), width), F32),
        ],
        2 * matmul,
        input_bytes + 3 * array_bytes,
    )(
        meta,
        counts,
        stats,
        jnp.stack([norm_gain, norm_shift]),
        select,
        grad_out,
        halo_g,
        out_weight,
        conv,
    )
    w_out = call(
        first_outer_kernel,
        "outer_w_out",
        (recs,),
        [per_record((frames, model)), per_record((frames, width))],
        whole((width, model)),
        sds((width, model), F32),
        [],
        matmul,
        input_bytes,
    )(grad_out, swished)
    sums = exchange(sums, "seq")
    grad_shift, grad_gain = jnp.sum(sums, axis=0)

    blocks = frames // chunk
    parts_in = frames // half_rows

    def back(first, size, *earlier):
        def window(i):
            return (first + i // blocks, pl.multiple_of(i % blocks * chunk, chunk), 0)

        def block(i):
            return (first + i // blocks, i % blocks, 0)

        return call(
            functools.partial(back_kernel, first, blocks),
            "back_conv",
            (size * blocks,),
            [
                smem(),
                smem(),
                whole((seqs, 2, width)),
                whole((seqs, 2, width)),
                whole((1, width)),
                pl.BlockSpec((pl.Element(1), pl.Element(chunk + 2 * EDGE), pl.Element(width)), window),
                pl.BlockSpec((pl.Element(1), pl.Element(chunk + 2 * EDGE), pl.Element(width)), window),
                pl.BlockSpec((1, chunk, width), block),
                pl.BlockSpec((1, chunk, width), block),
                whole((kernel, width)),
            ],
            [pl.BlockSpec((chunk, 2 * width), lambda i: (i, 0)), whole((16, width))],
            [sds((size * frames, 2 * width), BF16), sds((16, width), F32)],
            [
                pltpu.VMEM((halves, chunk + 2 * EDGE, LANES), F32),
                pltpu.VMEM((halves, kernel, 8, LANES), F32),
            ],
            0,
            1024,
        )(meta, counts, stats, sums, norm_gain[None], gn, conv, vl, sg, after(depth_taps, *earlier))

    def partials(first, size, mine, *earlier):
        sibling = lax.ppermute(mine, "tp", swap)
        out = sds((seqs, size, piece, frames), BF16)
        return call(
            partial_kernel,
            "partial_in",
            (size * parts_in,),
            [
                pl.BlockSpec((half_rows, 2 * width), lambda i: (i, 0)),
                pl.BlockSpec((half_rows, 2 * width), lambda i: (i, 0)),
                whole((chips * rows, 2 * width)),
                whole((chips * rows, 2 * width)),
                pl.BlockSpec(
                    (1, rows, half_rows), lambda i: (first + i // parts_in, 0, i % parts_in)
                ),
            ],
            [
                pl.BlockSpec(
                    (seqs, 1, piece, half_rows), lambda i: (0, i // parts_in, 0, i % parts_in)
                )
            ]
            * chips,
            [out] * chips,
            [],
            0,
            1024,
            vmem=20,
        )(mine, sibling, after(w_own, *earlier), w_sibling, picked)

    def deliver(part, *earlier):
        total = after(part[0], *earlier).astype(F32)
        for d in range(1, chips):
            send = [(i, ((i // 2 + d) % chips) * 2 + i % 2) for i in range(tps)]
            total = total + lax.ppermute(part[d], "tp", send).astype(F32)
        own = total.astype(BF16)
        return own, exchange(own, "seq")

    groups = ((0, 1), (1, 1), (2, recs - 2))
    grads = [None] * 3
    taps = [None] * 3
    parts = [None] * 3
    owns = [None] * 3
    moved = [None] * 3
    grads[0], taps[0] = back(*groups[0], w_out)
    grads[1], taps[1] = back(*groups[1], grads[0])
    parts[0] = partials(*groups[0], grads[0], grads[1])
    grads[2], taps[2] = back(*groups[2], *parts[0])
    parts[1] = partials(*groups[1], grads[1], grads[2])
    parts[2] = partials(*groups[2], grads[2], *parts[1])
    owns[0], moved[0] = deliver(parts[0], *parts[2])

    slots = 3 * width + 16 * (width // shard)
    half = sds((seqs // 2, slots, shard), BF16)
    keep, send = call(
        functools.partial(outer_kernel, groups),
        "outer_w_in",
        (recs,),
        [smem(), per_record((frames, model)), whole((width, model))]
        + [
            pl.BlockSpec(
                (frames, 2 * width),
                lambda r, first=first, size=size: (jnp.clip(r - first, 0, size - 1), 0),
            )
            for first, size in groups
        ]
        + [whole((16, width))] * len(groups),
        [whole(half.shape)] * 2,
        [half] * 2,
        [pltpu.VMEM((2 * width, model), F32)],
        0,
        1024,
    )(parity, after(normed, owns[0]), w_out, *grads, *taps)
    pairs = [(i, i ^ 1) for i in range(seqs)]
    others = lax.ppermute(send, "seq", pairs)
    owns[1], moved[1] = deliver(parts[1], keep)
    paired = (after(keep, owns[1]).astype(F32) + others.astype(F32)).astype(BF16)
    same = [[i for i in range(seqs) if i % 2 == odd] for odd in range(2)]
    got = lax.all_to_all(paired, "seq", 0, 0, axis_index_groups=same, tiled=True)
    owns[2], moved[2] = deliver(parts[2], paired)
    w_value, w_gate, w_out, grad_taps = call(
        functools.partial(finish_kernel, kernel),
        "finish",
        (1,),
        [whole(half.shape)],
        [whole((shard, width))] * 3 + [whole((kernel, width))],
        [sds((shard, width), F32)] * 3 + [sds((kernel, width), F32)],
        [],
        0,
        8 * seqs * slots * shard,
        vmem=20,
    )(got)
    grad_in = ()
    for (first, size), part in zip(groups, moved):
        grad_in = (
            call(
                place_kernel,
                "place",
                (size,),
                [pl.BlockSpec((seqs, 1, piece, frames), lambda i: (0, i, 0, 0))]
                + [anywhere()] * len(grad_in),
                pl.BlockSpec((1, piece, seqs * frames), lambda i, first=first: (first + i, 0, 0)),
                sds((recs, piece, seqs * frames), BF16),
                [],
                0,
                4 * size * piece * seqs * frames,
                {1: 0} if grad_in else None,
                vmem=20,
            )(part, *grad_in),
        )
    (grad_in,) = grad_in
    return (grad_in, w_value, w_gate, w_out, grad_taps, grad_gain, grad_shift)


def solution(mesh):
    placed = (
        P(None, "seq", None),
        P(None, "seq", None),
        P(None, "tp"),
        P(None, "tp"),
        P(None, "tp"),
        P("tp"),
        P("tp"),
        P(None, "tp"),
        P(),
    )
    return jax.shard_map(
        per_device,
        mesh=mesh,
        in_specs=placed,
        out_specs=(
            P(None, ("seq", "tp"), None),
            P("seq", "tp"),
            P("seq", "tp"),
            P("seq", "tp"),
            P(None, "tp"),
            P("tp"),
            P("tp"),
        ),
        check_vma=False,
    )
```

```python
import functools

import jax
import jax.numpy as jnp
from jax import lax
from jax.experimental import pallas as pl
from jax.experimental.pallas import tpu as pltpu
from jax.sharding import PartitionSpec as P

EPSILON = 1e-05
EDGE = 8
LANES = 128
F32 = jnp.float32
BF16 = jnp.bfloat16


def sigmoid(x):
    return 0.5 * jnp.tanh(0.5 * x) + 0.5


def dot(a, b):
    return jnp.dot(a, b, preferred_element_type=F32)


def dot_nt(a, b):
    return lax.dot_general(a, b, (((1,), (1,)), ((), ())), preferred_element_type=F32)


def dot_tn(a, b):
    return lax.dot_general(a, b, (((0,), (0,)), ((), ())), preferred_element_type=F32)


def rows_of(count, first):
    return first + lax.broadcasted_iota(jnp.int32, (count, 1), 0)


def fold_rows(x):
    return jnp.sum(x.reshape(x.shape[0] // 8, 8, x.shape[1]), axis=0)


def block_rows(total, most):
    return max(b for b in range(8, most + 1, 8) if total % b == 0)


def whole(shape):
    return pl.BlockSpec(shape, lambda *i: (0,) * len(shape))


def per_record(shape):
    return pl.BlockSpec((1,) + shape, lambda r: (r,) + (0,) * len(shape))


def smem():
    return pl.BlockSpec(memory_space=pltpu.SMEM)


def anywhere():
    return pl.BlockSpec(memory_space=pl.ANY)


def after(x, *earlier):
    return lax.optimization_barrier((x,) + earlier)[0]


def spread_sums(out, sums):
    for s in range(out.shape[0]):
        out[s] = sums


def call(
    kernel, name, grid, in_specs, out_specs, out_shape, scratch, flops, moved, aliases=None, vmem=60
):
    return pl.pallas_call(
        kernel,
        name=name,
        grid=grid,
        in_specs=in_specs,
        out_specs=out_specs,
        out_shape=out_shape,
        scratch_shapes=scratch,
        input_output_aliases=aliases or {},
        cost_estimate=pl.CostEstimate(flops=int(flops), bytes_accessed=int(moved), transcendentals=0),
        compiler_params=pltpu.CompilerParams(vmem_limit_bytes=vmem * 1024 * 1024),
    )


def gate_kernel(meta, x, halo, wv, wg, taps, vl_o, sg_o, conv_o, st_o, gp, st):
    r = pl.program_id(0)
    hi = meta[0, r]
    lo = meta[1, r]
    frames = x.shape[1]
    width = wv.shape[1]
    halves = width // LANES

    def put(row, value):
        for h in range(halves):
            gp[h, pl.ds(row, value.shape[0]), :] = value[:, h * LANES : (h + 1) * LANES]

    edge_v = dot(halo[0], wv[...])
    edge_g = dot(halo[0], wg[...])
    row = rows_of(2 * EDGE, 0)
    pos = jnp.where(row < EDGE, row - EDGE, row - EDGE + frames)
    edge = jnp.where((pos >= lo) & (pos < hi), edge_v * sigmoid(edge_g), 0.0)
    zero = jnp.zeros((EDGE, width), F32)
    put(0, zero)
    put(EDGE, edge[:EDGE])
    put(2 * EDGE + frames, edge[EDGE:])
    put(3 * EDGE + frames, zero)
    step = block_rows(frames, 512)
    small = block_rows(step, 64)
    for base in range(0, frames, step):
        xb = x[0, base : base + step, :]
        vl_o[0, base : base + step, :] = dot(xb, wv[...])
        sg_o[0, base : base + step, :] = dot(xb, wg[...])

    def gating(i, carry):
        base = pl.multiple_of(i * small, small)
        v = vl_o[0, pl.ds(base, small), :]
        s = sigmoid(sg_o[0, pl.ds(base, small), :])
        sg_o[0, pl.ds(base, small), :] = s
        put(2 * EDGE + base, jnp.where(rows_of(small, base) < hi, v * s, 0.0))
        return carry

    lax.fori_loop(0, frames // small, gating, 0)
    span = frames + 2 * EDGE
    cb = block_rows(span, 104)
    kernel = taps.shape[0]
    margin = (kernel - 1) // 2
    for h in range(halves):
        cols = slice(h * LANES, (h + 1) * LANES)

        def convolve(i, carry):
            s1, s2 = carry
            base = pl.multiple_of(i * cb, 8)
            acc = jnp.zeros((cb, LANES), F32)
            for k in range(kernel):
                acc = acc + taps[k : k + 1, cols] * gp[h, pl.ds(base + EDGE - margin + k, cb), :]
            conv_o[0, pl.ds(base, cb), cols] = acc
            pos = rows_of(cb, base - EDGE)
            kept = jnp.where((pos >= 0) & (pos < jnp.minimum(hi, frames)), acc, 0.0)
            return s1 + fold_rows(kept), s2 + fold_rows(kept * kept)

        none = jnp.zeros((8, LANES), F32)
        s1, s2 = lax.fori_loop(0, span // cb, convolve, (none, none))
        add = jnp.concatenate(
            [jnp.sum(s1, axis=0, keepdims=True), jnp.sum(s2, axis=0, keepdims=True)], axis=0
        )
        st[:, cols] = jnp.where(r == 0, 0.0, st[:, cols]) + add

    @pl.when(r == pl.num_programs(0) - 1)
    def _():
        spread_sums(st_o, st[...])


def batch_norm(stats, count):
    sums = jnp.sum(stats[...], axis=0)
    centre = sums[0:1] / count
    spread = sums[1:2] / count - centre * centre
    return centre, lax.rsqrt(spread + EPSILON)


def norm_kernel(
    meta, count, stats, affine, select, grads, halo, wo, conv,
    swished_o, gn_o, picked_o, st_o, st, ping, pong
):
    r = pl.program_id(0)
    hi = meta[0, r]
    lo = meta[1, r]
    frames = grads.shape[1]
    centre, inv = batch_norm(stats, count[0, 0])
    gain, shift = affine[0:1, :], affine[1:2, :]

    def part(row, swish_grad):
        size = swish_grad.shape[0]
        unit = (conv[0, pl.ds(row, size), :] - centre) * inv
        normalized = unit * gain + shift
        s = sigmoid(normalized)
        pos = rows_of(size, row - EDGE)
        keep = (pos >= lo) & (pos < hi)
        swished = jnp.where(keep, normalized * s, 0.0)
        gn = jnp.where(keep, swish_grad, 0.0) * (s + normalized * (s - s * s))
        gn_o[0, pl.ds(row, size), :] = gn
        return unit, swished, gn

    edge = dot(halo[0], wo[...])
    part(0, edge[:EDGE])
    part(frames + EDGE, edge[EDGE:])
    step = block_rows(frames, 512)
    small = block_rows(step, 32)
    s1 = jnp.zeros((8, conv.shape[2]), F32)
    s2 = s1
    held = (ping, pong)
    ping[...] = dot(grads[0, :step, :], wo[...])
    for i in range(frames // step):
        now = held[i % 2]
        if (i + 1) * step < frames:
            held[(i + 1) % 2][...] = dot(grads[0, (i + 1) * step : (i + 2) * step, :], wo[...])
        picked_o[0, :, i * step : (i + 1) * step] = dot_nt(
            select[...], grads[0, i * step : (i + 1) * step, :]
        ).astype(BF16)
        for j in range(step // small):
            base = i * step + j * small
            unit, swished, gn = part(base + EDGE, now[j * small : (j + 1) * small, :])
            swished_o[0, base : base + small, :] = swished.astype(BF16)
            s1 = s1 + fold_rows(gn)
            s2 = s2 + fold_rows(gn * unit)
    add = jnp.concatenate(
        [jnp.sum(s1, axis=0, keepdims=True), jnp.sum(s2, axis=0, keepdims=True)], axis=0
    )
    st[...] = jnp.where(r == 0, 0.0, st[...]) + add

    @pl.when(r == pl.num_programs(0) - 1)
    def _():
        spread_sums(st_o, st[...])


def back_kernel(
    record, blocks, meta, count, stats, sums, gain, gn, conv, vl, sg, taps, out, taps_o, gc, acc
):
    i = pl.program_id(0)
    frames, width = vl.shape[1:]
    hi = meta[0, record + i // blocks]
    lo = meta[1, record + i // blocks]
    halves = width // LANES
    span = frames + 2 * EDGE
    kernel = taps.shape[0]
    margin = (kernel - 1) // 2
    cb = block_rows(span, 144)
    step = block_rows(frames, 64)
    total_frames = count[0, 0]
    centre, inv = batch_norm(stats, total_frames)
    grad_sums = jnp.sum(sums[...], axis=0)
    scale = gain[...] * inv
    offset = scale * grad_sums[0:1] / total_frames
    slope = scale * inv * grad_sums[1:2] / total_frames
    first = i % blocks * frames

    @pl.when(i == 0)
    def _():
        acc[...] = jnp.zeros_like(acc)

    for h in range(halves):
        cols = slice(h * LANES, (h + 1) * LANES)
        for base in range(0, span, cb):
            pos = rows_of(cb, first + (base - EDGE))
            mean = offset[:, cols] + (conv[0, base : base + cb, cols] - centre[:, cols]) * slope[:, cols]
            gc[h, base : base + cb, :] = scale[:, cols] * gn[0, base : base + cb, cols] - jnp.where(
                (pos >= lo) & (pos < hi), mean, 0.0
            )
        sums_k = [acc[h, k] for k in range(kernel)]
        for base in range(0, frames, step):
            v = vl[0, base : base + step, cols]
            s = sg[0, base : base + step, cols]
            keep = rows_of(step, first + base) < hi
            vs = v * s
            gated = jnp.where(keep, vs, 0.0)
            total = jnp.zeros((step, LANES), F32)
            for k in range(kernel):
                window = gc[h, base + EDGE + margin - k : base + EDGE + margin - k + step, :]
                total = total + taps[k : k + 1, cols] * window
                sums_k[k] = sums_k[k] + fold_rows(window * gated)
            total = jnp.where(keep, total, 0.0)
            out[base : base + step, cols] = (total * s).astype(BF16)
            out[base : base + step, width + h * LANES : width + (h + 1) * LANES] = (
                total * (vs - vs * s)
            ).astype(BF16)
        for k in range(kernel):
            acc[h, k] = sums_k[k]

    @pl.when(i == pl.num_programs(0) - 1)
    def _():
        taps_o[...] = jnp.zeros_like(taps_o)
        for h in range(halves):
            for k in range(kernel):
                taps_o[k : k + 1, h * LANES : (h + 1) * LANES] = jnp.sum(
                    acc[h, k], axis=0, keepdims=True
                )


def partial_kernel(own, sibling, w_own, w_sibling, picked, mine, *others):
    total = dot_nt(w_own[...], own[...]) + dot_nt(w_sibling[...], sibling[...])
    rows = picked.shape[1]
    seqs, _, piece, frames = mine.shape
    mine[...] = (
        (total[:rows] + picked[0].astype(F32)).astype(BF16).reshape(seqs, 1, piece, frames)
    )
    for d, other in enumerate(others):
        other[...] = (
            total[(d + 1) * rows : (d + 2) * rows].astype(BF16).reshape(seqs, 1, piece, frames)
        )


def first_outer_kernel(grads, swished, out):
    r = pl.program_id(0)
    add = dot_tn(swished[0], grads[0])

    @pl.when(r == 0)
    def _():
        out[...] = add

    @pl.when(r > 0)
    def _():
        out[...] += add


def outer_kernel(groups, parity, x, w_out, *refs):
    lefts, taps = refs[: len(groups)], refs[len(groups) : 2 * len(groups)]
    keep, send, acc = refs[2 * len(groups) :]
    records = groups[-1][0] + groups[-1][1]
    width = w_out.shape[0]
    shard = keep.shape[2]
    r = pl.program_id(0)
    for (first, size), left in zip(groups, lefts):

        @pl.when((r >= first) & (r < first + size))
        def _(left=left):
            add = dot_tn(left[...], x[0])
            acc[...] = add + jnp.where(r == 0, 0.0, acc[...])

    @pl.when(r == records - 1)
    def _():
        tap_sums = taps[0][...]
        for part in taps[1:]:
            tap_sums = tap_sums + part[...]

        def write(place, odd):
            for j in range(place.shape[0]):
                at = (2 * j + odd) * shard
                place[j, : 2 * width, :] = acc[:, at : at + shard].astype(BF16)
                place[j, 2 * width : 3 * width, :] = w_out[:, at : at + shard].astype(BF16)
                for q in range(width // shard):
                    row = 3 * width + 16 * q
                    place[j, row : row + 16, :] = tap_sums[:, q * shard : (q + 1) * shard].astype(
                        BF16
                    )

        @pl.when(parity[0, 0] == 0)
        def _():
            write(keep, 0)
            write(send, 1)

        @pl.when(parity[0, 0] != 0)
        def _():
            write(keep, 1)
            write(send, 0)


def finish_kernel(kernel, got, value, gate, out, taps):
    width = value.shape[1]
    shard = value.shape[0]

    def total(row, size):
        sums = got[0, row : row + size, :].astype(F32)
        for j in range(1, got.shape[0]):
            sums = sums + got[j, row : row + size, :].astype(F32)
        return sums

    for i, place in enumerate((value, gate, out)):
        place[...] = total(i * width, width).T
    for q in range(width // shard):
        taps[:, q * shard : (q + 1) * shard] = total(3 * width + 16 * q, 16)[:kernel]


def place_kernel(moved, *refs):
    out = refs[-1]
    frames = moved.shape[3]
    for s in range(moved.shape[0]):
        out[0, :, s * frames : (s + 1) * frames] = moved[s, 0]


def exchange(copies, axis):
    return lax.all_to_all(copies, axis, 0, 0, tiled=True)


def per_device(
    normed,
    grad_out,
    value_weight,
    gate_weight,
    depth_taps,
    norm_gain,
    norm_shift,
    out_weight,
    lengths,
):
    recs, frames, model = normed.shape
    kernel = depth_taps.shape[0]
    width = value_weight.shape[1]
    seqs = lax.axis_size("seq")
    tps = lax.axis_size("tp")
    chips = tps // 2
    piece = model // (seqs * tps)
    rows = seqs * piece
    shard = model // seqs
    span = frames + 2 * EDGE
    seq_at = lax.axis_index("seq")
    tp_at = lax.axis_index("tp")
    chip_at, core_at = tp_at // 2, tp_at % 2
    count = jnp.sum(lengths).astype(F32)
    first = (seq_at * frames).astype(jnp.int32)
    meta = jnp.stack([lengths - first, jnp.full((recs,), 0, jnp.int32) - first])
    halves = width // LANES
    counts = count.reshape(1, 1)
    parity = (seq_at % 2).astype(jnp.int32).reshape(1, 1)
    sds = jax.ShapeDtypeStruct

    low_edge = jnp.concatenate([normed[:, -EDGE:], grad_out[:, -EDGE:]], axis=2)
    high_edge = jnp.concatenate([normed[:, :EDGE], grad_out[:, :EDGE]], axis=2)
    up = [(i, i + 1) for i in range(seqs - 1)]
    down = [(j, i) for i, j in up]
    halo = jnp.concatenate(
        [lax.ppermute(low_edge, "seq", up), lax.ppermute(high_edge, "seq", down)], axis=1
    )
    halo_x, halo_g = halo[:, :, :model], halo[:, :, model:]

    both = jnp.concatenate([value_weight, gate_weight], axis=1).reshape(seqs, tps, piece, 2 * width)

    def chosen(core):
        picks = [
            lax.dynamic_index_in_dim(both, ((chip_at + d) % chips) * 2 + core, 1, keepdims=False)
            for d in range(chips)
        ]
        return jnp.stack(picks).reshape(chips * rows, 2 * width)

    swap = [(i, i ^ 1) for i in range(tps)]
    w_own = chosen(core_at)
    w_sibling = lax.ppermute(chosen(1 - core_at), "tp", swap)

    channel = (
        jnp.arange(seqs, dtype=jnp.int32)[:, None] * (tps * piece)
        + tp_at * piece
        + jnp.arange(piece, dtype=jnp.int32)[None, :]
    ).reshape(rows, 1)
    select = (channel == jnp.arange(model, dtype=jnp.int32)[None, :]).astype(BF16)
    array_bytes = recs * frames * width * 4
    input_bytes = recs * frames * model * 2
    matmul = 2 * recs * frames * model * width

    vl, sg, conv, stats = call(
        gate_kernel,
        "gate_conv",
        (recs,),
        [
            smem(),
            per_record((frames, model)),
            per_record((2 * EDGE, model)),
            whole((model, width)),
            whole((model, width)),
            whole((kernel, width)),
        ],
        [
            per_record((frames, width)),
            per_record((frames, width)),
            per_record((span, width)),
            whole((seqs, 2, width)),
        ],
        [
            sds((recs, frames, width), F32),
            sds((recs, frames, width), F32),
            sds((recs, span, width), F32),
            sds((seqs, 2, width), F32),
        ],
        [pltpu.VMEM((halves, frames + 4 * EDGE, LANES), F32), pltpu.VMEM((2, width), F32)],
        2 * matmul,
        input_bytes + 3 * array_bytes,
    )(meta, normed, halo_x, value_weight, gate_weight, depth_taps)
    stats = exchange(stats, "seq")

    chunk = block_rows(frames, 256)
    half_rows = block_rows(frames, 512)
    swished, gn, picked, sums = call(
        norm_kernel,
        "swish_norm",
        (recs,),
        [
            smem(),
            smem(),
            whole((seqs, 2, width)),
            whole((2, width)),
            whole((rows, model)),
            per_record((frames, model)),
            per_record((2 * EDGE, model)),
            whole((model, width)),
            per_record((span, width)),
        ],
        [
            per_record((frames, width)),
            per_record((span, width)),
            per_record((rows, frames)),
            whole((seqs, 2, width)),
        ],
        [
            sds((recs, frames, width), BF16),
            sds((recs, span, width), F32),
            sds((recs, rows, frames), BF16),
            sds((seqs, 2, width), F32),
        ],
        [
            pltpu.VMEM((2, width), F32),
            pltpu.VMEM((block_rows(frames, 512), width), F32),
            pltpu.VMEM((block_rows(frames, 512), width), F32),
        ],
        2 * matmul,
        input_bytes + 3 * array_bytes,
    )(
        meta,
        counts,
        stats,
        jnp.stack([norm_gain, norm_shift]),
        select,
        grad_out,
        halo_g,
        out_weight,
        conv,
    )
    w_out = call(
        first_outer_kernel,
        "outer_w_out",
        (recs,),
        [per_record((frames, model)), per_record((frames, width))],
        whole((width, model)),
        sds((width, model), F32),
        [],
        matmul,
        input_bytes,
    )(grad_out, swished)
    sums = exchange(sums, "seq")
    grad_shift, grad_gain = jnp.sum(sums, axis=0)

    blocks = frames // chunk
    parts_in = frames // half_rows

    def back(first, size, *earlier):
        def window(i):
            return (first + i // blocks, pl.multiple_of(i % blocks * chunk, chunk), 0)

        def block(i):
            return (first + i // blocks, i % blocks, 0)

        return call(
            functools.partial(back_kernel, first, blocks),
            "back_conv",
            (size * blocks,),
            [
                smem(),
                smem(),
                whole((seqs, 2, width)),
                whole((seqs, 2, width)),
                whole((1, width)),
                pl.BlockSpec((pl.Element(1), pl.Element(chunk + 2 * EDGE), pl.Element(width)), window),
                pl.BlockSpec((pl.Element(1), pl.Element(chunk + 2 * EDGE), pl.Element(width)), window),
                pl.BlockSpec((1, chunk, width), block),
                pl.BlockSpec((1, chunk, width), block),
                whole((kernel, width)),
            ],
            [pl.BlockSpec((chunk, 2 * width), lambda i: (i, 0)), whole((16, width))],
            [sds((size * frames, 2 * width), BF16), sds((16, width), F32)],
            [
                pltpu.VMEM((halves, chunk + 2 * EDGE, LANES), F32),
                pltpu.VMEM((halves, kernel, 8, LANES), F32),
            ],
            0,
            1024,
        )(meta, counts, stats, sums, norm_gain[None], gn, conv, vl, sg, after(depth_taps, *earlier))

    def partials(first, size, mine, *earlier):
        sibling = lax.ppermute(mine, "tp", swap)
        out = sds((seqs, size, piece, frames), BF16)
        return call(
            partial_kernel,
            "partial_in",
            (size * parts_in,),
            [
                pl.BlockSpec((half_rows, 2 * width), lambda i: (i, 0)),
                pl.BlockSpec((half_rows, 2 * width), lambda i: (i, 0)),
                whole((chips * rows, 2 * width)),
                whole((chips * rows, 2 * width)),
                pl.BlockSpec(
                    (1, rows, half_rows), lambda i: (first + i // parts_in, 0, i % parts_in)
                ),
            ],
            [
                pl.BlockSpec(
                    (seqs, 1, piece, half_rows), lambda i: (0, i // parts_in, 0, i % parts_in)
                )
            ]
            * chips,
            [out] * chips,
            [],
            50_000_000_000,
            1024,
            vmem=20,
        )(mine, sibling, after(w_own, *earlier), w_sibling, picked)

    def deliver(part, *earlier):
        total = after(part[0], *earlier).astype(F32)
        for d in range(1, chips):
            send = [(i, ((i // 2 + d) % chips) * 2 + i % 2) for i in range(tps)]
            total = total + lax.ppermute(part[d], "tp", send).astype(F32)
        own = total.astype(BF16)
        return own, exchange(own, "seq")

    groups = ((0, 1), (1, 1), (2, recs - 2))
    grads = [None] * 3
    taps = [None] * 3
    parts = [None] * 3
    owns = [None] * 3
    moved = [None] * 3
    grads[0], taps[0] = back(*groups[0], w_out)
    grads[1], taps[1] = back(*groups[1], grads[0])
    parts[0] = partials(*groups[0], grads[0], grads[1])
    grads[2], taps[2] = back(*groups[2], *parts[0])
    owns[0], moved[0] = deliver(parts[0], grads[2])
    parts[1] = partials(*groups[1], grads[1], owns[0])
    parts[2] = partials(*groups[2], grads[2], *parts[1])
    owns[1], moved[1] = deliver(parts[1], *parts[2])

    slots = 3 * width + 16 * (width // shard)
    half = sds((seqs // 2, slots, shard), BF16)
    keep, send = call(
        functools.partial(outer_kernel, groups),
        "outer_w_in",
        (recs,),
        [smem(), per_record((frames, model)), whole((width, model))]
        + [
            pl.BlockSpec(
                (frames, 2 * width),
                lambda r, first=first, size=size: (jnp.clip(r - first, 0, size - 1), 0),
            )
            for first, size in groups
        ]
        + [whole((16, width))] * len(groups),
        [whole(half.shape)] * 2,
        [half] * 2,
        [pltpu.VMEM((2 * width, model), F32)],
        50_000_000_000,
        1024,
    )(parity, after(normed, owns[1]), w_out, *grads, *taps)
    pairs = [(i, i ^ 1) for i in range(seqs)]
    others = lax.ppermute(send, "seq", pairs)
    owns[2], moved[2] = deliver(parts[2], keep)
    paired = (after(keep, owns[2]).astype(F32) + others.astype(F32)).astype(BF16)
    same = [[i for i in range(seqs) if i % 2 == odd] for odd in range(2)]
    got = lax.all_to_all(paired, "seq", 0, 0, axis_index_groups=same, tiled=True)
    w_value, w_gate, w_out, grad_taps = call(
        functools.partial(finish_kernel, kernel),
        "finish",
        (1,),
        [whole(half.shape)],
        [whole((shard, width))] * 3 + [whole((kernel, width))],
        [sds((shard, width), F32)] * 3 + [sds((kernel, width), F32)],
        [],
        0,
        8 * seqs * slots * shard,
        vmem=20,
    )(got)
    grad_in = ()
    for (first, size), part in zip(groups, moved):
        grad_in = (
            call(
                place_kernel,
                "place",
                (size,),
                [pl.BlockSpec((seqs, 1, piece, frames), lambda i: (0, i, 0, 0))]
                + [anywhere()] * len(grad_in),
                pl.BlockSpec((1, piece, seqs * frames), lambda i, first=first: (first + i, 0, 0)),
                sds((recs, piece, seqs * frames), BF16),
                [],
                0,
                4 * size * piece * seqs * frames,
                {1: 0} if grad_in else None,
                vmem=20,
            )(part, *grad_in),
        )
    (grad_in,) = grad_in
    return (grad_in, w_value, w_gate, w_out, grad_taps, grad_gain, grad_shift)


def solution(mesh):
    placed = (
        P(None, "seq", None),
        P(None, "seq", None),
        P(None, "tp"),
        P(None, "tp"),
        P(None, "tp"),
        P("tp"),
        P("tp"),
        P(None, "tp"),
        P(),
    )
    return jax.shard_map(
        per_device,
        mesh=mesh,
        in_specs=placed,
        out_specs=(
            P(None, ("seq", "tp"), None),
            P("seq", "tp"),
            P("seq", "tp"),
            P("seq", "tp"),
            P(None, "tp"),
            P("tp"),
            P("tp"),
        ),
        check_vma=False,
    )
```

```python
import functools

import jax
import jax.numpy as jnp
from jax import lax
from jax.experimental import pallas as pl
from jax.experimental.pallas import tpu as pltpu
from jax.sharding import PartitionSpec as P

EPSILON = 1e-05
EDGE = 8
LANES = 128
F32 = jnp.float32
BF16 = jnp.bfloat16


def sigmoid(x):
    return 0.5 * jnp.tanh(0.5 * x) + 0.5


def dot(a, b):
    return jnp.dot(a, b, preferred_element_type=F32)


def dot_nt(a, b):
    return lax.dot_general(a, b, (((1,), (1,)), ((), ())), preferred_element_type=F32)


def dot_tn(a, b):
    return lax.dot_general(a, b, (((0,), (0,)), ((), ())), preferred_element_type=F32)


def rows_of(count, first):
    return first + lax.broadcasted_iota(jnp.int32, (count, 1), 0)


def fold_rows(x):
    return jnp.sum(x.reshape(x.shape[0] // 8, 8, x.shape[1]), axis=0)


def block_rows(total, most):
    return max(b for b in range(8, most + 1, 8) if total % b == 0)


def whole(shape):
    return pl.BlockSpec(shape, lambda *i: (0,) * len(shape))


def per_record(shape):
    return pl.BlockSpec((1,) + shape, lambda r: (r,) + (0,) * len(shape))


def smem():
    return pl.BlockSpec(memory_space=pltpu.SMEM)


def anywhere():
    return pl.BlockSpec(memory_space=pl.ANY)


def after(x, *earlier):
    return lax.optimization_barrier((x,) + earlier)[0]


def spread_sums(out, sums):
    for s in range(out.shape[0]):
        out[s] = sums


def call(
    kernel, name, grid, in_specs, out_specs, out_shape, scratch, flops, moved, aliases=None, vmem=63
):
    return pl.pallas_call(
        kernel,
        name=name,
        grid=grid,
        in_specs=in_specs,
        out_specs=out_specs,
        out_shape=out_shape,
        scratch_shapes=scratch,
        input_output_aliases=aliases or {},
        cost_estimate=pl.CostEstimate(flops=int(flops), bytes_accessed=int(moved), transcendentals=0),
        compiler_params=pltpu.CompilerParams(vmem_limit_bytes=vmem * 1024 * 1024),
    )


def gate_kernel(meta, x, halo, wv, wg, taps, vl_o, sg_o, conv_o, st_o, gp, st):
    r = pl.program_id(0)
    hi = meta[0, r]
    lo = meta[1, r]
    frames = x.shape[1]
    width = wv.shape[1]
    halves = width // LANES

    def put(row, value):
        for h in range(halves):
            gp[h, pl.ds(row, value.shape[0]), :] = value[:, h * LANES : (h + 1) * LANES]

    edge_v = dot(halo[0], wv[...])
    edge_g = dot(halo[0], wg[...])
    row = rows_of(2 * EDGE, 0)
    pos = jnp.where(row < EDGE, row - EDGE, row - EDGE + frames)
    edge = jnp.where((pos >= lo) & (pos < hi), edge_v * sigmoid(edge_g), 0.0)
    zero = jnp.zeros((EDGE, width), F32)
    put(0, zero)
    put(EDGE, edge[:EDGE])
    put(2 * EDGE + frames, edge[EDGE:])
    put(3 * EDGE + frames, zero)
    step = block_rows(frames, 512)
    small = block_rows(step, 64)
    for base in range(0, frames, step):
        xb = x[0, base : base + step, :]
        vl_o[0, base : base + step, :] = dot(xb, wv[...])
        sg_o[0, base : base + step, :] = dot(xb, wg[...])

    def gating(i, carry):
        base = pl.multiple_of(i * small, small)
        v = vl_o[0, pl.ds(base, small), :]
        s = sigmoid(sg_o[0, pl.ds(base, small), :])
        sg_o[0, pl.ds(base, small), :] = s
        put(2 * EDGE + base, jnp.where(rows_of(small, base) < hi, v * s, 0.0))
        return carry

    lax.fori_loop(0, frames // small, gating, 0)
    span = frames + 2 * EDGE
    cb = block_rows(span, 104)
    kernel = taps.shape[0]
    margin = (kernel - 1) // 2
    for h in range(halves):
        cols = slice(h * LANES, (h + 1) * LANES)

        def convolve(i, carry):
            s1, s2 = carry
            base = pl.multiple_of(i * cb, 8)
            acc = jnp.zeros((cb, LANES), F32)
            for k in range(kernel):
                acc = acc + taps[k : k + 1, cols] * gp[h, pl.ds(base + EDGE - margin + k, cb), :]
            conv_o[0, pl.ds(base, cb), cols] = acc
            pos = rows_of(cb, base - EDGE)
            kept = jnp.where((pos >= 0) & (pos < jnp.minimum(hi, frames)), acc, 0.0)
            return s1 + fold_rows(kept), s2 + fold_rows(kept * kept)

        none = jnp.zeros((8, LANES), F32)
        s1, s2 = lax.fori_loop(0, span // cb, convolve, (none, none))
        add = jnp.concatenate(
            [jnp.sum(s1, axis=0, keepdims=True), jnp.sum(s2, axis=0, keepdims=True)], axis=0
        )
        st[:, cols] = jnp.where(r == 0, 0.0, st[:, cols]) + add

    @pl.when(r == pl.num_programs(0) - 1)
    def _():
        spread_sums(st_o, st[...])


def batch_norm(stats, count):
    sums = jnp.sum(stats[...], axis=0)
    centre = sums[0:1] / count
    spread = sums[1:2] / count - centre * centre
    return centre, lax.rsqrt(spread + EPSILON)


def norm_kernel(
    meta, count, stats, affine, select, grads, halo, wo, conv,
    swished_o, gn_o, picked_o, st_o, st, ping, pong
):
    r = pl.program_id(0)
    hi = meta[0, r]
    lo = meta[1, r]
    frames = grads.shape[1]
    centre, inv = batch_norm(stats, count[0, 0])
    gain, shift = affine[0:1, :], affine[1:2, :]

    def part(row, swish_grad):
        size = swish_grad.shape[0]
        unit = (conv[0, pl.ds(row, size), :] - centre) * inv
        normalized = unit * gain + shift
        s = sigmoid(normalized)
        pos = rows_of(size, row - EDGE)
        keep = (pos >= lo) & (pos < hi)
        swished = jnp.where(keep, normalized * s, 0.0)
        gn = jnp.where(keep, swish_grad, 0.0) * (s + normalized * (s - s * s))
        gn_o[0, pl.ds(row, size), :] = gn
        return unit, swished, gn

    edge = dot(halo[0], wo[...])
    part(0, edge[:EDGE])
    part(frames + EDGE, edge[EDGE:])
    step = block_rows(frames, 512)
    small = block_rows(step, 32)
    s1 = jnp.zeros((8, conv.shape[2]), F32)
    s2 = s1
    held = (ping, pong)
    ping[...] = dot(grads[0, :step, :], wo[...])
    for i in range(frames // step):
        now = held[i % 2]
        if (i + 1) * step < frames:
            held[(i + 1) % 2][...] = dot(grads[0, (i + 1) * step : (i + 2) * step, :], wo[...])
        picked_o[0, :, i * step : (i + 1) * step] = dot_nt(
            select[...], grads[0, i * step : (i + 1) * step, :]
        ).astype(BF16)
        for j in range(step // small):
            base = i * step + j * small
            unit, swished, gn = part(base + EDGE, now[j * small : (j + 1) * small, :])
            swished_o[0, base : base + small, :] = swished.astype(BF16)
            s1 = s1 + fold_rows(gn)
            s2 = s2 + fold_rows(gn * unit)
    add = jnp.concatenate(
        [jnp.sum(s1, axis=0, keepdims=True), jnp.sum(s2, axis=0, keepdims=True)], axis=0
    )
    st[...] = jnp.where(r == 0, 0.0, st[...]) + add

    @pl.when(r == pl.num_programs(0) - 1)
    def _():
        spread_sums(st_o, st[...])


def back_kernel(
    record, blocks, meta, count, stats, sums, gain, gn, conv, vl, sg, taps, out, taps_o, gc, acc
):
    i = pl.program_id(0)
    frames, width = vl.shape[1:]
    hi = meta[0, record + i // blocks]
    lo = meta[1, record + i // blocks]
    halves = width // LANES
    span = frames + 2 * EDGE
    kernel = taps.shape[0]
    margin = (kernel - 1) // 2
    cb = block_rows(span, 144)
    step = block_rows(frames, 64)
    total_frames = count[0, 0]
    centre, inv = batch_norm(stats, total_frames)
    grad_sums = jnp.sum(sums[...], axis=0)
    scale = gain[...] * inv
    offset = scale * grad_sums[0:1] / total_frames
    slope = scale * inv * grad_sums[1:2] / total_frames
    first = i % blocks * frames

    @pl.when(i == 0)
    def _():
        acc[...] = jnp.zeros_like(acc)

    for h in range(halves):
        cols = slice(h * LANES, (h + 1) * LANES)
        for base in range(0, span, cb):
            pos = rows_of(cb, first + (base - EDGE))
            mean = offset[:, cols] + (conv[0, base : base + cb, cols] - centre[:, cols]) * slope[:, cols]
            gc[h, base : base + cb, :] = scale[:, cols] * gn[0, base : base + cb, cols] - jnp.where(
                (pos >= lo) & (pos < hi), mean, 0.0
            )
        sums_k = [acc[h, k] for k in range(kernel)]
        for base in range(0, frames, step):
            v = vl[0, base : base + step, cols]
            s = sg[0, base : base + step, cols]
            keep = rows_of(step, first + base) < hi
            vs = v * s
            gated = jnp.where(keep, vs, 0.0)
            total = jnp.zeros((step, LANES), F32)
            for k in range(kernel):
                window = gc[h, base + EDGE + margin - k : base + EDGE + margin - k + step, :]
                total = total + taps[k : k + 1, cols] * window
                sums_k[k] = sums_k[k] + fold_rows(window * gated)
            total = jnp.where(keep, total, 0.0)
            out[base : base + step, cols] = (total * s).astype(BF16)
            out[base : base + step, width + h * LANES : width + (h + 1) * LANES] = (
                total * (vs - vs * s)
            ).astype(BF16)
        for k in range(kernel):
            acc[h, k] = sums_k[k]

    @pl.when(i == pl.num_programs(0) - 1)
    def _():
        taps_o[...] = jnp.zeros_like(taps_o)
        for h in range(halves):
            for k in range(kernel):
                taps_o[k : k + 1, h * LANES : (h + 1) * LANES] = jnp.sum(
                    acc[h, k], axis=0, keepdims=True
                )


def partial_kernel(own, sibling, w_own, w_sibling, picked, mine, *others):
    total = dot_nt(w_own[...], own[...]) + dot_nt(w_sibling[...], sibling[...])
    rows = picked.shape[1]
    seqs, _, piece, frames = mine.shape
    mine[...] = (
        (total[:rows] + picked[0].astype(F32)).astype(BF16).reshape(seqs, 1, piece, frames)
    )
    for d, other in enumerate(others):
        other[...] = (
            total[(d + 1) * rows : (d + 2) * rows].astype(BF16).reshape(seqs, 1, piece, frames)
        )


def add_kernel(*refs):
    total = refs[0][...].astype(F32)
    for other in refs[1:-1]:
        total = total + other[...].astype(F32)
    refs[-1][...] = total.astype(BF16)


def first_outer_kernel(grads, swished, out):
    r = pl.program_id(0)
    add = dot_tn(swished[0], grads[0])

    @pl.when(r == 0)
    def _():
        out[...] = add

    @pl.when(r > 0)
    def _():
        out[...] += add


def outer_kernel(groups, parity, x, w_out, *refs):
    lefts, taps = refs[: len(groups)], refs[len(groups) : 2 * len(groups)]
    keep, send, acc = refs[2 * len(groups) :]
    records = groups[-1][0] + groups[-1][1]
    width = w_out.shape[0]
    shard = keep.shape[2]
    r = pl.program_id(0)
    for (first, size), left in zip(groups, lefts):

        @pl.when((r >= first) & (r < first + size))
        def _(left=left):
            add = dot_tn(left[...], x[0])
            acc[...] = add + jnp.where(r == 0, 0.0, acc[...])

    @pl.when(r == records - 1)
    def _():
        tap_sums = taps[0][...]
        for part in taps[1:]:
            tap_sums = tap_sums + part[...]

        def write(place, odd):
            for j in range(place.shape[0]):
                at = (2 * j + odd) * shard
                place[j, : 2 * width, :] = acc[:, at : at + shard].astype(BF16)
                place[j, 2 * width : 3 * width, :] = w_out[:, at : at + shard].astype(BF16)
                for q in range(width // shard):
                    row = 3 * width + 16 * q
                    place[j, row : row + 16, :] = tap_sums[:, q * shard : (q + 1) * shard].astype(
                        BF16
                    )

        @pl.when(parity[0, 0] == 0)
        def _():
            write(keep, 0)
            write(send, 1)

        @pl.when(parity[0, 0] != 0)
        def _():
            write(keep, 1)
            write(send, 0)


def finish_kernel(kernel, got, value, gate, out, taps):
    width = value.shape[1]
    shard = value.shape[0]

    def total(row, size):
        sums = got[0, row : row + size, :].astype(F32)
        for j in range(1, got.shape[0]):
            sums = sums + got[j, row : row + size, :].astype(F32)
        return sums

    for i, place in enumerate((value, gate, out)):
        place[...] = total(i * width, width).T
    for q in range(width // shard):
        taps[:, q * shard : (q + 1) * shard] = total(3 * width + 16 * q, 16)[:kernel]


def place_kernel(moved, *refs):
    out = refs[-1]
    frames = moved.shape[3]
    for s in range(moved.shape[0]):
        out[0, :, s * frames : (s + 1) * frames] = moved[s, 0]


def exchange(copies, axis):
    return lax.all_to_all(copies, axis, 0, 0, tiled=True)


def per_device(
    normed,
    grad_out,
    value_weight,
    gate_weight,
    depth_taps,
    norm_gain,
    norm_shift,
    out_weight,
    lengths,
):
    recs, frames, model = normed.shape
    kernel = depth_taps.shape[0]
    width = value_weight.shape[1]
    seqs = lax.axis_size("seq")
    tps = lax.axis_size("tp")
    chips = tps // 2
    piece = model // (seqs * tps)
    rows = seqs * piece
    shard = model // seqs
    span = frames + 2 * EDGE
    seq_at = lax.axis_index("seq")
    tp_at = lax.axis_index("tp")
    chip_at, core_at = tp_at // 2, tp_at % 2
    count = jnp.sum(lengths).astype(F32)
    first = (seq_at * frames).astype(jnp.int32)
    meta = jnp.stack([lengths - first, jnp.full((recs,), 0, jnp.int32) - first])
    halves = width // LANES
    counts = count.reshape(1, 1)
    parity = (seq_at % 2).astype(jnp.int32).reshape(1, 1)
    sds = jax.ShapeDtypeStruct

    low_edge = jnp.concatenate([normed[:, -EDGE:], grad_out[:, -EDGE:]], axis=2)
    high_edge = jnp.concatenate([normed[:, :EDGE], grad_out[:, :EDGE]], axis=2)
    up = [(i, i + 1) for i in range(seqs - 1)]
    down = [(j, i) for i, j in up]
    halo = jnp.concatenate(
        [lax.ppermute(low_edge, "seq", up), lax.ppermute(high_edge, "seq", down)], axis=1
    )
    halo_x, halo_g = halo[:, :, :model], halo[:, :, model:]

    both = jnp.concatenate([value_weight, gate_weight], axis=1).reshape(seqs, tps, piece, 2 * width)

    def chosen(core):
        picks = [
            lax.dynamic_index_in_dim(both, ((chip_at + d) % chips) * 2 + core, 1, keepdims=False)
            for d in range(chips)
        ]
        return jnp.stack(picks).reshape(chips * rows, 2 * width)

    swap = [(i, i ^ 1) for i in range(tps)]
    w_own = chosen(core_at)
    w_sibling = lax.ppermute(chosen(1 - core_at), "tp", swap)

    channel = (
        jnp.arange(seqs, dtype=jnp.int32)[:, None] * (tps * piece)
        + tp_at * piece
        + jnp.arange(piece, dtype=jnp.int32)[None, :]
    ).reshape(rows, 1)
    select = (channel == jnp.arange(model, dtype=jnp.int32)[None, :]).astype(BF16)
    array_bytes = recs * frames * width * 4
    input_bytes = recs * frames * model * 2
    matmul = 2 * recs * frames * model * width

    vl, sg, conv, stats = call(
        gate_kernel,
        "gate_conv",
        (recs,),
        [
            smem(),
            per_record((frames, model)),
            per_record((2 * EDGE, model)),
            whole((model, width)),
            whole((model, width)),
            whole((kernel, width)),
        ],
        [
            per_record((frames, width)),
            per_record((frames, width)),
            per_record((span, width)),
            whole((seqs, 2, width)),
        ],
        [
            sds((recs, frames, width), F32),
            sds((recs, frames, width), F32),
            sds((recs, span, width), F32),
            sds((seqs, 2, width), F32),
        ],
        [pltpu.VMEM((halves, frames + 4 * EDGE, LANES), F32), pltpu.VMEM((2, width), F32)],
        2 * matmul,
        input_bytes + 3 * array_bytes,
    )(meta, normed, halo_x, value_weight, gate_weight, depth_taps)
    stats = exchange(stats, "seq")

    chunk = block_rows(frames, 256)
    half_rows = block_rows(frames, 512)
    swished, gn, picked, sums = call(
        norm_kernel,
        "swish_norm",
        (recs,),
        [
            smem(),
            smem(),
            whole((seqs, 2, width)),
            whole((2, width)),
            whole((rows, model)),
            per_record((frames, model)),
            per_record((2 * EDGE, model)),
            whole((model, width)),
            per_record((span, width)),
        ],
        [
            per_record((frames, width)),
            per_record((span, width)),
            per_record((rows, frames)),
            whole((seqs, 2, width)),
        ],
        [
            sds((recs, frames, width), BF16),
            sds((recs, span, width), F32),
            sds((recs, rows, frames), BF16),
            sds((seqs, 2, width), F32),
        ],
        [
            pltpu.VMEM((2, width), F32),
            pltpu.VMEM((block_rows(frames, 512), width), F32),
            pltpu.VMEM((block_rows(frames, 512), width), F32),
        ],
        2 * matmul,
        input_bytes + 3 * array_bytes,
    )(
        meta,
        counts,
        stats,
        jnp.stack([norm_gain, norm_shift]),
        select,
        grad_out,
        halo_g,
        out_weight,
        conv,
    )
    w_out = call(
        first_outer_kernel,
        "outer_w_out",
        (recs,),
        [per_record((frames, model)), per_record((frames, width))],
        whole((width, model)),
        sds((width, model), F32),
        [],
        matmul,
        input_bytes,
    )(grad_out, swished)
    sums = exchange(sums, "seq")
    grad_shift, grad_gain = jnp.sum(sums, axis=0)

    blocks = frames // chunk
    parts_in = frames // half_rows

    def back(first, size, *earlier):
        def window(i):
            return (first + i // blocks, pl.multiple_of(i % blocks * chunk, chunk), 0)

        def block(i):
            return (first + i // blocks, i % blocks, 0)

        return call(
            functools.partial(back_kernel, first, blocks),
            "back_conv",
            (size * blocks,),
            [
                smem(),
                smem(),
                whole((seqs, 2, width)),
                whole((seqs, 2, width)),
                whole((1, width)),
                pl.BlockSpec((pl.Element(1), pl.Element(chunk + 2 * EDGE), pl.Element(width)), window),
                pl.BlockSpec((pl.Element(1), pl.Element(chunk + 2 * EDGE), pl.Element(width)), window),
                pl.BlockSpec((1, chunk, width), block),
                pl.BlockSpec((1, chunk, width), block),
                whole((kernel, width)),
            ],
            [pl.BlockSpec((chunk, 2 * width), lambda i: (i, 0)), whole((16, width))],
            [sds((size * frames, 2 * width), BF16), sds((16, width), F32)],
            [
                pltpu.VMEM((halves, chunk + 2 * EDGE, LANES), F32),
                pltpu.VMEM((halves, kernel, 8, LANES), F32),
            ],
            0,
            1024,
        )(meta, counts, stats, sums, norm_gain[None], gn, conv, vl, sg, after(depth_taps, *earlier))

    def partials(first, size, mine, *earlier):
        sibling = lax.ppermute(mine, "tp", swap)
        out = sds((seqs, size, piece, frames), BF16)
        return call(
            partial_kernel,
            "partial_in",
            (size * parts_in,),
            [
                pl.BlockSpec((half_rows, 2 * width), lambda i: (i, 0)),
                pl.BlockSpec((half_rows, 2 * width), lambda i: (i, 0)),
                whole((chips * rows, 2 * width)),
                whole((chips * rows, 2 * width)),
                pl.BlockSpec(
                    (1, rows, half_rows), lambda i: (first + i // parts_in, 0, i % parts_in)
                ),
            ],
            [
                pl.BlockSpec(
                    (seqs, 1, piece, half_rows), lambda i: (0, i // parts_in, 0, i % parts_in)
                )
            ]
            * chips,
            [out] * chips,
            [],
            0,
            1024,
        )(mine, sibling, after(w_own, *earlier), w_sibling, picked)

    def deliver(part, *earlier):
        arrived = []
        for d in range(1, chips):
            send = [(i, ((i // 2 + d) % chips) * 2 + i % 2) for i in range(tps)]
            arrived.append(lax.ppermute(part[d], "tp", send))
        size = part[0].shape[1]
        block = pl.BlockSpec(
            (seqs, 1, piece, half_rows), lambda i: (0, i // parts_in, 0, i % parts_in)
        )
        own = call(
            add_kernel,
            "add",
            (size * parts_in,),
            [block] * chips,
            block,
            sds(part[0].shape, BF16),
            [],
            50_000_000_000,
            1024,
        )(after(part[0], *earlier), *arrived)
        return own, exchange(own, "seq")

    groups = ((0, 1), (1, 1), (2, recs - 2))
    grads = [None] * 3
    taps = [None] * 3
    parts = [None] * 3
    owns = [None] * 3
    moved = [None] * 3
    grads[0], taps[0] = back(*groups[0], w_out)
    grads[1], taps[1] = back(*groups[1], grads[0])
    parts[0] = partials(*groups[0], grads[0], grads[1])
    grads[2], taps[2] = back(*groups[2], *parts[0])
    parts[1] = partials(*groups[1], grads[1], grads[2])
    owns[0], moved[0] = deliver(parts[0], *parts[1])
    parts[2] = partials(*groups[2], grads[2], owns[0])
    owns[1], moved[1] = deliver(parts[1], *parts[2])

    slots = 3 * width + 16 * (width // shard)
    half = sds((seqs // 2, slots, shard), BF16)
    keep, send = call(
        functools.partial(outer_kernel, groups),
        "outer_w_in",
        (recs,),
        [smem(), per_record((frames, model)), whole((width, model))]
        + [
            pl.BlockSpec(
                (frames, 2 * width),
                lambda r, first=first, size=size: (jnp.clip(r - first, 0, size - 1), 0),
            )
            for first, size in groups
        ]
        + [whole((16, width))] * len(groups),
        [whole(half.shape)] * 2,
        [half] * 2,
        [pltpu.VMEM((2 * width, model), F32)],
        50_000_000_000,
        1024,
    )(parity, after(normed, owns[1]), w_out, *grads, *taps)
    pairs = [(i, i ^ 1) for i in range(seqs)]
    others = lax.ppermute(send, "seq", pairs)
    owns[2], moved[2] = deliver(parts[2], keep)
    paired = (after(keep, owns[2]).astype(F32) + others.astype(F32)).astype(BF16)
    same = [[i for i in range(seqs) if i % 2 == odd] for odd in range(2)]
    got = lax.all_to_all(after(paired, moved[2]), "seq", 0, 0, axis_index_groups=same, tiled=True)
    w_value, w_gate, w_out, grad_taps = call(
        functools.partial(finish_kernel, kernel),
        "finish",
        (1,),
        [whole(half.shape)],
        [whole((shard, width))] * 3 + [whole((kernel, width))],
        [sds((shard, width), F32)] * 3 + [sds((kernel, width), F32)],
        [],
        0,
        8 * seqs * slots * shard,
        vmem=20,
    )(got)
    grad_in = ()
    for (first, size), part in zip(groups, moved):
        grad_in = (
            call(
                place_kernel,
                "place",
                (size,),
                [pl.BlockSpec((seqs, 1, piece, frames), lambda i: (0, i, 0, 0))]
                + [anywhere()] * len(grad_in),
                pl.BlockSpec((1, piece, seqs * frames), lambda i, first=first: (first + i, 0, 0)),
                sds((recs, piece, seqs * frames), BF16),
                [],
                0,
                4 * size * piece * seqs * frames,
                {1: 0} if grad_in else None,
                vmem=20,
            )(part, *grad_in),
        )
    (grad_in,) = grad_in
    return (grad_in, w_value, w_gate, w_out, grad_taps, grad_gain, grad_shift)


def solution(mesh):
    placed = (
        P(None, "seq", None),
        P(None, "seq", None),
        P(None, "tp"),
        P(None, "tp"),
        P(None, "tp"),
        P("tp"),
        P("tp"),
        P(None, "tp"),
        P(),
    )
    return jax.shard_map(
        per_device,
        mesh=mesh,
        in_specs=placed,
        out_specs=(
            P(None, ("seq", "tp"), None),
            P("seq", "tp"),
            P("seq", "tp"),
            P("seq", "tp"),
            P(None, "tp"),
            P("tp"),
            P("tp"),
        ),
        check_vma=False,
    )
```

```python
import functools

import jax
import jax.numpy as jnp
from jax import lax
from jax.experimental import pallas as pl
from jax.experimental.pallas import tpu as pltpu
from jax.sharding import PartitionSpec as P

EPSILON = 1e-05
EDGE = 8
LANES = 128
F32 = jnp.float32
BF16 = jnp.bfloat16


def sigmoid(x):
    return 0.5 * jnp.tanh(0.5 * x) + 0.5


def dot(a, b):
    return jnp.dot(a, b, preferred_element_type=F32)


def dot_nt(a, b):
    return lax.dot_general(a, b, (((1,), (1,)), ((), ())), preferred_element_type=F32)


def dot_tn(a, b):
    return lax.dot_general(a, b, (((0,), (0,)), ((), ())), preferred_element_type=F32)


def rows_of(count, first):
    return first + lax.broadcasted_iota(jnp.int32, (count, 1), 0)


def fold_rows(x):
    return jnp.sum(x.reshape(x.shape[0] // 8, 8, x.shape[1]), axis=0)


def block_rows(total, most):
    return max(b for b in range(8, most + 1, 8) if total % b == 0)


def whole(shape):
    return pl.BlockSpec(shape, lambda *i: (0,) * len(shape))


def per_record(shape):
    return pl.BlockSpec((1,) + shape, lambda r: (r,) + (0,) * len(shape))


def smem():
    return pl.BlockSpec(memory_space=pltpu.SMEM)


def anywhere():
    return pl.BlockSpec(memory_space=pl.ANY)


def after(x, *earlier):
    return lax.optimization_barrier((x,) + earlier)[0]


def spread_sums(out, sums):
    for s in range(out.shape[0]):
        out[s] = sums


def call(
    kernel, name, grid, in_specs, out_specs, out_shape, scratch, flops, moved, aliases=None, vmem=63
):
    return pl.pallas_call(
        kernel,
        name=name,
        grid=grid,
        in_specs=in_specs,
        out_specs=out_specs,
        out_shape=out_shape,
        scratch_shapes=scratch,
        input_output_aliases=aliases or {},
        cost_estimate=pl.CostEstimate(flops=int(flops), bytes_accessed=int(moved), transcendentals=0),
        compiler_params=pltpu.CompilerParams(vmem_limit_bytes=vmem * 1024 * 1024),
    )


def gate_kernel(meta, x, halo, wv, wg, taps, vl_o, sg_o, conv_o, st_o, gp, st):
    r = pl.program_id(0)
    hi = meta[0, r]
    lo = meta[1, r]
    frames = x.shape[1]
    width = wv.shape[1]
    halves = width // LANES

    def put(row, value):
        for h in range(halves):
            gp[h, pl.ds(row, value.shape[0]), :] = value[:, h * LANES : (h + 1) * LANES]

    edge_v = dot(halo[0], wv[...])
    edge_g = dot(halo[0], wg[...])
    row = rows_of(2 * EDGE, 0)
    pos = jnp.where(row < EDGE, row - EDGE, row - EDGE + frames)
    edge = jnp.where((pos >= lo) & (pos < hi), edge_v * sigmoid(edge_g), 0.0)
    zero = jnp.zeros((EDGE, width), F32)
    put(0, zero)
    put(EDGE, edge[:EDGE])
    put(2 * EDGE + frames, edge[EDGE:])
    put(3 * EDGE + frames, zero)
    step = block_rows(frames, 512)
    small = block_rows(step, 64)
    for base in range(0, frames, step):
        xb = x[0, base : base + step, :]
        vl_o[0, base : base + step, :] = dot(xb, wv[...])
        sg_o[0, base : base + step, :] = dot(xb, wg[...])

    def gating(i, carry):
        base = pl.multiple_of(i * small, small)
        v = vl_o[0, pl.ds(base, small), :]
        s = sigmoid(sg_o[0, pl.ds(base, small), :])
        sg_o[0, pl.ds(base, small), :] = s
        put(2 * EDGE + base, jnp.where(rows_of(small, base) < hi, v * s, 0.0))
        return carry

    lax.fori_loop(0, frames // small, gating, 0)
    span = frames + 2 * EDGE
    cb = block_rows(span, 104)
    kernel = taps.shape[0]
    margin = (kernel - 1) // 2
    for h in range(halves):
        cols = slice(h * LANES, (h + 1) * LANES)

        def convolve(i, carry):
            s1, s2 = carry
            base = pl.multiple_of(i * cb, 8)
            acc = jnp.zeros((cb, LANES), F32)
            for k in range(kernel):
                acc = acc + taps[k : k + 1, cols] * gp[h, pl.ds(base + EDGE - margin + k, cb), :]
            conv_o[0, pl.ds(base, cb), cols] = acc
            pos = rows_of(cb, base - EDGE)
            kept = jnp.where((pos >= 0) & (pos < jnp.minimum(hi, frames)), acc, 0.0)
            return s1 + fold_rows(kept), s2 + fold_rows(kept * kept)

        none = jnp.zeros((8, LANES), F32)
        s1, s2 = lax.fori_loop(0, span // cb, convolve, (none, none))
        add = jnp.concatenate(
            [jnp.sum(s1, axis=0, keepdims=True), jnp.sum(s2, axis=0, keepdims=True)], axis=0
        )
        st[:, cols] = jnp.where(r == 0, 0.0, st[:, cols]) + add

    @pl.when(r == pl.num_programs(0) - 1)
    def _():
        spread_sums(st_o, st[...])


def batch_norm(stats, count):
    sums = jnp.sum(stats[...], axis=0)
    centre = sums[0:1] / count
    spread = sums[1:2] / count - centre * centre
    return centre, lax.rsqrt(spread + EPSILON)


def norm_kernel(
    meta, count, stats, affine, select, grads, halo, wo, conv,
    swished_o, gn_o, picked_o, st_o, st, ping, pong
):
    r = pl.program_id(0)
    hi = meta[0, r]
    lo = meta[1, r]
    frames = grads.shape[1]
    centre, inv = batch_norm(stats, count[0, 0])
    gain, shift = affine[0:1, :], affine[1:2, :]

    def part(row, swish_grad):
        size = swish_grad.shape[0]
        unit = (conv[0, pl.ds(row, size), :] - centre) * inv
        normalized = unit * gain + shift
        s = sigmoid(normalized)
        pos = rows_of(size, row - EDGE)
        keep = (pos >= lo) & (pos < hi)
        swished = jnp.where(keep, normalized * s, 0.0)
        gn = jnp.where(keep, swish_grad, 0.0) * (s + normalized * (s - s * s))
        gn_o[0, pl.ds(row, size), :] = gn
        return unit, swished, gn

    edge = dot(halo[0], wo[...])
    part(0, edge[:EDGE])
    part(frames + EDGE, edge[EDGE:])
    step = block_rows(frames, 512)
    small = block_rows(step, 32)
    s1 = jnp.zeros((8, conv.shape[2]), F32)
    s2 = s1
    held = (ping, pong)
    ping[...] = dot(grads[0, :step, :], wo[...])
    for i in range(frames // step):
        now = held[i % 2]
        if (i + 1) * step < frames:
            held[(i + 1) % 2][...] = dot(grads[0, (i + 1) * step : (i + 2) * step, :], wo[...])
        picked_o[0, :, i * step : (i + 1) * step] = dot_nt(
            select[...], grads[0, i * step : (i + 1) * step, :]
        ).astype(BF16)
        for j in range(step // small):
            base = i * step + j * small
            unit, swished, gn = part(base + EDGE, now[j * small : (j + 1) * small, :])
            swished_o[0, base : base + small, :] = swished.astype(BF16)
            s1 = s1 + fold_rows(gn)
            s2 = s2 + fold_rows(gn * unit)
    add = jnp.concatenate(
        [jnp.sum(s1, axis=0, keepdims=True), jnp.sum(s2, axis=0, keepdims=True)], axis=0
    )
    st[...] = jnp.where(r == 0, 0.0, st[...]) + add

    @pl.when(r == pl.num_programs(0) - 1)
    def _():
        spread_sums(st_o, st[...])


def back_kernel(
    record, blocks, meta, count, stats, sums, gain, gn, conv, vl, sg, taps, out, taps_o, gc, acc
):
    i = pl.program_id(0)
    frames, width = vl.shape[1:]
    hi = meta[0, record + i // blocks]
    lo = meta[1, record + i // blocks]
    halves = width // LANES
    span = frames + 2 * EDGE
    kernel = taps.shape[0]
    margin = (kernel - 1) // 2
    cb = block_rows(span, 144)
    step = block_rows(frames, 64)
    total_frames = count[0, 0]
    centre, inv = batch_norm(stats, total_frames)
    grad_sums = jnp.sum(sums[...], axis=0)
    scale = gain[...] * inv
    offset = scale * grad_sums[0:1] / total_frames
    slope = scale * inv * grad_sums[1:2] / total_frames
    first = i % blocks * frames

    @pl.when(i == 0)
    def _():
        acc[...] = jnp.zeros_like(acc)

    for h in range(halves):
        cols = slice(h * LANES, (h + 1) * LANES)
        for base in range(0, span, cb):
            pos = rows_of(cb, first + (base - EDGE))
            mean = offset[:, cols] + (conv[0, base : base + cb, cols] - centre[:, cols]) * slope[:, cols]
            gc[h, base : base + cb, :] = scale[:, cols] * gn[0, base : base + cb, cols] - jnp.where(
                (pos >= lo) & (pos < hi), mean, 0.0
            )
        sums_k = [acc[h, k] for k in range(kernel)]
        for base in range(0, frames, step):
            v = vl[0, base : base + step, cols]
            s = sg[0, base : base + step, cols]
            keep = rows_of(step, first + base) < hi
            vs = v * s
            gated = jnp.where(keep, vs, 0.0)
            total = jnp.zeros((step, LANES), F32)
            for k in range(kernel):
                window = gc[h, base + EDGE + margin - k : base + EDGE + margin - k + step, :]
                total = total + taps[k : k + 1, cols] * window
                sums_k[k] = sums_k[k] + fold_rows(window * gated)
            total = jnp.where(keep, total, 0.0)
            out[base : base + step, cols] = (total * s).astype(BF16)
            out[base : base + step, width + h * LANES : width + (h + 1) * LANES] = (
                total * (vs - vs * s)
            ).astype(BF16)
        for k in range(kernel):
            acc[h, k] = sums_k[k]

    @pl.when(i == pl.num_programs(0) - 1)
    def _():
        taps_o[...] = jnp.zeros_like(taps_o)
        for h in range(halves):
            for k in range(kernel):
                taps_o[k : k + 1, h * LANES : (h + 1) * LANES] = jnp.sum(
                    acc[h, k], axis=0, keepdims=True
                )


def partial_kernel(own, sibling, w_own, w_sibling, picked, mine, *others):
    total = dot_nt(w_own[...], own[...]) + dot_nt(w_sibling[...], sibling[...])
    rows = picked.shape[1]
    seqs, _, piece, frames = mine.shape
    mine[...] = (
        (total[:rows] + picked[0].astype(F32)).astype(BF16).reshape(seqs, 1, piece, frames)
    )
    for d, other in enumerate(others):
        other[...] = (
            total[(d + 1) * rows : (d + 2) * rows].astype(BF16).reshape(seqs, 1, piece, frames)
        )


def add_kernel(*refs):
    total = refs[0][...].astype(F32)
    for other in refs[1:-1]:
        total = total + other[...].astype(F32)
    refs[-1][...] = total.astype(BF16)


def first_outer_kernel(grads, swished, out):
    r = pl.program_id(0)
    add = dot_tn(swished[0], grads[0])

    @pl.when(r == 0)
    def _():
        out[...] = add

    @pl.when(r > 0)
    def _():
        out[...] += add


def outer_kernel(groups, parity, x, w_out, *refs):
    lefts, taps = refs[: len(groups)], refs[len(groups) : 2 * len(groups)]
    keep, send, acc = refs[2 * len(groups) :]
    records = groups[-1][0] + groups[-1][1]
    width = w_out.shape[0]
    shard = keep.shape[2]
    r = pl.program_id(0)
    for (first, size), left in zip(groups, lefts):

        @pl.when((r >= first) & (r < first + size))
        def _(left=left):
            add = dot_tn(left[...], x[0])
            acc[...] = add + jnp.where(r == 0, 0.0, acc[...])

    @pl.when(r == records - 1)
    def _():
        tap_sums = taps[0][...]
        for part in taps[1:]:
            tap_sums = tap_sums + part[...]

        def write(place, odd):
            for j in range(place.shape[0]):
                at = (2 * j + odd) * shard
                place[j, : 2 * width, :] = acc[:, at : at + shard].astype(BF16)
                place[j, 2 * width : 3 * width, :] = w_out[:, at : at + shard].astype(BF16)
                for q in range(width // shard):
                    row = 3 * width + 16 * q
                    place[j, row : row + 16, :] = tap_sums[:, q * shard : (q + 1) * shard].astype(
                        BF16
                    )

        @pl.when(parity[0, 0] == 0)
        def _():
            write(keep, 0)
            write(send, 1)

        @pl.when(parity[0, 0] != 0)
        def _():
            write(keep, 1)
            write(send, 0)


def fold_kernel(parity, own, other, keep, send):
    def write(place, odd):
        for j in range(place.shape[0]):
            total = own[2 * j + odd].astype(F32) + other[2 * j + odd].astype(F32)
            place[j] = total.astype(BF16)

    @pl.when(parity[0, 0] == 0)
    def _():
        write(keep, 0)
        write(send, 1)

    @pl.when(parity[0, 0] != 0)
    def _():
        write(keep, 1)
        write(send, 0)


def finish_kernel(kernel, own, other, value, gate, out, taps):
    width = value.shape[1]
    shard = value.shape[0]

    def total(row, size):
        return own[0, row : row + size, :].astype(F32) + other[0, row : row + size, :].astype(F32)

    for i, place in enumerate((value, gate, out)):
        place[...] = total(i * width, width).T
    for q in range(width // shard):
        taps[:, q * shard : (q + 1) * shard] = total(3 * width + 16 * q, 16)[:kernel]


def place_kernel(moved, *refs):
    out = refs[-1]
    frames = moved.shape[3]
    for s in range(moved.shape[0]):
        out[0, :, s * frames : (s + 1) * frames] = moved[s, 0]


def exchange(copies, axis):
    return lax.all_to_all(copies, axis, 0, 0, tiled=True)


def per_device(
    normed,
    grad_out,
    value_weight,
    gate_weight,
    depth_taps,
    norm_gain,
    norm_shift,
    out_weight,
    lengths,
):
    recs, frames, model = normed.shape
    kernel = depth_taps.shape[0]
    width = value_weight.shape[1]
    seqs = lax.axis_size("seq")
    tps = lax.axis_size("tp")
    chips = tps // 2
    piece = model // (seqs * tps)
    rows = seqs * piece
    shard = model // seqs
    span = frames + 2 * EDGE
    seq_at = lax.axis_index("seq")
    tp_at = lax.axis_index("tp")
    chip_at, core_at = tp_at // 2, tp_at % 2
    count = jnp.sum(lengths).astype(F32)
    first = (seq_at * frames).astype(jnp.int32)
    meta = jnp.stack([lengths - first, jnp.full((recs,), 0, jnp.int32) - first])
    halves = width // LANES
    counts = count.reshape(1, 1)
    parity = (seq_at % 2).astype(jnp.int32).reshape(1, 1)
    sds = jax.ShapeDtypeStruct

    low_edge = jnp.concatenate([normed[:, -EDGE:], grad_out[:, -EDGE:]], axis=2)
    high_edge = jnp.concatenate([normed[:, :EDGE], grad_out[:, :EDGE]], axis=2)
    up = [(i, i + 1) for i in range(seqs - 1)]
    down = [(j, i) for i, j in up]
    halo = jnp.concatenate(
        [lax.ppermute(low_edge, "seq", up), lax.ppermute(high_edge, "seq", down)], axis=1
    )
    halo_x, halo_g = halo[:, :, :model], halo[:, :, model:]

    channel = (
        jnp.arange(seqs, dtype=jnp.int32)[:, None] * (tps * piece)
        + tp_at * piece
        + jnp.arange(piece, dtype=jnp.int32)[None, :]
    ).reshape(rows, 1)
    select = (channel == jnp.arange(model, dtype=jnp.int32)[None, :]).astype(BF16)
    array_bytes = recs * frames * width * 4
    input_bytes = recs * frames * model * 2
    matmul = 2 * recs * frames * model * width

    vl, sg, conv, stats = call(
        gate_kernel,
        "gate_conv",
        (recs,),
        [
            smem(),
            per_record((frames, model)),
            per_record((2 * EDGE, model)),
            whole((model, width)),
            whole((model, width)),
            whole((kernel, width)),
        ],
        [
            per_record((frames, width)),
            per_record((frames, width)),
            per_record((span, width)),
            whole((seqs, 2, width)),
        ],
        [
            sds((recs, frames, width), F32),
            sds((recs, frames, width), F32),
            sds((recs, span, width), F32),
            sds((seqs, 2, width), F32),
        ],
        [pltpu.VMEM((halves, frames + 4 * EDGE, LANES), F32), pltpu.VMEM((2, width), F32)],
        2 * matmul,
        input_bytes + 3 * array_bytes,
    )(meta, normed, halo_x, value_weight, gate_weight, depth_taps)
    both = jnp.concatenate([after(value_weight, stats), gate_weight], axis=1).reshape(seqs, tps, piece, 2 * width)

    def chosen(core):
        picks = [
            lax.dynamic_index_in_dim(both, ((chip_at + d) % chips) * 2 + core, 1, keepdims=False)
            for d in range(chips)
        ]
        return jnp.stack(picks).reshape(chips * rows, 2 * width)

    swap = [(i, i ^ 1) for i in range(tps)]
    w_own = chosen(core_at)
    w_sibling = lax.ppermute(chosen(1 - core_at), "tp", swap)

    stats = exchange(stats, "seq")

    chunk = block_rows(frames, 256)
    half_rows = block_rows(frames, 512)
    swished, gn, picked, sums = call(
        norm_kernel,
        "swish_norm",
        (recs,),
        [
            smem(),
            smem(),
            whole((seqs, 2, width)),
            whole((2, width)),
            whole((rows, model)),
            per_record((frames, model)),
            per_record((2 * EDGE, model)),
            whole((model, width)),
            per_record((span, width)),
        ],
        [
            per_record((frames, width)),
            per_record((span, width)),
            per_record((rows, frames)),
            whole((seqs, 2, width)),
        ],
        [
            sds((recs, frames, width), BF16),
            sds((recs, span, width), F32),
            sds((recs, rows, frames), BF16),
            sds((seqs, 2, width), F32),
        ],
        [
            pltpu.VMEM((2, width), F32),
            pltpu.VMEM((block_rows(frames, 512), width), F32),
            pltpu.VMEM((block_rows(frames, 512), width), F32),
        ],
        2 * matmul,
        input_bytes + 3 * array_bytes,
    )(
        meta,
        counts,
        stats,
        jnp.stack([norm_gain, norm_shift]),
        after(select, w_own, w_sibling),
        grad_out,
        halo_g,
        out_weight,
        conv,
    )
    w_out = call(
        first_outer_kernel,
        "outer_w_out",
        (recs,),
        [per_record((frames, model)), per_record((frames, width))],
        whole((width, model)),
        sds((width, model), F32),
        [],
        matmul,
        input_bytes,
    )(grad_out, swished)
    sums = exchange(sums, "seq")
    grad_shift, grad_gain = jnp.sum(sums, axis=0)

    blocks = frames // chunk
    parts_in = frames // half_rows

    def back(first, size, *earlier):
        def window(i):
            return (first + i // blocks, pl.multiple_of(i % blocks * chunk, chunk), 0)

        def block(i):
            return (first + i // blocks, i % blocks, 0)

        return call(
            functools.partial(back_kernel, first, blocks),
            "back_conv",
            (size * blocks,),
            [
                smem(),
                smem(),
                whole((seqs, 2, width)),
                whole((seqs, 2, width)),
                whole((1, width)),
                pl.BlockSpec((pl.Element(1), pl.Element(chunk + 2 * EDGE), pl.Element(width)), window),
                pl.BlockSpec((pl.Element(1), pl.Element(chunk + 2 * EDGE), pl.Element(width)), window),
                pl.BlockSpec((1, chunk, width), block),
                pl.BlockSpec((1, chunk, width), block),
                whole((kernel, width)),
            ],
            [pl.BlockSpec((chunk, 2 * width), lambda i: (i, 0)), whole((16, width))],
            [sds((size * frames, 2 * width), BF16), sds((16, width), F32)],
            [
                pltpu.VMEM((halves, chunk + 2 * EDGE, LANES), F32),
                pltpu.VMEM((halves, kernel, 8, LANES), F32),
            ],
            0,
            1024,
        )(meta, counts, stats, sums, norm_gain[None], gn, conv, vl, sg, after(depth_taps, *earlier))

    def partials(first, size, mine, *earlier):
        sibling = lax.ppermute(mine, "tp", swap)
        out = sds((seqs, size, piece, frames), BF16)
        return call(
            partial_kernel,
            "partial_in",
            (size * parts_in,),
            [
                pl.BlockSpec((half_rows, 2 * width), lambda i: (i, 0)),
                pl.BlockSpec((half_rows, 2 * width), lambda i: (i, 0)),
                whole((chips * rows, 2 * width)),
                whole((chips * rows, 2 * width)),
                pl.BlockSpec(
                    (1, rows, half_rows), lambda i: (first + i // parts_in, 0, i % parts_in)
                ),
            ],
            [
                pl.BlockSpec(
                    (seqs, 1, piece, half_rows), lambda i: (0, i // parts_in, 0, i % parts_in)
                )
            ]
            * chips,
            [out] * chips,
            [],
            0,
            1024,
        )(mine, sibling, after(w_own, *earlier), w_sibling, picked)

    def deliver(part, *earlier):
        arrived = []
        for d in range(1, chips):
            send = [(i, ((i // 2 + d) % chips) * 2 + i % 2) for i in range(tps)]
            arrived.append(lax.ppermute(part[d], "tp", send))
        size = part[0].shape[1]
        block = pl.BlockSpec(
            (seqs, 1, piece, half_rows), lambda i: (0, i // parts_in, 0, i % parts_in)
        )
        own = call(
            add_kernel,
            "add",
            (size * parts_in,),
            [block] * chips,
            block,
            sds(part[0].shape, BF16),
            [],
            50_000_000_000,
            1024,
        )(after(part[0], *earlier), *arrived)
        return own, exchange(own, "seq")

    groups = ((0, 1), (1, 1), (2, recs - 2))
    grads = [None] * 3
    taps = [None] * 3
    parts = [None] * 3
    owns = [None] * 3
    moved = [None] * 3
    grads[0], taps[0] = back(*groups[0], w_out)
    grads[1], taps[1] = back(*groups[1], grads[0])
    parts[0] = partials(*groups[0], grads[0], grads[1])
    grads[2], taps[2] = back(*groups[2], *parts[0])
    parts[1] = partials(*groups[1], grads[1], grads[2])
    owns[0], moved[0] = deliver(parts[0], *parts[1])
    parts[2] = partials(*groups[2], grads[2], owns[0])
    owns[1], moved[1] = deliver(parts[1], *parts[2])

    slots = 3 * width + 16 * (width // shard)
    half = sds((seqs // 2, slots, shard), BF16)
    keep, send = call(
        functools.partial(outer_kernel, groups),
        "outer_w_in",
        (recs,),
        [smem(), per_record((frames, model)), whole((width, model))]
        + [
            pl.BlockSpec(
                (frames, 2 * width),
                lambda r, first=first, size=size: (jnp.clip(r - first, 0, size - 1), 0),
            )
            for first, size in groups
        ]
        + [whole((16, width))] * len(groups),
        [whole(half.shape)] * 2,
        [half] * 2,
        [pltpu.VMEM((2 * width, model), F32)],
        50_000_000_000,
        1024,
    )(parity, after(normed, owns[1]), w_out, *grads, *taps)
    owns[2], moved[2] = deliver(parts[2], keep, moved[1])
    bit = 1
    while True:
        others = lax.ppermute(send, "seq", [(i, i ^ bit) for i in range(seqs)])
        bit *= 2
        if bit == seqs:
            break
        shape = (keep.shape[0] // 2,) + keep.shape[1:]
        side = ((seq_at // bit) % 2).astype(jnp.int32).reshape(1, 1)
        keep, send = call(
            fold_kernel,
            "fold",
            (1,),
            [smem()] + [whole(keep.shape)] * 2,
            [whole(shape)] * 2,
            [sds(shape, BF16)] * 2,
            [],
            0,
            1024,
            vmem=20,
        )(side, keep, others)
    w_value, w_gate, w_out, grad_taps = call(
        functools.partial(finish_kernel, kernel),
        "finish",
        (1,),
        [whole(keep.shape)] * 2,
        [whole((shard, width))] * 3 + [whole((kernel, width))],
        [sds((shard, width), F32)] * 3 + [sds((kernel, width), F32)],
        [],
        0,
        1024,
        vmem=20,
    )(keep, others)
    grad_in = ()
    for (first, size), part in zip(groups, moved):
        grad_in = (
            call(
                place_kernel,
                "place",
                (size,),
                [pl.BlockSpec((seqs, 1, piece, frames), lambda i: (0, i, 0, 0))]
                + [anywhere()] * len(grad_in),
                pl.BlockSpec((1, piece, seqs * frames), lambda i, first=first: (first + i, 0, 0)),
                sds((recs, piece, seqs * frames), BF16),
                [],
                0,
                4 * size * piece * seqs * frames,
                {1: 0} if grad_in else None,
                vmem=20,
            )(part, *grad_in),
        )
    (grad_in,) = grad_in
    return (grad_in, w_value, w_gate, w_out, grad_taps, grad_gain, grad_shift)


def solution(mesh):
    placed = (
        P(None, "seq", None),
        P(None, "seq", None),
        P(None, "tp"),
        P(None, "tp"),
        P(None, "tp"),
        P("tp"),
        P("tp"),
        P(None, "tp"),
        P(),
    )
    return jax.shard_map(
        per_device,
        mesh=mesh,
        in_specs=placed,
        out_specs=(
            P(None, ("seq", "tp"), None),
            P("seq", "tp"),
            P("seq", "tp"),
            P("seq", "tp"),
            P(None, "tp"),
            P("tp"),
            P("tp"),
        ),
        check_vma=False,
    )
```

```python
import functools

import jax
import jax.numpy as jnp
from jax import lax
from jax.experimental import pallas as pl
from jax.experimental.pallas import tpu as pltpu
from jax.sharding import PartitionSpec as P

EPSILON = 1e-05
EDGE = 8
LANES = 128
F32 = jnp.float32
BF16 = jnp.bfloat16


def sigmoid(x):
    return 0.5 * jnp.tanh(0.5 * x) + 0.5


def dot(a, b):
    return jnp.dot(a, b, preferred_element_type=F32)


def dot_nt(a, b):
    return lax.dot_general(a, b, (((1,), (1,)), ((), ())), preferred_element_type=F32)


def dot_tn(a, b):
    return lax.dot_general(a, b, (((0,), (0,)), ((), ())), preferred_element_type=F32)


def rows_of(count, first):
    return first + lax.broadcasted_iota(jnp.int32, (count, 1), 0)


def fold_rows(x):
    return jnp.sum(x.reshape(x.shape[0] // 8, 8, x.shape[1]), axis=0)


def block_rows(total, most):
    return max(b for b in range(8, most + 1, 8) if total % b == 0)


def whole(shape):
    return pl.BlockSpec(shape, lambda *i: (0,) * len(shape))


def per_record(shape):
    return pl.BlockSpec((1,) + shape, lambda r: (r,) + (0,) * len(shape))


def smem():
    return pl.BlockSpec(memory_space=pltpu.SMEM)


def anywhere():
    return pl.BlockSpec(memory_space=pl.ANY)


def after(x, *earlier):
    return lax.optimization_barrier((x,) + earlier)[0]


def spread_sums(out, sums):
    for s in range(out.shape[0]):
        out[s] = sums


def call(
    kernel, name, grid, in_specs, out_specs, out_shape, scratch, flops, moved, aliases=None, vmem=63
):
    return pl.pallas_call(
        kernel,
        name=name,
        grid=grid,
        in_specs=in_specs,
        out_specs=out_specs,
        out_shape=out_shape,
        scratch_shapes=scratch,
        input_output_aliases=aliases or {},
        cost_estimate=pl.CostEstimate(flops=int(flops), bytes_accessed=int(moved), transcendentals=0),
        compiler_params=pltpu.CompilerParams(vmem_limit_bytes=vmem * 1024 * 1024),
    )


def gate_kernel(meta, x, halo, wv, wg, taps, vl_o, sg_o, conv_o, st_o, gp, st):
    r = pl.program_id(0)
    hi = meta[0, r]
    lo = meta[1, r]
    frames = x.shape[1]
    width = wv.shape[1]
    halves = width // LANES

    def put(row, value):
        for h in range(halves):
            gp[h, pl.ds(row, value.shape[0]), :] = value[:, h * LANES : (h + 1) * LANES]

    edge_v = dot(halo[0], wv[...])
    edge_g = dot(halo[0], wg[...])
    row = rows_of(2 * EDGE, 0)
    pos = jnp.where(row < EDGE, row - EDGE, row - EDGE + frames)
    edge = jnp.where((pos >= lo) & (pos < hi), edge_v * sigmoid(edge_g), 0.0)
    zero = jnp.zeros((EDGE, width), F32)
    put(0, zero)
    put(EDGE, edge[:EDGE])
    put(2 * EDGE + frames, edge[EDGE:])
    put(3 * EDGE + frames, zero)
    step = block_rows(frames, 512)
    small = block_rows(step, 64)
    for base in range(0, frames, step):
        xb = x[0, base : base + step, :]
        vl_o[0, base : base + step, :] = dot(xb, wv[...])
        sg_o[0, base : base + step, :] = dot(xb, wg[...])

    def gating(i, carry):
        base = pl.multiple_of(i * small, small)
        v = vl_o[0, pl.ds(base, small), :]
        s = sigmoid(sg_o[0, pl.ds(base, small), :])
        sg_o[0, pl.ds(base, small), :] = s
        put(2 * EDGE + base, jnp.where(rows_of(small, base) < hi, v * s, 0.0))
        return carry

    lax.fori_loop(0, frames // small, gating, 0)
    span = frames + 2 * EDGE
    cb = block_rows(span, 104)
    kernel = taps.shape[0]
    margin = (kernel - 1) // 2
    for h in range(halves):
        cols = slice(h * LANES, (h + 1) * LANES)

        def convolve(i, carry):
            s1, s2 = carry
            base = pl.multiple_of(i * cb, 8)
            acc = jnp.zeros((cb, LANES), F32)
            for k in range(kernel):
                acc = acc + taps[k : k + 1, cols] * gp[h, pl.ds(base + EDGE - margin + k, cb), :]
            conv_o[0, pl.ds(base, cb), cols] = acc
            pos = rows_of(cb, base - EDGE)
            kept = jnp.where((pos >= 0) & (pos < jnp.minimum(hi, frames)), acc, 0.0)
            return s1 + fold_rows(kept), s2 + fold_rows(kept * kept)

        none = jnp.zeros((8, LANES), F32)
        s1, s2 = lax.fori_loop(0, span // cb, convolve, (none, none))
        add = jnp.concatenate(
            [jnp.sum(s1, axis=0, keepdims=True), jnp.sum(s2, axis=0, keepdims=True)], axis=0
        )
        st[:, cols] = jnp.where(r == 0, 0.0, st[:, cols]) + add

    @pl.when(r == pl.num_programs(0) - 1)
    def _():
        spread_sums(st_o, st[...])


def batch_norm(stats, count):
    sums = jnp.sum(stats[...], axis=0)
    centre = sums[0:1] / count
    spread = sums[1:2] / count - centre * centre
    return centre, lax.rsqrt(spread + EPSILON)


def norm_kernel(
    meta, count, stats, affine, select, grads, halo, wo, conv,
    swished_o, gn_o, picked_o, st_o, st, ping, pong
):
    r = pl.program_id(0)
    hi = meta[0, r]
    lo = meta[1, r]
    frames = grads.shape[1]
    centre, inv = batch_norm(stats, count[0, 0])
    gain, shift = affine[0:1, :], affine[1:2, :]

    def part(row, swish_grad):
        size = swish_grad.shape[0]
        unit = (conv[0, pl.ds(row, size), :] - centre) * inv
        normalized = unit * gain + shift
        s = sigmoid(normalized)
        pos = rows_of(size, row - EDGE)
        keep = (pos >= lo) & (pos < hi)
        swished = jnp.where(keep, normalized * s, 0.0)
        gn = jnp.where(keep, swish_grad, 0.0) * (s + normalized * (s - s * s))
        gn_o[0, pl.ds(row, size), :] = gn
        return unit, swished, gn

    edge = dot(halo[0], wo[...])
    part(0, edge[:EDGE])
    part(frames + EDGE, edge[EDGE:])
    step = block_rows(frames, 512)
    small = block_rows(step, 32)
    s1 = jnp.zeros((8, conv.shape[2]), F32)
    s2 = s1
    held = (ping, pong)
    ping[...] = dot(grads[0, :step, :], wo[...])
    for i in range(frames // step):
        now = held[i % 2]
        if (i + 1) * step < frames:
            held[(i + 1) % 2][...] = dot(grads[0, (i + 1) * step : (i + 2) * step, :], wo[...])
        picked_o[0, :, i * step : (i + 1) * step] = dot_nt(
            select[...], grads[0, i * step : (i + 1) * step, :]
        ).astype(BF16)
        for j in range(step // small):
            base = i * step + j * small
            unit, swished, gn = part(base + EDGE, now[j * small : (j + 1) * small, :])
            swished_o[0, base : base + small, :] = swished.astype(BF16)
            s1 = s1 + fold_rows(gn)
            s2 = s2 + fold_rows(gn * unit)
    add = jnp.concatenate(
        [jnp.sum(s1, axis=0, keepdims=True), jnp.sum(s2, axis=0, keepdims=True)], axis=0
    )
    st[...] = jnp.where(r == 0, 0.0, st[...]) + add

    @pl.when(r == pl.num_programs(0) - 1)
    def _():
        spread_sums(st_o, st[...])


def back_kernel(
    record, blocks, meta, count, stats, sums, gain, gn, conv, vl, sg, taps, out, taps_o, gc, acc
):
    i = pl.program_id(0)
    frames, width = vl.shape[1:]
    hi = meta[0, record + i // blocks]
    lo = meta[1, record + i // blocks]
    halves = width // LANES
    span = frames + 2 * EDGE
    kernel = taps.shape[0]
    margin = (kernel - 1) // 2
    cb = block_rows(span, 144)
    step = block_rows(frames, 64)
    total_frames = count[0, 0]
    centre, inv = batch_norm(stats, total_frames)
    grad_sums = jnp.sum(sums[...], axis=0)
    scale = gain[...] * inv
    offset = scale * grad_sums[0:1] / total_frames
    slope = scale * inv * grad_sums[1:2] / total_frames
    first = i % blocks * frames

    @pl.when(i == 0)
    def _():
        acc[...] = jnp.zeros_like(acc)

    for h in range(halves):
        cols = slice(h * LANES, (h + 1) * LANES)
        for base in range(0, span, cb):
            pos = rows_of(cb, first + (base - EDGE))
            mean = offset[:, cols] + (conv[0, base : base + cb, cols] - centre[:, cols]) * slope[:, cols]
            gc[h, base : base + cb, :] = scale[:, cols] * gn[0, base : base + cb, cols] - jnp.where(
                (pos >= lo) & (pos < hi), mean, 0.0
            )
        sums_k = [acc[h, k] for k in range(kernel)]
        for base in range(0, frames, step):
            v = vl[0, base : base + step, cols]
            s = sg[0, base : base + step, cols]
            keep = rows_of(step, first + base) < hi
            vs = v * s
            gated = jnp.where(keep, vs, 0.0)
            total = jnp.zeros((step, LANES), F32)
            for k in range(kernel):
                window = gc[h, base + EDGE + margin - k : base + EDGE + margin - k + step, :]
                total = total + taps[k : k + 1, cols] * window
                sums_k[k] = sums_k[k] + fold_rows(window * gated)
            total = jnp.where(keep, total, 0.0)
            out[base : base + step, cols] = (total * s).astype(BF16)
            out[base : base + step, width + h * LANES : width + (h + 1) * LANES] = (
                total * (vs - vs * s)
            ).astype(BF16)
        for k in range(kernel):
            acc[h, k] = sums_k[k]

    @pl.when(i == pl.num_programs(0) - 1)
    def _():
        taps_o[...] = jnp.zeros_like(taps_o)
        for h in range(halves):
            for k in range(kernel):
                taps_o[k : k + 1, h * LANES : (h + 1) * LANES] = jnp.sum(
                    acc[h, k], axis=0, keepdims=True
                )


def partial_kernel(own, sibling, w_own, w_sibling, picked, mine, *others):
    total = dot_nt(w_own[...], own[...]) + dot_nt(w_sibling[...], sibling[...])
    rows = picked.shape[1]
    seqs, _, piece, frames = mine.shape
    mine[...] = (
        (total[:rows] + picked[0].astype(F32)).astype(BF16).reshape(seqs, 1, piece, frames)
    )
    for d, other in enumerate(others):
        other[...] = (
            total[(d + 1) * rows : (d + 2) * rows].astype(BF16).reshape(seqs, 1, piece, frames)
        )


def add_kernel(*refs):
    total = refs[0][...].astype(F32)
    for other in refs[1:-1]:
        total = total + other[...].astype(F32)
    refs[-1][...] = total.astype(BF16)


def first_outer_kernel(grads, swished, out):
    r = pl.program_id(0)
    add = dot_tn(swished[0], grads[0])

    @pl.when(r == 0)
    def _():
        out[...] = add

    @pl.when(r > 0)
    def _():
        out[...] += add


def outer_kernel(groups, parity, x, w_out, *refs):
    lefts, taps = refs[: len(groups)], refs[len(groups) : 2 * len(groups)]
    keep, send, acc = refs[2 * len(groups) :]
    records = groups[-1][0] + groups[-1][1]
    width = w_out.shape[0]
    shard = keep.shape[2]
    r = pl.program_id(0)
    for (first, size), left in zip(groups, lefts):

        @pl.when((r >= first) & (r < first + size))
        def _(left=left):
            add = dot_tn(left[...], x[0])
            acc[...] = add + jnp.where(r == 0, 0.0, acc[...])

    @pl.when(r == records - 1)
    def _():
        tap_sums = taps[0][...]
        for part in taps[1:]:
            tap_sums = tap_sums + part[...]

        def write(place, odd):
            for j in range(place.shape[0]):
                at = (2 * j + odd) * shard
                place[j, : 2 * width, :] = acc[:, at : at + shard].astype(BF16)
                place[j, 2 * width : 3 * width, :] = w_out[:, at : at + shard].astype(BF16)
                for q in range(width // shard):
                    row = 3 * width + 16 * q
                    place[j, row : row + 16, :] = tap_sums[:, q * shard : (q + 1) * shard].astype(
                        BF16
                    )

        @pl.when(parity[0, 0] == 0)
        def _():
            write(keep, 0)
            write(send, 1)

        @pl.when(parity[0, 0] != 0)
        def _():
            write(keep, 1)
            write(send, 0)


def fold_kernel(parity, own, other, keep, send):
    def write(place, odd):
        for j in range(place.shape[0]):
            total = own[2 * j + odd].astype(F32) + other[2 * j + odd].astype(F32)
            place[j] = total.astype(BF16)

    @pl.when(parity[0, 0] == 0)
    def _():
        write(keep, 0)
        write(send, 1)

    @pl.when(parity[0, 0] != 0)
    def _():
        write(keep, 1)
        write(send, 0)


def finish_kernel(kernel, own, other, value, gate, out, taps):
    width = value.shape[1]
    shard = value.shape[0]

    def total(row, size):
        return own[0, row : row + size, :].astype(F32) + other[0, row : row + size, :].astype(F32)

    for i, place in enumerate((value, gate, out)):
        place[...] = total(i * width, width).T
    for q in range(width // shard):
        taps[:, q * shard : (q + 1) * shard] = total(3 * width + 16 * q, 16)[:kernel]


def place_kernel(moved, *refs):
    out = refs[-1]
    frames = moved.shape[3]
    for s in range(moved.shape[0]):
        out[0, :, s * frames : (s + 1) * frames] = moved[s, 0]


def exchange(copies, axis):
    return lax.all_to_all(copies, axis, 0, 0, tiled=True)


def per_device(
    normed,
    grad_out,
    value_weight,
    gate_weight,
    depth_taps,
    norm_gain,
    norm_shift,
    out_weight,
    lengths,
):
    recs, frames, model = normed.shape
    kernel = depth_taps.shape[0]
    width = value_weight.shape[1]
    seqs = lax.axis_size("seq")
    tps = lax.axis_size("tp")
    chips = tps // 2
    piece = model // (seqs * tps)
    rows = seqs * piece
    shard = model // seqs
    span = frames + 2 * EDGE
    seq_at = lax.axis_index("seq")
    tp_at = lax.axis_index("tp")
    chip_at, core_at = tp_at // 2, tp_at % 2
    count = jnp.sum(lengths).astype(F32)
    first = (seq_at * frames).astype(jnp.int32)
    meta = jnp.stack([lengths - first, jnp.full((recs,), 0, jnp.int32) - first])
    halves = width // LANES
    counts = count.reshape(1, 1)
    parity = (seq_at % 2).astype(jnp.int32).reshape(1, 1)
    sds = jax.ShapeDtypeStruct

    low_edge = jnp.concatenate([normed[:, -EDGE:], grad_out[:, -EDGE:]], axis=2)
    high_edge = jnp.concatenate([normed[:, :EDGE], grad_out[:, :EDGE]], axis=2)
    up = [(i, i + 1) for i in range(seqs - 1)]
    down = [(j, i) for i, j in up]
    halo = jnp.concatenate(
        [lax.ppermute(low_edge, "seq", up), lax.ppermute(high_edge, "seq", down)], axis=1
    )
    halo_x, halo_g = halo[:, :, :model], halo[:, :, model:]

    channel = (
        jnp.arange(seqs, dtype=jnp.int32)[:, None] * (tps * piece)
        + tp_at * piece
        + jnp.arange(piece, dtype=jnp.int32)[None, :]
    ).reshape(rows, 1)
    select = (channel == jnp.arange(model, dtype=jnp.int32)[None, :]).astype(BF16)
    array_bytes = recs * frames * width * 4
    input_bytes = recs * frames * model * 2
    matmul = 2 * recs * frames * model * width

    vl, sg, conv, stats = call(
        gate_kernel,
        "gate_conv",
        (recs,),
        [
            smem(),
            per_record((frames, model)),
            per_record((2 * EDGE, model)),
            whole((model, width)),
            whole((model, width)),
            whole((kernel, width)),
        ],
        [
            per_record((frames, width)),
            per_record((frames, width)),
            per_record((span, width)),
            whole((seqs, 2, width)),
        ],
        [
            sds((recs, frames, width), F32),
            sds((recs, frames, width), F32),
            sds((recs, span, width), F32),
            sds((seqs, 2, width), F32),
        ],
        [pltpu.VMEM((halves, frames + 4 * EDGE, LANES), F32), pltpu.VMEM((2, width), F32)],
        2 * matmul,
        input_bytes + 3 * array_bytes,
    )(meta, normed, halo_x, value_weight, gate_weight, depth_taps)
    both = jnp.concatenate([after(value_weight, stats), gate_weight], axis=1).reshape(seqs, tps, piece, 2 * width)

    def chosen(core):
        picks = [
            lax.dynamic_index_in_dim(both, ((chip_at + d) % chips) * 2 + core, 1, keepdims=False)
            for d in range(chips)
        ]
        return jnp.stack(picks).reshape(chips * rows, 2 * width)

    swap = [(i, i ^ 1) for i in range(tps)]
    w_own = chosen(core_at)
    w_sibling = lax.ppermute(chosen(1 - core_at), "tp", swap)

    stats = exchange(stats, "seq")

    chunk = block_rows(frames, 256)
    half_rows = block_rows(frames, 512)
    swished, gn, picked, sums = call(
        norm_kernel,
        "swish_norm",
        (recs,),
        [
            smem(),
            smem(),
            whole((seqs, 2, width)),
            whole((2, width)),
            whole((rows, model)),
            per_record((frames, model)),
            per_record((2 * EDGE, model)),
            whole((model, width)),
            per_record((span, width)),
        ],
        [
            per_record((frames, width)),
            per_record((span, width)),
            per_record((rows, frames)),
            whole((seqs, 2, width)),
        ],
        [
            sds((recs, frames, width), BF16),
            sds((recs, span, width), F32),
            sds((recs, rows, frames), BF16),
            sds((seqs, 2, width), F32),
        ],
        [
            pltpu.VMEM((2, width), F32),
            pltpu.VMEM((block_rows(frames, 512), width), F32),
            pltpu.VMEM((block_rows(frames, 512), width), F32),
        ],
        2 * matmul,
        input_bytes + 3 * array_bytes,
    )(
        meta,
        counts,
        stats,
        jnp.stack([norm_gain, norm_shift]),
        after(select, w_own, w_sibling),
        grad_out,
        halo_g,
        out_weight,
        conv,
    )
    w_out = call(
        first_outer_kernel,
        "outer_w_out",
        (recs,),
        [per_record((frames, model)), per_record((frames, width))],
        whole((width, model)),
        sds((width, model), F32),
        [],
        matmul,
        input_bytes,
    )(grad_out, swished)
    sums = exchange(sums, "seq")
    grad_shift, grad_gain = jnp.sum(sums, axis=0)

    blocks = frames // chunk
    parts_in = frames // half_rows

    def back(first, size, *earlier):
        def window(i):
            return (first + i // blocks, pl.multiple_of(i % blocks * chunk, chunk), 0)

        def block(i):
            return (first + i // blocks, i % blocks, 0)

        return call(
            functools.partial(back_kernel, first, blocks),
            "back_conv",
            (size * blocks,),
            [
                smem(),
                smem(),
                whole((seqs, 2, width)),
                whole((seqs, 2, width)),
                whole((1, width)),
                pl.BlockSpec((pl.Element(1), pl.Element(chunk + 2 * EDGE), pl.Element(width)), window),
                pl.BlockSpec((pl.Element(1), pl.Element(chunk + 2 * EDGE), pl.Element(width)), window),
                pl.BlockSpec((1, chunk, width), block),
                pl.BlockSpec((1, chunk, width), block),
                whole((kernel, width)),
            ],
            [pl.BlockSpec((chunk, 2 * width), lambda i: (i, 0)), whole((16, width))],
            [sds((size * frames, 2 * width), BF16), sds((16, width), F32)],
            [
                pltpu.VMEM((halves, chunk + 2 * EDGE, LANES), F32),
                pltpu.VMEM((halves, kernel, 8, LANES), F32),
            ],
            0,
            1024,
        )(meta, counts, stats, sums, norm_gain[None], gn, conv, vl, sg, after(depth_taps, *earlier))

    def partials(first, size, mine, *earlier):
        sibling = lax.ppermute(mine, "tp", swap)
        out = sds((seqs, size, piece, frames), BF16)
        return call(
            partial_kernel,
            "partial_in",
            (size * parts_in,),
            [
                pl.BlockSpec((half_rows, 2 * width), lambda i: (i, 0)),
                pl.BlockSpec((half_rows, 2 * width), lambda i: (i, 0)),
                whole((chips * rows, 2 * width)),
                whole((chips * rows, 2 * width)),
                pl.BlockSpec(
                    (1, rows, half_rows), lambda i: (first + i // parts_in, 0, i % parts_in)
                ),
            ],
            [
                pl.BlockSpec(
                    (seqs, 1, piece, half_rows), lambda i: (0, i // parts_in, 0, i % parts_in)
                )
            ]
            * chips,
            [out] * chips,
            [],
            0,
            1024,
        )(mine, sibling, after(w_own, *earlier), w_sibling, picked)

    def deliver(part, *earlier):
        arrived = []
        for d in range(1, chips):
            send = [(i, ((i // 2 + d) % chips) * 2 + i % 2) for i in range(tps)]
            arrived.append(lax.ppermute(part[d], "tp", send))
        size = part[0].shape[1]
        block = pl.BlockSpec(
            (seqs, 1, piece, half_rows), lambda i: (0, i // parts_in, 0, i % parts_in)
        )
        own = call(
            add_kernel,
            "add",
            (size * parts_in,),
            [block] * chips,
            block,
            sds(part[0].shape, BF16),
            [],
            50_000_000_000,
            1024,
        )(after(part[0], *earlier), *arrived)
        return own

    groups = ((0, 1), (1, 1), (2, recs - 2))
    grads = [None] * 3
    taps = [None] * 3
    parts = [None] * 3
    owns = [None] * 3
    moved = [None] * 3
    grads[0], taps[0] = back(*groups[0], w_out)
    grads[1], taps[1] = back(*groups[1], grads[0])
    parts[0] = partials(*groups[0], grads[0], grads[1])
    grads[2], taps[2] = back(*groups[2], *parts[0])
    parts[1] = partials(*groups[1], grads[1], grads[2])
    owns[0] = deliver(parts[0], *parts[1])
    moved[0] = exchange(owns[0], "seq")
    owns[1] = deliver(parts[1], owns[0])
    parts[2] = partials(*groups[2], grads[2], owns[1])

    slots = 3 * width + 16 * (width // shard)
    half = sds((seqs // 2, slots, shard), BF16)
    keep, send = call(
        functools.partial(outer_kernel, groups),
        "outer_w_in",
        (recs,),
        [smem(), per_record((frames, model)), whole((width, model))]
        + [
            pl.BlockSpec(
                (frames, 2 * width),
                lambda r, first=first, size=size: (jnp.clip(r - first, 0, size - 1), 0),
            )
            for first, size in groups
        ]
        + [whole((16, width))] * len(groups),
        [whole(half.shape)] * 2,
        [half] * 2,
        [pltpu.VMEM((2 * width, model), F32)],
        50_000_000_000,
        1024,
    )(parity, after(normed, *parts[2]), w_out, *grads, *taps)
    moved[1] = exchange(after(owns[1], keep, moved[0]), "seq")
    bit = 1
    while True:
        others = lax.ppermute(send, "seq", [(i, i ^ bit) for i in range(seqs)])
        if bit == 1:
            owns[2] = deliver(parts[2], others)
            moved[2] = exchange(after(owns[2], moved[1]), "seq")
        bit *= 2
        if bit == seqs:
            break
        shape = (keep.shape[0] // 2,) + keep.shape[1:]
        side = ((seq_at // bit) % 2).astype(jnp.int32).reshape(1, 1)
        keep, send = call(
            fold_kernel,
            "fold",
            (1,),
            [smem()] + [whole(keep.shape)] * 2,
            [whole(shape)] * 2,
            [sds(shape, BF16)] * 2,
            [],
            0,
            1024,
            vmem=20,
        )(side, keep, others)
    w_value, w_gate, w_out, grad_taps = call(
        functools.partial(finish_kernel, kernel),
        "finish",
        (1,),
        [whole(keep.shape)] * 2,
        [whole((shard, width))] * 3 + [whole((kernel, width))],
        [sds((shard, width), F32)] * 3 + [sds((kernel, width), F32)],
        [],
        0,
        1024,
        vmem=20,
    )(keep, others)
    grad_in = ()
    for (first, size), part in zip(groups, moved):
        grad_in = (
            call(
                place_kernel,
                "place",
                (size,),
                [pl.BlockSpec((seqs, 1, piece, frames), lambda i: (0, i, 0, 0))]
                + [anywhere()] * len(grad_in),
                pl.BlockSpec((1, piece, seqs * frames), lambda i, first=first: (first + i, 0, 0)),
                sds((recs, piece, seqs * frames), BF16),
                [],
                0,
                4 * size * piece * seqs * frames,
                {1: 0} if grad_in else None,
                vmem=20,
            )(part, *grad_in),
        )
    (grad_in,) = grad_in
    return (grad_in, w_value, w_gate, w_out, grad_taps, grad_gain, grad_shift)


def solution(mesh):
    placed = (
        P(None, "seq", None),
        P(None, "seq", None),
        P(None, "tp"),
        P(None, "tp"),
        P(None, "tp"),
        P("tp"),
        P("tp"),
        P(None, "tp"),
        P(),
    )
    return jax.shard_map(
        per_device,
        mesh=mesh,
        in_specs=placed,
        out_specs=(
            P(None, ("seq", "tp"), None),
            P("seq", "tp"),
            P("seq", "tp"),
            P("seq", "tp"),
            P(None, "tp"),
            P("tp"),
            P("tp"),
        ),
        check_vma=False,
    )
```

```python
import functools

import jax
import jax.numpy as jnp
from jax import lax
from jax.experimental import pallas as pl
from jax.experimental.pallas import tpu as pltpu
from jax.sharding import PartitionSpec as P

EPSILON = 1e-05
EDGE = 8
LANES = 128
F32 = jnp.float32
BF16 = jnp.bfloat16


def sigmoid(x):
    return 0.5 * jnp.tanh(0.5 * x) + 0.5


def dot(a, b):
    return jnp.dot(a, b, preferred_element_type=F32)


def dot_nt(a, b):
    return lax.dot_general(a, b, (((1,), (1,)), ((), ())), preferred_element_type=F32)


def dot_tn(a, b):
    return lax.dot_general(a, b, (((0,), (0,)), ((), ())), preferred_element_type=F32)


def rows_of(count, first):
    return first + lax.broadcasted_iota(jnp.int32, (count, 1), 0)


def fold_rows(x):
    return jnp.sum(x.reshape(x.shape[0] // 8, 8, x.shape[1]), axis=0)


def block_rows(total, most):
    return max(b for b in range(8, most + 1, 8) if total % b == 0)


def whole(shape):
    return pl.BlockSpec(shape, lambda *i: (0,) * len(shape))


def per_record(shape):
    return pl.BlockSpec((1,) + shape, lambda r: (r,) + (0,) * len(shape))


def smem():
    return pl.BlockSpec(memory_space=pltpu.SMEM)


def anywhere():
    return pl.BlockSpec(memory_space=pl.ANY)


def after(x, *earlier):
    return lax.optimization_barrier((x,) + earlier)[0]


def spread_sums(out, sums):
    for s in range(out.shape[0]):
        out[s] = sums


def call(
    kernel, name, grid, in_specs, out_specs, out_shape, scratch, flops, moved, aliases=None, vmem=63
):
    return pl.pallas_call(
        kernel,
        name=name,
        grid=grid,
        in_specs=in_specs,
        out_specs=out_specs,
        out_shape=out_shape,
        scratch_shapes=scratch,
        input_output_aliases=aliases or {},
        cost_estimate=pl.CostEstimate(flops=int(flops), bytes_accessed=int(moved), transcendentals=0),
        compiler_params=pltpu.CompilerParams(vmem_limit_bytes=vmem * 1024 * 1024),
    )


def gate_kernel(meta, x, halo, wv, wg, taps, vl_o, sg_o, conv_o, st_o, gp, st):
    r = pl.program_id(0)
    hi = meta[0, r]
    lo = meta[1, r]
    frames = x.shape[1]
    width = wv.shape[1]
    halves = width // LANES

    def put(row, value):
        for h in range(halves):
            gp[h, pl.ds(row, value.shape[0]), :] = value[:, h * LANES : (h + 1) * LANES]

    edge_v = dot(halo[0], wv[...])
    edge_g = dot(halo[0], wg[...])
    row = rows_of(2 * EDGE, 0)
    pos = jnp.where(row < EDGE, row - EDGE, row - EDGE + frames)
    edge = jnp.where((pos >= lo) & (pos < hi), edge_v * sigmoid(edge_g), 0.0)
    zero = jnp.zeros((EDGE, width), F32)
    put(0, zero)
    put(EDGE, edge[:EDGE])
    put(2 * EDGE + frames, edge[EDGE:])
    put(3 * EDGE + frames, zero)
    step = block_rows(frames, 512)
    small = block_rows(step, 64)
    for base in range(0, frames, step):
        xb = x[0, base : base + step, :]
        vl_o[0, base : base + step, :] = dot(xb, wv[...])
        sg_o[0, base : base + step, :] = dot(xb, wg[...])

    def gating(i, carry):
        base = pl.multiple_of(i * small, small)
        v = vl_o[0, pl.ds(base, small), :]
        s = sigmoid(sg_o[0, pl.ds(base, small), :])
        sg_o[0, pl.ds(base, small), :] = s
        put(2 * EDGE + base, jnp.where(rows_of(small, base) < hi, v * s, 0.0))
        return carry

    lax.fori_loop(0, frames // small, gating, 0)
    span = frames + 2 * EDGE
    cb = block_rows(span, 104)
    kernel = taps.shape[0]
    margin = (kernel - 1) // 2
    for h in range(halves):
        cols = slice(h * LANES, (h + 1) * LANES)

        def convolve(i, carry):
            s1, s2 = carry
            base = pl.multiple_of(i * cb, 8)
            acc = jnp.zeros((cb, LANES), F32)
            for k in range(kernel):
                acc = acc + taps[k : k + 1, cols] * gp[h, pl.ds(base + EDGE - margin + k, cb), :]
            conv_o[0, pl.ds(base, cb), cols] = acc
            pos = rows_of(cb, base - EDGE)
            kept = jnp.where((pos >= 0) & (pos < jnp.minimum(hi, frames)), acc, 0.0)
            return s1 + fold_rows(kept), s2 + fold_rows(kept * kept)

        none = jnp.zeros((8, LANES), F32)
        s1, s2 = lax.fori_loop(0, span // cb, convolve, (none, none))
        add = jnp.concatenate(
            [jnp.sum(s1, axis=0, keepdims=True), jnp.sum(s2, axis=0, keepdims=True)], axis=0
        )
        st[:, cols] = jnp.where(r == 0, 0.0, st[:, cols]) + add

    @pl.when(r == pl.num_programs(0) - 1)
    def _():
        spread_sums(st_o, st[...])


def batch_norm(stats, count):
    sums = jnp.sum(stats[...], axis=0)
    centre = sums[0:1] / count
    spread = sums[1:2] / count - centre * centre
    return centre, lax.rsqrt(spread + EPSILON)


def norm_kernel(
    meta, count, stats, affine, select, grads, halo, wo, conv,
    swished_o, gn_o, picked_o, st_o, st, ping, pong
):
    r = pl.program_id(0)
    hi = meta[0, r]
    lo = meta[1, r]
    frames = grads.shape[1]
    centre, inv = batch_norm(stats, count[0, 0])
    gain, shift = affine[0:1, :], affine[1:2, :]

    def part(row, swish_grad):
        size = swish_grad.shape[0]
        unit = (conv[0, pl.ds(row, size), :] - centre) * inv
        normalized = unit * gain + shift
        s = sigmoid(normalized)
        pos = rows_of(size, row - EDGE)
        keep = (pos >= lo) & (pos < hi)
        swished = jnp.where(keep, normalized * s, 0.0)
        gn = jnp.where(keep, swish_grad, 0.0) * (s + normalized * (s - s * s))
        gn_o[0, pl.ds(row, size), :] = gn
        return unit, swished, gn

    edge = dot(halo[0], wo[...])
    part(0, edge[:EDGE])
    part(frames + EDGE, edge[EDGE:])
    step = block_rows(frames, 512)
    small = block_rows(step, 32)
    s1 = jnp.zeros((8, conv.shape[2]), F32)
    s2 = s1
    held = (ping, pong)
    ping[...] = dot(grads[0, :step, :], wo[...])
    for i in range(frames // step):
        now = held[i % 2]
        if (i + 1) * step < frames:
            held[(i + 1) % 2][...] = dot(grads[0, (i + 1) * step : (i + 2) * step, :], wo[...])
        picked_o[0, :, i * step : (i + 1) * step] = dot_nt(
            select[...], grads[0, i * step : (i + 1) * step, :]
        ).astype(BF16)
        for j in range(step // small):
            base = i * step + j * small
            unit, swished, gn = part(base + EDGE, now[j * small : (j + 1) * small, :])
            swished_o[0, base : base + small, :] = swished.astype(BF16)
            s1 = s1 + fold_rows(gn)
            s2 = s2 + fold_rows(gn * unit)
    add = jnp.concatenate(
        [jnp.sum(s1, axis=0, keepdims=True), jnp.sum(s2, axis=0, keepdims=True)], axis=0
    )
    st[...] = jnp.where(r == 0, 0.0, st[...]) + add

    @pl.when(r == pl.num_programs(0) - 1)
    def _():
        spread_sums(st_o, st[...])


def back_kernel(
    record, blocks, meta, count, stats, sums, gain, gn, conv, vl, sg, taps, out, taps_o, gc, acc
):
    i = pl.program_id(0)
    frames, width = vl.shape[1:]
    hi = meta[0, record + i // blocks]
    lo = meta[1, record + i // blocks]
    halves = width // LANES
    span = frames + 2 * EDGE
    kernel = taps.shape[0]
    margin = (kernel - 1) // 2
    cb = block_rows(span, 144)
    step = block_rows(frames, 64)
    total_frames = count[0, 0]
    centre, inv = batch_norm(stats, total_frames)
    grad_sums = jnp.sum(sums[...], axis=0)
    scale = gain[...] * inv
    offset = scale * grad_sums[0:1] / total_frames
    slope = scale * inv * grad_sums[1:2] / total_frames
    first = i % blocks * frames

    @pl.when(i == 0)
    def _():
        acc[...] = jnp.zeros_like(acc)

    for h in range(halves):
        cols = slice(h * LANES, (h + 1) * LANES)
        for base in range(0, span, cb):
            pos = rows_of(cb, first + (base - EDGE))
            mean = offset[:, cols] + (conv[0, base : base + cb, cols] - centre[:, cols]) * slope[:, cols]
            gc[h, base : base + cb, :] = scale[:, cols] * gn[0, base : base + cb, cols] - jnp.where(
                (pos >= lo) & (pos < hi), mean, 0.0
            )
        sums_k = [acc[h, k] for k in range(kernel)]
        for base in range(0, frames, step):
            v = vl[0, base : base + step, cols]
            s = sg[0, base : base + step, cols]
            keep = rows_of(step, first + base) < hi
            vs = v * s
            gated = jnp.where(keep, vs, 0.0)
            total = jnp.zeros((step, LANES), F32)
            for k in range(kernel):
                window = gc[h, base + EDGE + margin - k : base + EDGE + margin - k + step, :]
                total = total + taps[k : k + 1, cols] * window
                sums_k[k] = sums_k[k] + fold_rows(window * gated)
            total = jnp.where(keep, total, 0.0)
            out[base : base + step, cols] = (total * s).astype(BF16)
            out[base : base + step, width + h * LANES : width + (h + 1) * LANES] = (
                total * (vs - vs * s)
            ).astype(BF16)
        for k in range(kernel):
            acc[h, k] = sums_k[k]

    @pl.when(i == pl.num_programs(0) - 1)
    def _():
        taps_o[...] = jnp.zeros_like(taps_o)
        for h in range(halves):
            for k in range(kernel):
                taps_o[k : k + 1, h * LANES : (h + 1) * LANES] = jnp.sum(
                    acc[h, k], axis=0, keepdims=True
                )


def partial_kernel(own, sibling, w_own, w_sibling, picked, mine, *others):
    total = dot_nt(w_own[...], own[...]) + dot_nt(w_sibling[...], sibling[...])
    rows = picked.shape[1]
    seqs, _, piece, frames = mine.shape
    mine[...] = (
        (total[:rows] + picked[0].astype(F32)).astype(BF16).reshape(seqs, 1, piece, frames)
    )
    for d, other in enumerate(others):
        other[...] = (
            total[(d + 1) * rows : (d + 2) * rows].astype(BF16).reshape(seqs, 1, piece, frames)
        )


def add_kernel(*refs):
    total = refs[0][...].astype(F32)
    for other in refs[1:-1]:
        total = total + other[...].astype(F32)
    refs[-1][...] = total.astype(BF16)


def first_outer_kernel(grads, swished, out, acc):
    r = pl.program_id(0)
    add = dot_tn(swished[0], grads[0])
    acc[...] = add + jnp.where(r == 0, 0.0, acc[...])

    @pl.when(r == pl.num_programs(0) - 1)
    def _():
        shard = out.shape[2]
        for s in range(out.shape[0]):
            out[s] = acc[:, s * shard : (s + 1) * shard].astype(BF16)


def outer_kernel(groups, parity, x, *refs):
    lefts, taps = refs[: len(groups)], refs[len(groups) : 2 * len(groups)]
    keep, send, acc = refs[2 * len(groups) :]
    records = groups[-1][0] + groups[-1][1]
    width = acc.shape[0] // 2
    shard = keep.shape[2]
    r = pl.program_id(0)
    for (first, size), left in zip(groups, lefts):

        @pl.when((r >= first) & (r < first + size))
        def _(left=left):
            add = dot_tn(left[...], x[0])
            acc[...] = add + jnp.where(r == 0, 0.0, acc[...])

    @pl.when(r == records - 1)
    def _():
        tap_sums = taps[0][...]
        for part in taps[1:]:
            tap_sums = tap_sums + part[...]

        def write(place, odd):
            for j in range(place.shape[0]):
                at = (2 * j + odd) * shard
                place[j, : 2 * width, :] = acc[:, at : at + shard].astype(BF16)
                for q in range(width // shard):
                    row = 2 * width + 16 * q
                    place[j, row : row + 16, :] = tap_sums[:, q * shard : (q + 1) * shard].astype(
                        BF16
                    )

        @pl.when(parity[0, 0] == 0)
        def _():
            write(keep, 0)
            write(send, 1)

        @pl.when(parity[0, 0] != 0)
        def _():
            write(keep, 1)
            write(send, 0)


def fold_kernel(parity, own, other, keep, send):
    def write(place, odd):
        for j in range(place.shape[0]):
            total = own[2 * j + odd].astype(F32) + other[2 * j + odd].astype(F32)
            place[j] = total.astype(BF16)

    @pl.when(parity[0, 0] == 0)
    def _():
        write(keep, 0)
        write(send, 1)

    @pl.when(parity[0, 0] != 0)
    def _():
        write(keep, 1)
        write(send, 0)


def finish_kernel(kernel, own, other, ready, value, gate, out, taps):
    width = value.shape[1]
    shard = value.shape[0]

    def total(row, size):
        return own[0, row : row + size, :].astype(F32) + other[0, row : row + size, :].astype(F32)

    value[...] = total(0, width).T
    gate[...] = total(width, width).T
    out[...] = ready[0].astype(F32).T
    for q in range(width // shard):
        taps[:, q * shard : (q + 1) * shard] = total(2 * width + 16 * q, 16)[:kernel]


def place_kernel(moved, *refs):
    out = refs[-1]
    frames = moved.shape[3]
    for s in range(moved.shape[0]):
        out[0, :, s * frames : (s + 1) * frames] = moved[s, 0]


def exchange(copies, axis):
    return lax.all_to_all(copies, axis, 0, 0, tiled=True)


def per_device(
    normed,
    grad_out,
    value_weight,
    gate_weight,
    depth_taps,
    norm_gain,
    norm_shift,
    out_weight,
    lengths,
):
    recs, frames, model = normed.shape
    kernel = depth_taps.shape[0]
    width = value_weight.shape[1]
    seqs = lax.axis_size("seq")
    tps = lax.axis_size("tp")
    chips = tps // 2
    piece = model // (seqs * tps)
    rows = seqs * piece
    shard = model // seqs
    span = frames + 2 * EDGE
    seq_at = lax.axis_index("seq")
    tp_at = lax.axis_index("tp")
    chip_at, core_at = tp_at // 2, tp_at % 2
    count = jnp.sum(lengths).astype(F32)
    first = (seq_at * frames).astype(jnp.int32)
    meta = jnp.stack([lengths - first, jnp.full((recs,), 0, jnp.int32) - first])
    halves = width // LANES
    counts = count.reshape(1, 1)
    parity = (seq_at % 2).astype(jnp.int32).reshape(1, 1)
    sds = jax.ShapeDtypeStruct

    low_edge = jnp.concatenate([normed[:, -EDGE:], grad_out[:, -EDGE:]], axis=2)
    high_edge = jnp.concatenate([normed[:, :EDGE], grad_out[:, :EDGE]], axis=2)
    up = [(i, i + 1) for i in range(seqs - 1)]
    down = [(j, i) for i, j in up]
    halo = jnp.concatenate(
        [lax.ppermute(low_edge, "seq", up), lax.ppermute(high_edge, "seq", down)], axis=1
    )
    halo_x, halo_g = halo[:, :, :model], halo[:, :, model:]

    channel = (
        jnp.arange(seqs, dtype=jnp.int32)[:, None] * (tps * piece)
        + tp_at * piece
        + jnp.arange(piece, dtype=jnp.int32)[None, :]
    ).reshape(rows, 1)
    select = (channel == jnp.arange(model, dtype=jnp.int32)[None, :]).astype(BF16)
    array_bytes = recs * frames * width * 4
    input_bytes = recs * frames * model * 2
    matmul = 2 * recs * frames * model * width

    vl, sg, conv, stats = call(
        gate_kernel,
        "gate_conv",
        (recs,),
        [
            smem(),
            per_record((frames, model)),
            per_record((2 * EDGE, model)),
            whole((model, width)),
            whole((model, width)),
            whole((kernel, width)),
        ],
        [
            per_record((frames, width)),
            per_record((frames, width)),
            per_record((span, width)),
            whole((seqs, 2, width)),
        ],
        [
            sds((recs, frames, width), F32),
            sds((recs, frames, width), F32),
            sds((recs, span, width), F32),
            sds((seqs, 2, width), F32),
        ],
        [pltpu.VMEM((halves, frames + 4 * EDGE, LANES), F32), pltpu.VMEM((2, width), F32)],
        2 * matmul,
        input_bytes + 3 * array_bytes,
    )(meta, normed, halo_x, value_weight, gate_weight, depth_taps)
    both = jnp.concatenate([after(value_weight, stats), gate_weight], axis=1).reshape(seqs, tps, piece, 2 * width)

    def chosen(core):
        picks = [
            lax.dynamic_index_in_dim(both, ((chip_at + d) % chips) * 2 + core, 1, keepdims=False)
            for d in range(chips)
        ]
        return jnp.stack(picks).reshape(chips * rows, 2 * width)

    swap = [(i, i ^ 1) for i in range(tps)]
    w_own = chosen(core_at)
    w_sibling = lax.ppermute(chosen(1 - core_at), "tp", swap)

    stats = exchange(stats, "seq")

    chunk = block_rows(frames, 256)
    half_rows = block_rows(frames, 512)
    swished, gn, picked, sums = call(
        norm_kernel,
        "swish_norm",
        (recs,),
        [
            smem(),
            smem(),
            whole((seqs, 2, width)),
            whole((2, width)),
            whole((rows, model)),
            per_record((frames, model)),
            per_record((2 * EDGE, model)),
            whole((model, width)),
            per_record((span, width)),
        ],
        [
            per_record((frames, width)),
            per_record((span, width)),
            per_record((rows, frames)),
            whole((seqs, 2, width)),
        ],
        [
            sds((recs, frames, width), BF16),
            sds((recs, span, width), F32),
            sds((recs, rows, frames), BF16),
            sds((seqs, 2, width), F32),
        ],
        [
            pltpu.VMEM((2, width), F32),
            pltpu.VMEM((block_rows(frames, 512), width), F32),
            pltpu.VMEM((block_rows(frames, 512), width), F32),
        ],
        2 * matmul,
        input_bytes + 3 * array_bytes,
    )(
        meta,
        counts,
        stats,
        jnp.stack([norm_gain, norm_shift]),
        after(select, w_own, w_sibling),
        grad_out,
        halo_g,
        out_weight,
        conv,
    )
    w_out = call(
        first_outer_kernel,
        "outer_w_out",
        (recs,),
        [per_record((frames, model)), per_record((frames, width))],
        whole((seqs, width, shard)),
        sds((seqs, width, shard), BF16),
        [pltpu.VMEM((width, model), F32)],
        matmul,
        input_bytes,
    )(grad_out, swished)
    sums = exchange(sums, "seq")
    grad_shift, grad_gain = jnp.sum(sums, axis=0)

    blocks = frames // chunk
    parts_in = frames // half_rows

    def back(first, size, *earlier):
        def window(i):
            return (first + i // blocks, pl.multiple_of(i % blocks * chunk, chunk), 0)

        def block(i):
            return (first + i // blocks, i % blocks, 0)

        return call(
            functools.partial(back_kernel, first, blocks),
            "back_conv",
            (size * blocks,),
            [
                smem(),
                smem(),
                whole((seqs, 2, width)),
                whole((seqs, 2, width)),
                whole((1, width)),
                pl.BlockSpec((pl.Element(1), pl.Element(chunk + 2 * EDGE), pl.Element(width)), window),
                pl.BlockSpec((pl.Element(1), pl.Element(chunk + 2 * EDGE), pl.Element(width)), window),
                pl.BlockSpec((1, chunk, width), block),
                pl.BlockSpec((1, chunk, width), block),
                whole((kernel, width)),
            ],
            [pl.BlockSpec((chunk, 2 * width), lambda i: (i, 0)), whole((16, width))],
            [sds((size * frames, 2 * width), BF16), sds((16, width), F32)],
            [
                pltpu.VMEM((halves, chunk + 2 * EDGE, LANES), F32),
                pltpu.VMEM((halves, kernel, 8, LANES), F32),
            ],
            0,
            1024,
        )(meta, counts, stats, sums, norm_gain[None], gn, conv, vl, sg, after(depth_taps, *earlier))

    def partials(first, size, mine, *earlier):
        sibling = lax.ppermute(mine, "tp", swap)
        out = sds((seqs, size, piece, frames), BF16)
        return call(
            partial_kernel,
            "partial_in",
            (size * parts_in,),
            [
                pl.BlockSpec((half_rows, 2 * width), lambda i: (i, 0)),
                pl.BlockSpec((half_rows, 2 * width), lambda i: (i, 0)),
                whole((chips * rows, 2 * width)),
                whole((chips * rows, 2 * width)),
                pl.BlockSpec(
                    (1, rows, half_rows), lambda i: (first + i // parts_in, 0, i % parts_in)
                ),
            ],
            [
                pl.BlockSpec(
                    (seqs, 1, piece, half_rows), lambda i: (0, i // parts_in, 0, i % parts_in)
                )
            ]
            * chips,
            [out] * chips,
            [],
            0,
            1024,
        )(mine, sibling, after(w_own, *earlier), w_sibling, picked)

    def deliver(part, *earlier):
        arrived = []
        for d in range(1, chips):
            send = [(i, ((i // 2 + d) % chips) * 2 + i % 2) for i in range(tps)]
            arrived.append(lax.ppermute(part[d], "tp", send))
        size = part[0].shape[1]
        block = pl.BlockSpec(
            (seqs, 1, piece, half_rows), lambda i: (0, i // parts_in, 0, i % parts_in)
        )
        own = call(
            add_kernel,
            "add",
            (size * parts_in,),
            [block] * chips,
            block,
            sds(part[0].shape, BF16),
            [],
            50_000_000_000,
            1024,
        )(after(part[0], *earlier), *arrived)
        return own

    groups = ((0, 1), (1, 1), (2, recs - 2))
    grads = [None] * 3
    taps = [None] * 3
    parts = [None] * 3
    owns = [None] * 3
    moved = [None] * 3
    w_out_sum = lax.psum_scatter(w_out, "seq", scatter_dimension=0, tiled=True)
    grads[0], taps[0] = back(*groups[0], w_out)
    grads[1], taps[1] = back(*groups[1], grads[0])
    parts[0] = partials(*groups[0], grads[0], grads[1])
    grads[2], taps[2] = back(*groups[2], *parts[0])
    parts[1] = partials(*groups[1], grads[1], grads[2])
    owns[0] = deliver(parts[0], *parts[1])
    moved[0] = exchange(owns[0], "seq")
    owns[1] = deliver(parts[1], owns[0])
    parts[2] = partials(*groups[2], grads[2], owns[1])

    slots = 2 * width + 16 * (width // shard)
    half = sds((seqs // 2, slots, shard), BF16)
    keep, send = call(
        functools.partial(outer_kernel, groups),
        "outer_w_in",
        (recs,),
        [smem(), per_record((frames, model))]
        + [
            pl.BlockSpec(
                (frames, 2 * width),
                lambda r, first=first, size=size: (jnp.clip(r - first, 0, size - 1), 0),
            )
            for first, size in groups
        ]
        + [whole((16, width))] * len(groups),
        [whole(half.shape)] * 2,
        [half] * 2,
        [pltpu.VMEM((2 * width, model), F32)],
        50_000_000_000,
        1024,
    )(parity, after(normed, *parts[2]), *grads, *taps)
    moved[1] = exchange(after(owns[1], keep, moved[0]), "seq")
    bit = 1
    while True:
        others = lax.ppermute(send, "seq", [(i, i ^ bit) for i in range(seqs)])
        if bit == 1:
            owns[2] = deliver(parts[2], others)
            moved[2] = exchange(after(owns[2], moved[1]), "seq")
        bit *= 2
        if bit == seqs:
            break
        shape = (keep.shape[0] // 2,) + keep.shape[1:]
        side = ((seq_at // bit) % 2).astype(jnp.int32).reshape(1, 1)
        keep, send = call(
            fold_kernel,
            "fold",
            (1,),
            [smem()] + [whole(keep.shape)] * 2,
            [whole(shape)] * 2,
            [sds(shape, BF16)] * 2,
            [],
            0,
            1024,
            vmem=20,
        )(side, keep, others)
    w_value, w_gate, w_out, grad_taps = call(
        functools.partial(finish_kernel, kernel),
        "finish",
        (1,),
        [whole(keep.shape)] * 2 + [whole((1, width, shard))],
        [whole((shard, width))] * 3 + [whole((kernel, width))],
        [sds((shard, width), F32)] * 3 + [sds((kernel, width), F32)],
        [],
        0,
        1024,
        vmem=20,
    )(keep, others, w_out_sum)
    grad_in = ()
    for (first, size), part in zip(groups, moved):
        grad_in = (
            call(
                place_kernel,
                "place",
                (size,),
                [pl.BlockSpec((seqs, 1, piece, frames), lambda i: (0, i, 0, 0))]
                + [anywhere()] * len(grad_in),
                pl.BlockSpec((1, piece, seqs * frames), lambda i, first=first: (first + i, 0, 0)),
                sds((recs, piece, seqs * frames), BF16),
                [],
                0,
                4 * size * piece * seqs * frames,
                {1: 0} if grad_in else None,
                vmem=20,
            )(part, *grad_in),
        )
    (grad_in,) = grad_in
    return (grad_in, w_value, w_gate, w_out, grad_taps, grad_gain, grad_shift)


def solution(mesh):
    placed = (
        P(None, "seq", None),
        P(None, "seq", None),
        P(None, "tp"),
        P(None, "tp"),
        P(None, "tp"),
        P("tp"),
        P("tp"),
        P(None, "tp"),
        P(),
    )
    return jax.shard_map(
        per_device,
        mesh=mesh,
        in_specs=placed,
        out_specs=(
            P(None, ("seq", "tp"), None),
            P("seq", "tp"),
            P("seq", "tp"),
            P("seq", "tp"),
            P(None, "tp"),
            P("tp"),
            P("tp"),
        ),
        check_vma=False,
    )
```

```python
import functools

import jax
import jax.numpy as jnp
from jax import lax
from jax.experimental import pallas as pl
from jax.experimental.pallas import tpu as pltpu
from jax.sharding import PartitionSpec as P

EPSILON = 1e-05
EDGE = 8
LANES = 128
LONG = 50_000_000_000
F32 = jnp.float32
BF16 = jnp.bfloat16


def sigmoid(x):
    return 0.5 * jnp.tanh(0.5 * x) + 0.5


def dot(a, b):
    return jnp.dot(a, b, preferred_element_type=F32)


def dot_nt(a, b):
    return lax.dot_general(a, b, (((1,), (1,)), ((), ())), preferred_element_type=F32)


def dot_tn(a, b):
    return lax.dot_general(a, b, (((0,), (0,)), ((), ())), preferred_element_type=F32)


def rows_of(count, first):
    return first + lax.broadcasted_iota(jnp.int32, (count, 1), 0)


def fold_rows(x):
    return jnp.sum(x.reshape(x.shape[0] // 8, 8, x.shape[1]), axis=0)


def block_rows(total, most):
    return max(b for b in range(8, most + 1, 8) if total % b == 0)


def whole(shape):
    return pl.BlockSpec(shape, lambda *i: (0,) * len(shape))


def per_record(shape):
    return pl.BlockSpec((1,) + shape, lambda r: (r,) + (0,) * len(shape))


def smem():
    return pl.BlockSpec(memory_space=pltpu.SMEM)


def anywhere():
    return pl.BlockSpec(memory_space=pl.ANY)


def after(x, *earlier):
    return lax.optimization_barrier((x,) + earlier)[0]


def spread_sums(out, sums):
    for s in range(out.shape[0]):
        out[s] = sums


def call(
    kernel, name, grid, in_specs, out_specs, out_shape, scratch, flops, moved, aliases=None, vmem=63
):
    return pl.pallas_call(
        kernel,
        name=name,
        grid=grid,
        in_specs=in_specs,
        out_specs=out_specs,
        out_shape=out_shape,
        scratch_shapes=scratch,
        input_output_aliases=aliases or {},
        cost_estimate=pl.CostEstimate(flops=int(flops), bytes_accessed=int(moved), transcendentals=0),
        compiler_params=pltpu.CompilerParams(vmem_limit_bytes=vmem * 1024 * 1024),
    )


def gate_kernel(meta, x, halo, wv, wg, taps, vl_o, sg_o, conv_o, st_o, gp, st):
    r = pl.program_id(0)
    hi = meta[0, r]
    lo = meta[1, r]
    frames = x.shape[1]
    width = wv.shape[1]
    halves = width // LANES

    def put(row, value):
        for h in range(halves):
            gp[h, pl.ds(row, value.shape[0]), :] = value[:, h * LANES : (h + 1) * LANES]

    edge_v = dot(halo[0], wv[...])
    edge_g = dot(halo[0], wg[...])
    row = rows_of(2 * EDGE, 0)
    pos = jnp.where(row < EDGE, row - EDGE, row - EDGE + frames)
    edge = jnp.where((pos >= lo) & (pos < hi), edge_v * sigmoid(edge_g), 0.0)
    zero = jnp.zeros((EDGE, width), F32)
    put(0, zero)
    put(EDGE, edge[:EDGE])
    put(2 * EDGE + frames, edge[EDGE:])
    put(3 * EDGE + frames, zero)
    step = block_rows(frames, 512)
    small = block_rows(step, 64)
    for base in range(0, frames, step):
        xb = x[0, base : base + step, :]
        vl_o[0, base : base + step, :] = dot(xb, wv[...])
        sg_o[0, base : base + step, :] = dot(xb, wg[...])

    def gating(i, carry):
        base = pl.multiple_of(i * small, small)
        v = vl_o[0, pl.ds(base, small), :]
        s = sigmoid(sg_o[0, pl.ds(base, small), :])
        sg_o[0, pl.ds(base, small), :] = s
        put(2 * EDGE + base, jnp.where(rows_of(small, base) < hi, v * s, 0.0))
        return carry

    lax.fori_loop(0, frames // small, gating, 0)
    span = frames + 2 * EDGE
    cb = block_rows(span, 104)
    kernel = taps.shape[0]
    margin = (kernel - 1) // 2
    for h in range(halves):
        cols = slice(h * LANES, (h + 1) * LANES)

        def convolve(i, carry):
            s1, s2 = carry
            base = pl.multiple_of(i * cb, 8)
            acc = jnp.zeros((cb, LANES), F32)
            for k in range(kernel):
                acc = acc + taps[k : k + 1, cols] * gp[h, pl.ds(base + EDGE - margin + k, cb), :]
            conv_o[0, pl.ds(base, cb), cols] = acc
            pos = rows_of(cb, base - EDGE)
            kept = jnp.where((pos >= 0) & (pos < jnp.minimum(hi, frames)), acc, 0.0)
            return s1 + fold_rows(kept), s2 + fold_rows(kept * kept)

        none = jnp.zeros((8, LANES), F32)
        s1, s2 = lax.fori_loop(0, span // cb, convolve, (none, none))
        add = jnp.concatenate(
            [jnp.sum(s1, axis=0, keepdims=True), jnp.sum(s2, axis=0, keepdims=True)], axis=0
        )
        st[:, cols] = jnp.where(r == 0, 0.0, st[:, cols]) + add

    @pl.when(r == pl.num_programs(0) - 1)
    def _():
        spread_sums(st_o, st[...])


def batch_norm(stats, count):
    sums = jnp.sum(stats[...], axis=0)
    centre = sums[0:1] / count
    spread = sums[1:2] / count - centre * centre
    return centre, lax.rsqrt(spread + EPSILON)


def norm_kernel(
    meta, count, stats, affine, select, grads, halo, wo, conv,
    swished_o, gn_o, picked_o, st_o, st, ping, pong
):
    r = pl.program_id(0)
    hi = meta[0, r]
    lo = meta[1, r]
    frames = grads.shape[1]
    centre, inv = batch_norm(stats, count[0, 0])
    gain, shift = affine[0:1, :], affine[1:2, :]

    def part(row, swish_grad):
        size = swish_grad.shape[0]
        unit = (conv[0, pl.ds(row, size), :] - centre) * inv
        normalized = unit * gain + shift
        s = sigmoid(normalized)
        pos = rows_of(size, row - EDGE)
        keep = (pos >= lo) & (pos < hi)
        swished = jnp.where(keep, normalized * s, 0.0)
        gn = jnp.where(keep, swish_grad, 0.0) * (s + normalized * (s - s * s))
        gn_o[0, pl.ds(row, size), :] = gn
        return unit, swished, gn

    edge = dot(halo[0], wo[...])
    part(0, edge[:EDGE])
    part(frames + EDGE, edge[EDGE:])
    step = block_rows(frames, 512)
    small = block_rows(step, 32)
    s1 = jnp.zeros((8, conv.shape[2]), F32)
    s2 = s1
    held = (ping, pong)
    ping[...] = dot(grads[0, :step, :], wo[...])
    for i in range(frames // step):
        now = held[i % 2]
        if (i + 1) * step < frames:
            held[(i + 1) % 2][...] = dot(grads[0, (i + 1) * step : (i + 2) * step, :], wo[...])
        picked_o[0, :, i * step : (i + 1) * step] = dot_nt(
            select[...], grads[0, i * step : (i + 1) * step, :]
        ).astype(BF16)
        for j in range(step // small):
            base = i * step + j * small
            unit, swished, gn = part(base + EDGE, now[j * small : (j + 1) * small, :])
            swished_o[0, base : base + small, :] = swished.astype(BF16)
            s1 = s1 + fold_rows(gn)
            s2 = s2 + fold_rows(gn * unit)
    add = jnp.concatenate(
        [jnp.sum(s1, axis=0, keepdims=True), jnp.sum(s2, axis=0, keepdims=True)], axis=0
    )
    st[...] = jnp.where(r == 0, 0.0, st[...]) + add

    @pl.when(r == pl.num_programs(0) - 1)
    def _():
        spread_sums(st_o, st[...])


def back_kernel(
    record, blocks, meta, count, stats, sums, gain, gn, conv, vl, sg, taps, out, taps_o, gc, acc
):
    i = pl.program_id(0)
    frames, width = vl.shape[1:]
    hi = meta[0, record + i // blocks]
    lo = meta[1, record + i // blocks]
    halves = width // LANES
    span = frames + 2 * EDGE
    kernel = taps.shape[0]
    margin = (kernel - 1) // 2
    cb = block_rows(span, 144)
    step = block_rows(frames, 64)
    total_frames = count[0, 0]
    centre, inv = batch_norm(stats, total_frames)
    grad_sums = jnp.sum(sums[...], axis=0)
    scale = gain[...] * inv
    offset = scale * grad_sums[0:1] / total_frames
    slope = scale * inv * grad_sums[1:2] / total_frames
    first = i % blocks * frames

    @pl.when(i == 0)
    def _():
        acc[...] = jnp.zeros_like(acc)

    for h in range(halves):
        cols = slice(h * LANES, (h + 1) * LANES)
        for base in range(0, span, cb):
            pos = rows_of(cb, first + (base - EDGE))
            mean = offset[:, cols] + (conv[0, base : base + cb, cols] - centre[:, cols]) * slope[:, cols]
            gc[h, base : base + cb, :] = scale[:, cols] * gn[0, base : base + cb, cols] - jnp.where(
                (pos >= lo) & (pos < hi), mean, 0.0
            )
        sums_k = [acc[h, k] for k in range(kernel)]
        for base in range(0, frames, step):
            v = vl[0, base : base + step, cols]
            s = sg[0, base : base + step, cols]
            keep = rows_of(step, first + base) < hi
            vs = v * s
            gated = jnp.where(keep, vs, 0.0)
            total = jnp.zeros((step, LANES), F32)
            for k in range(kernel):
                window = gc[h, base + EDGE + margin - k : base + EDGE + margin - k + step, :]
                total = total + taps[k : k + 1, cols] * window
                sums_k[k] = sums_k[k] + fold_rows(window * gated)
            total = jnp.where(keep, total, 0.0)
            out[base : base + step, cols] = (total * s).astype(BF16)
            out[base : base + step, width + h * LANES : width + (h + 1) * LANES] = (
                total * (vs - vs * s)
            ).astype(BF16)
        for k in range(kernel):
            acc[h, k] = sums_k[k]

    @pl.when(i == pl.num_programs(0) - 1)
    def _():
        taps_o[...] = jnp.zeros_like(taps_o)
        for h in range(halves):
            for k in range(kernel):
                taps_o[k : k + 1, h * LANES : (h + 1) * LANES] = jnp.sum(
                    acc[h, k], axis=0, keepdims=True
                )


def partial_kernel(own, sibling, w_own, w_sibling, picked, mine, *others):
    total = dot_nt(w_own[...], own[...]) + dot_nt(w_sibling[...], sibling[...])
    rows = picked.shape[1]
    seqs, _, piece, frames = mine.shape
    mine[...] = (
        (total[:rows] + picked[0].astype(F32)).astype(BF16).reshape(seqs, 1, piece, frames)
    )
    for d, other in enumerate(others):
        other[...] = (
            total[(d + 1) * rows : (d + 2) * rows].astype(BF16).reshape(seqs, 1, piece, frames)
        )


def add_kernel(*refs):
    total = refs[0][...].astype(F32)
    for other in refs[1:-1]:
        total = total + other[...].astype(F32)
    refs[-1][...] = total.astype(BF16)


def first_outer_kernel(grads, swished, out):
    r = pl.program_id(0)
    add = dot_tn(swished[0], grads[0])

    @pl.when(r == 0)
    def _():
        out[...] = add

    @pl.when(r > 0)
    def _():
        out[...] += add


def outer_kernel(groups, parity, x, w_out, *refs):
    lefts, taps = refs[: len(groups)], refs[len(groups) : 2 * len(groups)]
    keep, send, acc = refs[2 * len(groups) :]
    records = groups[-1][0] + groups[-1][1]
    width = w_out.shape[0]
    shard = keep.shape[2]
    r = pl.program_id(0)
    for (first, size), left in zip(groups, lefts):

        @pl.when((r >= first) & (r < first + size))
        def _(left=left):
            add = dot_tn(left[...], x[0])
            acc[...] = add + jnp.where(r == 0, 0.0, acc[...])

    @pl.when(r == records - 1)
    def _():
        tap_sums = taps[0][...]
        for part in taps[1:]:
            tap_sums = tap_sums + part[...]

        def write(place, odd):
            for j in range(place.shape[0]):
                at = (2 * j + odd) * shard
                place[j, : 2 * width, :] = acc[:, at : at + shard].astype(BF16)
                place[j, 2 * width : 3 * width, :] = w_out[:, at : at + shard].astype(BF16)
                for q in range(width // shard):
                    row = 3 * width + 16 * q
                    place[j, row : row + 16, :] = tap_sums[:, q * shard : (q + 1) * shard].astype(
                        BF16
                    )

        @pl.when(parity[0, 0] == 0)
        def _():
            write(keep, 0)
            write(send, 1)

        @pl.when(parity[0, 0] != 0)
        def _():
            write(keep, 1)
            write(send, 0)


def fold_kernel(parity, own, other, keep, send):
    def write(place, odd):
        for j in range(place.shape[0]):
            total = own[2 * j + odd].astype(F32) + other[2 * j + odd].astype(F32)
            place[j] = total.astype(BF16)

    @pl.when(parity[0, 0] == 0)
    def _():
        write(keep, 0)
        write(send, 1)

    @pl.when(parity[0, 0] != 0)
    def _():
        write(keep, 1)
        write(send, 0)


def finish_kernel(kernel, own, other, value, gate, out, taps):
    width = value.shape[1]
    shard = value.shape[0]

    def total(row, size):
        return own[0, row : row + size, :].astype(F32) + other[0, row : row + size, :].astype(F32)

    for i, place in enumerate((value, gate, out)):
        place[...] = total(i * width, width).T
    for q in range(width // shard):
        taps[:, q * shard : (q + 1) * shard] = total(3 * width + 16 * q, 16)[:kernel]


def place_kernel(moved, *refs):
    out = refs[-1]
    frames = moved.shape[3]
    for s in range(moved.shape[0]):
        out[0, :, s * frames : (s + 1) * frames] = moved[s, 0]


def exchange(copies, axis):
    return lax.all_to_all(copies, axis, 0, 0, tiled=True)


def per_device(
    normed,
    grad_out,
    value_weight,
    gate_weight,
    depth_taps,
    norm_gain,
    norm_shift,
    out_weight,
    lengths,
):
    recs, frames, model = normed.shape
    kernel = depth_taps.shape[0]
    width = value_weight.shape[1]
    seqs = lax.axis_size("seq")
    tps = lax.axis_size("tp")
    chips = tps // 2
    piece = model // (seqs * tps)
    rows = seqs * piece
    shard = model // seqs
    span = frames + 2 * EDGE
    seq_at = lax.axis_index("seq")
    tp_at = lax.axis_index("tp")
    chip_at, core_at = tp_at // 2, tp_at % 2
    count = jnp.sum(lengths).astype(F32)
    first = (seq_at * frames).astype(jnp.int32)
    meta = jnp.stack([lengths - first, jnp.full((recs,), 0, jnp.int32) - first])
    halves = width // LANES
    counts = count.reshape(1, 1)
    parity = (seq_at % 2).astype(jnp.int32).reshape(1, 1)
    sds = jax.ShapeDtypeStruct

    low_edge = jnp.concatenate([normed[:, -EDGE:], grad_out[:, -EDGE:]], axis=2)
    high_edge = jnp.concatenate([normed[:, :EDGE], grad_out[:, :EDGE]], axis=2)
    up = [(i, i + 1) for i in range(seqs - 1)]
    down = [(j, i) for i, j in up]
    halo = jnp.concatenate(
        [lax.ppermute(low_edge, "seq", up), lax.ppermute(high_edge, "seq", down)], axis=1
    )
    halo_x, halo_g = halo[:, :, :model], halo[:, :, model:]

    channel = (
        jnp.arange(seqs, dtype=jnp.int32)[:, None] * (tps * piece)
        + tp_at * piece
        + jnp.arange(piece, dtype=jnp.int32)[None, :]
    ).reshape(rows, 1)
    select = (channel == jnp.arange(model, dtype=jnp.int32)[None, :]).astype(BF16)
    array_bytes = recs * frames * width * 4
    input_bytes = recs * frames * model * 2
    matmul = 2 * recs * frames * model * width

    vl, sg, conv, stats = call(
        gate_kernel,
        "gate_conv",
        (recs,),
        [
            smem(),
            per_record((frames, model)),
            per_record((2 * EDGE, model)),
            whole((model, width)),
            whole((model, width)),
            whole((kernel, width)),
        ],
        [
            per_record((frames, width)),
            per_record((frames, width)),
            per_record((span, width)),
            whole((seqs, 2, width)),
        ],
        [
            sds((recs, frames, width), F32),
            sds((recs, frames, width), F32),
            sds((recs, span, width), F32),
            sds((seqs, 2, width), F32),
        ],
        [pltpu.VMEM((halves, frames + 4 * EDGE, LANES), F32), pltpu.VMEM((2, width), F32)],
        2 * matmul,
        input_bytes + 3 * array_bytes,
    )(meta, normed, halo_x, value_weight, gate_weight, depth_taps)
    both = jnp.concatenate([after(value_weight, stats), gate_weight], axis=1).reshape(seqs, tps, piece, 2 * width)

    def chosen(core):
        picks = [
            lax.dynamic_index_in_dim(both, ((chip_at + d) % chips) * 2 + core, 1, keepdims=False)
            for d in range(chips)
        ]
        return jnp.stack(picks).reshape(chips * rows, 2 * width)

    swap = [(i, i ^ 1) for i in range(tps)]
    w_own = chosen(core_at)
    w_sibling = lax.ppermute(chosen(1 - core_at), "tp", swap)

    stats = exchange(stats, "seq")

    chunk = block_rows(frames, 256)
    half_rows = block_rows(frames, 512)
    swished, gn, picked, sums = call(
        norm_kernel,
        "swish_norm",
        (recs,),
        [
            smem(),
            smem(),
            whole((seqs, 2, width)),
            whole((2, width)),
            whole((rows, model)),
            per_record((frames, model)),
            per_record((2 * EDGE, model)),
            whole((model, width)),
            per_record((span, width)),
        ],
        [
            per_record((frames, width)),
            per_record((span, width)),
            per_record((rows, frames)),
            whole((seqs, 2, width)),
        ],
        [
            sds((recs, frames, width), BF16),
            sds((recs, span, width), F32),
            sds((recs, rows, frames), BF16),
            sds((seqs, 2, width), F32),
        ],
        [
            pltpu.VMEM((2, width), F32),
            pltpu.VMEM((block_rows(frames, 512), width), F32),
            pltpu.VMEM((block_rows(frames, 512), width), F32),
        ],
        2 * matmul,
        input_bytes + 3 * array_bytes,
    )(
        meta,
        counts,
        stats,
        jnp.stack([norm_gain, norm_shift]),
        after(select, w_own, w_sibling),
        grad_out,
        halo_g,
        out_weight,
        conv,
    )
    w_out = call(
        first_outer_kernel,
        "outer_w_out",
        (recs,),
        [per_record((frames, model)), per_record((frames, width))],
        whole((width, model)),
        sds((width, model), F32),
        [],
        matmul,
        input_bytes,
    )(grad_out, swished)
    sums = exchange(sums, "seq")
    grad_shift, grad_gain = jnp.sum(sums, axis=0)

    blocks = frames // chunk
    parts_in = frames // half_rows

    def back(first, size, *earlier):
        def window(i):
            return (first + i // blocks, pl.multiple_of(i % blocks * chunk, chunk), 0)

        def block(i):
            return (first + i // blocks, i % blocks, 0)

        return call(
            functools.partial(back_kernel, first, blocks),
            "back_conv",
            (size * blocks,),
            [
                smem(),
                smem(),
                whole((seqs, 2, width)),
                whole((seqs, 2, width)),
                whole((1, width)),
                pl.BlockSpec((pl.Element(1), pl.Element(chunk + 2 * EDGE), pl.Element(width)), window),
                pl.BlockSpec((pl.Element(1), pl.Element(chunk + 2 * EDGE), pl.Element(width)), window),
                pl.BlockSpec((1, chunk, width), block),
                pl.BlockSpec((1, chunk, width), block),
                whole((kernel, width)),
            ],
            [pl.BlockSpec((chunk, 2 * width), lambda i: (i, 0)), whole((16, width))],
            [sds((size * frames, 2 * width), BF16), sds((16, width), F32)],
            [
                pltpu.VMEM((halves, chunk + 2 * EDGE, LANES), F32),
                pltpu.VMEM((halves, kernel, 8, LANES), F32),
            ],
            0,
            1024,
        )(meta, counts, stats, sums, norm_gain[None], gn, conv, vl, sg, after(depth_taps, *earlier))

    def partials(first, size, mine, *earlier):
        sibling = lax.ppermute(mine, "tp", swap)
        out = sds((seqs, size, piece, frames), BF16)
        return call(
            partial_kernel,
            "partial_in",
            (size * parts_in,),
            [
                pl.BlockSpec((half_rows, 2 * width), lambda i: (i, 0)),
                pl.BlockSpec((half_rows, 2 * width), lambda i: (i, 0)),
                whole((chips * rows, 2 * width)),
                whole((chips * rows, 2 * width)),
                pl.BlockSpec(
                    (1, rows, half_rows), lambda i: (first + i // parts_in, 0, i % parts_in)
                ),
            ],
            [
                pl.BlockSpec(
                    (seqs, 1, piece, half_rows), lambda i: (0, i // parts_in, 0, i % parts_in)
                )
            ]
            * chips,
            [out] * chips,
            [],
            0,
            1024,
        )(mine, sibling, after(w_own, *earlier), w_sibling, picked)

    def deliver(part, weight, *earlier):
        arrived = []
        for d in range(1, chips):
            send = [(i, ((i // 2 + d) % chips) * 2 + i % 2) for i in range(tps)]
            arrived.append(lax.ppermute(part[d], "tp", send))
        size = part[0].shape[1]
        block = pl.BlockSpec(
            (seqs, 1, piece, half_rows), lambda i: (0, i // parts_in, 0, i % parts_in)
        )
        own = call(
            add_kernel,
            "add",
            (size * parts_in,),
            [block] * chips,
            block,
            sds(part[0].shape, BF16),
            [],
            weight,
            1024,
        )(after(part[0], *earlier), *arrived)
        return own

    groups = ((0, 1), (1, 1), (2, recs - 2))
    grads = [None] * 3
    taps = [None] * 3
    parts = [None] * 3
    owns = [None] * 3
    moved = [None] * 3
    grads[0], taps[0] = back(*groups[0], w_out)
    grads[1], taps[1] = back(*groups[1], grads[0])
    parts[0] = partials(*groups[0], grads[0], grads[1])
    grads[2], taps[2] = back(*groups[2], *parts[0])
    parts[1] = partials(*groups[1], grads[1], grads[2])
    owns[0] = deliver(parts[0], LONG, *parts[1])
    moved[0] = exchange(owns[0], "seq")

    slots = 3 * width + 16 * (width // shard)
    half = sds((seqs // 2, slots, shard), BF16)
    keep, send = call(
        functools.partial(outer_kernel, groups),
        "outer_w_in",
        (recs,),
        [smem(), per_record((frames, model)), whole((width, model))]
        + [
            pl.BlockSpec(
                (frames, 2 * width),
                lambda r, first=first, size=size: (jnp.clip(r - first, 0, size - 1), 0),
            )
            for first, size in groups
        ]
        + [whole((16, width))] * len(groups),
        [whole(half.shape)] * 2,
        [half] * 2,
        [pltpu.VMEM((2 * width, model), F32)],
        LONG,
        1024,
    )(parity, after(normed, owns[0]), w_out, *grads, *taps)
    owns[1] = deliver(parts[1], LONG, keep)
    moved[1] = exchange(after(owns[1], moved[0]), "seq")
    parts[2] = partials(*groups[2], grads[2], owns[1])
    bit = 1
    while True:
        others = lax.ppermute(send, "seq", [(i, i ^ bit) for i in range(seqs)])
        bit *= 2
        if bit == seqs:
            break
        if bit == 2:
            keep = after(keep, *parts[2])
        shape = (keep.shape[0] // 2,) + keep.shape[1:]
        side = ((seq_at // bit) % 2).astype(jnp.int32).reshape(1, 1)
        keep, send = call(
            fold_kernel,
            "fold",
            (1,),
            [smem()] + [whole(keep.shape)] * 2,
            [whole(shape)] * 2,
            [sds(shape, BF16)] * 2,
            [],
            LONG if bit == 2 else 0,
            1024,
            vmem=20,
        )(side, keep, others)
        if bit == min(4, seqs // 2):
            owns[2] = deliver(parts[2], 0, keep, moved[1])
            moved[2] = exchange(owns[2], "seq")
    w_value, w_gate, w_out, grad_taps = call(
        functools.partial(finish_kernel, kernel),
        "finish",
        (1,),
        [whole(keep.shape)] * 2,
        [whole((shard, width))] * 3 + [whole((kernel, width))],
        [sds((shard, width), F32)] * 3 + [sds((kernel, width), F32)],
        [],
        0,
        1024,
        vmem=20,
    )(keep, others)
    grad_in = ()
    for (first, size), part in zip(groups, moved):
        grad_in = (
            call(
                place_kernel,
                "place",
                (size,),
                [pl.BlockSpec((seqs, 1, piece, frames), lambda i: (0, i, 0, 0))]
                + [anywhere()] * len(grad_in),
                pl.BlockSpec((1, piece, seqs * frames), lambda i, first=first: (first + i, 0, 0)),
                sds((recs, piece, seqs * frames), BF16),
                [],
                0,
                4 * size * piece * seqs * frames,
                {1: 0} if grad_in else None,
                vmem=20,
            )(part, *grad_in),
        )
    (grad_in,) = grad_in
    return (grad_in, w_value, w_gate, w_out, grad_taps, grad_gain, grad_shift)


def solution(mesh):
    placed = (
        P(None, "seq", None),
        P(None, "seq", None),
        P(None, "tp"),
        P(None, "tp"),
        P(None, "tp"),
        P("tp"),
        P("tp"),
        P(None, "tp"),
        P(),
    )
    return jax.shard_map(
        per_device,
        mesh=mesh,
        in_specs=placed,
        out_specs=(
            P(None, ("seq", "tp"), None),
            P("seq", "tp"),
            P("seq", "tp"),
            P("seq", "tp"),
            P(None, "tp"),
            P("tp"),
            P("tp"),
        ),
        check_vma=False,
    )
```

```python
import functools

import jax
import jax.numpy as jnp
from jax import lax
from jax.experimental import pallas as pl
from jax.experimental.pallas import tpu as pltpu
from jax.sharding import PartitionSpec as P

EPSILON = 1e-05
EDGE = 8
LANES = 128
LONG = 50_000_000_000
F32 = jnp.float32
BF16 = jnp.bfloat16


def sigmoid(x):
    return 0.5 * jnp.tanh(0.5 * x) + 0.5


def dot(a, b):
    return jnp.dot(a, b, preferred_element_type=F32)


def dot_nt(a, b):
    return lax.dot_general(a, b, (((1,), (1,)), ((), ())), preferred_element_type=F32)


def dot_tn(a, b):
    return lax.dot_general(a, b, (((0,), (0,)), ((), ())), preferred_element_type=F32)


def rows_of(count, first):
    return first + lax.broadcasted_iota(jnp.int32, (count, 1), 0)


def fold_rows(x):
    return jnp.sum(x.reshape(x.shape[0] // 8, 8, x.shape[1]), axis=0)


def block_rows(total, most):
    return max(b for b in range(8, most + 1, 8) if total % b == 0)


def whole(shape):
    return pl.BlockSpec(shape, lambda *i: (0,) * len(shape))


def per_record(shape):
    return pl.BlockSpec((1,) + shape, lambda r: (r,) + (0,) * len(shape))


def smem():
    return pl.BlockSpec(memory_space=pltpu.SMEM)


def anywhere():
    return pl.BlockSpec(memory_space=pl.ANY)


def after(x, *earlier):
    return lax.optimization_barrier((x,) + earlier)[0]


def spread_sums(out, sums):
    for s in range(out.shape[0]):
        out[s] = sums


def call(
    kernel, name, grid, in_specs, out_specs, out_shape, scratch, flops, moved, aliases=None, vmem=63
):
    return pl.pallas_call(
        kernel,
        name=name,
        grid=grid,
        in_specs=in_specs,
        out_specs=out_specs,
        out_shape=out_shape,
        scratch_shapes=scratch,
        input_output_aliases=aliases or {},
        cost_estimate=pl.CostEstimate(flops=int(flops), bytes_accessed=int(moved), transcendentals=0),
        compiler_params=pltpu.CompilerParams(vmem_limit_bytes=vmem * 1024 * 1024),
    )


def gate_kernel(meta, x, halo, wv, wg, taps, vl_o, sg_o, conv_o, st_o, gp, st):
    r = pl.program_id(0)
    hi = meta[0, r]
    lo = meta[1, r]
    frames = x.shape[1]
    width = wv.shape[1]
    halves = width // LANES

    def put(row, value):
        for h in range(halves):
            gp[h, pl.ds(row, value.shape[0]), :] = value[:, h * LANES : (h + 1) * LANES]

    edge_v = dot(halo[0], wv[...])
    edge_g = dot(halo[0], wg[...])
    row = rows_of(2 * EDGE, 0)
    pos = jnp.where(row < EDGE, row - EDGE, row - EDGE + frames)
    edge = jnp.where((pos >= lo) & (pos < hi), edge_v * sigmoid(edge_g), 0.0)
    zero = jnp.zeros((EDGE, width), F32)
    put(0, zero)
    put(EDGE, edge[:EDGE])
    put(2 * EDGE + frames, edge[EDGE:])
    put(3 * EDGE + frames, zero)
    step = block_rows(frames, 512)
    small = block_rows(step, 64)
    for base in range(0, frames, step):
        xb = x[0, base : base + step, :]
        vl_o[0, base : base + step, :] = dot(xb, wv[...])
        sg_o[0, base : base + step, :] = dot(xb, wg[...])

    def gating(i, carry):
        base = pl.multiple_of(i * small, small)
        v = vl_o[0, pl.ds(base, small), :]
        s = sigmoid(sg_o[0, pl.ds(base, small), :])
        sg_o[0, pl.ds(base, small), :] = s
        put(2 * EDGE + base, jnp.where(rows_of(small, base) < hi, v * s, 0.0))
        return carry

    lax.fori_loop(0, frames // small, gating, 0)
    span = frames + 2 * EDGE
    cb = block_rows(span, 104)
    kernel = taps.shape[0]
    margin = (kernel - 1) // 2
    for h in range(halves):
        cols = slice(h * LANES, (h + 1) * LANES)

        def convolve(i, carry):
            s1, s2 = carry
            base = pl.multiple_of(i * cb, 8)
            acc = jnp.zeros((cb, LANES), F32)
            for k in range(kernel):
                acc = acc + taps[k : k + 1, cols] * gp[h, pl.ds(base + EDGE - margin + k, cb), :]
            conv_o[0, pl.ds(base, cb), cols] = acc
            pos = rows_of(cb, base - EDGE)
            kept = jnp.where((pos >= 0) & (pos < jnp.minimum(hi, frames)), acc, 0.0)
            return s1 + fold_rows(kept), s2 + fold_rows(kept * kept)

        none = jnp.zeros((8, LANES), F32)
        s1, s2 = lax.fori_loop(0, span // cb, convolve, (none, none))
        add = jnp.concatenate(
            [jnp.sum(s1, axis=0, keepdims=True), jnp.sum(s2, axis=0, keepdims=True)], axis=0
        )
        st[:, cols] = jnp.where(r == 0, 0.0, st[:, cols]) + add

    @pl.when(r == pl.num_programs(0) - 1)
    def _():
        spread_sums(st_o, st[...])


def batch_norm(stats, count):
    sums = jnp.sum(stats[...], axis=0)
    centre = sums[0:1] / count
    spread = sums[1:2] / count - centre * centre
    return centre, lax.rsqrt(spread + EPSILON)


def norm_kernel(
    meta, count, stats, affine, select, grads, halo, wo, conv,
    swished_o, gn_o, picked_o, st_o, st, ping, pong
):
    r = pl.program_id(0)
    hi = meta[0, r]
    lo = meta[1, r]
    frames = grads.shape[1]
    centre, inv = batch_norm(stats, count[0, 0])
    gain, shift = affine[0:1, :], affine[1:2, :]

    def part(row, swish_grad):
        size = swish_grad.shape[0]
        unit = (conv[0, pl.ds(row, size), :] - centre) * inv
        normalized = unit * gain + shift
        s = sigmoid(normalized)
        pos = rows_of(size, row - EDGE)
        keep = (pos >= lo) & (pos < hi)
        swished = jnp.where(keep, normalized * s, 0.0)
        gn = jnp.where(keep, swish_grad, 0.0) * (s + normalized * (s - s * s))
        gn_o[0, pl.ds(row, size), :] = gn
        return unit, swished, gn

    edge = dot(halo[0], wo[...])
    part(0, edge[:EDGE])
    part(frames + EDGE, edge[EDGE:])
    step = block_rows(frames, 512)
    small = block_rows(step, 32)
    s1 = jnp.zeros((8, conv.shape[2]), F32)
    s2 = s1
    held = (ping, pong)
    ping[...] = dot(grads[0, :step, :], wo[...])
    for i in range(frames // step):
        now = held[i % 2]
        if (i + 1) * step < frames:
            held[(i + 1) % 2][...] = dot(grads[0, (i + 1) * step : (i + 2) * step, :], wo[...])
        picked_o[0, :, i * step : (i + 1) * step] = dot_nt(
            select[...], grads[0, i * step : (i + 1) * step, :]
        ).astype(BF16)
        for j in range(step // small):
            base = i * step + j * small
            unit, swished, gn = part(base + EDGE, now[j * small : (j + 1) * small, :])
            swished_o[0, base : base + small, :] = swished.astype(BF16)
            s1 = s1 + fold_rows(gn)
            s2 = s2 + fold_rows(gn * unit)
    add = jnp.concatenate(
        [jnp.sum(s1, axis=0, keepdims=True), jnp.sum(s2, axis=0, keepdims=True)], axis=0
    )
    st[...] = jnp.where(r == 0, 0.0, st[...]) + add

    @pl.when(r == pl.num_programs(0) - 1)
    def _():
        spread_sums(st_o, st[...])


def back_kernel(
    record, blocks, meta, count, stats, sums, gain, gn, conv, vl, sg, taps, out, taps_o, gc, acc
):
    i = pl.program_id(0)
    frames, width = vl.shape[1:]
    hi = meta[0, record + i // blocks]
    lo = meta[1, record + i // blocks]
    halves = width // LANES
    span = frames + 2 * EDGE
    kernel = taps.shape[0]
    margin = (kernel - 1) // 2
    cb = block_rows(span, 144)
    step = block_rows(frames, 64)
    total_frames = count[0, 0]
    centre, inv = batch_norm(stats, total_frames)
    grad_sums = jnp.sum(sums[...], axis=0)
    scale = gain[...] * inv
    offset = scale * grad_sums[0:1] / total_frames
    slope = scale * inv * grad_sums[1:2] / total_frames
    first = i % blocks * frames

    @pl.when(i == 0)
    def _():
        acc[...] = jnp.zeros_like(acc)

    for h in range(halves):
        cols = slice(h * LANES, (h + 1) * LANES)
        for base in range(0, span, cb):
            pos = rows_of(cb, first + (base - EDGE))
            mean = offset[:, cols] + (conv[0, base : base + cb, cols] - centre[:, cols]) * slope[:, cols]
            gc[h, base : base + cb, :] = scale[:, cols] * gn[0, base : base + cb, cols] - jnp.where(
                (pos >= lo) & (pos < hi), mean, 0.0
            )
        sums_k = [acc[h, k] for k in range(kernel)]
        for base in range(0, frames, step):
            v = vl[0, base : base + step, cols]
            s = sg[0, base : base + step, cols]
            keep = rows_of(step, first + base) < hi
            vs = v * s
            gated = jnp.where(keep, vs, 0.0)
            total = jnp.zeros((step, LANES), F32)
            for k in range(kernel):
                window = gc[h, base + EDGE + margin - k : base + EDGE + margin - k + step, :]
                total = total + taps[k : k + 1, cols] * window
                sums_k[k] = sums_k[k] + fold_rows(window * gated)
            total = jnp.where(keep, total, 0.0)
            out[base : base + step, cols] = (total * s).astype(BF16)
            out[base : base + step, width + h * LANES : width + (h + 1) * LANES] = (
                total * (vs - vs * s)
            ).astype(BF16)
        for k in range(kernel):
            acc[h, k] = sums_k[k]

    @pl.when(i == pl.num_programs(0) - 1)
    def _():
        taps_o[...] = jnp.zeros_like(taps_o)
        for h in range(halves):
            for k in range(kernel):
                taps_o[k : k + 1, h * LANES : (h + 1) * LANES] = jnp.sum(
                    acc[h, k], axis=0, keepdims=True
                )


def partial_kernel(own, sibling, w_own, w_sibling, picked, mine, *others):
    total = dot_nt(w_own[...], own[...]) + dot_nt(w_sibling[...], sibling[...])
    rows = picked.shape[1]
    seqs, _, piece, frames = mine.shape
    mine[...] = (
        (total[:rows] + picked[0].astype(F32)).astype(BF16).reshape(seqs, 1, piece, frames)
    )
    for d, other in enumerate(others):
        other[...] = (
            total[(d + 1) * rows : (d + 2) * rows].astype(BF16).reshape(seqs, 1, piece, frames)
        )


def add_kernel(*refs):
    total = refs[0][...].astype(F32)
    for other in refs[1:-1]:
        total = total + other[...].astype(F32)
    refs[-1][...] = total.astype(BF16)


def first_outer_kernel(grads, swished, out):
    r = pl.program_id(0)
    add = dot_tn(swished[0], grads[0])

    @pl.when(r == 0)
    def _():
        out[...] = add

    @pl.when(r > 0)
    def _():
        out[...] += add


def outer_kernel(groups, parity, x, w_out, *refs):
    lefts, taps = refs[: len(groups)], refs[len(groups) : 2 * len(groups)]
    keep, send, acc = refs[2 * len(groups) :]
    records = groups[-1][0] + groups[-1][1]
    width = w_out.shape[0]
    shard = keep.shape[2]
    r = pl.program_id(0)
    for (first, size), left in zip(groups, lefts):

        @pl.when((r >= first) & (r < first + size))
        def _(left=left):
            add = dot_tn(left[...], x[0])
            acc[...] = add + jnp.where(r == 0, 0.0, acc[...])

    @pl.when(r == records - 1)
    def _():
        tap_sums = taps[0][...]
        for part in taps[1:]:
            tap_sums = tap_sums + part[...]

        def write(place, odd):
            for j in range(place.shape[0]):
                at = (2 * j + odd) * shard
                place[j, : 2 * width, :] = acc[:, at : at + shard].astype(BF16)
                place[j, 2 * width : 3 * width, :] = w_out[:, at : at + shard].astype(BF16)
                for q in range(width // shard):
                    row = 3 * width + 16 * q
                    place[j, row : row + 16, :] = tap_sums[:, q * shard : (q + 1) * shard].astype(
                        BF16
                    )

        @pl.when(parity[0, 0] == 0)
        def _():
            write(keep, 0)
            write(send, 1)

        @pl.when(parity[0, 0] != 0)
        def _():
            write(keep, 1)
            write(send, 0)


def fold_kernel(parity, own, other, keep, send):
    def write(place, odd):
        for j in range(place.shape[0]):
            total = own[2 * j + odd].astype(F32) + other[2 * j + odd].astype(F32)
            place[j] = total.astype(BF16)

    @pl.when(parity[0, 0] == 0)
    def _():
        write(keep, 0)
        write(send, 1)

    @pl.when(parity[0, 0] != 0)
    def _():
        write(keep, 1)
        write(send, 0)


def finish_kernel(kernel, own, other, value, gate, out, taps):
    width = value.shape[1]
    shard = value.shape[0]

    def total(row, size):
        return own[0, row : row + size, :].astype(F32) + other[0, row : row + size, :].astype(F32)

    for i, place in enumerate((value, gate, out)):
        place[...] = total(i * width, width).T
    for q in range(width // shard):
        taps[:, q * shard : (q + 1) * shard] = total(3 * width + 16 * q, 16)[:kernel]


def place_kernel(moved, *refs):
    out = refs[-1]
    frames = moved.shape[3]
    for s in range(moved.shape[0]):
        out[0, :, s * frames : (s + 1) * frames] = moved[s, 0]


def exchange(copies, axis):
    return lax.all_to_all(copies, axis, 0, 0, tiled=True)


def per_device(
    normed,
    grad_out,
    value_weight,
    gate_weight,
    depth_taps,
    norm_gain,
    norm_shift,
    out_weight,
    lengths,
):
    recs, frames, model = normed.shape
    kernel = depth_taps.shape[0]
    width = value_weight.shape[1]
    seqs = lax.axis_size("seq")
    tps = lax.axis_size("tp")
    chips = tps // 2
    piece = model // (seqs * tps)
    rows = seqs * piece
    shard = model // seqs
    span = frames + 2 * EDGE
    seq_at = lax.axis_index("seq")
    tp_at = lax.axis_index("tp")
    chip_at, core_at = tp_at // 2, tp_at % 2
    count = jnp.sum(lengths).astype(F32)
    first = (seq_at * frames).astype(jnp.int32)
    meta = jnp.stack([lengths - first, jnp.full((recs,), 0, jnp.int32) - first])
    halves = width // LANES
    counts = count.reshape(1, 1)
    parity = (seq_at % 2).astype(jnp.int32).reshape(1, 1)
    sds = jax.ShapeDtypeStruct

    low_edge = jnp.concatenate([normed[:, -EDGE:], grad_out[:, -EDGE:]], axis=2)
    high_edge = jnp.concatenate([normed[:, :EDGE], grad_out[:, :EDGE]], axis=2)
    up = [(i, i + 1) for i in range(seqs - 1)]
    down = [(j, i) for i, j in up]
    halo = jnp.concatenate(
        [lax.ppermute(low_edge, "seq", up), lax.ppermute(high_edge, "seq", down)], axis=1
    )
    halo_x, halo_g = halo[:, :, :model], halo[:, :, model:]

    channel = (
        jnp.arange(seqs, dtype=jnp.int32)[:, None] * (tps * piece)
        + tp_at * piece
        + jnp.arange(piece, dtype=jnp.int32)[None, :]
    ).reshape(rows, 1)
    select = (channel == jnp.arange(model, dtype=jnp.int32)[None, :]).astype(BF16)
    array_bytes = recs * frames * width * 4
    input_bytes = recs * frames * model * 2
    matmul = 2 * recs * frames * model * width

    vl, sg, conv, stats = call(
        gate_kernel,
        "gate_conv",
        (recs,),
        [
            smem(),
            per_record((frames, model)),
            per_record((2 * EDGE, model)),
            whole((model, width)),
            whole((model, width)),
            whole((kernel, width)),
        ],
        [
            per_record((frames, width)),
            per_record((frames, width)),
            per_record((span, width)),
            whole((seqs, 2, width)),
        ],
        [
            sds((recs, frames, width), F32),
            sds((recs, frames, width), F32),
            sds((recs, span, width), F32),
            sds((seqs, 2, width), F32),
        ],
        [pltpu.VMEM((halves, frames + 4 * EDGE, LANES), F32), pltpu.VMEM((2, width), F32)],
        2 * matmul,
        input_bytes + 3 * array_bytes,
    )(meta, normed, halo_x, value_weight, gate_weight, depth_taps)
    both = jnp.concatenate([after(value_weight, stats), gate_weight], axis=1).reshape(seqs, tps, piece, 2 * width)

    def chosen(core):
        picks = [
            lax.dynamic_index_in_dim(both, ((chip_at + d) % chips) * 2 + core, 1, keepdims=False)
            for d in range(chips)
        ]
        return jnp.stack(picks).reshape(chips * rows, 2 * width)

    swap = [(i, i ^ 1) for i in range(tps)]
    w_own = chosen(core_at)
    w_sibling = lax.ppermute(chosen(1 - core_at), "tp", swap)

    stats = exchange(stats, "seq")

    chunk = block_rows(frames, 256)
    half_rows = block_rows(frames, 512)
    swished, gn, picked, sums = call(
        norm_kernel,
        "swish_norm",
        (recs,),
        [
            smem(),
            smem(),
            whole((seqs, 2, width)),
            whole((2, width)),
            whole((rows, model)),
            per_record((frames, model)),
            per_record((2 * EDGE, model)),
            whole((model, width)),
            per_record((span, width)),
        ],
        [
            per_record((frames, width)),
            per_record((span, width)),
            per_record((rows, frames)),
            whole((seqs, 2, width)),
        ],
        [
            sds((recs, frames, width), BF16),
            sds((recs, span, width), F32),
            sds((recs, rows, frames), BF16),
            sds((seqs, 2, width), F32),
        ],
        [
            pltpu.VMEM((2, width), F32),
            pltpu.VMEM((block_rows(frames, 512), width), F32),
            pltpu.VMEM((block_rows(frames, 512), width), F32),
        ],
        2 * matmul,
        input_bytes + 3 * array_bytes,
    )(
        meta,
        counts,
        stats,
        jnp.stack([norm_gain, norm_shift]),
        after(select, w_own, w_sibling),
        grad_out,
        halo_g,
        out_weight,
        conv,
    )
    w_out = call(
        first_outer_kernel,
        "outer_w_out",
        (recs,),
        [per_record((frames, model)), per_record((frames, width))],
        whole((width, model)),
        sds((width, model), F32),
        [],
        matmul,
        input_bytes,
    )(grad_out, swished)
    sums = exchange(sums, "seq")
    grad_shift, grad_gain = jnp.sum(sums, axis=0)

    blocks = frames // chunk
    parts_in = frames // half_rows

    def back(first, size, *earlier):
        def window(i):
            return (first + i // blocks, pl.multiple_of(i % blocks * chunk, chunk), 0)

        def block(i):
            return (first + i // blocks, i % blocks, 0)

        return call(
            functools.partial(back_kernel, first, blocks),
            "back_conv",
            (size * blocks,),
            [
                smem(),
                smem(),
                whole((seqs, 2, width)),
                whole((seqs, 2, width)),
                whole((1, width)),
                pl.BlockSpec((pl.Element(1), pl.Element(chunk + 2 * EDGE), pl.Element(width)), window),
                pl.BlockSpec((pl.Element(1), pl.Element(chunk + 2 * EDGE), pl.Element(width)), window),
                pl.BlockSpec((1, chunk, width), block),
                pl.BlockSpec((1, chunk, width), block),
                whole((kernel, width)),
            ],
            [pl.BlockSpec((chunk, 2 * width), lambda i: (i, 0)), whole((16, width))],
            [sds((size * frames, 2 * width), BF16), sds((16, width), F32)],
            [
                pltpu.VMEM((halves, chunk + 2 * EDGE, LANES), F32),
                pltpu.VMEM((halves, kernel, 8, LANES), F32),
            ],
            0,
            1024,
        )(meta, counts, stats, sums, norm_gain[None], gn, conv, vl, sg, after(depth_taps, *earlier))

    def partials(first, size, mine, *earlier):
        sibling = lax.ppermute(mine, "tp", swap)
        out = sds((seqs, size, piece, frames), BF16)
        return call(
            partial_kernel,
            "partial_in",
            (size * parts_in,),
            [
                pl.BlockSpec((half_rows, 2 * width), lambda i: (i, 0)),
                pl.BlockSpec((half_rows, 2 * width), lambda i: (i, 0)),
                whole((chips * rows, 2 * width)),
                whole((chips * rows, 2 * width)),
                pl.BlockSpec(
                    (1, rows, half_rows), lambda i: (first + i // parts_in, 0, i % parts_in)
                ),
            ],
            [
                pl.BlockSpec(
                    (seqs, 1, piece, half_rows), lambda i: (0, i // parts_in, 0, i % parts_in)
                )
            ]
            * chips,
            [out] * chips,
            [],
            0,
            1024,
        )(mine, sibling, after(w_own, *earlier), w_sibling, picked)

    def deliver(part, weight, *earlier):
        arrived = []
        for d in range(1, chips):
            send = [(i, ((i // 2 + d) % chips) * 2 + i % 2) for i in range(tps)]
            arrived.append(lax.ppermute(part[d], "tp", send))
        size = part[0].shape[1]
        block = pl.BlockSpec(
            (seqs, 1, piece, half_rows), lambda i: (0, i // parts_in, 0, i % parts_in)
        )
        own = call(
            add_kernel,
            "add",
            (size * parts_in,),
            [block] * chips,
            block,
            sds(part[0].shape, BF16),
            [],
            weight,
            1024,
        )(after(part[0], *earlier), *arrived)
        return own

    groups = ((0, 1), (1, 1), (2, recs - 2))
    grads = [None] * 3
    taps = [None] * 3
    parts = [None] * 3
    owns = [None] * 3
    moved = [None] * 3
    grads[0], taps[0] = back(*groups[0], w_out)
    grads[1], taps[1] = back(*groups[1], grads[0])
    parts[0] = partials(*groups[0], grads[0], grads[1])
    grads[2], taps[2] = back(*groups[2], *parts[0])
    parts[1] = partials(*groups[1], grads[1], grads[2])
    owns[0] = deliver(parts[0], LONG, *parts[1])
    parts[2] = partials(*groups[2], grads[2], owns[0])
    moved[0] = exchange(after(owns[0], *parts[2]), "seq")
    owns[1] = deliver(parts[1], 0, *parts[2])

    slots = 3 * width + 16 * (width // shard)
    half = sds((seqs // 2, slots, shard), BF16)
    keep, send = call(
        functools.partial(outer_kernel, groups),
        "outer_w_in",
        (recs,),
        [smem(), per_record((frames, model)), whole((width, model))]
        + [
            pl.BlockSpec(
                (frames, 2 * width),
                lambda r, first=first, size=size: (jnp.clip(r - first, 0, size - 1), 0),
            )
            for first, size in groups
        ]
        + [whole((16, width))] * len(groups),
        [whole(half.shape)] * 2,
        [half] * 2,
        [pltpu.VMEM((2 * width, model), F32)],
        LONG,
        1024,
    )(parity, after(normed, owns[1]), w_out, *grads, *taps)
    moved[1] = exchange(after(owns[1], keep, moved[0]), "seq")
    owns[2] = deliver(parts[2], 0, keep)
    moved[2] = exchange(after(owns[2], moved[1]), "seq")
    bit = 1
    while True:
        others = lax.ppermute(send, "seq", [(i, i ^ bit) for i in range(seqs)])
        bit *= 2
        if bit == seqs:
            break
        if bit == 2:
            keep = after(keep, owns[2])
        shape = (keep.shape[0] // 2,) + keep.shape[1:]
        side = ((seq_at // bit) % 2).astype(jnp.int32).reshape(1, 1)
        keep, send = call(
            fold_kernel,
            "fold",
            (1,),
            [smem()] + [whole(keep.shape)] * 2,
            [whole(shape)] * 2,
            [sds(shape, BF16)] * 2,
            [],
            0,
            1024,
            vmem=20,
        )(side, keep, others)
    w_value, w_gate, w_out, grad_taps = call(
        functools.partial(finish_kernel, kernel),
        "finish",
        (1,),
        [whole(keep.shape)] * 2,
        [whole((shard, width))] * 3 + [whole((kernel, width))],
        [sds((shard, width), F32)] * 3 + [sds((kernel, width), F32)],
        [],
        0,
        1024,
        vmem=20,
    )(keep, others)
    grad_in = ()
    for (first, size), part in zip(groups, moved):
        grad_in = (
            call(
                place_kernel,
                "place",
                (size,),
                [pl.BlockSpec((seqs, 1, piece, frames), lambda i: (0, i, 0, 0))]
                + [anywhere()] * len(grad_in),
                pl.BlockSpec((1, piece, seqs * frames), lambda i, first=first: (first + i, 0, 0)),
                sds((recs, piece, seqs * frames), BF16),
                [],
                0,
                4 * size * piece * seqs * frames,
                {1: 0} if grad_in else None,
                vmem=20,
            )(part, *grad_in),
        )
    (grad_in,) = grad_in
    return (grad_in, w_value, w_gate, w_out, grad_taps, grad_gain, grad_shift)


def solution(mesh):
    placed = (
        P(None, "seq", None),
        P(None, "seq", None),
        P(None, "tp"),
        P(None, "tp"),
        P(None, "tp"),
        P("tp"),
        P("tp"),
        P(None, "tp"),
        P(),
    )
    return jax.shard_map(
        per_device,
        mesh=mesh,
        in_specs=placed,
        out_specs=(
            P(None, ("seq", "tp"), None),
            P("seq", "tp"),
            P("seq", "tp"),
            P("seq", "tp"),
            P(None, "tp"),
            P("tp"),
            P("tp"),
        ),
        check_vma=False,
    )
```

```python
import functools

import jax
import jax.numpy as jnp
from jax import lax
from jax.experimental import pallas as pl
from jax.experimental.pallas import tpu as pltpu
from jax.sharding import PartitionSpec as P

EPSILON = 1e-05
EDGE = 8
LANES = 128
LONG = 50_000_000_000
F32 = jnp.float32
BF16 = jnp.bfloat16


def sigmoid(x):
    return 0.5 * jnp.tanh(0.5 * x) + 0.5


def dot(a, b):
    return jnp.dot(a, b, preferred_element_type=F32)


def dot_nt(a, b):
    return lax.dot_general(a, b, (((1,), (1,)), ((), ())), preferred_element_type=F32)


def dot_tn(a, b):
    return lax.dot_general(a, b, (((0,), (0,)), ((), ())), preferred_element_type=F32)


def rows_of(count, first):
    return first + lax.broadcasted_iota(jnp.int32, (count, 1), 0)


def fold_rows(x):
    return jnp.sum(x.reshape(x.shape[0] // 8, 8, x.shape[1]), axis=0)


def block_rows(total, most):
    return max(b for b in range(8, most + 1, 8) if total % b == 0)


def whole(shape):
    return pl.BlockSpec(shape, lambda *i: (0,) * len(shape))


def per_record(shape):
    return pl.BlockSpec((1,) + shape, lambda r: (r,) + (0,) * len(shape))


def smem():
    return pl.BlockSpec(memory_space=pltpu.SMEM)


def anywhere():
    return pl.BlockSpec(memory_space=pl.ANY)


def after(x, *earlier):
    return lax.optimization_barrier((x,) + earlier)[0]


def spread_sums(out, sums):
    for s in range(out.shape[0]):
        out[s] = sums


def call(
    kernel, name, grid, in_specs, out_specs, out_shape, scratch, flops, moved, aliases=None, vmem=63
):
    return pl.pallas_call(
        kernel,
        name=name,
        grid=grid,
        in_specs=in_specs,
        out_specs=out_specs,
        out_shape=out_shape,
        scratch_shapes=scratch,
        input_output_aliases=aliases or {},
        cost_estimate=pl.CostEstimate(flops=int(flops), bytes_accessed=int(moved), transcendentals=0),
        compiler_params=pltpu.CompilerParams(vmem_limit_bytes=vmem * 1024 * 1024),
    )


def gate_kernel(meta, x, halo, wv, wg, taps, vl_o, sg_o, conv_o, st_o, gp, st):
    r = pl.program_id(0)
    hi = meta[0, r]
    lo = meta[1, r]
    frames = x.shape[1]
    width = wv.shape[1]
    halves = width // LANES

    def put(row, value):
        for h in range(halves):
            gp[h, pl.ds(row, value.shape[0]), :] = value[:, h * LANES : (h + 1) * LANES]

    edge_v = dot(halo[0], wv[...])
    edge_g = dot(halo[0], wg[...])
    row = rows_of(2 * EDGE, 0)
    pos = jnp.where(row < EDGE, row - EDGE, row - EDGE + frames)
    edge = jnp.where((pos >= lo) & (pos < hi), edge_v * sigmoid(edge_g), 0.0)
    zero = jnp.zeros((EDGE, width), F32)
    put(0, zero)
    put(EDGE, edge[:EDGE])
    put(2 * EDGE + frames, edge[EDGE:])
    put(3 * EDGE + frames, zero)
    step = block_rows(frames, 512)
    small = block_rows(step, 64)
    for base in range(0, frames, step):
        xb = x[0, base : base + step, :]
        vl_o[0, base : base + step, :] = dot(xb, wv[...])
        sg_o[0, base : base + step, :] = dot(xb, wg[...])

    def gating(i, carry):
        base = pl.multiple_of(i * small, small)
        v = vl_o[0, pl.ds(base, small), :]
        s = sigmoid(sg_o[0, pl.ds(base, small), :])
        sg_o[0, pl.ds(base, small), :] = s
        put(2 * EDGE + base, jnp.where(rows_of(small, base) < hi, v * s, 0.0))
        return carry

    lax.fori_loop(0, frames // small, gating, 0)
    span = frames + 2 * EDGE
    cb = block_rows(span, 104)
    kernel = taps.shape[0]
    margin = (kernel - 1) // 2
    for h in range(halves):
        cols = slice(h * LANES, (h + 1) * LANES)

        def convolve(i, carry):
            s1, s2 = carry
            base = pl.multiple_of(i * cb, 8)
            acc = jnp.zeros((cb, LANES), F32)
            for k in range(kernel):
                acc = acc + taps[k : k + 1, cols] * gp[h, pl.ds(base + EDGE - margin + k, cb), :]
            conv_o[0, pl.ds(base, cb), cols] = acc
            pos = rows_of(cb, base - EDGE)
            kept = jnp.where((pos >= 0) & (pos < jnp.minimum(hi, frames)), acc, 0.0)
            return s1 + fold_rows(kept), s2 + fold_rows(kept * kept)

        none = jnp.zeros((8, LANES), F32)
        s1, s2 = lax.fori_loop(0, span // cb, convolve, (none, none))
        add = jnp.concatenate(
            [jnp.sum(s1, axis=0, keepdims=True), jnp.sum(s2, axis=0, keepdims=True)], axis=0
        )
        st[:, cols] = jnp.where(r == 0, 0.0, st[:, cols]) + add

    @pl.when(r == pl.num_programs(0) - 1)
    def _():
        spread_sums(st_o, st[...])


def batch_norm(stats, count):
    sums = jnp.sum(stats[...], axis=0)
    centre = sums[0:1] / count
    spread = sums[1:2] / count - centre * centre
    return centre, lax.rsqrt(spread + EPSILON)


def norm_kernel(
    meta, count, stats, affine, select, grads, halo, wo, conv,
    swished_o, gn_o, picked_o, st_o, st, ping, pong
):
    r = pl.program_id(0)
    hi = meta[0, r]
    lo = meta[1, r]
    frames = grads.shape[1]
    centre, inv = batch_norm(stats, count[0, 0])
    gain, shift = affine[0:1, :], affine[1:2, :]

    def part(row, swish_grad):
        size = swish_grad.shape[0]
        unit = (conv[0, pl.ds(row, size), :] - centre) * inv
        normalized = unit * gain + shift
        s = sigmoid(normalized)
        pos = rows_of(size, row - EDGE)
        keep = (pos >= lo) & (pos < hi)
        swished = jnp.where(keep, normalized * s, 0.0)
        gn = jnp.where(keep, swish_grad, 0.0) * (s + normalized * (s - s * s))
        gn_o[0, pl.ds(row, size), :] = gn
        return unit, swished, gn

    edge = dot(halo[0], wo[...])
    part(0, edge[:EDGE])
    part(frames + EDGE, edge[EDGE:])
    step = block_rows(frames, 512)
    small = block_rows(step, 32)
    s1 = jnp.zeros((8, conv.shape[2]), F32)
    s2 = s1
    held = (ping, pong)
    ping[...] = dot(grads[0, :step, :], wo[...])
    for i in range(frames // step):
        now = held[i % 2]
        if (i + 1) * step < frames:
            held[(i + 1) % 2][...] = dot(grads[0, (i + 1) * step : (i + 2) * step, :], wo[...])
        picked_o[0, :, i * step : (i + 1) * step] = dot_nt(
            select[...], grads[0, i * step : (i + 1) * step, :]
        ).astype(BF16)
        for j in range(step // small):
            base = i * step + j * small
            unit, swished, gn = part(base + EDGE, now[j * small : (j + 1) * small, :])
            swished_o[0, base : base + small, :] = swished.astype(BF16)
            s1 = s1 + fold_rows(gn)
            s2 = s2 + fold_rows(gn * unit)
    add = jnp.concatenate(
        [jnp.sum(s1, axis=0, keepdims=True), jnp.sum(s2, axis=0, keepdims=True)], axis=0
    )
    st[...] = jnp.where(r == 0, 0.0, st[...]) + add

    @pl.when(r == pl.num_programs(0) - 1)
    def _():
        spread_sums(st_o, st[...])


def back_kernel(
    record, blocks, meta, count, stats, sums, gain, gn, conv, vl, sg, taps, out, taps_o, gc, acc
):
    i = pl.program_id(0)
    frames, width = vl.shape[1:]
    hi = meta[0, record + i // blocks]
    lo = meta[1, record + i // blocks]
    halves = width // LANES
    span = frames + 2 * EDGE
    kernel = taps.shape[0]
    margin = (kernel - 1) // 2
    cb = block_rows(span, 144)
    step = block_rows(frames, 64)
    total_frames = count[0, 0]
    centre, inv = batch_norm(stats, total_frames)
    grad_sums = jnp.sum(sums[...], axis=0)
    scale = gain[...] * inv
    offset = scale * grad_sums[0:1] / total_frames
    slope = scale * inv * grad_sums[1:2] / total_frames
    first = i % blocks * frames

    @pl.when(i == 0)
    def _():
        acc[...] = jnp.zeros_like(acc)

    for h in range(halves):
        cols = slice(h * LANES, (h + 1) * LANES)
        for base in range(0, span, cb):
            pos = rows_of(cb, first + (base - EDGE))
            mean = offset[:, cols] + (conv[0, base : base + cb, cols] - centre[:, cols]) * slope[:, cols]
            gc[h, base : base + cb, :] = scale[:, cols] * gn[0, base : base + cb, cols] - jnp.where(
                (pos >= lo) & (pos < hi), mean, 0.0
            )
        sums_k = [acc[h, k] for k in range(kernel)]
        for base in range(0, frames, step):
            v = vl[0, base : base + step, cols]
            s = sg[0, base : base + step, cols]
            keep = rows_of(step, first + base) < hi
            vs = v * s
            gated = jnp.where(keep, vs, 0.0)
            total = jnp.zeros((step, LANES), F32)
            for k in range(kernel):
                window = gc[h, base + EDGE + margin - k : base + EDGE + margin - k + step, :]
                total = total + taps[k : k + 1, cols] * window
                sums_k[k] = sums_k[k] + fold_rows(window * gated)
            total = jnp.where(keep, total, 0.0)
            out[base : base + step, cols] = (total * s).astype(BF16)
            out[base : base + step, width + h * LANES : width + (h + 1) * LANES] = (
                total * (vs - vs * s)
            ).astype(BF16)
        for k in range(kernel):
            acc[h, k] = sums_k[k]

    @pl.when(i == pl.num_programs(0) - 1)
    def _():
        taps_o[...] = jnp.zeros_like(taps_o)
        for h in range(halves):
            for k in range(kernel):
                taps_o[k : k + 1, h * LANES : (h + 1) * LANES] = jnp.sum(
                    acc[h, k], axis=0, keepdims=True
                )


def partial_kernel(own, sibling, w_own, w_sibling, picked, mine, *others):
    total = dot_nt(w_own[...], own[...]) + dot_nt(w_sibling[...], sibling[...])
    rows = picked.shape[1]
    seqs, _, piece, frames = mine.shape
    mine[...] = (
        (total[:rows] + picked[0].astype(F32)).astype(BF16).reshape(seqs, 1, piece, frames)
    )
    for d, other in enumerate(others):
        other[...] = (
            total[(d + 1) * rows : (d + 2) * rows].astype(BF16).reshape(seqs, 1, piece, frames)
        )


def add_kernel(*refs):
    total = refs[0][...].astype(F32)
    for other in refs[1:-1]:
        total = total + other[...].astype(F32)
    refs[-1][...] = total.astype(BF16)


def first_outer_kernel(grads, swished, out, acc):
    r = pl.program_id(0)
    add = dot_tn(swished[0], grads[0])
    acc[...] = add + jnp.where(r == 0, 0.0, acc[...])

    @pl.when(r == pl.num_programs(0) - 1)
    def _():
        shard = out.shape[2]
        for s in range(out.shape[0]):
            out[s] = acc[:, s * shard : (s + 1) * shard].astype(BF16)


def outer_kernel(groups, parity, x, *refs):
    lefts, taps = refs[: len(groups)], refs[len(groups) : 2 * len(groups)]
    keep, send, acc = refs[2 * len(groups) :]
    records = groups[-1][0] + groups[-1][1]
    width = acc.shape[0] // 2
    shard = keep.shape[2]
    r = pl.program_id(0)
    for (first, size), left in zip(groups, lefts):

        @pl.when((r >= first) & (r < first + size))
        def _(left=left):
            add = dot_tn(left[...], x[0])
            acc[...] = add + jnp.where(r == 0, 0.0, acc[...])

    @pl.when(r == records - 1)
    def _():
        tap_sums = taps[0][...]
        for part in taps[1:]:
            tap_sums = tap_sums + part[...]

        def write(place, odd):
            for j in range(place.shape[0]):
                at = (2 * j + odd) * shard
                place[j, : 2 * width, :] = acc[:, at : at + shard].astype(BF16)
                for q in range(width // shard):
                    row = 2 * width + 16 * q
                    place[j, row : row + 16, :] = tap_sums[:, q * shard : (q + 1) * shard].astype(
                        BF16
                    )

        @pl.when(parity[0, 0] == 0)
        def _():
            write(keep, 0)
            write(send, 1)

        @pl.when(parity[0, 0] != 0)
        def _():
            write(keep, 1)
            write(send, 0)


def fold_kernel(parity, own, other, keep, send):
    def write(place, odd):
        for j in range(place.shape[0]):
            total = own[2 * j + odd].astype(F32) + other[2 * j + odd].astype(F32)
            place[j] = total.astype(BF16)

    @pl.when(parity[0, 0] == 0)
    def _():
        write(keep, 0)
        write(send, 1)

    @pl.when(parity[0, 0] != 0)
    def _():
        write(keep, 1)
        write(send, 0)


def finish_kernel(kernel, own, other, pieces, value, gate, out, taps):
    width = value.shape[1]
    shard = value.shape[0]

    def total(row, size):
        return own[0, row : row + size, :].astype(F32) + other[0, row : row + size, :].astype(F32)

    value[...] = total(0, width).T
    gate[...] = total(width, width).T
    out[...] = jnp.sum(pieces[...].astype(F32), axis=0).T
    for q in range(width // shard):
        taps[:, q * shard : (q + 1) * shard] = total(2 * width + 16 * q, 16)[:kernel]


def place_kernel(moved, *refs):
    out = refs[-1]
    frames = moved.shape[3]
    for s in range(moved.shape[0]):
        out[0, :, s * frames : (s + 1) * frames] = moved[s, 0]


def exchange(copies, axis):
    return lax.all_to_all(copies, axis, 0, 0, tiled=True)


def per_device(
    normed,
    grad_out,
    value_weight,
    gate_weight,
    depth_taps,
    norm_gain,
    norm_shift,
    out_weight,
    lengths,
):
    recs, frames, model = normed.shape
    kernel = depth_taps.shape[0]
    width = value_weight.shape[1]
    seqs = lax.axis_size("seq")
    tps = lax.axis_size("tp")
    chips = tps // 2
    piece = model // (seqs * tps)
    rows = seqs * piece
    shard = model // seqs
    span = frames + 2 * EDGE
    seq_at = lax.axis_index("seq")
    tp_at = lax.axis_index("tp")
    chip_at, core_at = tp_at // 2, tp_at % 2
    count = jnp.sum(lengths).astype(F32)
    first = (seq_at * frames).astype(jnp.int32)
    meta = jnp.stack([lengths - first, jnp.full((recs,), 0, jnp.int32) - first])
    halves = width // LANES
    counts = count.reshape(1, 1)
    parity = (seq_at % 2).astype(jnp.int32).reshape(1, 1)
    sds = jax.ShapeDtypeStruct

    low_edge = jnp.concatenate([normed[:, -EDGE:], grad_out[:, -EDGE:]], axis=2)
    high_edge = jnp.concatenate([normed[:, :EDGE], grad_out[:, :EDGE]], axis=2)
    up = [(i, i + 1) for i in range(seqs - 1)]
    down = [(j, i) for i, j in up]
    halo = jnp.concatenate(
        [lax.ppermute(low_edge, "seq", up), lax.ppermute(high_edge, "seq", down)], axis=1
    )
    halo_x, halo_g = halo[:, :, :model], halo[:, :, model:]

    channel = (
        jnp.arange(seqs, dtype=jnp.int32)[:, None] * (tps * piece)
        + tp_at * piece
        + jnp.arange(piece, dtype=jnp.int32)[None, :]
    ).reshape(rows, 1)
    select = (channel == jnp.arange(model, dtype=jnp.int32)[None, :]).astype(BF16)
    array_bytes = recs * frames * width * 4
    input_bytes = recs * frames * model * 2
    matmul = 2 * recs * frames * model * width

    vl, sg, conv, stats = call(
        gate_kernel,
        "gate_conv",
        (recs,),
        [
            smem(),
            per_record((frames, model)),
            per_record((2 * EDGE, model)),
            whole((model, width)),
            whole((model, width)),
            whole((kernel, width)),
        ],
        [
            per_record((frames, width)),
            per_record((frames, width)),
            per_record((span, width)),
            whole((seqs, 2, width)),
        ],
        [
            sds((recs, frames, width), F32),
            sds((recs, frames, width), F32),
            sds((recs, span, width), F32),
            sds((seqs, 2, width), F32),
        ],
        [pltpu.VMEM((halves, frames + 4 * EDGE, LANES), F32), pltpu.VMEM((2, width), F32)],
        2 * matmul,
        input_bytes + 3 * array_bytes,
    )(meta, normed, halo_x, value_weight, gate_weight, depth_taps)
    both = jnp.concatenate([after(value_weight, stats), gate_weight], axis=1).reshape(seqs, tps, piece, 2 * width)

    def chosen(core):
        picks = [
            lax.dynamic_index_in_dim(both, ((chip_at + d) % chips) * 2 + core, 1, keepdims=False)
            for d in range(chips)
        ]
        return jnp.stack(picks).reshape(chips * rows, 2 * width)

    swap = [(i, i ^ 1) for i in range(tps)]
    w_own = chosen(core_at)
    w_sibling = lax.ppermute(chosen(1 - core_at), "tp", swap)

    stats = exchange(stats, "seq")

    chunk = block_rows(frames, 256)
    half_rows = block_rows(frames, 512)
    swished, gn, picked, sums = call(
        norm_kernel,
        "swish_norm",
        (recs,),
        [
            smem(),
            smem(),
            whole((seqs, 2, width)),
            whole((2, width)),
            whole((rows, model)),
            per_record((frames, model)),
            per_record((2 * EDGE, model)),
            whole((model, width)),
            per_record((span, width)),
        ],
        [
            per_record((frames, width)),
            per_record((span, width)),
            per_record((rows, frames)),
            whole((seqs, 2, width)),
        ],
        [
            sds((recs, frames, width), BF16),
            sds((recs, span, width), F32),
            sds((recs, rows, frames), BF16),
            sds((seqs, 2, width), F32),
        ],
        [
            pltpu.VMEM((2, width), F32),
            pltpu.VMEM((block_rows(frames, 512), width), F32),
            pltpu.VMEM((block_rows(frames, 512), width), F32),
        ],
        2 * matmul,
        input_bytes + 3 * array_bytes,
    )(
        meta,
        counts,
        stats,
        jnp.stack([norm_gain, norm_shift]),
        after(select, w_own, w_sibling),
        grad_out,
        halo_g,
        out_weight,
        conv,
    )
    w_out = call(
        first_outer_kernel,
        "outer_w_out",
        (recs,),
        [per_record((frames, model)), per_record((frames, width))],
        whole((seqs, width, shard)),
        sds((seqs, width, shard), BF16),
        [pltpu.VMEM((width, model), F32)],
        matmul,
        input_bytes,
    )(grad_out, swished)
    sums = exchange(sums, "seq")
    grad_shift, grad_gain = jnp.sum(sums, axis=0)

    blocks = frames // chunk
    parts_in = frames // half_rows

    def back(first, size, *earlier):
        def window(i):
            return (first + i // blocks, pl.multiple_of(i % blocks * chunk, chunk), 0)

        def block(i):
            return (first + i // blocks, i % blocks, 0)

        return call(
            functools.partial(back_kernel, first, blocks),
            "back_conv",
            (size * blocks,),
            [
                smem(),
                smem(),
                whole((seqs, 2, width)),
                whole((seqs, 2, width)),
                whole((1, width)),
                pl.BlockSpec((pl.Element(1), pl.Element(chunk + 2 * EDGE), pl.Element(width)), window),
                pl.BlockSpec((pl.Element(1), pl.Element(chunk + 2 * EDGE), pl.Element(width)), window),
                pl.BlockSpec((1, chunk, width), block),
                pl.BlockSpec((1, chunk, width), block),
                whole((kernel, width)),
            ],
            [pl.BlockSpec((chunk, 2 * width), lambda i: (i, 0)), whole((16, width))],
            [sds((size * frames, 2 * width), BF16), sds((16, width), F32)],
            [
                pltpu.VMEM((halves, chunk + 2 * EDGE, LANES), F32),
                pltpu.VMEM((halves, kernel, 8, LANES), F32),
            ],
            0,
            1024,
        )(meta, counts, stats, sums, norm_gain[None], gn, conv, vl, sg, after(depth_taps, *earlier))

    def partials(first, size, mine, *earlier):
        sibling = lax.ppermute(mine, "tp", swap)
        out = sds((seqs, size, piece, frames), BF16)
        return call(
            partial_kernel,
            "partial_in",
            (size * parts_in,),
            [
                pl.BlockSpec((half_rows, 2 * width), lambda i: (i, 0)),
                pl.BlockSpec((half_rows, 2 * width), lambda i: (i, 0)),
                whole((chips * rows, 2 * width)),
                whole((chips * rows, 2 * width)),
                pl.BlockSpec(
                    (1, rows, half_rows), lambda i: (first + i // parts_in, 0, i % parts_in)
                ),
            ],
            [
                pl.BlockSpec(
                    (seqs, 1, piece, half_rows), lambda i: (0, i // parts_in, 0, i % parts_in)
                )
            ]
            * chips,
            [out] * chips,
            [],
            0,
            1024,
        )(mine, sibling, after(w_own, *earlier), w_sibling, picked)

    def deliver(part, weight, *earlier):
        arrived = []
        for d in range(1, chips):
            send = [(i, ((i // 2 + d) % chips) * 2 + i % 2) for i in range(tps)]
            arrived.append(lax.ppermute(part[d], "tp", send))
        size = part[0].shape[1]
        block = pl.BlockSpec(
            (seqs, 1, piece, half_rows), lambda i: (0, i // parts_in, 0, i % parts_in)
        )
        own = call(
            add_kernel,
            "add",
            (size * parts_in,),
            [block] * chips,
            block,
            sds(part[0].shape, BF16),
            [],
            weight,
            1024,
        )(after(part[0], *earlier), *arrived)
        return own

    groups = ((0, 1), (1, 1), (2, recs - 2))
    grads = [None] * 3
    taps = [None] * 3
    parts = [None] * 3
    owns = [None] * 3
    moved = [None] * 3
    w_out_pieces = exchange(w_out, "seq")
    grads[0], taps[0] = back(*groups[0], w_out)
    grads[1], taps[1] = back(*groups[1], grads[0])
    parts[0] = partials(*groups[0], grads[0], grads[1])
    grads[2], taps[2] = back(*groups[2], *parts[0])
    parts[1] = partials(*groups[1], grads[1], grads[2])
    owns[0] = deliver(parts[0], LONG, w_out_pieces, *parts[1])
    parts[2] = partials(*groups[2], grads[2], owns[0])
    moved[0] = exchange(after(owns[0], *parts[2]), "seq")
    owns[1] = deliver(parts[1], 0, *parts[2])

    slots = 2 * width + 16 * (width // shard)
    half = sds((seqs // 2, slots, shard), BF16)
    keep, send = call(
        functools.partial(outer_kernel, groups),
        "outer_w_in",
        (recs,),
        [smem(), per_record((frames, model))]
        + [
            pl.BlockSpec(
                (frames, 2 * width),
                lambda r, first=first, size=size: (jnp.clip(r - first, 0, size - 1), 0),
            )
            for first, size in groups
        ]
        + [whole((16, width))] * len(groups),
        [whole(half.shape)] * 2,
        [half] * 2,
        [pltpu.VMEM((2 * width, model), F32)],
        LONG,
        1024,
    )(parity, after(normed, owns[1]), *grads, *taps)
    moved[1] = exchange(after(owns[1], keep, moved[0]), "seq")
    bit = 1
    while True:
        others = lax.ppermute(send, "seq", [(i, i ^ bit) for i in range(seqs)])
        if bit == 1:
            owns[2] = deliver(parts[2], 0, others)
            moved[2] = exchange(after(owns[2], moved[1]), "seq")
        bit *= 2
        if bit == seqs:
            break
        if bit == 2:
            keep = after(keep, owns[2])
        shape = (keep.shape[0] // 2,) + keep.shape[1:]
        side = ((seq_at // bit) % 2).astype(jnp.int32).reshape(1, 1)
        keep, send = call(
            fold_kernel,
            "fold",
            (1,),
            [smem()] + [whole(keep.shape)] * 2,
            [whole(shape)] * 2,
            [sds(shape, BF16)] * 2,
            [],
            0,
            1024,
            vmem=20,
        )(side, keep, others)
    w_value, w_gate, w_out, grad_taps = call(
        functools.partial(finish_kernel, kernel),
        "finish",
        (1,),
        [whole(keep.shape)] * 2 + [whole((seqs, width, shard))],
        [whole((shard, width))] * 3 + [whole((kernel, width))],
        [sds((shard, width), F32)] * 3 + [sds((kernel, width), F32)],
        [],
        0,
        1024,
        vmem=20,
    )(keep, others, w_out_pieces)
    grad_in = ()
    for (first, size), part in zip(groups, moved):
        grad_in = (
            call(
                place_kernel,
                "place",
                (size,),
                [pl.BlockSpec((seqs, 1, piece, frames), lambda i: (0, i, 0, 0))]
                + [anywhere()] * len(grad_in),
                pl.BlockSpec((1, piece, seqs * frames), lambda i, first=first: (first + i, 0, 0)),
                sds((recs, piece, seqs * frames), BF16),
                [],
                0,
                4 * size * piece * seqs * frames,
                {1: 0} if grad_in else None,
                vmem=20,
            )(part, *grad_in),
        )
    (grad_in,) = grad_in
    return (grad_in, w_value, w_gate, w_out, grad_taps, grad_gain, grad_shift)


def solution(mesh):
    placed = (
        P(None, "seq", None),
        P(None, "seq", None),
        P(None, "tp"),
        P(None, "tp"),
        P(None, "tp"),
        P("tp"),
        P("tp"),
        P(None, "tp"),
        P(),
    )
    return jax.shard_map(
        per_device,
        mesh=mesh,
        in_specs=placed,
        out_specs=(
            P(None, ("seq", "tp"), None),
            P("seq", "tp"),
            P("seq", "tp"),
            P("seq", "tp"),
            P(None, "tp"),
            P("tp"),
            P("tp"),
        ),
        check_vma=False,
    )
```

```python
import functools

import jax
import jax.numpy as jnp
from jax import lax
from jax.experimental import pallas as pl
from jax.experimental.pallas import tpu as pltpu
from jax.sharding import PartitionSpec as P

EPSILON = 1e-05
EDGE = 8
LANES = 128
LONG = 50_000_000_000
F32 = jnp.float32
BF16 = jnp.bfloat16


def sigmoid(x):
    return 0.5 * jnp.tanh(0.5 * x) + 0.5


def dot(a, b):
    return jnp.dot(a, b, preferred_element_type=F32)


def dot_nt(a, b):
    return lax.dot_general(a, b, (((1,), (1,)), ((), ())), preferred_element_type=F32)


def dot_tn(a, b):
    return lax.dot_general(a, b, (((0,), (0,)), ((), ())), preferred_element_type=F32)


def rows_of(count, first):
    return first + lax.broadcasted_iota(jnp.int32, (count, 1), 0)


def fold_rows(x):
    return jnp.sum(x.reshape(x.shape[0] // 8, 8, x.shape[1]), axis=0)


def block_rows(total, most):
    return max(b for b in range(8, most + 1, 8) if total % b == 0)


def whole(shape):
    return pl.BlockSpec(shape, lambda *i: (0,) * len(shape))


def per_record(shape):
    return pl.BlockSpec((1,) + shape, lambda r: (r,) + (0,) * len(shape))


def smem():
    return pl.BlockSpec(memory_space=pltpu.SMEM)


def anywhere():
    return pl.BlockSpec(memory_space=pl.ANY)


def after(x, *earlier):
    return lax.optimization_barrier((x,) + earlier)[0]


def spread_sums(out, sums):
    for s in range(out.shape[0]):
        out[s] = sums


def call(
    kernel, name, grid, in_specs, out_specs, out_shape, scratch, flops, moved, aliases=None, vmem=63
):
    return pl.pallas_call(
        kernel,
        name=name,
        grid=grid,
        in_specs=in_specs,
        out_specs=out_specs,
        out_shape=out_shape,
        scratch_shapes=scratch,
        input_output_aliases=aliases or {},
        cost_estimate=pl.CostEstimate(flops=int(flops), bytes_accessed=int(moved), transcendentals=0),
        compiler_params=pltpu.CompilerParams(vmem_limit_bytes=vmem * 1024 * 1024),
    )


def gate_kernel(meta, x, halo, wv, wg, taps, vl_o, sg_o, conv_o, st_o, gp, st):
    r = pl.program_id(0)
    hi = meta[0, r]
    lo = meta[1, r]
    frames = x.shape[1]
    width = wv.shape[1]
    halves = width // LANES

    def put(row, value):
        for h in range(halves):
            gp[h, pl.ds(row, value.shape[0]), :] = value[:, h * LANES : (h + 1) * LANES]

    edge_v = dot(halo[0], wv[...])
    edge_g = dot(halo[0], wg[...])
    row = rows_of(2 * EDGE, 0)
    pos = jnp.where(row < EDGE, row - EDGE, row - EDGE + frames)
    edge = jnp.where((pos >= lo) & (pos < hi), edge_v * sigmoid(edge_g), 0.0)
    zero = jnp.zeros((EDGE, width), F32)
    put(0, zero)
    put(EDGE, edge[:EDGE])
    put(2 * EDGE + frames, edge[EDGE:])
    put(3 * EDGE + frames, zero)
    step = block_rows(frames, 512)
    small = block_rows(step, 64)
    for base in range(0, frames, step):
        xb = x[0, base : base + step, :]
        vl_o[0, base : base + step, :] = dot(xb, wv[...])
        sg_o[0, base : base + step, :] = dot(xb, wg[...])

    def gating(i, carry):
        base = pl.multiple_of(i * small, small)
        v = vl_o[0, pl.ds(base, small), :]
        s = sigmoid(sg_o[0, pl.ds(base, small), :])
        sg_o[0, pl.ds(base, small), :] = s
        put(2 * EDGE + base, jnp.where(rows_of(small, base) < hi, v * s, 0.0))
        return carry

    lax.fori_loop(0, frames // small, gating, 0)
    span = frames + 2 * EDGE
    cb = block_rows(span, 104)
    kernel = taps.shape[0]
    margin = (kernel - 1) // 2
    for h in range(halves):
        cols = slice(h * LANES, (h + 1) * LANES)

        def convolve(i, carry):
            s1, s2 = carry
            base = pl.multiple_of(i * cb, 8)
            acc = jnp.zeros((cb, LANES), F32)
            for k in range(kernel):
                acc = acc + taps[k : k + 1, cols] * gp[h, pl.ds(base + EDGE - margin + k, cb), :]
            conv_o[0, pl.ds(base, cb), cols] = acc
            pos = rows_of(cb, base - EDGE)
            kept = jnp.where((pos >= 0) & (pos < jnp.minimum(hi, frames)), acc, 0.0)
            return s1 + fold_rows(kept), s2 + fold_rows(kept * kept)

        none = jnp.zeros((8, LANES), F32)
        s1, s2 = lax.fori_loop(0, span // cb, convolve, (none, none))
        add = jnp.concatenate(
            [jnp.sum(s1, axis=0, keepdims=True), jnp.sum(s2, axis=0, keepdims=True)], axis=0
        )
        st[:, cols] = jnp.where(r == 0, 0.0, st[:, cols]) + add

    @pl.when(r == pl.num_programs(0) - 1)
    def _():
        spread_sums(st_o, st[...])


def batch_norm(stats, count):
    sums = jnp.sum(stats[...], axis=0)
    centre = sums[0:1] / count
    spread = sums[1:2] / count - centre * centre
    return centre, lax.rsqrt(spread + EPSILON)


def norm_kernel(
    meta, count, stats, affine, select, grads, halo, wo, conv,
    swished_o, gn_o, picked_o, st_o, st, ping, pong
):
    r = pl.program_id(0)
    hi = meta[0, r]
    lo = meta[1, r]
    frames = grads.shape[1]
    centre, inv = batch_norm(stats, count[0, 0])
    gain, shift = affine[0:1, :], affine[1:2, :]

    def part(row, swish_grad):
        size = swish_grad.shape[0]
        unit = (conv[0, pl.ds(row, size), :] - centre) * inv
        normalized = unit * gain + shift
        s = sigmoid(normalized)
        pos = rows_of(size, row - EDGE)
        keep = (pos >= lo) & (pos < hi)
        swished = jnp.where(keep, normalized * s, 0.0)
        gn = jnp.where(keep, swish_grad, 0.0) * (s + normalized * (s - s * s))
        gn_o[0, pl.ds(row, size), :] = gn
        return unit, swished, gn

    edge = dot(halo[0], wo[...])
    part(0, edge[:EDGE])
    part(frames + EDGE, edge[EDGE:])
    step = block_rows(frames, 512)
    small = block_rows(step, 32)
    s1 = jnp.zeros((8, conv.shape[2]), F32)
    s2 = s1
    held = (ping, pong)
    ping[...] = dot(grads[0, :step, :], wo[...])
    for i in range(frames // step):
        now = held[i % 2]
        if (i + 1) * step < frames:
            held[(i + 1) % 2][...] = dot(grads[0, (i + 1) * step : (i + 2) * step, :], wo[...])
        picked_o[0, :, i * step : (i + 1) * step] = dot_nt(
            select[...], grads[0, i * step : (i + 1) * step, :]
        ).astype(BF16)
        for j in range(step // small):
            base = i * step + j * small
            unit, swished, gn = part(base + EDGE, now[j * small : (j + 1) * small, :])
            swished_o[0, base : base + small, :] = swished.astype(BF16)
            s1 = s1 + fold_rows(gn)
            s2 = s2 + fold_rows(gn * unit)
    add = jnp.concatenate(
        [jnp.sum(s1, axis=0, keepdims=True), jnp.sum(s2, axis=0, keepdims=True)], axis=0
    )
    st[...] = jnp.where(r == 0, 0.0, st[...]) + add

    @pl.when(r == pl.num_programs(0) - 1)
    def _():
        spread_sums(st_o, st[...])


def back_kernel(
    record, blocks, meta, count, stats, sums, gain, gn, conv, vl, sg, taps, out, taps_o, gc, acc
):
    i = pl.program_id(0)
    frames, width = vl.shape[1:]
    hi = meta[0, record + i // blocks]
    lo = meta[1, record + i // blocks]
    halves = width // LANES
    span = frames + 2 * EDGE
    kernel = taps.shape[0]
    margin = (kernel - 1) // 2
    cb = block_rows(span, 144)
    step = block_rows(frames, 64)
    total_frames = count[0, 0]
    centre, inv = batch_norm(stats, total_frames)
    grad_sums = jnp.sum(sums[...], axis=0)
    scale = gain[...] * inv
    offset = scale * grad_sums[0:1] / total_frames
    slope = scale * inv * grad_sums[1:2] / total_frames
    first = i % blocks * frames

    @pl.when(i == 0)
    def _():
        acc[...] = jnp.zeros_like(acc)

    for h in range(halves):
        cols = slice(h * LANES, (h + 1) * LANES)
        for base in range(0, span, cb):
            pos = rows_of(cb, first + (base - EDGE))
            mean = offset[:, cols] + (conv[0, base : base + cb, cols] - centre[:, cols]) * slope[:, cols]
            gc[h, base : base + cb, :] = scale[:, cols] * gn[0, base : base + cb, cols] - jnp.where(
                (pos >= lo) & (pos < hi), mean, 0.0
            )
        sums_k = [acc[h, k] for k in range(kernel)]
        for base in range(0, frames, step):
            v = vl[0, base : base + step, cols]
            s = sg[0, base : base + step, cols]
            keep = rows_of(step, first + base) < hi
            vs = v * s
            gated = jnp.where(keep, vs, 0.0)
            total = jnp.zeros((step, LANES), F32)
            for k in range(kernel):
                window = gc[h, base + EDGE + margin - k : base + EDGE + margin - k + step, :]
                total = total + taps[k : k + 1, cols] * window
                sums_k[k] = sums_k[k] + fold_rows(window * gated)
            total = jnp.where(keep, total, 0.0)
            out[base : base + step, cols] = (total * s).astype(BF16)
            out[base : base + step, width + h * LANES : width + (h + 1) * LANES] = (
                total * (vs - vs * s)
            ).astype(BF16)
        for k in range(kernel):
            acc[h, k] = sums_k[k]

    @pl.when(i == pl.num_programs(0) - 1)
    def _():
        taps_o[...] = jnp.zeros_like(taps_o)
        for h in range(halves):
            for k in range(kernel):
                taps_o[k : k + 1, h * LANES : (h + 1) * LANES] = jnp.sum(
                    acc[h, k], axis=0, keepdims=True
                )


def partial_kernel(own, sibling, w_own, w_sibling, picked, mine, *others):
    total = dot_nt(w_own[...], own[...]) + dot_nt(w_sibling[...], sibling[...])
    rows = picked.shape[1]
    seqs, _, piece, frames = mine.shape
    mine[...] = (
        (total[:rows] + picked[0].astype(F32)).astype(BF16).reshape(seqs, 1, piece, frames)
    )
    for d, other in enumerate(others):
        other[...] = (
            total[(d + 1) * rows : (d + 2) * rows].astype(BF16).reshape(seqs, 1, piece, frames)
        )


def add_kernel(*refs):
    total = refs[0][...].astype(F32)
    for other in refs[1:-1]:
        total = total + other[...].astype(F32)
    refs[-1][...] = total.astype(BF16)


def first_outer_kernel(grads, swished, out):
    r = pl.program_id(0)
    add = dot_tn(swished[0], grads[0])

    @pl.when(r == 0)
    def _():
        out[...] = add

    @pl.when(r > 0)
    def _():
        out[...] += add


def outer_kernel(groups, parity, x, w_out, *refs):
    lefts, taps = refs[: len(groups)], refs[len(groups) : 2 * len(groups)]
    keep, send, acc = refs[2 * len(groups) :]
    records = groups[-1][0] + groups[-1][1]
    width = w_out.shape[0]
    shard = keep.shape[2]
    r = pl.program_id(0)
    for (first, size), left in zip(groups, lefts):

        @pl.when((r >= first) & (r < first + size))
        def _(left=left):
            add = dot_tn(left[...], x[0])
            acc[...] = add + jnp.where(r == 0, 0.0, acc[...])

    @pl.when(r == records - 1)
    def _():
        tap_sums = taps[0][...]
        for part in taps[1:]:
            tap_sums = tap_sums + part[...]

        def write(place, odd):
            for j in range(place.shape[0]):
                at = (2 * j + odd) * shard
                place[j, : 2 * width, :] = acc[:, at : at + shard].astype(BF16)
                place[j, 2 * width : 3 * width, :] = w_out[:, at : at + shard].astype(BF16)
                for q in range(width // shard):
                    row = 3 * width + 16 * q
                    place[j, row : row + 16, :] = tap_sums[:, q * shard : (q + 1) * shard].astype(
                        BF16
                    )

        @pl.when(parity[0, 0] == 0)
        def _():
            write(keep, 0)
            write(send, 1)

        @pl.when(parity[0, 0] != 0)
        def _():
            write(keep, 1)
            write(send, 0)


def fold_kernel(parity, own, other, keep, send):
    def write(place, odd):
        for j in range(place.shape[0]):
            total = own[2 * j + odd].astype(F32) + other[2 * j + odd].astype(F32)
            place[j] = total.astype(BF16)

    @pl.when(parity[0, 0] == 0)
    def _():
        write(keep, 0)
        write(send, 1)

    @pl.when(parity[0, 0] != 0)
    def _():
        write(keep, 1)
        write(send, 0)


def finish_kernel(kernel, own, other, value, gate, out, taps):
    width = value.shape[1]
    shard = value.shape[0]

    def total(row, size):
        return own[0, row : row + size, :].astype(F32) + other[0, row : row + size, :].astype(F32)

    for i, place in enumerate((value, gate, out)):
        place[...] = total(i * width, width).T
    for q in range(width // shard):
        taps[:, q * shard : (q + 1) * shard] = total(3 * width + 16 * q, 16)[:kernel]


def place_kernel(moved, *refs):
    out = refs[-1]
    frames = moved.shape[3]
    for s in range(moved.shape[0]):
        out[0, :, s * frames : (s + 1) * frames] = moved[s, 0]


def exchange(copies, axis):
    return lax.all_to_all(copies, axis, 0, 0, tiled=True)


def per_device(
    normed,
    grad_out,
    value_weight,
    gate_weight,
    depth_taps,
    norm_gain,
    norm_shift,
    out_weight,
    lengths,
):
    recs, frames, model = normed.shape
    kernel = depth_taps.shape[0]
    width = value_weight.shape[1]
    seqs = lax.axis_size("seq")
    tps = lax.axis_size("tp")
    chips = tps // 2
    piece = model // (seqs * tps)
    rows = seqs * piece
    shard = model // seqs
    span = frames + 2 * EDGE
    seq_at = lax.axis_index("seq")
    tp_at = lax.axis_index("tp")
    chip_at, core_at = tp_at // 2, tp_at % 2
    count = jnp.sum(lengths).astype(F32)
    first = (seq_at * frames).astype(jnp.int32)
    meta = jnp.stack([lengths - first, jnp.full((recs,), 0, jnp.int32) - first])
    halves = width // LANES
    counts = count.reshape(1, 1)
    parity = (seq_at % 2).astype(jnp.int32).reshape(1, 1)
    sds = jax.ShapeDtypeStruct

    low_edge = jnp.concatenate([normed[:, -EDGE:], grad_out[:, -EDGE:]], axis=2)
    high_edge = jnp.concatenate([normed[:, :EDGE], grad_out[:, :EDGE]], axis=2)
    up = [(i, i + 1) for i in range(seqs - 1)]
    down = [(j, i) for i, j in up]
    halo = jnp.concatenate(
        [lax.ppermute(low_edge, "seq", up), lax.ppermute(high_edge, "seq", down)], axis=1
    )
    halo_x, halo_g = halo[:, :, :model], halo[:, :, model:]

    channel = (
        jnp.arange(seqs, dtype=jnp.int32)[:, None] * (tps * piece)
        + tp_at * piece
        + jnp.arange(piece, dtype=jnp.int32)[None, :]
    ).reshape(rows, 1)
    select = (channel == jnp.arange(model, dtype=jnp.int32)[None, :]).astype(BF16)
    array_bytes = recs * frames * width * 4
    input_bytes = recs * frames * model * 2
    matmul = 2 * recs * frames * model * width

    vl, sg, conv, stats = call(
        gate_kernel,
        "gate_conv",
        (recs,),
        [
            smem(),
            per_record((frames, model)),
            per_record((2 * EDGE, model)),
            whole((model, width)),
            whole((model, width)),
            whole((kernel, width)),
        ],
        [
            per_record((frames, width)),
            per_record((frames, width)),
            per_record((span, width)),
            whole((seqs, 2, width)),
        ],
        [
            sds((recs, frames, width), F32),
            sds((recs, frames, width), F32),
            sds((recs, span, width), F32),
            sds((seqs, 2, width), F32),
        ],
        [pltpu.VMEM((halves, frames + 4 * EDGE, LANES), F32), pltpu.VMEM((2, width), F32)],
        2 * matmul,
        input_bytes + 3 * array_bytes,
    )(meta, normed, halo_x, value_weight, gate_weight, depth_taps)
    both = jnp.concatenate([after(value_weight, stats), gate_weight], axis=1).reshape(seqs, tps, piece, 2 * width)

    def chosen(core):
        picks = [
            lax.dynamic_index_in_dim(both, ((chip_at + d) % chips) * 2 + core, 1, keepdims=False)
            for d in range(chips)
        ]
        return jnp.stack(picks).reshape(chips * rows, 2 * width)

    swap = [(i, i ^ 1) for i in range(tps)]
    w_own = chosen(core_at)
    w_sibling = lax.ppermute(chosen(1 - core_at), "tp", swap)

    stats = exchange(stats, "seq")

    chunk = block_rows(frames, 256)
    half_rows = block_rows(frames, 512)
    swished, gn, picked, sums = call(
        norm_kernel,
        "swish_norm",
        (recs,),
        [
            smem(),
            smem(),
            whole((seqs, 2, width)),
            whole((2, width)),
            whole((rows, model)),
            per_record((frames, model)),
            per_record((2 * EDGE, model)),
            whole((model, width)),
            per_record((span, width)),
        ],
        [
            per_record((frames, width)),
            per_record((span, width)),
            per_record((rows, frames)),
            whole((seqs, 2, width)),
        ],
        [
            sds((recs, frames, width), BF16),
            sds((recs, span, width), F32),
            sds((recs, rows, frames), BF16),
            sds((seqs, 2, width), F32),
        ],
        [
            pltpu.VMEM((2, width), F32),
            pltpu.VMEM((block_rows(frames, 512), width), F32),
            pltpu.VMEM((block_rows(frames, 512), width), F32),
        ],
        2 * matmul,
        input_bytes + 3 * array_bytes,
    )(
        meta,
        counts,
        stats,
        jnp.stack([norm_gain, norm_shift]),
        after(select, w_own, w_sibling),
        grad_out,
        halo_g,
        out_weight,
        conv,
    )
    w_out = call(
        first_outer_kernel,
        "outer_w_out",
        (recs,),
        [per_record((frames, model)), per_record((frames, width))],
        whole((width, model)),
        sds((width, model), F32),
        [],
        matmul,
        input_bytes,
    )(grad_out, swished)
    sums = exchange(sums, "seq")
    grad_shift, grad_gain = jnp.sum(sums, axis=0)

    blocks = frames // chunk
    parts_in = frames // half_rows

    def back(first, size, *earlier):
        def window(i):
            return (first + i // blocks, pl.multiple_of(i % blocks * chunk, chunk), 0)

        def block(i):
            return (first + i // blocks, i % blocks, 0)

        return call(
            functools.partial(back_kernel, first, blocks),
            "back_conv",
            (size * blocks,),
            [
                smem(),
                smem(),
                whole((seqs, 2, width)),
                whole((seqs, 2, width)),
                whole((1, width)),
                pl.BlockSpec((pl.Element(1), pl.Element(chunk + 2 * EDGE), pl.Element(width)), window),
                pl.BlockSpec((pl.Element(1), pl.Element(chunk + 2 * EDGE), pl.Element(width)), window),
                pl.BlockSpec((1, chunk, width), block),
                pl.BlockSpec((1, chunk, width), block),
                whole((kernel, width)),
            ],
            [pl.BlockSpec((chunk, 2 * width), lambda i: (i, 0)), whole((16, width))],
            [sds((size * frames, 2 * width), BF16), sds((16, width), F32)],
            [
                pltpu.VMEM((halves, chunk + 2 * EDGE, LANES), F32),
                pltpu.VMEM((halves, kernel, 8, LANES), F32),
            ],
            0,
            1024,
        )(meta, counts, stats, sums, norm_gain[None], gn, conv, vl, sg, after(depth_taps, *earlier))

    def partials(first, size, mine, *earlier):
        sibling = lax.ppermute(mine, "tp", swap)
        out = sds((seqs, size, piece, frames), BF16)
        return call(
            partial_kernel,
            "partial_in",
            (size * parts_in,),
            [
                pl.BlockSpec((half_rows, 2 * width), lambda i: (i, 0)),
                pl.BlockSpec((half_rows, 2 * width), lambda i: (i, 0)),
                whole((chips * rows, 2 * width)),
                whole((chips * rows, 2 * width)),
                pl.BlockSpec(
                    (1, rows, half_rows), lambda i: (first + i // parts_in, 0, i % parts_in)
                ),
            ],
            [
                pl.BlockSpec(
                    (seqs, 1, piece, half_rows), lambda i: (0, i // parts_in, 0, i % parts_in)
                )
            ]
            * chips,
            [out] * chips,
            [],
            0,
            1024,
        )(mine, sibling, after(w_own, *earlier), w_sibling, picked)

    def deliver(part, weight, *earlier):
        arrived = []
        for d in range(1, chips):
            send = [(i, ((i // 2 + d) % chips) * 2 + i % 2) for i in range(tps)]
            arrived.append(lax.ppermute(part[d], "tp", send))
        size = part[0].shape[1]
        block = pl.BlockSpec(
            (seqs, 1, piece, half_rows), lambda i: (0, i // parts_in, 0, i % parts_in)
        )
        own = call(
            add_kernel,
            "add",
            (size * parts_in,),
            [block] * chips,
            block,
            sds(part[0].shape, BF16),
            [],
            weight,
            1024,
        )(after(part[0], *earlier), *arrived)
        return own

    groups = ((0, recs // 2), (recs // 2, recs - recs // 2))
    grads, taps, parts, owns, moved = ([None] * 2 for _ in range(5))
    grads[0], taps[0] = back(*groups[0], w_out)
    grads[1], taps[1] = back(*groups[1], grads[0])
    parts[0] = partials(*groups[0], grads[0], grads[1])
    parts[1] = partials(*groups[1], grads[1], *parts[0])

    slots = 3 * width + 16 * (width // shard)
    half = sds((seqs // 2, slots, shard), BF16)
    keep, send = call(
        functools.partial(outer_kernel, groups),
        "outer_w_in",
        (recs,),
        [smem(), per_record((frames, model)), whole((width, model))]
        + [
            pl.BlockSpec(
                (frames, 2 * width),
                lambda r, first=first, size=size: (jnp.clip(r - first, 0, size - 1), 0),
            )
            for first, size in groups
        ]
        + [whole((16, width))] * len(groups),
        [whole(half.shape)] * 2,
        [half] * 2,
        [pltpu.VMEM((2 * width, model), F32)],
        0,
        1024,
    )(parity, after(normed, *parts[1]), w_out, *grads, *taps)
    owns[0] = deliver(parts[0], LONG, keep)
    moved[0] = exchange(owns[0], "seq")
    bit = 1
    while True:
        others = lax.ppermute(send, "seq", [(i, i ^ bit) for i in range(seqs)])
        bit *= 2
        if bit == seqs:
            break
        if bit == 2:
            keep = after(keep, owns[0])
        shape = (keep.shape[0] // 2,) + keep.shape[1:]
        side = ((seq_at // bit) % 2).astype(jnp.int32).reshape(1, 1)
        keep, send = call(
            fold_kernel,
            "fold",
            (1,),
            [smem()] + [whole(keep.shape)] * 2,
            [whole(shape)] * 2,
            [sds(shape, BF16)] * 2,
            [],
            0,
            1024,
            vmem=20,
        )(side, keep, others)
        if bit == 2:
            owns[1] = deliver(parts[1], 0, keep)
        if bit == min(4, seqs // 2):
            moved[1] = exchange(after(owns[1], moved[0], keep), "seq")
    w_value, w_gate, w_out, grad_taps = call(
        functools.partial(finish_kernel, kernel),
        "finish",
        (1,),
        [whole(keep.shape)] * 2,
        [whole((shard, width))] * 3 + [whole((kernel, width))],
        [sds((shard, width), F32)] * 3 + [sds((kernel, width), F32)],
        [],
        0,
        1024,
        vmem=20,
    )(keep, others)
    grad_in = ()
    for (first, size), part in zip(groups, moved):
        grad_in = (
            call(
                place_kernel,
                "place",
                (size,),
                [pl.BlockSpec((seqs, 1, piece, frames), lambda i: (0, i, 0, 0))]
                + [anywhere()] * len(grad_in),
                pl.BlockSpec((1, piece, seqs * frames), lambda i, first=first: (first + i, 0, 0)),
                sds((recs, piece, seqs * frames), BF16),
                [],
                0,
                4 * size * piece * seqs * frames,
                {1: 0} if grad_in else None,
                vmem=20,
            )(part, *grad_in),
        )
    (grad_in,) = grad_in
    return (grad_in, w_value, w_gate, w_out, grad_taps, grad_gain, grad_shift)


def solution(mesh):
    placed = (
        P(None, "seq", None),
        P(None, "seq", None),
        P(None, "tp"),
        P(None, "tp"),
        P(None, "tp"),
        P("tp"),
        P("tp"),
        P(None, "tp"),
        P(),
    )
    return jax.shard_map(
        per_device,
        mesh=mesh,
        in_specs=placed,
        out_specs=(
            P(None, ("seq", "tp"), None),
            P("seq", "tp"),
            P("seq", "tp"),
            P("seq", "tp"),
            P(None, "tp"),
            P("tp"),
            P("tp"),
        ),
        check_vma=False,
    )
```

```python
import functools

import jax
import jax.numpy as jnp
from jax import lax
from jax.experimental import pallas as pl
from jax.experimental.pallas import tpu as pltpu
from jax.sharding import PartitionSpec as P

EPSILON = 1e-05
EDGE = 8
LANES = 128
LONG = 50_000_000_000
F32 = jnp.float32
BF16 = jnp.bfloat16


def sigmoid(x):
    return 0.5 * jnp.tanh(0.5 * x) + 0.5


def dot(a, b):
    return jnp.dot(a, b, preferred_element_type=F32)


def dot_nt(a, b):
    return lax.dot_general(a, b, (((1,), (1,)), ((), ())), preferred_element_type=F32)


def dot_tn(a, b):
    return lax.dot_general(a, b, (((0,), (0,)), ((), ())), preferred_element_type=F32)


def rows_of(count, first):
    return first + lax.broadcasted_iota(jnp.int32, (count, 1), 0)


def fold_rows(x):
    return jnp.sum(x.reshape(x.shape[0] // 8, 8, x.shape[1]), axis=0)


def block_rows(total, most):
    return max(b for b in range(8, most + 1, 8) if total % b == 0)


def whole(shape):
    return pl.BlockSpec(shape, lambda *i: (0,) * len(shape))


def per_record(shape):
    return pl.BlockSpec((1,) + shape, lambda r: (r,) + (0,) * len(shape))


def smem():
    return pl.BlockSpec(memory_space=pltpu.SMEM)


def anywhere():
    return pl.BlockSpec(memory_space=pl.ANY)


def after(x, *earlier):
    return lax.optimization_barrier((x,) + earlier)[0]


def spread_sums(out, sums):
    for s in range(out.shape[0]):
        out[s] = sums


def call(
    kernel, name, grid, in_specs, out_specs, out_shape, scratch, flops, moved, aliases=None, vmem=63
):
    return pl.pallas_call(
        kernel,
        name=name,
        grid=grid,
        in_specs=in_specs,
        out_specs=out_specs,
        out_shape=out_shape,
        scratch_shapes=scratch,
        input_output_aliases=aliases or {},
        cost_estimate=pl.CostEstimate(flops=int(flops), bytes_accessed=int(moved), transcendentals=0),
        compiler_params=pltpu.CompilerParams(vmem_limit_bytes=vmem * 1024 * 1024),
    )


def gate_kernel(meta, x, halo, wv, wg, taps, vl_o, sg_o, conv_o, st_o, gp, st):
    r = pl.program_id(0)
    hi = meta[0, r]
    lo = meta[1, r]
    frames = x.shape[1]
    width = wv.shape[1]
    halves = width // LANES

    def put(row, value):
        for h in range(halves):
            gp[h, pl.ds(row, value.shape[0]), :] = value[:, h * LANES : (h + 1) * LANES]

    edge_v = dot(halo[0], wv[...])
    edge_g = dot(halo[0], wg[...])
    row = rows_of(2 * EDGE, 0)
    pos = jnp.where(row < EDGE, row - EDGE, row - EDGE + frames)
    edge = jnp.where((pos >= lo) & (pos < hi), edge_v * sigmoid(edge_g), 0.0)
    zero = jnp.zeros((EDGE, width), F32)
    put(0, zero)
    put(EDGE, edge[:EDGE])
    put(2 * EDGE + frames, edge[EDGE:])
    put(3 * EDGE + frames, zero)
    step = block_rows(frames, 512)
    small = block_rows(step, 64)
    for base in range(0, frames, step):
        xb = x[0, base : base + step, :]
        vl_o[0, base : base + step, :] = dot(xb, wv[...])
        sg_o[0, base : base + step, :] = dot(xb, wg[...])

    def gating(i, carry):
        base = pl.multiple_of(i * small, small)
        v = vl_o[0, pl.ds(base, small), :]
        s = sigmoid(sg_o[0, pl.ds(base, small), :])
        sg_o[0, pl.ds(base, small), :] = s
        put(2 * EDGE + base, jnp.where(rows_of(small, base) < hi, v * s, 0.0))
        return carry

    lax.fori_loop(0, frames // small, gating, 0)
    span = frames + 2 * EDGE
    cb = block_rows(span, 104)
    kernel = taps.shape[0]
    margin = (kernel - 1) // 2
    for h in range(halves):
        cols = slice(h * LANES, (h + 1) * LANES)

        def convolve(i, carry):
            s1, s2 = carry
            base = pl.multiple_of(i * cb, 8)
            acc = jnp.zeros((cb, LANES), F32)
            for k in range(kernel):
                acc = acc + taps[k : k + 1, cols] * gp[h, pl.ds(base + EDGE - margin + k, cb), :]
            conv_o[0, pl.ds(base, cb), cols] = acc
            pos = rows_of(cb, base - EDGE)
            kept = jnp.where((pos >= 0) & (pos < jnp.minimum(hi, frames)), acc, 0.0)
            return s1 + fold_rows(kept), s2 + fold_rows(kept * kept)

        none = jnp.zeros((8, LANES), F32)
        s1, s2 = lax.fori_loop(0, span // cb, convolve, (none, none))
        add = jnp.concatenate(
            [jnp.sum(s1, axis=0, keepdims=True), jnp.sum(s2, axis=0, keepdims=True)], axis=0
        )
        st[:, cols] = jnp.where(r == 0, 0.0, st[:, cols]) + add

    @pl.when(r == pl.num_programs(0) - 1)
    def _():
        spread_sums(st_o, st[...])


def swish_kernel(grads, halo, wo, sw_o):
    frames = grads.shape[1]
    edge = dot(halo[0], wo[...])
    sw_o[0, :EDGE, :] = edge[:EDGE]
    sw_o[0, EDGE + frames :, :] = edge[EDGE:]
    step = block_rows(frames, 512)
    for base in range(0, frames, step):
        sw_o[0, EDGE + base : EDGE + base + step, :] = dot(grads[0, base : base + step, :], wo[...])


def batch_norm(stats, count):
    sums = jnp.sum(stats[...], axis=0)
    centre = sums[0:1] / count
    spread = sums[1:2] / count - centre * centre
    return centre, lax.rsqrt(spread + EPSILON)


def norm_kernel(
    meta, count, stats, affine, select, grads, sw, conv, swished_o, gn_o, picked_o, st_o, st
):
    r = pl.program_id(0)
    hi = meta[0, r]
    lo = meta[1, r]
    frames = grads.shape[1]
    centre, inv = batch_norm(stats, count[0, 0])
    gain, shift = affine[0:1, :], affine[1:2, :]

    def part(row, size):
        unit = (conv[0, pl.ds(row, size), :] - centre) * inv
        normalized = unit * gain + shift
        s = sigmoid(normalized)
        pos = rows_of(size, row - EDGE)
        keep = (pos >= lo) & (pos < hi)
        swished = jnp.where(keep, normalized * s, 0.0)
        swish_grad = sw[0, pl.ds(row, size), :]
        gn = jnp.where(keep, swish_grad, 0.0) * (s + normalized * (s - s * s))
        gn_o[0, pl.ds(row, size), :] = gn
        return unit, swished, gn

    part(0, EDGE)
    part(frames + EDGE, EDGE)
    step = block_rows(frames, 512)
    small = block_rows(step, 32)
    s1 = jnp.zeros((8, conv.shape[2]), F32)
    s2 = s1
    for i in range(frames // step):
        picked_o[0, :, i * step : (i + 1) * step] = dot_nt(
            select[...], grads[0, i * step : (i + 1) * step, :]
        ).astype(BF16)
        for j in range(step // small):
            base = i * step + j * small
            unit, swished, gn = part(base + EDGE, small)
            swished_o[0, base : base + small, :] = swished.astype(BF16)
            s1 = s1 + fold_rows(gn)
            s2 = s2 + fold_rows(gn * unit)
    add = jnp.concatenate(
        [jnp.sum(s1, axis=0, keepdims=True), jnp.sum(s2, axis=0, keepdims=True)], axis=0
    )
    st[...] = jnp.where(r == 0, 0.0, st[...]) + add

    @pl.when(r == pl.num_programs(0) - 1)
    def _():
        spread_sums(st_o, st[...])


def back_kernel(
    record, blocks, meta, count, stats, sums, gain, gn, conv, vl, sg, taps, out, taps_o, gc, acc
):
    i = pl.program_id(0)
    frames, width = vl.shape[1:]
    hi = meta[0, record + i // blocks]
    lo = meta[1, record + i // blocks]
    halves = width // LANES
    span = frames + 2 * EDGE
    kernel = taps.shape[0]
    margin = (kernel - 1) // 2
    cb = block_rows(span, 144)
    step = block_rows(frames, 64)
    total_frames = count[0, 0]
    centre, inv = batch_norm(stats, total_frames)
    grad_sums = jnp.sum(sums[...], axis=0)
    scale = gain[...] * inv
    offset = scale * grad_sums[0:1] / total_frames
    slope = scale * inv * grad_sums[1:2] / total_frames
    first = i % blocks * frames

    @pl.when(i == 0)
    def _():
        acc[...] = jnp.zeros_like(acc)

    for h in range(halves):
        cols = slice(h * LANES, (h + 1) * LANES)
        for base in range(0, span, cb):
            pos = rows_of(cb, first + (base - EDGE))
            mean = offset[:, cols] + (conv[0, base : base + cb, cols] - centre[:, cols]) * slope[:, cols]
            gc[h, base : base + cb, :] = scale[:, cols] * gn[0, base : base + cb, cols] - jnp.where(
                (pos >= lo) & (pos < hi), mean, 0.0
            )
        sums_k = [acc[h, k] for k in range(kernel)]
        for base in range(0, frames, step):
            v = vl[0, base : base + step, cols]
            s = sg[0, base : base + step, cols]
            keep = rows_of(step, first + base) < hi
            vs = v * s
            gated = jnp.where(keep, vs, 0.0)
            total = jnp.zeros((step, LANES), F32)
            for k in range(kernel):
                window = gc[h, base + EDGE + margin - k : base + EDGE + margin - k + step, :]
                total = total + taps[k : k + 1, cols] * window
                sums_k[k] = sums_k[k] + fold_rows(window * gated)
            total = jnp.where(keep, total, 0.0)
            out[base : base + step, cols] = (total * s).astype(BF16)
            out[base : base + step, width + h * LANES : width + (h + 1) * LANES] = (
                total * (vs - vs * s)
            ).astype(BF16)
        for k in range(kernel):
            acc[h, k] = sums_k[k]

    @pl.when(i == pl.num_programs(0) - 1)
    def _():
        taps_o[...] = jnp.zeros_like(taps_o)
        for h in range(halves):
            for k in range(kernel):
                taps_o[k : k + 1, h * LANES : (h + 1) * LANES] = jnp.sum(
                    acc[h, k], axis=0, keepdims=True
                )


def partial_kernel(own, sibling, w_own, w_sibling, picked, mine, *others):
    total = dot_nt(w_own[...], own[...]) + dot_nt(w_sibling[...], sibling[...])
    rows = picked.shape[1]
    seqs, _, piece, frames = mine.shape
    mine[...] = (
        (total[:rows] + picked[0].astype(F32)).astype(BF16).reshape(seqs, 1, piece, frames)
    )
    for d, other in enumerate(others):
        other[...] = (
            total[(d + 1) * rows : (d + 2) * rows].astype(BF16).reshape(seqs, 1, piece, frames)
        )


def add_kernel(*refs):
    total = refs[0][...].astype(F32)
    for other in refs[1:-1]:
        total = total + other[...].astype(F32)
    refs[-1][...] = total.astype(BF16)


def first_outer_kernel(grads, swished, out):
    r = pl.program_id(0)
    add = dot_tn(swished[0], grads[0])

    @pl.when(r == 0)
    def _():
        out[...] = add

    @pl.when(r > 0)
    def _():
        out[...] += add


def outer_kernel(groups, parity, x, w_out, *refs):
    lefts, taps = refs[: len(groups)], refs[len(groups) : 2 * len(groups)]
    keep, send, acc = refs[2 * len(groups) :]
    records = groups[-1][0] + groups[-1][1]
    width = w_out.shape[0]
    shard = keep.shape[2]
    r = pl.program_id(0)
    for (first, size), left in zip(groups, lefts):

        @pl.when((r >= first) & (r < first + size))
        def _(left=left):
            add = dot_tn(left[...], x[0])
            acc[...] = add + jnp.where(r == 0, 0.0, acc[...])

    @pl.when(r == records - 1)
    def _():
        tap_sums = taps[0][...]
        for part in taps[1:]:
            tap_sums = tap_sums + part[...]

        def write(place, odd):
            for j in range(place.shape[0]):
                at = (2 * j + odd) * shard
                place[j, : 2 * width, :] = acc[:, at : at + shard].astype(BF16)
                place[j, 2 * width : 3 * width, :] = w_out[:, at : at + shard].astype(BF16)
                for q in range(width // shard):
                    row = 3 * width + 16 * q
                    place[j, row : row + 16, :] = tap_sums[:, q * shard : (q + 1) * shard].astype(
                        BF16
                    )

        @pl.when(parity[0, 0] == 0)
        def _():
            write(keep, 0)
            write(send, 1)

        @pl.when(parity[0, 0] != 0)
        def _():
            write(keep, 1)
            write(send, 0)


def fold_kernel(parity, own, other, keep, send):
    def write(place, odd):
        for j in range(place.shape[0]):
            total = own[2 * j + odd].astype(F32) + other[2 * j + odd].astype(F32)
            place[j] = total.astype(BF16)

    @pl.when(parity[0, 0] == 0)
    def _():
        write(keep, 0)
        write(send, 1)

    @pl.when(parity[0, 0] != 0)
    def _():
        write(keep, 1)
        write(send, 0)


def finish_kernel(kernel, own, other, value, gate, out, taps):
    width = value.shape[1]
    shard = value.shape[0]

    def total(row, size):
        return own[0, row : row + size, :].astype(F32) + other[0, row : row + size, :].astype(F32)

    for i, place in enumerate((value, gate, out)):
        place[...] = total(i * width, width).T
    for q in range(width // shard):
        taps[:, q * shard : (q + 1) * shard] = total(3 * width + 16 * q, 16)[:kernel]


def place_kernel(moved, *refs):
    out = refs[-1]
    frames = moved.shape[3]
    for s in range(moved.shape[0]):
        out[0, :, s * frames : (s + 1) * frames] = moved[s, 0]


def exchange(copies, axis):
    return lax.all_to_all(copies, axis, 0, 0, tiled=True)


def per_device(
    normed,
    grad_out,
    value_weight,
    gate_weight,
    depth_taps,
    norm_gain,
    norm_shift,
    out_weight,
    lengths,
):
    recs, frames, model = normed.shape
    kernel = depth_taps.shape[0]
    width = value_weight.shape[1]
    seqs = lax.axis_size("seq")
    tps = lax.axis_size("tp")
    chips = tps // 2
    piece = model // (seqs * tps)
    rows = seqs * piece
    shard = model // seqs
    span = frames + 2 * EDGE
    seq_at = lax.axis_index("seq")
    tp_at = lax.axis_index("tp")
    chip_at, core_at = tp_at // 2, tp_at % 2
    count = jnp.sum(lengths).astype(F32)
    first = (seq_at * frames).astype(jnp.int32)
    meta = jnp.stack([lengths - first, jnp.full((recs,), 0, jnp.int32) - first])
    halves = width // LANES
    counts = count.reshape(1, 1)
    parity = (seq_at % 2).astype(jnp.int32).reshape(1, 1)
    sds = jax.ShapeDtypeStruct

    low_edge = jnp.concatenate([normed[:, -EDGE:], grad_out[:, -EDGE:]], axis=2)
    high_edge = jnp.concatenate([normed[:, :EDGE], grad_out[:, :EDGE]], axis=2)
    up = [(i, i + 1) for i in range(seqs - 1)]
    down = [(j, i) for i, j in up]
    halo = jnp.concatenate(
        [lax.ppermute(low_edge, "seq", up), lax.ppermute(high_edge, "seq", down)], axis=1
    )
    halo_x, halo_g = halo[:, :, :model], halo[:, :, model:]

    channel = (
        jnp.arange(seqs, dtype=jnp.int32)[:, None] * (tps * piece)
        + tp_at * piece
        + jnp.arange(piece, dtype=jnp.int32)[None, :]
    ).reshape(rows, 1)
    select = (channel == jnp.arange(model, dtype=jnp.int32)[None, :]).astype(BF16)
    array_bytes = recs * frames * width * 4
    input_bytes = recs * frames * model * 2
    matmul = 2 * recs * frames * model * width

    vl, sg, conv, stats = call(
        gate_kernel,
        "gate_conv",
        (recs,),
        [
            smem(),
            per_record((frames, model)),
            per_record((2 * EDGE, model)),
            whole((model, width)),
            whole((model, width)),
            whole((kernel, width)),
        ],
        [
            per_record((frames, width)),
            per_record((frames, width)),
            per_record((span, width)),
            whole((seqs, 2, width)),
        ],
        [
            sds((recs, frames, width), F32),
            sds((recs, frames, width), F32),
            sds((recs, span, width), F32),
            sds((seqs, 2, width), F32),
        ],
        [pltpu.VMEM((halves, frames + 4 * EDGE, LANES), F32), pltpu.VMEM((2, width), F32)],
        2 * matmul,
        input_bytes + 3 * array_bytes,
    )(meta, normed, halo_x, value_weight, gate_weight, depth_taps)
    both = jnp.concatenate([after(value_weight, stats), gate_weight], axis=1).reshape(seqs, tps, piece, 2 * width)

    def chosen(core):
        picks = [
            lax.dynamic_index_in_dim(both, ((chip_at + d) % chips) * 2 + core, 1, keepdims=False)
            for d in range(chips)
        ]
        return jnp.stack(picks).reshape(chips * rows, 2 * width)

    swap = [(i, i ^ 1) for i in range(tps)]
    w_own = chosen(core_at)
    w_sibling = lax.ppermute(chosen(1 - core_at), "tp", swap)

    stats = exchange(stats, "seq")

    chunk = block_rows(frames, 256)
    half_rows = block_rows(frames, 512)
    sw = call(
        swish_kernel,
        "swish_grad",
        (recs,),
        [per_record((frames, model)), per_record((2 * EDGE, model)), whole((model, width))],
        per_record((span, width)),
        sds((recs, span, width), F32),
        [],
        matmul,
        input_bytes + array_bytes,
    )(grad_out, halo_g, after(out_weight, w_own))

    swished, gn, picked, sums = call(
        norm_kernel,
        "norm",
        (recs,),
        [
            smem(),
            smem(),
            whole((seqs, 2, width)),
            whole((2, width)),
            whole((rows, model)),
            per_record((frames, model)),
            per_record((span, width)),
            per_record((span, width)),
        ],
        [
            per_record((frames, width)),
            per_record((span, width)),
            per_record((rows, frames)),
            whole((seqs, 2, width)),
        ],
        [
            sds((recs, frames, width), BF16),
            sds((recs, span, width), F32),
            sds((recs, rows, frames), BF16),
            sds((seqs, 2, width), F32),
        ],
        [pltpu.VMEM((2, width), F32)],
        matmul,
        input_bytes + 3 * array_bytes,
    )(
        meta,
        counts,
        stats,
        jnp.stack([norm_gain, norm_shift]),
        after(select, w_own, w_sibling),
        grad_out,
        sw,
        conv,
    )
    w_out = call(
        first_outer_kernel,
        "outer_w_out",
        (recs,),
        [per_record((frames, model)), per_record((frames, width))],
        whole((width, model)),
        sds((width, model), F32),
        [],
        matmul,
        input_bytes,
    )(grad_out, swished)
    sums = exchange(sums, "seq")
    grad_shift, grad_gain = jnp.sum(sums, axis=0)

    blocks = frames // chunk
    parts_in = frames // half_rows

    def back(first, size, *earlier):
        def window(i):
            return (first + i // blocks, pl.multiple_of(i % blocks * chunk, chunk), 0)

        def block(i):
            return (first + i // blocks, i % blocks, 0)

        return call(
            functools.partial(back_kernel, first, blocks),
            "back_conv",
            (size * blocks,),
            [
                smem(),
                smem(),
                whole((seqs, 2, width)),
                whole((seqs, 2, width)),
                whole((1, width)),
                pl.BlockSpec((pl.Element(1), pl.Element(chunk + 2 * EDGE), pl.Element(width)), window),
                pl.BlockSpec((pl.Element(1), pl.Element(chunk + 2 * EDGE), pl.Element(width)), window),
                pl.BlockSpec((1, chunk, width), block),
                pl.BlockSpec((1, chunk, width), block),
                whole((kernel, width)),
            ],
            [pl.BlockSpec((chunk, 2 * width), lambda i: (i, 0)), whole((16, width))],
            [sds((size * frames, 2 * width), BF16), sds((16, width), F32)],
            [
                pltpu.VMEM((halves, chunk + 2 * EDGE, LANES), F32),
                pltpu.VMEM((halves, kernel, 8, LANES), F32),
            ],
            0,
            1024,
        )(meta, counts, stats, sums, norm_gain[None], gn, conv, vl, sg, after(depth_taps, *earlier))

    def partials(first, size, mine, *earlier):
        sibling = lax.ppermute(mine, "tp", swap)
        out = sds((seqs, size, piece, frames), BF16)
        return call(
            partial_kernel,
            "partial_in",
            (size * parts_in,),
            [
                pl.BlockSpec((half_rows, 2 * width), lambda i: (i, 0)),
                pl.BlockSpec((half_rows, 2 * width), lambda i: (i, 0)),
                whole((chips * rows, 2 * width)),
                whole((chips * rows, 2 * width)),
                pl.BlockSpec(
                    (1, rows, half_rows), lambda i: (first + i // parts_in, 0, i % parts_in)
                ),
            ],
            [
                pl.BlockSpec(
                    (seqs, 1, piece, half_rows), lambda i: (0, i // parts_in, 0, i % parts_in)
                )
            ]
            * chips,
            [out] * chips,
            [],
            0,
            1024,
        )(mine, sibling, after(w_own, *earlier), w_sibling, picked)

    def deliver(part, weight, *earlier):
        arrived = []
        for d in range(1, chips):
            send = [(i, ((i // 2 + d) % chips) * 2 + i % 2) for i in range(tps)]
            arrived.append(lax.ppermute(part[d], "tp", send))
        size = part[0].shape[1]
        block = pl.BlockSpec(
            (seqs, 1, piece, half_rows), lambda i: (0, i // parts_in, 0, i % parts_in)
        )
        own = call(
            add_kernel,
            "add",
            (size * parts_in,),
            [block] * chips,
            block,
            sds(part[0].shape, BF16),
            [],
            weight,
            1024,
        )(after(part[0], *earlier), *arrived)
        return own

    groups = ((0, 1), (1, 1), (2, recs - 2))
    grads = [None] * 3
    taps = [None] * 3
    parts = [None] * 3
    owns = [None] * 3
    moved = [None] * 3
    grads[0], taps[0] = back(*groups[0], w_out)
    grads[1], taps[1] = back(*groups[1], grads[0])
    parts[0] = partials(*groups[0], grads[0], grads[1])
    grads[2], taps[2] = back(*groups[2], *parts[0])
    parts[1] = partials(*groups[1], grads[1], grads[2])
    owns[0] = deliver(parts[0], LONG, *parts[1])
    moved[0] = exchange(owns[0], "seq")
    parts[2] = partials(*groups[2], grads[2], owns[0])

    slots = 3 * width + 16 * (width // shard)
    half = sds((seqs // 2, slots, shard), BF16)
    keep, send = call(
        functools.partial(outer_kernel, groups),
        "outer_w_in",
        (recs,),
        [smem(), per_record((frames, model)), whole((width, model))]
        + [
            pl.BlockSpec(
                (frames, 2 * width),
                lambda r, first=first, size=size: (jnp.clip(r - first, 0, size - 1), 0),
            )
            for first, size in groups
        ]
        + [whole((16, width))] * len(groups),
        [whole(half.shape)] * 2,
        [half] * 2,
        [pltpu.VMEM((2 * width, model), F32)],
        LONG,
        1024,
    )(parity, after(normed, *parts[2]), w_out, *grads, *taps)
    owns[1] = deliver(parts[1], LONG, keep)
    moved[1] = exchange(after(owns[1], moved[0]), "seq")
    bit = 1
    while True:
        others = lax.ppermute(send, "seq", [(i, i ^ bit) for i in range(seqs)])
        bit *= 2
        if bit == seqs:
            break
        if bit == 2:
            keep = after(keep, owns[1])
        shape = (keep.shape[0] // 2,) + keep.shape[1:]
        side = ((seq_at // bit) % 2).astype(jnp.int32).reshape(1, 1)
        keep, send = call(
            fold_kernel,
            "fold",
            (1,),
            [smem()] + [whole(keep.shape)] * 2,
            [whole(shape)] * 2,
            [sds(shape, BF16)] * 2,
            [],
            0,
            1024,
            vmem=20,
        )(side, keep, others)
        if bit == 2:
            owns[2] = deliver(parts[2], 0, keep)
        if bit == min(4, seqs // 2):
            moved[2] = exchange(after(owns[2], moved[1], keep), "seq")
    w_value, w_gate, w_out, grad_taps = call(
        functools.partial(finish_kernel, kernel),
        "finish",
        (1,),
        [whole(keep.shape)] * 2,
        [whole((shard, width))] * 3 + [whole((kernel, width))],
        [sds((shard, width), F32)] * 3 + [sds((kernel, width), F32)],
        [],
        0,
        1024,
        vmem=20,
    )(keep, others)
    grad_in = ()
    for (first, size), part in zip(groups, moved):
        grad_in = (
            call(
                place_kernel,
                "place",
                (size,),
                [pl.BlockSpec((seqs, 1, piece, frames), lambda i: (0, i, 0, 0))]
                + [anywhere()] * len(grad_in),
                pl.BlockSpec((1, piece, seqs * frames), lambda i, first=first: (first + i, 0, 0)),
                sds((recs, piece, seqs * frames), BF16),
                [],
                0,
                4 * size * piece * seqs * frames,
                {1: 0} if grad_in else None,
                vmem=20,
            )(part, *grad_in),
        )
    (grad_in,) = grad_in
    return (grad_in, w_value, w_gate, w_out, grad_taps, grad_gain, grad_shift)


def solution(mesh):
    placed = (
        P(None, "seq", None),
        P(None, "seq", None),
        P(None, "tp"),
        P(None, "tp"),
        P(None, "tp"),
        P("tp"),
        P("tp"),
        P(None, "tp"),
        P(),
    )
    return jax.shard_map(
        per_device,
        mesh=mesh,
        in_specs=placed,
        out_specs=(
            P(None, ("seq", "tp"), None),
            P("seq", "tp"),
            P("seq", "tp"),
            P("seq", "tp"),
            P(None, "tp"),
            P("tp"),
            P("tp"),
        ),
        check_vma=False,
    )
```

```python
import functools

import jax
import jax.numpy as jnp
from jax import lax
from jax.experimental import pallas as pl
from jax.experimental.pallas import tpu as pltpu
from jax.sharding import PartitionSpec as P

EPSILON = 1e-05
EDGE = 8
LANES = 128
LONG = 50_000_000_000
F32 = jnp.float32
BF16 = jnp.bfloat16


def sigmoid(x):
    return 0.5 * jnp.tanh(0.5 * x) + 0.5


def dot(a, b):
    return jnp.dot(a, b, preferred_element_type=F32)


def dot_nt(a, b):
    return lax.dot_general(a, b, (((1,), (1,)), ((), ())), preferred_element_type=F32)


def dot_tn(a, b):
    return lax.dot_general(a, b, (((0,), (0,)), ((), ())), preferred_element_type=F32)


def rows_of(count, first):
    return first + lax.broadcasted_iota(jnp.int32, (count, 1), 0)


def fold_rows(x):
    return jnp.sum(x.reshape(x.shape[0] // 8, 8, x.shape[1]), axis=0)


def block_rows(total, most):
    return max(b for b in range(8, most + 1, 8) if total % b == 0)


def whole(shape):
    return pl.BlockSpec(shape, lambda *i: (0,) * len(shape))


def per_record(shape):
    return pl.BlockSpec((1,) + shape, lambda r: (r,) + (0,) * len(shape))


def smem():
    return pl.BlockSpec(memory_space=pltpu.SMEM)


def anywhere():
    return pl.BlockSpec(memory_space=pl.ANY)


def after(x, *earlier):
    return lax.optimization_barrier((x,) + earlier)[0]


def spread_sums(out, sums):
    for s in range(out.shape[0]):
        out[s] = sums


def call(
    kernel, name, grid, in_specs, out_specs, out_shape, scratch, flops, moved, aliases=None, vmem=63
):
    return pl.pallas_call(
        kernel,
        name=name,
        grid=grid,
        in_specs=in_specs,
        out_specs=out_specs,
        out_shape=out_shape,
        scratch_shapes=scratch,
        input_output_aliases=aliases or {},
        cost_estimate=pl.CostEstimate(flops=int(flops), bytes_accessed=int(moved), transcendentals=0),
        compiler_params=pltpu.CompilerParams(vmem_limit_bytes=vmem * 1024 * 1024),
    )


def gate_kernel(meta, x, halo, wv, wg, taps, vl_o, sg_o, conv_o, st_o, gp, st):
    r = pl.program_id(0)
    hi = meta[0, r]
    lo = meta[1, r]
    frames = x.shape[1]
    width = wv.shape[1]
    halves = width // LANES

    def put(row, value):
        for h in range(halves):
            gp[h, pl.ds(row, value.shape[0]), :] = value[:, h * LANES : (h + 1) * LANES]

    edge_v = dot(halo[0], wv[...])
    edge_g = dot(halo[0], wg[...])
    row = rows_of(2 * EDGE, 0)
    pos = jnp.where(row < EDGE, row - EDGE, row - EDGE + frames)
    edge = jnp.where((pos >= lo) & (pos < hi), edge_v * sigmoid(edge_g), 0.0)
    zero = jnp.zeros((EDGE, width), F32)
    put(0, zero)
    put(EDGE, edge[:EDGE])
    put(2 * EDGE + frames, edge[EDGE:])
    put(3 * EDGE + frames, zero)
    step = block_rows(frames, 512)
    small = block_rows(step, 64)
    for base in range(0, frames, step):
        xb = x[0, base : base + step, :]
        vl_o[0, base : base + step, :] = dot(xb, wv[...])
        sg_o[0, base : base + step, :] = dot(xb, wg[...])

    def gating(i, carry):
        base = pl.multiple_of(i * small, small)
        v = vl_o[0, pl.ds(base, small), :]
        s = sigmoid(sg_o[0, pl.ds(base, small), :])
        sg_o[0, pl.ds(base, small), :] = s
        put(2 * EDGE + base, jnp.where(rows_of(small, base) < hi, v * s, 0.0))
        return carry

    lax.fori_loop(0, frames // small, gating, 0)
    span = frames + 2 * EDGE
    cb = block_rows(span, 104)
    kernel = taps.shape[0]
    margin = (kernel - 1) // 2
    for h in range(halves):
        cols = slice(h * LANES, (h + 1) * LANES)

        def convolve(i, carry):
            s1, s2 = carry
            base = pl.multiple_of(i * cb, 8)
            acc = jnp.zeros((cb, LANES), F32)
            for k in range(kernel):
                acc = acc + taps[k : k + 1, cols] * gp[h, pl.ds(base + EDGE - margin + k, cb), :]
            conv_o[0, pl.ds(base, cb), cols] = acc
            pos = rows_of(cb, base - EDGE)
            kept = jnp.where((pos >= 0) & (pos < jnp.minimum(hi, frames)), acc, 0.0)
            return s1 + fold_rows(kept), s2 + fold_rows(kept * kept)

        none = jnp.zeros((8, LANES), F32)
        s1, s2 = lax.fori_loop(0, span // cb, convolve, (none, none))
        add = jnp.concatenate(
            [jnp.sum(s1, axis=0, keepdims=True), jnp.sum(s2, axis=0, keepdims=True)], axis=0
        )
        st[:, cols] = jnp.where(r == 0, 0.0, st[:, cols]) + add

    @pl.when(r == pl.num_programs(0) - 1)
    def _():
        spread_sums(st_o, st[...])


def batch_norm(stats, count):
    sums = jnp.sum(stats[...], axis=0)
    centre = sums[0:1] / count
    spread = sums[1:2] / count - centre * centre
    return centre, lax.rsqrt(spread + EPSILON)


def norm_kernel(
    meta, count, stats, affine, select, grads, halo, wo, conv,
    swished_o, gn_o, picked_o, st_o, st, ping, pong
):
    r = pl.program_id(0)
    hi = meta[0, r]
    lo = meta[1, r]
    frames = grads.shape[1]
    centre, inv = batch_norm(stats, count[0, 0])
    gain, shift = affine[0:1, :], affine[1:2, :]

    def part(row, swish_grad):
        size = swish_grad.shape[0]
        unit = (conv[0, pl.ds(row, size), :] - centre) * inv
        normalized = unit * gain + shift
        s = sigmoid(normalized)
        pos = rows_of(size, row - EDGE)
        keep = (pos >= lo) & (pos < hi)
        swished = jnp.where(keep, normalized * s, 0.0)
        gn = jnp.where(keep, swish_grad, 0.0) * (s + normalized * (s - s * s))
        gn_o[0, pl.ds(row, size), :] = gn
        return unit, swished, gn

    edge = dot(halo[0], wo[...])
    part(0, edge[:EDGE])
    part(frames + EDGE, edge[EDGE:])
    step = block_rows(frames, 512)
    small = block_rows(step, 32)
    s1 = jnp.zeros((8, conv.shape[2]), F32)
    s2 = s1
    held = (ping, pong)
    ping[...] = dot(grads[0, :step, :], wo[...])
    for i in range(frames // step):
        now = held[i % 2]
        if (i + 1) * step < frames:
            held[(i + 1) % 2][...] = dot(grads[0, (i + 1) * step : (i + 2) * step, :], wo[...])
        picked_o[0, :, i * step : (i + 1) * step] = dot_nt(
            select[...], grads[0, i * step : (i + 1) * step, :]
        ).astype(BF16)
        for j in range(step // small):
            base = i * step + j * small
            unit, swished, gn = part(base + EDGE, now[j * small : (j + 1) * small, :])
            swished_o[0, base : base + small, :] = swished.astype(BF16)
            s1 = s1 + fold_rows(gn)
            s2 = s2 + fold_rows(gn * unit)
    add = jnp.concatenate(
        [jnp.sum(s1, axis=0, keepdims=True), jnp.sum(s2, axis=0, keepdims=True)], axis=0
    )
    st[...] = jnp.where(r == 0, 0.0, st[...]) + add

    @pl.when(r == pl.num_programs(0) - 1)
    def _():
        spread_sums(st_o, st[...])


def back_kernel(
    record, blocks, meta, count, stats, sums, gain, gn, conv, vl, sg, taps, out, taps_o, gc, acc
):
    i = pl.program_id(0)
    frames, width = vl.shape[1:]
    hi = meta[0, record + i // blocks]
    lo = meta[1, record + i // blocks]
    halves = width // LANES
    span = frames + 2 * EDGE
    kernel = taps.shape[0]
    margin = (kernel - 1) // 2
    cb = block_rows(span, 144)
    step = block_rows(frames, 64)
    total_frames = count[0, 0]
    centre, inv = batch_norm(stats, total_frames)
    grad_sums = jnp.sum(sums[...], axis=0)
    scale = gain[...] * inv
    offset = scale * grad_sums[0:1] / total_frames
    slope = scale * inv * grad_sums[1:2] / total_frames
    first = i % blocks * frames

    @pl.when(i == 0)
    def _():
        acc[...] = jnp.zeros_like(acc)

    for h in range(halves):
        cols = slice(h * LANES, (h + 1) * LANES)
        for base in range(0, span, cb):
            pos = rows_of(cb, first + (base - EDGE))
            mean = offset[:, cols] + (conv[0, base : base + cb, cols] - centre[:, cols]) * slope[:, cols]
            gc[h, base : base + cb, :] = scale[:, cols] * gn[0, base : base + cb, cols] - jnp.where(
                (pos >= lo) & (pos < hi), mean, 0.0
            )
        sums_k = [acc[h, k] for k in range(kernel)]
        for base in range(0, frames, step):
            v = vl[0, base : base + step, cols]
            s = sg[0, base : base + step, cols]
            keep = rows_of(step, first + base) < hi
            vs = v * s
            gated = jnp.where(keep, vs, 0.0)
            total = jnp.zeros((step, LANES), F32)
            for k in range(kernel):
                window = gc[h, base + EDGE + margin - k : base + EDGE + margin - k + step, :]
                total = total + taps[k : k + 1, cols] * window
                sums_k[k] = sums_k[k] + fold_rows(window * gated)
            total = jnp.where(keep, total, 0.0)
            out[base : base + step, cols] = (total * s).astype(BF16)
            out[base : base + step, width + h * LANES : width + (h + 1) * LANES] = (
                total * (vs - vs * s)
            ).astype(BF16)
        for k in range(kernel):
            acc[h, k] = sums_k[k]

    @pl.when(i == pl.num_programs(0) - 1)
    def _():
        taps_o[...] = jnp.zeros_like(taps_o)
        for h in range(halves):
            for k in range(kernel):
                taps_o[k : k + 1, h * LANES : (h + 1) * LANES] = jnp.sum(
                    acc[h, k], axis=0, keepdims=True
                )


def partial_kernel(own, sibling, w_own, w_sibling, picked, mine, *others):
    total = dot_nt(w_own[...], own[...]) + dot_nt(w_sibling[...], sibling[...])
    rows = picked.shape[1]
    seqs, _, piece, frames = mine.shape
    mine[...] = (
        (total[:rows] + picked[0].astype(F32)).astype(BF16).reshape(seqs, 1, piece, frames)
    )
    for d, other in enumerate(others):
        other[...] = (
            total[(d + 1) * rows : (d + 2) * rows].astype(BF16).reshape(seqs, 1, piece, frames)
        )


def add_kernel(*refs):
    total = refs[0][...].astype(F32)
    for other in refs[1:-1]:
        total = total + other[...].astype(F32)
    refs[-1][...] = total.astype(BF16)


def first_outer_kernel(grads, swished, out):
    r = pl.program_id(0)
    add = dot_tn(swished[0], grads[0])

    @pl.when(r == 0)
    def _():
        out[...] = add

    @pl.when(r > 0)
    def _():
        out[...] += add


def outer_kernel(groups, parity, x, w_out, *refs):
    lefts, taps = refs[: len(groups)], refs[len(groups) : 2 * len(groups)]
    keep, send, acc = refs[2 * len(groups) :]
    records = groups[-1][0] + groups[-1][1]
    width = w_out.shape[0]
    shard = keep.shape[2]
    r = pl.program_id(0)
    for (first, size), left in zip(groups, lefts):

        @pl.when((r >= first) & (r < first + size))
        def _(left=left):
            add = dot_tn(left[...], x[0])
            acc[...] = add + jnp.where(r == 0, 0.0, acc[...])

    @pl.when(r == records - 1)
    def _():
        tap_sums = taps[0][...]
        for part in taps[1:]:
            tap_sums = tap_sums + part[...]

        def write(place, odd):
            for j in range(place.shape[0]):
                at = (2 * j + odd) * shard
                place[j, : 2 * width, :] = acc[:, at : at + shard].astype(BF16)
                place[j, 2 * width : 3 * width, :] = w_out[:, at : at + shard].astype(BF16)
                for q in range(width // shard):
                    row = 3 * width + 16 * q
                    place[j, row : row + 16, :] = tap_sums[:, q * shard : (q + 1) * shard].astype(
                        BF16
                    )

        @pl.when(parity[0, 0] == 0)
        def _():
            write(keep, 0)
            write(send, 1)

        @pl.when(parity[0, 0] != 0)
        def _():
            write(keep, 1)
            write(send, 0)


def fold_kernel(parity, own, other, keep, send):
    def write(place, odd):
        for j in range(place.shape[0]):
            total = own[2 * j + odd].astype(F32) + other[2 * j + odd].astype(F32)
            place[j] = total.astype(BF16)

    @pl.when(parity[0, 0] == 0)
    def _():
        write(keep, 0)
        write(send, 1)

    @pl.when(parity[0, 0] != 0)
    def _():
        write(keep, 1)
        write(send, 0)


def finish_kernel(kernel, own, other, value, gate, out, taps):
    width = value.shape[1]
    shard = value.shape[0]

    def total(row, size):
        return own[0, row : row + size, :].astype(F32) + other[0, row : row + size, :].astype(F32)

    for i, place in enumerate((value, gate, out)):
        place[...] = total(i * width, width).T
    for q in range(width // shard):
        taps[:, q * shard : (q + 1) * shard] = total(3 * width + 16 * q, 16)[:kernel]


def place_kernel(moved, *refs):
    out = refs[-1]
    frames = moved.shape[3]
    for s in range(moved.shape[0]):
        out[0, :, s * frames : (s + 1) * frames] = moved[s, 0]


def exchange(copies, axis):
    return lax.all_to_all(copies, axis, 0, 0, tiled=True)


def per_device(
    normed,
    grad_out,
    value_weight,
    gate_weight,
    depth_taps,
    norm_gain,
    norm_shift,
    out_weight,
    lengths,
):
    recs, frames, model = normed.shape
    kernel = depth_taps.shape[0]
    width = value_weight.shape[1]
    seqs = lax.axis_size("seq")
    tps = lax.axis_size("tp")
    chips = tps // 2
    piece = model // (seqs * tps)
    rows = seqs * piece
    shard = model // seqs
    span = frames + 2 * EDGE
    seq_at = lax.axis_index("seq")
    tp_at = lax.axis_index("tp")
    chip_at, core_at = tp_at // 2, tp_at % 2
    count = jnp.sum(lengths).astype(F32)
    first = (seq_at * frames).astype(jnp.int32)
    meta = jnp.stack([lengths - first, jnp.full((recs,), 0, jnp.int32) - first])
    halves = width // LANES
    counts = count.reshape(1, 1)
    parity = (seq_at % 2).astype(jnp.int32).reshape(1, 1)
    sds = jax.ShapeDtypeStruct

    low_edge = jnp.concatenate([normed[:, -EDGE:], grad_out[:, -EDGE:]], axis=2)
    high_edge = jnp.concatenate([normed[:, :EDGE], grad_out[:, :EDGE]], axis=2)
    up = [(i, i + 1) for i in range(seqs - 1)]
    down = [(j, i) for i, j in up]
    halo = jnp.concatenate(
        [lax.ppermute(low_edge, "seq", up), lax.ppermute(high_edge, "seq", down)], axis=1
    )
    halo_x, halo_g = halo[:, :, :model], halo[:, :, model:]

    channel = (
        jnp.arange(seqs, dtype=jnp.int32)[:, None] * (tps * piece)
        + tp_at * piece
        + jnp.arange(piece, dtype=jnp.int32)[None, :]
    ).reshape(rows, 1)
    select = (channel == jnp.arange(model, dtype=jnp.int32)[None, :]).astype(BF16)
    array_bytes = recs * frames * width * 4
    input_bytes = recs * frames * model * 2
    matmul = 2 * recs * frames * model * width

    vl, sg, conv, stats = call(
        gate_kernel,
        "gate_conv",
        (recs,),
        [
            smem(),
            per_record((frames, model)),
            per_record((2 * EDGE, model)),
            whole((model, width)),
            whole((model, width)),
            whole((kernel, width)),
        ],
        [
            per_record((frames, width)),
            per_record((frames, width)),
            per_record((span, width)),
            whole((seqs, 2, width)),
        ],
        [
            sds((recs, frames, width), F32),
            sds((recs, frames, width), F32),
            sds((recs, span, width), F32),
            sds((seqs, 2, width), F32),
        ],
        [pltpu.VMEM((halves, frames + 4 * EDGE, LANES), F32), pltpu.VMEM((2, width), F32)],
        2 * matmul,
        input_bytes + 3 * array_bytes,
    )(meta, normed, halo_x, value_weight, gate_weight, depth_taps)
    both = jnp.concatenate([after(value_weight, stats), gate_weight], axis=1).reshape(seqs, tps, piece, 2 * width)

    def chosen(core):
        picks = [
            lax.dynamic_index_in_dim(both, ((chip_at + d) % chips) * 2 + core, 1, keepdims=False)
            for d in range(chips)
        ]
        return jnp.stack(picks).reshape(chips * rows, 2 * width)

    swap = [(i, i ^ 1) for i in range(tps)]
    w_own = chosen(core_at)
    w_sibling = lax.ppermute(chosen(1 - core_at), "tp", swap)

    stats = exchange(stats, "seq")

    chunk = block_rows(frames, 256)
    half_rows = block_rows(frames, 512)
    swished, gn, picked, sums = call(
        norm_kernel,
        "swish_norm",
        (recs,),
        [
            smem(),
            smem(),
            whole((seqs, 2, width)),
            whole((2, width)),
            whole((rows, model)),
            per_record((frames, model)),
            per_record((2 * EDGE, model)),
            whole((model, width)),
            per_record((span, width)),
        ],
        [
            per_record((frames, width)),
            per_record((span, width)),
            per_record((rows, frames)),
            whole((seqs, 2, width)),
        ],
        [
            sds((recs, frames, width), BF16),
            sds((recs, span, width), F32),
            sds((recs, rows, frames), BF16),
            sds((seqs, 2, width), F32),
        ],
        [
            pltpu.VMEM((2, width), F32),
            pltpu.VMEM((block_rows(frames, 512), width), F32),
            pltpu.VMEM((block_rows(frames, 512), width), F32),
        ],
        2 * matmul,
        input_bytes + 3 * array_bytes,
    )(
        meta,
        counts,
        stats,
        jnp.stack([norm_gain, norm_shift]),
        after(select, w_own, w_sibling),
        grad_out,
        halo_g,
        out_weight,
        conv,
    )
    w_out = call(
        first_outer_kernel,
        "outer_w_out",
        (recs,),
        [per_record((frames, model)), per_record((frames, width))],
        whole((width, model)),
        sds((width, model), F32),
        [],
        matmul,
        input_bytes,
    )(grad_out, swished)
    sums = exchange(sums, "seq")
    grad_shift, grad_gain = jnp.sum(sums, axis=0)

    blocks = frames // chunk
    parts_in = frames // half_rows

    def back(first, size, *earlier):
        def window(i):
            return (first + i // blocks, pl.multiple_of(i % blocks * chunk, chunk), 0)

        def block(i):
            return (first + i // blocks, i % blocks, 0)

        return call(
            functools.partial(back_kernel, first, blocks),
            "back_conv",
            (size * blocks,),
            [
                smem(),
                smem(),
                whole((seqs, 2, width)),
                whole((seqs, 2, width)),
                whole((1, width)),
                pl.BlockSpec((pl.Element(1), pl.Element(chunk + 2 * EDGE), pl.Element(width)), window),
                pl.BlockSpec((pl.Element(1), pl.Element(chunk + 2 * EDGE), pl.Element(width)), window),
                pl.BlockSpec((1, chunk, width), block),
                pl.BlockSpec((1, chunk, width), block),
                whole((kernel, width)),
            ],
            [pl.BlockSpec((chunk, 2 * width), lambda i: (i, 0)), whole((16, width))],
            [sds((size * frames, 2 * width), BF16), sds((16, width), F32)],
            [
                pltpu.VMEM((halves, chunk + 2 * EDGE, LANES), F32),
                pltpu.VMEM((halves, kernel, 8, LANES), F32),
            ],
            0,
            1024,
        )(meta, counts, stats, sums, norm_gain[None], gn, conv, vl, sg, after(depth_taps, *earlier))

    def partials(first, size, mine, *earlier):
        sibling = lax.ppermute(mine, "tp", swap)
        out = sds((seqs, size, piece, frames), BF16)
        return call(
            partial_kernel,
            "partial_in",
            (size * parts_in,),
            [
                pl.BlockSpec((half_rows, 2 * width), lambda i: (i, 0)),
                pl.BlockSpec((half_rows, 2 * width), lambda i: (i, 0)),
                whole((chips * rows, 2 * width)),
                whole((chips * rows, 2 * width)),
                pl.BlockSpec(
                    (1, rows, half_rows), lambda i: (first + i // parts_in, 0, i % parts_in)
                ),
            ],
            [
                pl.BlockSpec(
                    (seqs, 1, piece, half_rows), lambda i: (0, i // parts_in, 0, i % parts_in)
                )
            ]
            * chips,
            [out] * chips,
            [],
            0,
            1024,
        )(mine, sibling, after(w_own, *earlier), w_sibling, picked)

    def deliver(part, weight, *earlier):
        arrived = []
        for d in range(1, chips):
            send = [(i, ((i // 2 + d) % chips) * 2 + i % 2) for i in range(tps)]
            arrived.append(lax.ppermute(part[d], "tp", send))
        size = part[0].shape[1]
        block = pl.BlockSpec(
            (seqs, 1, piece, half_rows), lambda i: (0, i // parts_in, 0, i % parts_in)
        )
        own = call(
            add_kernel,
            "add",
            (size * parts_in,),
            [block] * chips,
            block,
            sds(part[0].shape, BF16),
            [],
            weight,
            1024,
        )(after(part[0], *earlier), *arrived)
        return own

    groups = ((0, 1), (1, 1), (2, recs - 2))
    grads = [None] * 3
    taps = [None] * 3
    parts = [None] * 3
    owns = [None] * 3
    moved = [None] * 3
    grads[0], taps[0] = back(*groups[0], w_out)
    grads[1], taps[1] = back(*groups[1], grads[0])
    parts[0] = partials(*groups[0], grads[0], grads[1])
    grads[2], taps[2] = back(*groups[2], *parts[0])
    parts[1] = partials(*groups[1], grads[1], grads[2])
    owns[0] = deliver(parts[0], LONG, *parts[1])
    moved[0] = exchange(owns[0], "seq")
    parts[2] = partials(*groups[2], grads[2], owns[0])

    slots = 3 * width + 16 * (width // shard)
    half = sds((seqs // 2, slots, shard), BF16)
    keep, send = call(
        functools.partial(outer_kernel, groups),
        "outer_w_in",
        (recs,),
        [smem(), per_record((frames, model)), whole((width, model))]
        + [
            pl.BlockSpec(
                (frames, 2 * width),
                lambda r, first=first, size=size: (jnp.clip(r - first, 0, size - 1), 0),
            )
            for first, size in groups
        ]
        + [whole((16, width))] * len(groups),
        [whole(half.shape)] * 2,
        [half] * 2,
        [pltpu.VMEM((2 * width, model), F32)],
        LONG,
        1024,
    )(parity, after(normed, *parts[2]), w_out, *grads, *taps)
    owns[1] = deliver(parts[1], LONG, keep)
    moved[1] = exchange(after(owns[1], moved[0]), "seq")
    owns[2] = deliver(parts[2], 0, owns[1])
    moved[2] = exchange(after(owns[2], moved[1]), "seq")
    bit = 1
    while True:
        others = lax.ppermute(send, "seq", [(i, i ^ bit) for i in range(seqs)])
        bit *= 2
        if bit == seqs:
            break
        if bit == 2:
            keep = after(keep, owns[2])
        shape = (keep.shape[0] // 2,) + keep.shape[1:]
        side = ((seq_at // bit) % 2).astype(jnp.int32).reshape(1, 1)
        keep, send = call(
            fold_kernel,
            "fold",
            (1,),
            [smem()] + [whole(keep.shape)] * 2,
            [whole(shape)] * 2,
            [sds(shape, BF16)] * 2,
            [],
            0,
            1024,
            vmem=20,
        )(side, keep, others)
    w_value, w_gate, w_out, grad_taps = call(
        functools.partial(finish_kernel, kernel),
        "finish",
        (1,),
        [whole(keep.shape)] * 2,
        [whole((shard, width))] * 3 + [whole((kernel, width))],
        [sds((shard, width), F32)] * 3 + [sds((kernel, width), F32)],
        [],
        0,
        1024,
        vmem=20,
    )(keep, others)
    grad_in = ()
    for (first, size), part in zip(groups, moved):
        grad_in = (
            call(
                place_kernel,
                "place",
                (size,),
                [pl.BlockSpec((seqs, 1, piece, frames), lambda i: (0, i, 0, 0))]
                + [anywhere()] * len(grad_in),
                pl.BlockSpec((1, piece, seqs * frames), lambda i, first=first: (first + i, 0, 0)),
                sds((recs, piece, seqs * frames), BF16),
                [],
                0,
                4 * size * piece * seqs * frames,
                {1: 0} if grad_in else None,
                vmem=20,
            )(part, *grad_in),
        )
    (grad_in,) = grad_in
    return (grad_in, w_value, w_gate, w_out, grad_taps, grad_gain, grad_shift)


def solution(mesh):
    placed = (
        P(None, "seq", None),
        P(None, "seq", None),
        P(None, "tp"),
        P(None, "tp"),
        P(None, "tp"),
        P("tp"),
        P("tp"),
        P(None, "tp"),
        P(),
    )
    return jax.shard_map(
        per_device,
        mesh=mesh,
        in_specs=placed,
        out_specs=(
            P(None, ("seq", "tp"), None),
            P("seq", "tp"),
            P("seq", "tp"),
            P("seq", "tp"),
            P(None, "tp"),
            P("tp"),
            P("tp"),
        ),
        check_vma=False,
    )
```

```python
import functools

import jax
import jax.numpy as jnp
from jax import lax
from jax.experimental import pallas as pl
from jax.experimental.pallas import tpu as pltpu
from jax.sharding import PartitionSpec as P

EPSILON = 1e-05
EDGE = 8
LANES = 128
LONG = 50_000_000_000
F32 = jnp.float32
BF16 = jnp.bfloat16


def sigmoid(x):
    return 0.5 * jnp.tanh(0.5 * x) + 0.5


def dot(a, b):
    return jnp.dot(a, b, preferred_element_type=F32)


def dot_nt(a, b):
    return lax.dot_general(a, b, (((1,), (1,)), ((), ())), preferred_element_type=F32)


def dot_tn(a, b):
    return lax.dot_general(a, b, (((0,), (0,)), ((), ())), preferred_element_type=F32)


def rows_of(count, first):
    return first + lax.broadcasted_iota(jnp.int32, (count, 1), 0)


def fold_rows(x):
    return jnp.sum(x.reshape(x.shape[0] // 8, 8, x.shape[1]), axis=0)


def block_rows(total, most):
    return max(b for b in range(8, most + 1, 8) if total % b == 0)


def whole(shape):
    return pl.BlockSpec(shape, lambda *i: (0,) * len(shape))


def per_record(shape):
    return pl.BlockSpec((1,) + shape, lambda r: (r,) + (0,) * len(shape))


def smem():
    return pl.BlockSpec(memory_space=pltpu.SMEM)


def anywhere():
    return pl.BlockSpec(memory_space=pl.ANY)


def after(x, *earlier):
    return lax.optimization_barrier((x,) + earlier)[0]


def spread_sums(out, sums):
    for s in range(out.shape[0]):
        out[s] = sums


def call(
    kernel, name, grid, in_specs, out_specs, out_shape, scratch, flops, moved, aliases=None, vmem=63
):
    return pl.pallas_call(
        kernel,
        name=name,
        grid=grid,
        in_specs=in_specs,
        out_specs=out_specs,
        out_shape=out_shape,
        scratch_shapes=scratch,
        input_output_aliases=aliases or {},
        cost_estimate=pl.CostEstimate(flops=int(flops), bytes_accessed=int(moved), transcendentals=0),
        compiler_params=pltpu.CompilerParams(vmem_limit_bytes=vmem * 1024 * 1024),
    )


def gate_kernel(meta, x, halo, wv, wg, taps, vl_o, sg_o, conv_o, st_o, gp, st):
    r = pl.program_id(0)
    hi = meta[0, r]
    lo = meta[1, r]
    frames = x.shape[1]
    width = wv.shape[1]
    halves = width // LANES

    def put(row, value):
        for h in range(halves):
            gp[h, pl.ds(row, value.shape[0]), :] = value[:, h * LANES : (h + 1) * LANES]

    edge_v = dot(halo[0], wv[...])
    edge_g = dot(halo[0], wg[...])
    row = rows_of(2 * EDGE, 0)
    pos = jnp.where(row < EDGE, row - EDGE, row - EDGE + frames)
    edge = jnp.where((pos >= lo) & (pos < hi), edge_v * sigmoid(edge_g), 0.0)
    zero = jnp.zeros((EDGE, width), F32)
    put(0, zero)
    put(EDGE, edge[:EDGE])
    put(2 * EDGE + frames, edge[EDGE:])
    put(3 * EDGE + frames, zero)
    step = block_rows(frames, 512)
    small = block_rows(step, 64)
    for base in range(0, frames, step):
        xb = x[0, base : base + step, :]
        vl_o[0, base : base + step, :] = dot(xb, wv[...])
        sg_o[0, base : base + step, :] = dot(xb, wg[...])

    def gating(i, carry):
        base = pl.multiple_of(i * small, small)
        v = vl_o[0, pl.ds(base, small), :]
        s = sigmoid(sg_o[0, pl.ds(base, small), :])
        sg_o[0, pl.ds(base, small), :] = s
        put(2 * EDGE + base, jnp.where(rows_of(small, base) < hi, v * s, 0.0))
        return carry

    lax.fori_loop(0, frames // small, gating, 0)
    span = frames + 2 * EDGE
    cb = block_rows(span, 104)
    kernel = taps.shape[0]
    margin = (kernel - 1) // 2
    for h in range(halves):
        cols = slice(h * LANES, (h + 1) * LANES)

        def convolve(i, carry):
            s1, s2 = carry
            base = pl.multiple_of(i * cb, 8)
            acc = jnp.zeros((cb, LANES), F32)
            for k in range(kernel):
                acc = acc + taps[k : k + 1, cols] * gp[h, pl.ds(base + EDGE - margin + k, cb), :]
            conv_o[0, pl.ds(base, cb), cols] = acc
            pos = rows_of(cb, base - EDGE)
            kept = jnp.where((pos >= 0) & (pos < jnp.minimum(hi, frames)), acc, 0.0)
            return s1 + fold_rows(kept), s2 + fold_rows(kept * kept)

        none = jnp.zeros((8, LANES), F32)
        s1, s2 = lax.fori_loop(0, span // cb, convolve, (none, none))
        add = jnp.concatenate(
            [jnp.sum(s1, axis=0, keepdims=True), jnp.sum(s2, axis=0, keepdims=True)], axis=0
        )
        st[:, cols] = jnp.where(r == 0, 0.0, st[:, cols]) + add

    @pl.when(r == pl.num_programs(0) - 1)
    def _():
        spread_sums(st_o, st[...])


def batch_norm(stats, count):
    sums = jnp.sum(stats[...], axis=0)
    centre = sums[0:1] / count
    spread = sums[1:2] / count - centre * centre
    return centre, lax.rsqrt(spread + EPSILON)


def norm_kernel(
    meta, count, stats, affine, select, grads, halo, wo, conv,
    swished_o, gn_o, picked_o, st_o, st, ping, pong
):
    r = pl.program_id(0)
    hi = meta[0, r]
    lo = meta[1, r]
    frames = grads.shape[1]
    centre, inv = batch_norm(stats, count[0, 0])
    gain, shift = affine[0:1, :], affine[1:2, :]

    def part(row, swish_grad):
        size = swish_grad.shape[0]
        unit = (conv[0, pl.ds(row, size), :] - centre) * inv
        normalized = unit * gain + shift
        s = sigmoid(normalized)
        pos = rows_of(size, row - EDGE)
        keep = (pos >= lo) & (pos < hi)
        swished = jnp.where(keep, normalized * s, 0.0)
        gn = jnp.where(keep, swish_grad, 0.0) * (s + normalized * (s - s * s))
        gn_o[0, pl.ds(row, size), :] = gn
        return unit, swished, gn

    edge = dot(halo[0], wo[...])
    part(0, edge[:EDGE])
    part(frames + EDGE, edge[EDGE:])
    step = block_rows(frames, 512)
    small = block_rows(step, 32)
    s1 = jnp.zeros((8, conv.shape[2]), F32)
    s2 = s1
    held = (ping, pong)
    ping[...] = dot(grads[0, :step, :], wo[...])
    for i in range(frames // step):
        now = held[i % 2]
        if (i + 1) * step < frames:
            held[(i + 1) % 2][...] = dot(grads[0, (i + 1) * step : (i + 2) * step, :], wo[...])
        picked_o[0, :, i * step : (i + 1) * step] = dot_nt(
            select[...], grads[0, i * step : (i + 1) * step, :]
        ).astype(BF16)
        for j in range(step // small):
            base = i * step + j * small
            unit, swished, gn = part(base + EDGE, now[j * small : (j + 1) * small, :])
            swished_o[0, base : base + small, :] = swished.astype(BF16)
            s1 = s1 + fold_rows(gn)
            s2 = s2 + fold_rows(gn * unit)
    add = jnp.concatenate(
        [jnp.sum(s1, axis=0, keepdims=True), jnp.sum(s2, axis=0, keepdims=True)], axis=0
    )
    st[...] = jnp.where(r == 0, 0.0, st[...]) + add

    @pl.when(r == pl.num_programs(0) - 1)
    def _():
        spread_sums(st_o, st[...])


def back_kernel(
    record, blocks, meta, count, stats, sums, gain, gn, conv, vl, sg, taps, out, taps_o, gc, acc
):
    i = pl.program_id(0)
    frames, width = vl.shape[1:]
    hi = meta[0, record + i // blocks]
    lo = meta[1, record + i // blocks]
    halves = width // LANES
    span = frames + 2 * EDGE
    kernel = taps.shape[0]
    margin = (kernel - 1) // 2
    cb = block_rows(span, 144)
    step = block_rows(frames, 64)
    total_frames = count[0, 0]
    centre, inv = batch_norm(stats, total_frames)
    grad_sums = jnp.sum(sums[...], axis=0)
    scale = gain[...] * inv
    offset = scale * grad_sums[0:1] / total_frames
    slope = scale * inv * grad_sums[1:2] / total_frames
    first = i % blocks * frames

    @pl.when(i == 0)
    def _():
        acc[...] = jnp.zeros_like(acc)

    for h in range(halves):
        cols = slice(h * LANES, (h + 1) * LANES)
        for base in range(0, span, cb):
            pos = rows_of(cb, first + (base - EDGE))
            mean = offset[:, cols] + (conv[0, base : base + cb, cols] - centre[:, cols]) * slope[:, cols]
            gc[h, base : base + cb, :] = scale[:, cols] * gn[0, base : base + cb, cols] - jnp.where(
                (pos >= lo) & (pos < hi), mean, 0.0
            )
        sums_k = [acc[h, k] for k in range(kernel)]
        for base in range(0, frames, step):
            v = vl[0, base : base + step, cols]
            s = sg[0, base : base + step, cols]
            keep = rows_of(step, first + base) < hi
            vs = v * s
            gated = jnp.where(keep, vs, 0.0)
            total = jnp.zeros((step, LANES), F32)
            for k in range(kernel):
                window = gc[h, base + EDGE + margin - k : base + EDGE + margin - k + step, :]
                total = total + taps[k : k + 1, cols] * window
                sums_k[k] = sums_k[k] + fold_rows(window * gated)
            total = jnp.where(keep, total, 0.0)
            out[base : base + step, cols] = (total * s).astype(BF16)
            out[base : base + step, width + h * LANES : width + (h + 1) * LANES] = (
                total * (vs - vs * s)
            ).astype(BF16)
        for k in range(kernel):
            acc[h, k] = sums_k[k]

    @pl.when(i == pl.num_programs(0) - 1)
    def _():
        taps_o[...] = jnp.zeros_like(taps_o)
        for h in range(halves):
            for k in range(kernel):
                taps_o[k : k + 1, h * LANES : (h + 1) * LANES] = jnp.sum(
                    acc[h, k], axis=0, keepdims=True
                )


def partial_kernel(own, sibling, w_own, w_sibling, picked, mine, *others):
    total = dot_nt(w_own[...], own[...]) + dot_nt(w_sibling[...], sibling[...])
    rows = picked.shape[1]
    seqs, _, piece, frames = mine.shape
    mine[...] = (
        (total[:rows] + picked[0].astype(F32)).astype(BF16).reshape(seqs, 1, piece, frames)
    )
    for d, other in enumerate(others):
        other[...] = (
            total[(d + 1) * rows : (d + 2) * rows].astype(BF16).reshape(seqs, 1, piece, frames)
        )


def add_kernel(*refs):
    total = refs[0][...].astype(F32)
    for other in refs[1:-1]:
        total = total + other[...].astype(F32)
    refs[-1][...] = total.astype(BF16)


def first_outer_kernel(grads, swished, out):
    r = pl.program_id(0)
    add = dot_tn(swished[0], grads[0])

    @pl.when(r == 0)
    def _():
        out[...] = add

    @pl.when(r > 0)
    def _():
        out[...] += add


def outer_kernel(groups, parity, x, w_out, *refs):
    lefts, taps = refs[: len(groups)], refs[len(groups) : 2 * len(groups)]
    keep, send, acc = refs[2 * len(groups) :]
    records = groups[-1][0] + groups[-1][1]
    width = w_out.shape[0]
    shard = keep.shape[2]
    r = pl.program_id(0)
    for (first, size), left in zip(groups, lefts):

        @pl.when((r >= first) & (r < first + size))
        def _(left=left):
            add = dot_tn(left[...], x[0])
            acc[...] = add + jnp.where(r == 0, 0.0, acc[...])

    @pl.when(r == records - 1)
    def _():
        tap_sums = taps[0][...]
        for part in taps[1:]:
            tap_sums = tap_sums + part[...]

        def write(place, odd):
            for j in range(place.shape[0]):
                at = (2 * j + odd) * shard
                place[j, : 2 * width, :] = acc[:, at : at + shard].astype(BF16)
                place[j, 2 * width : 3 * width, :] = w_out[:, at : at + shard].astype(BF16)
                for q in range(width // shard):
                    row = 3 * width + 16 * q
                    place[j, row : row + 16, :] = tap_sums[:, q * shard : (q + 1) * shard].astype(
                        BF16
                    )

        @pl.when(parity[0, 0] == 0)
        def _():
            write(keep, 0)
            write(send, 1)

        @pl.when(parity[0, 0] != 0)
        def _():
            write(keep, 1)
            write(send, 0)


def fold_kernel(parity, own, other, keep, send):
    def write(place, odd):
        for j in range(place.shape[0]):
            total = own[2 * j + odd].astype(F32) + other[2 * j + odd].astype(F32)
            place[j] = total.astype(BF16)

    @pl.when(parity[0, 0] == 0)
    def _():
        write(keep, 0)
        write(send, 1)

    @pl.when(parity[0, 0] != 0)
    def _():
        write(keep, 1)
        write(send, 0)


def finish_kernel(kernel, own, other, value, gate, out, taps):
    width = value.shape[1]
    shard = value.shape[0]

    def total(row, size):
        return own[0, row : row + size, :].astype(F32) + other[0, row : row + size, :].astype(F32)

    for i, place in enumerate((value, gate, out)):
        place[...] = total(i * width, width).T
    for q in range(width // shard):
        taps[:, q * shard : (q + 1) * shard] = total(3 * width + 16 * q, 16)[:kernel]


def place_kernel(moved, *refs):
    out = refs[-1]
    frames = moved.shape[3]
    for s in range(moved.shape[0]):
        out[0, :, s * frames : (s + 1) * frames] = moved[s, 0]


def exchange(copies, axis):
    return lax.all_to_all(copies, axis, 0, 0, tiled=True)


def per_device(
    normed,
    grad_out,
    value_weight,
    gate_weight,
    depth_taps,
    norm_gain,
    norm_shift,
    out_weight,
    lengths,
):
    recs, frames, model = normed.shape
    kernel = depth_taps.shape[0]
    width = value_weight.shape[1]
    seqs = lax.axis_size("seq")
    tps = lax.axis_size("tp")
    chips = tps // 2
    piece = model // (seqs * tps)
    rows = seqs * piece
    shard = model // seqs
    span = frames + 2 * EDGE
    seq_at = lax.axis_index("seq")
    tp_at = lax.axis_index("tp")
    chip_at, core_at = tp_at // 2, tp_at % 2
    count = jnp.sum(lengths).astype(F32)
    first = (seq_at * frames).astype(jnp.int32)
    meta = jnp.stack([lengths - first, jnp.full((recs,), 0, jnp.int32) - first])
    halves = width // LANES
    counts = count.reshape(1, 1)
    parity = (seq_at % 2).astype(jnp.int32).reshape(1, 1)
    sds = jax.ShapeDtypeStruct

    low_edge = jnp.concatenate([normed[:, -EDGE:], grad_out[:, -EDGE:]], axis=2)
    high_edge = jnp.concatenate([normed[:, :EDGE], grad_out[:, :EDGE]], axis=2)
    up = [(i, i + 1) for i in range(seqs - 1)]
    down = [(j, i) for i, j in up]
    halo = jnp.concatenate(
        [lax.ppermute(low_edge, "seq", up), lax.ppermute(high_edge, "seq", down)], axis=1
    )
    halo_x, halo_g = halo[:, :, :model], halo[:, :, model:]

    channel = (
        jnp.arange(seqs, dtype=jnp.int32)[:, None] * (tps * piece)
        + tp_at * piece
        + jnp.arange(piece, dtype=jnp.int32)[None, :]
    ).reshape(rows, 1)
    select = (channel == jnp.arange(model, dtype=jnp.int32)[None, :]).astype(BF16)
    array_bytes = recs * frames * width * 4
    input_bytes = recs * frames * model * 2
    matmul = 2 * recs * frames * model * width

    vl, sg, conv, stats = call(
        gate_kernel,
        "gate_conv",
        (recs,),
        [
            smem(),
            per_record((frames, model)),
            per_record((2 * EDGE, model)),
            whole((model, width)),
            whole((model, width)),
            whole((kernel, width)),
        ],
        [
            per_record((frames, width)),
            per_record((frames, width)),
            per_record((span, width)),
            whole((seqs, 2, width)),
        ],
        [
            sds((recs, frames, width), F32),
            sds((recs, frames, width), F32),
            sds((recs, span, width), F32),
            sds((seqs, 2, width), F32),
        ],
        [pltpu.VMEM((halves, frames + 4 * EDGE, LANES), F32), pltpu.VMEM((2, width), F32)],
        2 * matmul,
        input_bytes + 3 * array_bytes,
    )(meta, normed, halo_x, value_weight, gate_weight, depth_taps)
    both = jnp.concatenate([after(value_weight, stats), gate_weight], axis=1).reshape(seqs, tps, piece, 2 * width)

    def chosen(core):
        picks = [
            lax.dynamic_index_in_dim(both, ((chip_at + d) % chips) * 2 + core, 1, keepdims=False)
            for d in range(chips)
        ]
        return jnp.stack(picks).reshape(chips * rows, 2 * width)

    swap = [(i, i ^ 1) for i in range(tps)]
    w_own = chosen(core_at)
    w_sibling = lax.ppermute(chosen(1 - core_at), "tp", swap)

    stats = exchange(stats, "seq")

    chunk = block_rows(frames, 256)
    half_rows = block_rows(frames, 512)
    swished, gn, picked, sums = call(
        norm_kernel,
        "swish_norm",
        (recs,),
        [
            smem(),
            smem(),
            whole((seqs, 2, width)),
            whole((2, width)),
            whole((rows, model)),
            per_record((frames, model)),
            per_record((2 * EDGE, model)),
            whole((model, width)),
            per_record((span, width)),
        ],
        [
            per_record((frames, width)),
            per_record((span, width)),
            per_record((rows, frames)),
            whole((seqs, 2, width)),
        ],
        [
            sds((recs, frames, width), BF16),
            sds((recs, span, width), F32),
            sds((recs, rows, frames), BF16),
            sds((seqs, 2, width), F32),
        ],
        [
            pltpu.VMEM((2, width), F32),
            pltpu.VMEM((block_rows(frames, 512), width), F32),
            pltpu.VMEM((block_rows(frames, 512), width), F32),
        ],
        2 * matmul,
        input_bytes + 3 * array_bytes,
    )(
        meta,
        counts,
        stats,
        jnp.stack([norm_gain, norm_shift]),
        after(select, w_own, w_sibling),
        grad_out,
        halo_g,
        out_weight,
        conv,
    )
    w_out = call(
        first_outer_kernel,
        "outer_w_out",
        (recs,),
        [per_record((frames, model)), per_record((frames, width))],
        whole((width, model)),
        sds((width, model), F32),
        [],
        matmul,
        input_bytes,
    )(grad_out, swished)
    sums = exchange(sums, "seq")
    grad_shift, grad_gain = jnp.sum(sums, axis=0)

    blocks = frames // chunk
    parts_in = frames // half_rows

    def back(first, size, *earlier):
        def window(i):
            return (first + i // blocks, pl.multiple_of(i % blocks * chunk, chunk), 0)

        def block(i):
            return (first + i // blocks, i % blocks, 0)

        return call(
            functools.partial(back_kernel, first, blocks),
            "back_conv",
            (size * blocks,),
            [
                smem(),
                smem(),
                whole((seqs, 2, width)),
                whole((seqs, 2, width)),
                whole((1, width)),
                pl.BlockSpec((pl.Element(1), pl.Element(chunk + 2 * EDGE), pl.Element(width)), window),
                pl.BlockSpec((pl.Element(1), pl.Element(chunk + 2 * EDGE), pl.Element(width)), window),
                pl.BlockSpec((1, chunk, width), block),
                pl.BlockSpec((1, chunk, width), block),
                whole((kernel, width)),
            ],
            [pl.BlockSpec((chunk, 2 * width), lambda i: (i, 0)), whole((16, width))],
            [sds((size * frames, 2 * width), BF16), sds((16, width), F32)],
            [
                pltpu.VMEM((halves, chunk + 2 * EDGE, LANES), F32),
                pltpu.VMEM((halves, kernel, 8, LANES), F32),
            ],
            0,
            1024,
        )(meta, counts, stats, sums, norm_gain[None], gn, conv, vl, sg, after(depth_taps, *earlier))

    def partials(first, size, mine, *earlier):
        sibling = lax.ppermute(mine, "tp", swap)
        out = sds((seqs, size, piece, frames), BF16)
        return call(
            partial_kernel,
            "partial_in",
            (size * parts_in,),
            [
                pl.BlockSpec((half_rows, 2 * width), lambda i: (i, 0)),
                pl.BlockSpec((half_rows, 2 * width), lambda i: (i, 0)),
                whole((chips * rows, 2 * width)),
                whole((chips * rows, 2 * width)),
                pl.BlockSpec(
                    (1, rows, half_rows), lambda i: (first + i // parts_in, 0, i % parts_in)
                ),
            ],
            [
                pl.BlockSpec(
                    (seqs, 1, piece, half_rows), lambda i: (0, i // parts_in, 0, i % parts_in)
                )
            ]
            * chips,
            [out] * chips,
            [],
            0,
            1024,
        )(mine, sibling, after(w_own, *earlier), w_sibling, picked)

    def deliver(part, weight, *earlier):
        arrived = []
        for d in range(1, chips):
            send = [(i, ((i // 2 + d) % chips) * 2 + i % 2) for i in range(tps)]
            arrived.append(lax.ppermute(part[d], "tp", send))
        size = part[0].shape[1]
        block = pl.BlockSpec(
            (seqs, 1, piece, half_rows), lambda i: (0, i // parts_in, 0, i % parts_in)
        )
        own = call(
            add_kernel,
            "add",
            (size * parts_in,),
            [block] * chips,
            block,
            sds(part[0].shape, BF16),
            [],
            weight,
            1024,
        )(after(part[0], *earlier), *arrived)
        return own

    groups = ((0, 1), (1, 1), (2, recs - 2))
    grads = [None] * 3
    taps = [None] * 3
    parts = [None] * 3
    owns = [None] * 3
    moved = [None] * 3
    grads[0], taps[0] = back(*groups[0], w_out)
    grads[1], taps[1] = back(*groups[1], grads[0])
    parts[0] = partials(*groups[0], grads[0], grads[1])
    grads[2], taps[2] = back(*groups[2], *parts[0])
    parts[1] = partials(*groups[1], grads[1], grads[2])
    owns[0] = deliver(parts[0], LONG, *parts[1])
    moved[0] = exchange(owns[0], "seq")
    parts[2] = partials(*groups[2], grads[2], owns[0])

    slots = 3 * width + 16 * (width // shard)
    half = sds((seqs // 2, slots, shard), BF16)
    keep, send = call(
        functools.partial(outer_kernel, groups),
        "outer_w_in",
        (recs,),
        [smem(), per_record((frames, model)), whole((width, model))]
        + [
            pl.BlockSpec(
                (frames, 2 * width),
                lambda r, first=first, size=size: (jnp.clip(r - first, 0, size - 1), 0),
            )
            for first, size in groups
        ]
        + [whole((16, width))] * len(groups),
        [whole(half.shape)] * 2,
        [half] * 2,
        [pltpu.VMEM((2 * width, model), F32)],
        LONG,
        1024,
    )(parity, after(normed, *parts[2]), w_out, *grads, *taps)
    owns[1] = deliver(parts[1], LONG, keep)
    moved[1] = exchange(after(owns[1], moved[0]), "seq")
    owns[2] = deliver(parts[2], 0, owns[1])
    bit = 1
    while True:
        others = lax.ppermute(send, "seq", [(i, i ^ bit) for i in range(seqs)])
        if bit == 1:
            moved[2] = exchange(after(owns[2], moved[1], others), "seq")
        bit *= 2
        if bit == seqs:
            break
        if bit == 2:
            keep = after(keep, owns[2])
        shape = (keep.shape[0] // 2,) + keep.shape[1:]
        side = ((seq_at // bit) % 2).astype(jnp.int32).reshape(1, 1)
        keep, send = call(
            fold_kernel,
            "fold",
            (1,),
            [smem()] + [whole(keep.shape)] * 2,
            [whole(shape)] * 2,
            [sds(shape, BF16)] * 2,
            [],
            0,
            1024,
            vmem=20,
        )(side, keep, others)
    w_value, w_gate, w_out, grad_taps = call(
        functools.partial(finish_kernel, kernel),
        "finish",
        (1,),
        [whole(keep.shape)] * 2,
        [whole((shard, width))] * 3 + [whole((kernel, width))],
        [sds((shard, width), F32)] * 3 + [sds((kernel, width), F32)],
        [],
        0,
        1024,
        vmem=20,
    )(keep, others)
    grad_in = ()
    for (first, size), part in zip(groups, moved):
        grad_in = (
            call(
                place_kernel,
                "place",
                (size,),
                [pl.BlockSpec((seqs, 1, piece, frames), lambda i: (0, i, 0, 0))]
                + [anywhere()] * len(grad_in),
                pl.BlockSpec((1, piece, seqs * frames), lambda i, first=first: (first + i, 0, 0)),
                sds((recs, piece, seqs * frames), BF16),
                [],
                0,
                4 * size * piece * seqs * frames,
                {1: 0} if grad_in else None,
                vmem=20,
            )(part, *grad_in),
        )
    (grad_in,) = grad_in
    return (grad_in, w_value, w_gate, w_out, grad_taps, grad_gain, grad_shift)


def solution(mesh):
    placed = (
        P(None, "seq", None),
        P(None, "seq", None),
        P(None, "tp"),
        P(None, "tp"),
        P(None, "tp"),
        P("tp"),
        P("tp"),
        P(None, "tp"),
        P(),
    )
    return jax.shard_map(
        per_device,
        mesh=mesh,
        in_specs=placed,
        out_specs=(
            P(None, ("seq", "tp"), None),
            P("seq", "tp"),
            P("seq", "tp"),
            P("seq", "tp"),
            P(None, "tp"),
            P("tp"),
            P("tp"),
        ),
        check_vma=False,
    )
```

```python
import functools

import jax
import jax.numpy as jnp
from jax import lax
from jax.experimental import pallas as pl
from jax.experimental.pallas import tpu as pltpu
from jax.sharding import PartitionSpec as P

EPSILON = 1e-05
EDGE = 8
LANES = 128
LONG = 50_000_000_000
F32 = jnp.float32
BF16 = jnp.bfloat16


def sigmoid(x):
    return 0.5 * jnp.tanh(0.5 * x) + 0.5


def dot(a, b):
    return jnp.dot(a, b, preferred_element_type=F32)


def dot_nt(a, b):
    return lax.dot_general(a, b, (((1,), (1,)), ((), ())), preferred_element_type=F32)


def dot_tn(a, b):
    return lax.dot_general(a, b, (((0,), (0,)), ((), ())), preferred_element_type=F32)


def rows_of(count, first):
    return first + lax.broadcasted_iota(jnp.int32, (count, 1), 0)


def fold_rows(x):
    return jnp.sum(x.reshape(x.shape[0] // 8, 8, x.shape[1]), axis=0)


def block_rows(total, most):
    return max(b for b in range(8, most + 1, 8) if total % b == 0)


def whole(shape):
    return pl.BlockSpec(shape, lambda *i: (0,) * len(shape))


def per_record(shape):
    return pl.BlockSpec((1,) + shape, lambda r: (r,) + (0,) * len(shape))


def smem():
    return pl.BlockSpec(memory_space=pltpu.SMEM)


def anywhere():
    return pl.BlockSpec(memory_space=pl.ANY)


def after(x, *earlier):
    return lax.optimization_barrier((x,) + earlier)[0]


def spread_sums(out, sums):
    for s in range(out.shape[0]):
        out[s] = sums


def call(
    kernel, name, grid, in_specs, out_specs, out_shape, scratch, flops, moved, aliases=None, vmem=63
):
    return pl.pallas_call(
        kernel,
        name=name,
        grid=grid,
        in_specs=in_specs,
        out_specs=out_specs,
        out_shape=out_shape,
        scratch_shapes=scratch,
        input_output_aliases=aliases or {},
        cost_estimate=pl.CostEstimate(flops=int(flops), bytes_accessed=int(moved), transcendentals=0),
        compiler_params=pltpu.CompilerParams(vmem_limit_bytes=vmem * 1024 * 1024),
    )


def gate_kernel(meta, x, halo, wv, wg, taps, vl_o, sg_o, conv_o, st_o, gp, st):
    r = pl.program_id(0)
    hi = meta[0, r]
    lo = meta[1, r]
    frames = x.shape[1]
    width = wv.shape[1]
    halves = width // LANES

    def put(row, value):
        for h in range(halves):
            gp[h, pl.ds(row, value.shape[0]), :] = value[:, h * LANES : (h + 1) * LANES]

    edge_v = dot(halo[0], wv[...])
    edge_g = dot(halo[0], wg[...])
    row = rows_of(2 * EDGE, 0)
    pos = jnp.where(row < EDGE, row - EDGE, row - EDGE + frames)
    edge = jnp.where((pos >= lo) & (pos < hi), edge_v * sigmoid(edge_g), 0.0)
    zero = jnp.zeros((EDGE, width), F32)
    put(0, zero)
    put(EDGE, edge[:EDGE])
    put(2 * EDGE + frames, edge[EDGE:])
    put(3 * EDGE + frames, zero)
    step = block_rows(frames, 512)
    small = block_rows(step, 64)
    for base in range(0, frames, step):
        xb = x[0, base : base + step, :]
        vl_o[0, base : base + step, :] = dot(xb, wv[...])
        sg_o[0, base : base + step, :] = dot(xb, wg[...])

    def gating(i, carry):
        base = pl.multiple_of(i * small, small)
        v = vl_o[0, pl.ds(base, small), :]
        s = sigmoid(sg_o[0, pl.ds(base, small), :])
        sg_o[0, pl.ds(base, small), :] = s
        put(2 * EDGE + base, jnp.where(rows_of(small, base) < hi, v * s, 0.0))
        return carry

    lax.fori_loop(0, frames // small, gating, 0)
    span = frames + 2 * EDGE
    cb = block_rows(span, 104)
    kernel = taps.shape[0]
    margin = (kernel - 1) // 2
    for h in range(halves):
        cols = slice(h * LANES, (h + 1) * LANES)

        def convolve(i, carry):
            s1, s2 = carry
            base = pl.multiple_of(i * cb, 8)
            acc = jnp.zeros((cb, LANES), F32)
            for k in range(kernel):
                acc = acc + taps[k : k + 1, cols] * gp[h, pl.ds(base + EDGE - margin + k, cb), :]
            conv_o[0, pl.ds(base, cb), cols] = acc
            pos = rows_of(cb, base - EDGE)
            kept = jnp.where((pos >= 0) & (pos < jnp.minimum(hi, frames)), acc, 0.0)
            return s1 + fold_rows(kept), s2 + fold_rows(kept * kept)

        none = jnp.zeros((8, LANES), F32)
        s1, s2 = lax.fori_loop(0, span // cb, convolve, (none, none))
        add = jnp.concatenate(
            [jnp.sum(s1, axis=0, keepdims=True), jnp.sum(s2, axis=0, keepdims=True)], axis=0
        )
        st[:, cols] = jnp.where(r == 0, 0.0, st[:, cols]) + add

    @pl.when(r == pl.num_programs(0) - 1)
    def _():
        spread_sums(st_o, st[...])


def batch_norm(stats, count):
    sums = jnp.sum(stats[...], axis=0)
    centre = sums[0:1] / count
    spread = sums[1:2] / count - centre * centre
    return centre, lax.rsqrt(spread + EPSILON)


def norm_kernel(
    meta, count, stats, affine, select, grads, halo, wo, conv,
    swished_o, gn_o, picked_o, st_o, st, ping, pong
):
    r = pl.program_id(0)
    hi = meta[0, r]
    lo = meta[1, r]
    frames = grads.shape[1]
    centre, inv = batch_norm(stats, count[0, 0])
    gain, shift = affine[0:1, :], affine[1:2, :]

    def part(row, swish_grad):
        size = swish_grad.shape[0]
        unit = (conv[0, pl.ds(row, size), :] - centre) * inv
        normalized = unit * gain + shift
        s = sigmoid(normalized)
        pos = rows_of(size, row - EDGE)
        keep = (pos >= lo) & (pos < hi)
        swished = jnp.where(keep, normalized * s, 0.0)
        gn = jnp.where(keep, swish_grad, 0.0) * (s + normalized * (s - s * s))
        gn_o[0, pl.ds(row, size), :] = gn
        return unit, swished, gn

    edge = dot(halo[0], wo[...])
    part(0, edge[:EDGE])
    part(frames + EDGE, edge[EDGE:])
    step = block_rows(frames, 512)
    small = block_rows(step, 32)
    s1 = jnp.zeros((8, conv.shape[2]), F32)
    s2 = s1
    held = (ping, pong)
    ping[...] = dot(grads[0, :step, :], wo[...])
    for i in range(frames // step):
        now = held[i % 2]
        if (i + 1) * step < frames:
            held[(i + 1) % 2][...] = dot(grads[0, (i + 1) * step : (i + 2) * step, :], wo[...])
        picked_o[0, :, i * step : (i + 1) * step] = dot_nt(
            select[...], grads[0, i * step : (i + 1) * step, :]
        ).astype(BF16)
        for j in range(step // small):
            base = i * step + j * small
            unit, swished, gn = part(base + EDGE, now[j * small : (j + 1) * small, :])
            swished_o[0, base : base + small, :] = swished.astype(BF16)
            s1 = s1 + fold_rows(gn)
            s2 = s2 + fold_rows(gn * unit)
    add = jnp.concatenate(
        [jnp.sum(s1, axis=0, keepdims=True), jnp.sum(s2, axis=0, keepdims=True)], axis=0
    )
    st[...] = jnp.where(r == 0, 0.0, st[...]) + add

    @pl.when(r == pl.num_programs(0) - 1)
    def _():
        spread_sums(st_o, st[...])


def back_kernel(
    record, blocks, meta, count, stats, sums, gain, gn, conv, vl, sg, taps, out, taps_o, gc, acc
):
    i = pl.program_id(0)
    frames, width = vl.shape[1:]
    hi = meta[0, record + i // blocks]
    lo = meta[1, record + i // blocks]
    halves = width // LANES
    span = frames + 2 * EDGE
    kernel = taps.shape[0]
    margin = (kernel - 1) // 2
    cb = block_rows(span, 144)
    step = block_rows(frames, 64)
    total_frames = count[0, 0]
    centre, inv = batch_norm(stats, total_frames)
    grad_sums = jnp.sum(sums[...], axis=0)
    scale = gain[...] * inv
    offset = scale * grad_sums[0:1] / total_frames
    slope = scale * inv * grad_sums[1:2] / total_frames
    first = i % blocks * frames

    @pl.when(i == 0)
    def _():
        acc[...] = jnp.zeros_like(acc)

    for h in range(halves):
        cols = slice(h * LANES, (h + 1) * LANES)
        for base in range(0, span, cb):
            pos = rows_of(cb, first + (base - EDGE))
            mean = offset[:, cols] + (conv[0, base : base + cb, cols] - centre[:, cols]) * slope[:, cols]
            gc[h, base : base + cb, :] = scale[:, cols] * gn[0, base : base + cb, cols] - jnp.where(
                (pos >= lo) & (pos < hi), mean, 0.0
            )
        sums_k = [acc[h, k] for k in range(kernel)]
        for base in range(0, frames, step):
            v = vl[0, base : base + step, cols]
            s = sg[0, base : base + step, cols]
            keep = rows_of(step, first + base) < hi
            vs = v * s
            gated = jnp.where(keep, vs, 0.0)
            total = jnp.zeros((step, LANES), F32)
            for k in range(kernel):
                window = gc[h, base + EDGE + margin - k : base + EDGE + margin - k + step, :]
                total = total + taps[k : k + 1, cols] * window
                sums_k[k] = sums_k[k] + fold_rows(window * gated)
            total = jnp.where(keep, total, 0.0)
            out[base : base + step, cols] = (total * s).astype(BF16)
            out[base : base + step, width + h * LANES : width + (h + 1) * LANES] = (
                total * (vs - vs * s)
            ).astype(BF16)
        for k in range(kernel):
            acc[h, k] = sums_k[k]

    @pl.when(i == pl.num_programs(0) - 1)
    def _():
        taps_o[...] = jnp.zeros_like(taps_o)
        for h in range(halves):
            for k in range(kernel):
                taps_o[k : k + 1, h * LANES : (h + 1) * LANES] = jnp.sum(
                    acc[h, k], axis=0, keepdims=True
                )


def partial_kernel(own, sibling, w_own, w_sibling, picked, mine, *others):
    total = dot_nt(w_own[...], own[...]) + dot_nt(w_sibling[...], sibling[...])
    rows = picked.shape[1]
    seqs, _, piece, frames = mine.shape
    mine[...] = (
        (total[:rows] + picked[0].astype(F32)).astype(BF16).reshape(seqs, 1, piece, frames)
    )
    for d, other in enumerate(others):
        other[...] = (
            total[(d + 1) * rows : (d + 2) * rows].astype(BF16).reshape(seqs, 1, piece, frames)
        )


def add_kernel(*refs):
    total = refs[0][...].astype(F32)
    for other in refs[1:-1]:
        total = total + other[...].astype(F32)
    refs[-1][...] = total.astype(BF16)


def first_outer_kernel(grads, swished, out, acc):
    r = pl.program_id(0)
    add = dot_tn(swished[0], grads[0])
    acc[...] = add + jnp.where(r == 0, 0.0, acc[...])

    @pl.when(r == pl.num_programs(0) - 1)
    def _():
        shard = out.shape[2]
        for s in range(out.shape[0]):
            out[s] = acc[:, s * shard : (s + 1) * shard].astype(BF16)


def outer_kernel(groups, parity, x, *refs):
    lefts, taps = refs[: len(groups)], refs[len(groups) : 2 * len(groups)]
    keep, send, acc = refs[2 * len(groups) :]
    records = groups[-1][0] + groups[-1][1]
    width = acc.shape[0] // 2
    shard = keep.shape[2]
    r = pl.program_id(0)
    for (first, size), left in zip(groups, lefts):

        @pl.when((r >= first) & (r < first + size))
        def _(left=left):
            add = dot_tn(left[...], x[0])
            acc[...] = add + jnp.where(r == 0, 0.0, acc[...])

    @pl.when(r == records - 1)
    def _():
        tap_sums = taps[0][...]
        for part in taps[1:]:
            tap_sums = tap_sums + part[...]

        def write(place, odd):
            for j in range(place.shape[0]):
                at = (2 * j + odd) * shard
                place[j, : 2 * width, :] = acc[:, at : at + shard].astype(BF16)
                for q in range(width // shard):
                    row = 2 * width + 16 * q
                    place[j, row : row + 16, :] = tap_sums[:, q * shard : (q + 1) * shard].astype(
                        BF16
                    )

        @pl.when(parity[0, 0] == 0)
        def _():
            write(keep, 0)
            write(send, 1)

        @pl.when(parity[0, 0] != 0)
        def _():
            write(keep, 1)
            write(send, 0)


def fold_kernel(parity, own, other, keep, send):
    def write(place, odd):
        for j in range(place.shape[0]):
            total = own[2 * j + odd].astype(F32) + other[2 * j + odd].astype(F32)
            place[j] = total.astype(BF16)

    @pl.when(parity[0, 0] == 0)
    def _():
        write(keep, 0)
        write(send, 1)

    @pl.when(parity[0, 0] != 0)
    def _():
        write(keep, 1)
        write(send, 0)


def finish_kernel(kernel, own, other, pieces, value, gate, out, taps):
    width = value.shape[1]
    shard = value.shape[0]

    def total(row, size):
        return own[0, row : row + size, :].astype(F32) + other[0, row : row + size, :].astype(F32)

    value[...] = total(0, width).T
    gate[...] = total(width, width).T
    out[...] = jnp.sum(pieces[...].astype(F32), axis=0).T
    for q in range(width // shard):
        taps[:, q * shard : (q + 1) * shard] = total(2 * width + 16 * q, 16)[:kernel]


def place_kernel(moved, *refs):
    out = refs[-1]
    frames = moved.shape[3]
    for s in range(moved.shape[0]):
        out[0, :, s * frames : (s + 1) * frames] = moved[s, 0]


def exchange(copies, axis):
    return lax.all_to_all(copies, axis, 0, 0, tiled=True)


def per_device(
    normed,
    grad_out,
    value_weight,
    gate_weight,
    depth_taps,
    norm_gain,
    norm_shift,
    out_weight,
    lengths,
):
    recs, frames, model = normed.shape
    kernel = depth_taps.shape[0]
    width = value_weight.shape[1]
    seqs = lax.axis_size("seq")
    tps = lax.axis_size("tp")
    chips = tps // 2
    piece = model // (seqs * tps)
    rows = seqs * piece
    shard = model // seqs
    span = frames + 2 * EDGE
    seq_at = lax.axis_index("seq")
    tp_at = lax.axis_index("tp")
    chip_at, core_at = tp_at // 2, tp_at % 2
    count = jnp.sum(lengths).astype(F32)
    first = (seq_at * frames).astype(jnp.int32)
    meta = jnp.stack([lengths - first, jnp.full((recs,), 0, jnp.int32) - first])
    halves = width // LANES
    counts = count.reshape(1, 1)
    parity = (seq_at % 2).astype(jnp.int32).reshape(1, 1)
    sds = jax.ShapeDtypeStruct

    low_edge = jnp.concatenate([normed[:, -EDGE:], grad_out[:, -EDGE:]], axis=2)
    high_edge = jnp.concatenate([normed[:, :EDGE], grad_out[:, :EDGE]], axis=2)
    up = [(i, i + 1) for i in range(seqs - 1)]
    down = [(j, i) for i, j in up]
    halo = jnp.concatenate(
        [lax.ppermute(low_edge, "seq", up), lax.ppermute(high_edge, "seq", down)], axis=1
    )
    halo_x, halo_g = halo[:, :, :model], halo[:, :, model:]

    channel = (
        jnp.arange(seqs, dtype=jnp.int32)[:, None] * (tps * piece)
        + tp_at * piece
        + jnp.arange(piece, dtype=jnp.int32)[None, :]
    ).reshape(rows, 1)
    select = (channel == jnp.arange(model, dtype=jnp.int32)[None, :]).astype(BF16)
    array_bytes = recs * frames * width * 4
    input_bytes = recs * frames * model * 2
    matmul = 2 * recs * frames * model * width

    vl, sg, conv, stats = call(
        gate_kernel,
        "gate_conv",
        (recs,),
        [
            smem(),
            per_record((frames, model)),
            per_record((2 * EDGE, model)),
            whole((model, width)),
            whole((model, width)),
            whole((kernel, width)),
        ],
        [
            per_record((frames, width)),
            per_record((frames, width)),
            per_record((span, width)),
            whole((seqs, 2, width)),
        ],
        [
            sds((recs, frames, width), F32),
            sds((recs, frames, width), F32),
            sds((recs, span, width), F32),
            sds((seqs, 2, width), F32),
        ],
        [pltpu.VMEM((halves, frames + 4 * EDGE, LANES), F32), pltpu.VMEM((2, width), F32)],
        2 * matmul,
        input_bytes + 3 * array_bytes,
    )(meta, normed, halo_x, value_weight, gate_weight, depth_taps)
    both = jnp.concatenate([after(value_weight, stats), gate_weight], axis=1).reshape(seqs, tps, piece, 2 * width)

    def chosen(core):
        picks = [
            lax.dynamic_index_in_dim(both, ((chip_at + d) % chips) * 2 + core, 1, keepdims=False)
            for d in range(chips)
        ]
        return jnp.stack(picks).reshape(chips * rows, 2 * width)

    swap = [(i, i ^ 1) for i in range(tps)]
    w_own = chosen(core_at)
    w_sibling = lax.ppermute(chosen(1 - core_at), "tp", swap)

    stats = exchange(stats, "seq")

    chunk = block_rows(frames, 256)
    half_rows = block_rows(frames, 512)
    swished, gn, picked, sums = call(
        norm_kernel,
        "swish_norm",
        (recs,),
        [
            smem(),
            smem(),
            whole((seqs, 2, width)),
            whole((2, width)),
            whole((rows, model)),
            per_record((frames, model)),
            per_record((2 * EDGE, model)),
            whole((model, width)),
            per_record((span, width)),
        ],
        [
            per_record((frames, width)),
            per_record((span, width)),
            per_record((rows, frames)),
            whole((seqs, 2, width)),
        ],
        [
            sds((recs, frames, width), BF16),
            sds((recs, span, width), F32),
            sds((recs, rows, frames), BF16),
            sds((seqs, 2, width), F32),
        ],
        [
            pltpu.VMEM((2, width), F32),
            pltpu.VMEM((block_rows(frames, 512), width), F32),
            pltpu.VMEM((block_rows(frames, 512), width), F32),
        ],
        2 * matmul,
        input_bytes + 3 * array_bytes,
    )(
        meta,
        counts,
        stats,
        jnp.stack([norm_gain, norm_shift]),
        after(select, w_own, w_sibling),
        grad_out,
        halo_g,
        out_weight,
        conv,
    )
    w_out = call(
        first_outer_kernel,
        "outer_w_out",
        (recs,),
        [per_record((frames, model)), per_record((frames, width))],
        whole((seqs, width, shard)),
        sds((seqs, width, shard), BF16),
        [pltpu.VMEM((width, model), F32)],
        matmul,
        input_bytes,
    )(grad_out, swished)
    sums = exchange(sums, "seq")
    grad_shift, grad_gain = jnp.sum(sums, axis=0)

    blocks = frames // chunk
    parts_in = frames // half_rows

    def back(first, size, *earlier):
        def window(i):
            return (first + i // blocks, pl.multiple_of(i % blocks * chunk, chunk), 0)

        def block(i):
            return (first + i // blocks, i % blocks, 0)

        return call(
            functools.partial(back_kernel, first, blocks),
            "back_conv",
            (size * blocks,),
            [
                smem(),
                smem(),
                whole((seqs, 2, width)),
                whole((seqs, 2, width)),
                whole((1, width)),
                pl.BlockSpec((pl.Element(1), pl.Element(chunk + 2 * EDGE), pl.Element(width)), window),
                pl.BlockSpec((pl.Element(1), pl.Element(chunk + 2 * EDGE), pl.Element(width)), window),
                pl.BlockSpec((1, chunk, width), block),
                pl.BlockSpec((1, chunk, width), block),
                whole((kernel, width)),
            ],
            [pl.BlockSpec((chunk, 2 * width), lambda i: (i, 0)), whole((16, width))],
            [sds((size * frames, 2 * width), BF16), sds((16, width), F32)],
            [
                pltpu.VMEM((halves, chunk + 2 * EDGE, LANES), F32),
                pltpu.VMEM((halves, kernel, 8, LANES), F32),
            ],
            0,
            1024,
        )(meta, counts, stats, sums, norm_gain[None], gn, conv, vl, sg, after(depth_taps, *earlier))

    def partials(first, size, mine, *earlier):
        sibling = lax.ppermute(mine, "tp", swap)
        out = sds((seqs, size, piece, frames), BF16)
        return call(
            partial_kernel,
            "partial_in",
            (size * parts_in,),
            [
                pl.BlockSpec((half_rows, 2 * width), lambda i: (i, 0)),
                pl.BlockSpec((half_rows, 2 * width), lambda i: (i, 0)),
                whole((chips * rows, 2 * width)),
                whole((chips * rows, 2 * width)),
                pl.BlockSpec(
                    (1, rows, half_rows), lambda i: (first + i // parts_in, 0, i % parts_in)
                ),
            ],
            [
                pl.BlockSpec(
                    (seqs, 1, piece, half_rows), lambda i: (0, i // parts_in, 0, i % parts_in)
                )
            ]
            * chips,
            [out] * chips,
            [],
            0,
            1024,
        )(mine, sibling, after(w_own, *earlier), w_sibling, picked)

    def deliver(part, weight, *earlier):
        arrived = []
        for d in range(1, chips):
            send = [(i, ((i // 2 + d) % chips) * 2 + i % 2) for i in range(tps)]
            arrived.append(lax.ppermute(part[d], "tp", send))
        size = part[0].shape[1]
        block = pl.BlockSpec(
            (seqs, 1, piece, half_rows), lambda i: (0, i // parts_in, 0, i % parts_in)
        )
        own = call(
            add_kernel,
            "add",
            (size * parts_in,),
            [block] * chips,
            block,
            sds(part[0].shape, BF16),
            [],
            weight,
            1024,
        )(after(part[0], *earlier), *arrived)
        return own

    groups = ((0, 1), (1, 1), (2, recs - 2))
    grads = [None] * 3
    taps = [None] * 3
    parts = [None] * 3
    owns = [None] * 3
    moved = [None] * 3
    w_out_pieces = exchange(w_out, "seq")
    grads[0], taps[0] = back(*groups[0], w_out)
    grads[1], taps[1] = back(*groups[1], grads[0])
    parts[0] = partials(*groups[0], grads[0], grads[1])
    grads[2], taps[2] = back(*groups[2], *parts[0])
    parts[1] = partials(*groups[1], grads[1], grads[2])
    owns[0] = deliver(parts[0], LONG, w_out_pieces, *parts[1])
    moved[0] = exchange(owns[0], "seq")
    parts[2] = partials(*groups[2], grads[2], owns[0])

    slots = 2 * width + 16 * (width // shard)
    half = sds((seqs // 2, slots, shard), BF16)
    keep, send = call(
        functools.partial(outer_kernel, groups),
        "outer_w_in",
        (recs,),
        [smem(), per_record((frames, model))]
        + [
            pl.BlockSpec(
                (frames, 2 * width),
                lambda r, first=first, size=size: (jnp.clip(r - first, 0, size - 1), 0),
            )
            for first, size in groups
        ]
        + [whole((16, width))] * len(groups),
        [whole(half.shape)] * 2,
        [half] * 2,
        [pltpu.VMEM((2 * width, model), F32)],
        LONG,
        1024,
    )(parity, after(normed, *parts[2]), *grads, *taps)
    owns[1] = deliver(parts[1], LONG, keep)
    moved[1] = exchange(after(owns[1], moved[0]), "seq")
    owns[2] = deliver(parts[2], 0, owns[1])
    bit = 1
    while True:
        others = lax.ppermute(send, "seq", [(i, i ^ bit) for i in range(seqs)])
        if bit == 1:
            moved[2] = exchange(after(owns[2], moved[1], others), "seq")
        bit *= 2
        if bit == seqs:
            break
        if bit == 2:
            keep = after(keep, owns[2])
        shape = (keep.shape[0] // 2,) + keep.shape[1:]
        side = ((seq_at // bit) % 2).astype(jnp.int32).reshape(1, 1)
        keep, send = call(
            fold_kernel,
            "fold",
            (1,),
            [smem()] + [whole(keep.shape)] * 2,
            [whole(shape)] * 2,
            [sds(shape, BF16)] * 2,
            [],
            0,
            1024,
            vmem=20,
        )(side, keep, others)
    w_value, w_gate, w_out, grad_taps = call(
        functools.partial(finish_kernel, kernel),
        "finish",
        (1,),
        [whole(keep.shape)] * 2 + [whole((seqs, width, shard))],
        [whole((shard, width))] * 3 + [whole((kernel, width))],
        [sds((shard, width), F32)] * 3 + [sds((kernel, width), F32)],
        [],
        0,
        1024,
        vmem=20,
    )(keep, others, w_out_pieces)
    grad_in = ()
    for (first, size), part in zip(groups, moved):
        grad_in = (
            call(
                place_kernel,
                "place",
                (size,),
                [pl.BlockSpec((seqs, 1, piece, frames), lambda i: (0, i, 0, 0))]
                + [anywhere()] * len(grad_in),
                pl.BlockSpec((1, piece, seqs * frames), lambda i, first=first: (first + i, 0, 0)),
                sds((recs, piece, seqs * frames), BF16),
                [],
                0,
                4 * size * piece * seqs * frames,
                {1: 0} if grad_in else None,
                vmem=20,
            )(part, *grad_in),
        )
    (grad_in,) = grad_in
    return (grad_in, w_value, w_gate, w_out, grad_taps, grad_gain, grad_shift)


def solution(mesh):
    placed = (
        P(None, "seq", None),
        P(None, "seq", None),
        P(None, "tp"),
        P(None, "tp"),
        P(None, "tp"),
        P("tp"),
        P("tp"),
        P(None, "tp"),
        P(),
    )
    return jax.shard_map(
        per_device,
        mesh=mesh,
        in_specs=placed,
        out_specs=(
            P(None, ("seq", "tp"), None),
            P("seq", "tp"),
            P("seq", "tp"),
            P("seq", "tp"),
            P(None, "tp"),
            P("tp"),
            P("tp"),
        ),
        check_vma=False,
    )
```

```python
import functools

import jax
import jax.numpy as jnp
from jax import lax
from jax.experimental import pallas as pl
from jax.experimental.pallas import tpu as pltpu
from jax.sharding import PartitionSpec as P

EPSILON = 1e-05
EDGE = 8
LANES = 128
LONG = 50_000_000_000
F32 = jnp.float32
BF16 = jnp.bfloat16


def sigmoid(x):
    return 0.5 * jnp.tanh(0.5 * x) + 0.5


def dot(a, b):
    return jnp.dot(a, b, preferred_element_type=F32)


def dot_nt(a, b):
    return lax.dot_general(a, b, (((1,), (1,)), ((), ())), preferred_element_type=F32)


def dot_tn(a, b):
    return lax.dot_general(a, b, (((0,), (0,)), ((), ())), preferred_element_type=F32)


def rows_of(count, first):
    return first + lax.broadcasted_iota(jnp.int32, (count, 1), 0)


def fold_rows(x):
    return jnp.sum(x.reshape(x.shape[0] // 8, 8, x.shape[1]), axis=0)


def block_rows(total, most):
    return max(b for b in range(8, most + 1, 8) if total % b == 0)


def whole(shape):
    return pl.BlockSpec(shape, lambda *i: (0,) * len(shape))


def per_record(shape):
    return pl.BlockSpec((1,) + shape, lambda r: (r,) + (0,) * len(shape))


def smem():
    return pl.BlockSpec(memory_space=pltpu.SMEM)


def anywhere():
    return pl.BlockSpec(memory_space=pl.ANY)


def after(x, *earlier):
    return lax.optimization_barrier((x,) + earlier)[0]


def spread_sums(out, sums):
    for s in range(out.shape[0]):
        out[s] = sums


def call(
    kernel, name, grid, in_specs, out_specs, out_shape, scratch, flops, moved, aliases=None, vmem=63
):
    return pl.pallas_call(
        kernel,
        name=name,
        grid=grid,
        in_specs=in_specs,
        out_specs=out_specs,
        out_shape=out_shape,
        scratch_shapes=scratch,
        input_output_aliases=aliases or {},
        cost_estimate=pl.CostEstimate(flops=int(flops), bytes_accessed=int(moved), transcendentals=0),
        compiler_params=pltpu.CompilerParams(vmem_limit_bytes=vmem * 1024 * 1024),
    )


def gate_kernel(meta, x, halo, wv, wg, taps, vl_o, sg_o, conv_o, st_o, gp, st):
    r = pl.program_id(0)
    hi = meta[0, r]
    lo = meta[1, r]
    frames = x.shape[1]
    width = wv.shape[1]
    halves = width // LANES

    def put(row, value):
        for h in range(halves):
            gp[h, pl.ds(row, value.shape[0]), :] = value[:, h * LANES : (h + 1) * LANES]

    edge_v = dot(halo[0], wv[...])
    edge_g = dot(halo[0], wg[...])
    row = rows_of(2 * EDGE, 0)
    pos = jnp.where(row < EDGE, row - EDGE, row - EDGE + frames)
    edge = jnp.where((pos >= lo) & (pos < hi), edge_v * sigmoid(edge_g), 0.0)
    zero = jnp.zeros((EDGE, width), F32)
    put(0, zero)
    put(EDGE, edge[:EDGE])
    put(2 * EDGE + frames, edge[EDGE:])
    put(3 * EDGE + frames, zero)
    step = block_rows(frames, 512)
    small = block_rows(step, 64)
    for base in range(0, frames, step):
        xb = x[0, base : base + step, :]
        vl_o[0, base : base + step, :] = dot(xb, wv[...])
        sg_o[0, base : base + step, :] = dot(xb, wg[...])

    def gating(i, carry):
        base = pl.multiple_of(i * small, small)
        v = vl_o[0, pl.ds(base, small), :]
        s = sigmoid(sg_o[0, pl.ds(base, small), :])
        sg_o[0, pl.ds(base, small), :] = s
        put(2 * EDGE + base, jnp.where(rows_of(small, base) < hi, v * s, 0.0))
        return carry

    lax.fori_loop(0, frames // small, gating, 0)
    span = frames + 2 * EDGE
    cb = block_rows(span, 104)
    kernel = taps.shape[0]
    margin = (kernel - 1) // 2
    for h in range(halves):
        cols = slice(h * LANES, (h + 1) * LANES)

        def convolve(i, carry):
            s1, s2 = carry
            base = pl.multiple_of(i * cb, 8)
            acc = jnp.zeros((cb, LANES), F32)
            for k in range(kernel):
                acc = acc + taps[k : k + 1, cols] * gp[h, pl.ds(base + EDGE - margin + k, cb), :]
            conv_o[0, pl.ds(base, cb), cols] = acc
            pos = rows_of(cb, base - EDGE)
            kept = jnp.where((pos >= 0) & (pos < jnp.minimum(hi, frames)), acc, 0.0)
            return s1 + fold_rows(kept), s2 + fold_rows(kept * kept)

        none = jnp.zeros((8, LANES), F32)
        s1, s2 = lax.fori_loop(0, span // cb, convolve, (none, none))
        add = jnp.concatenate(
            [jnp.sum(s1, axis=0, keepdims=True), jnp.sum(s2, axis=0, keepdims=True)], axis=0
        )
        st[:, cols] = jnp.where(r == 0, 0.0, st[:, cols]) + add

    @pl.when(r == pl.num_programs(0) - 1)
    def _():
        spread_sums(st_o, st[...])


def batch_norm(stats, count):
    sums = jnp.sum(stats[...], axis=0)
    centre = sums[0:1] / count
    spread = sums[1:2] / count - centre * centre
    return centre, lax.rsqrt(spread + EPSILON)


def norm_kernel(
    meta, count, stats, affine, select, grads, halo, wo, conv,
    swished_o, gn_o, picked_o, st_o, st, ping, pong
):
    r = pl.program_id(0)
    hi = meta[0, r]
    lo = meta[1, r]
    frames = grads.shape[1]
    centre, inv = batch_norm(stats, count[0, 0])
    gain, shift = affine[0:1, :], affine[1:2, :]

    def part(row, swish_grad):
        size = swish_grad.shape[0]
        unit = (conv[0, pl.ds(row, size), :] - centre) * inv
        normalized = unit * gain + shift
        s = sigmoid(normalized)
        pos = rows_of(size, row - EDGE)
        keep = (pos >= lo) & (pos < hi)
        swished = jnp.where(keep, normalized * s, 0.0)
        gn = jnp.where(keep, swish_grad, 0.0) * (s + normalized * (s - s * s))
        gn_o[0, pl.ds(row, size), :] = gn
        return unit, swished, gn

    edge = dot(halo[0], wo[...])
    part(0, edge[:EDGE])
    part(frames + EDGE, edge[EDGE:])
    step = block_rows(frames, 512)
    small = block_rows(step, 32)
    s1 = jnp.zeros((8, conv.shape[2]), F32)
    s2 = s1
    held = (ping, pong)
    ping[...] = dot(grads[0, :step, :], wo[...])
    for i in range(frames // step):
        now = held[i % 2]
        if (i + 1) * step < frames:
            held[(i + 1) % 2][...] = dot(grads[0, (i + 1) * step : (i + 2) * step, :], wo[...])
        picked_o[0, :, i * step : (i + 1) * step] = dot_nt(
            select[...], grads[0, i * step : (i + 1) * step, :]
        ).astype(BF16)
        for j in range(step // small):
            base = i * step + j * small
            unit, swished, gn = part(base + EDGE, now[j * small : (j + 1) * small, :])
            swished_o[0, base : base + small, :] = swished.astype(BF16)
            s1 = s1 + fold_rows(gn)
            s2 = s2 + fold_rows(gn * unit)
    add = jnp.concatenate(
        [jnp.sum(s1, axis=0, keepdims=True), jnp.sum(s2, axis=0, keepdims=True)], axis=0
    )
    st[...] = jnp.where(r == 0, 0.0, st[...]) + add

    @pl.when(r == pl.num_programs(0) - 1)
    def _():
        spread_sums(st_o, st[...])


def back_kernel(
    record, blocks, meta, count, stats, sums, gain, gn, conv, vl, sg, taps, out, taps_o, gc, acc
):
    i = pl.program_id(0)
    frames, width = vl.shape[1:]
    hi = meta[0, record + i // blocks]
    lo = meta[1, record + i // blocks]
    halves = width // LANES
    span = frames + 2 * EDGE
    kernel = taps.shape[0]
    margin = (kernel - 1) // 2
    cb = block_rows(span, 144)
    step = block_rows(frames, 32)
    total_frames = count[0, 0]
    centre, inv = batch_norm(stats, total_frames)
    grad_sums = jnp.sum(sums[...], axis=0)
    scale = gain[...] * inv
    offset = scale * grad_sums[0:1] / total_frames
    slope = scale * inv * grad_sums[1:2] / total_frames
    first = i % blocks * frames

    @pl.when(i == 0)
    def _():
        acc[...] = jnp.zeros_like(acc)

    for h in range(halves):
        cols = slice(h * LANES, (h + 1) * LANES)
        for base in range(0, span, cb):
            pos = rows_of(cb, first + (base - EDGE))
            mean = offset[:, cols] + (conv[0, base : base + cb, cols] - centre[:, cols]) * slope[:, cols]
            gc[h, base : base + cb, :] = scale[:, cols] * gn[0, base : base + cb, cols] - jnp.where(
                (pos >= lo) & (pos < hi), mean, 0.0
            )
        sums_k = [acc[h, k] for k in range(kernel)]
        for base in range(0, frames, step):
            v = vl[0, base : base + step, cols]
            s = sg[0, base : base + step, cols]
            keep = rows_of(step, first + base) < hi
            vs = v * s
            gated = jnp.where(keep, vs, 0.0)
            total = jnp.zeros((step, LANES), F32)
            for k in range(kernel):
                window = gc[h, base + EDGE + margin - k : base + EDGE + margin - k + step, :]
                total = total + taps[k : k + 1, cols] * window
                sums_k[k] = sums_k[k] + fold_rows(window * gated)
            total = jnp.where(keep, total, 0.0)
            out[base : base + step, cols] = (total * s).astype(BF16)
            out[base : base + step, width + h * LANES : width + (h + 1) * LANES] = (
                total * (vs - vs * s)
            ).astype(BF16)
        for k in range(kernel):
            acc[h, k] = sums_k[k]

    @pl.when(i == pl.num_programs(0) - 1)
    def _():
        taps_o[...] = jnp.zeros_like(taps_o)
        for h in range(halves):
            for k in range(kernel):
                taps_o[k : k + 1, h * LANES : (h + 1) * LANES] = jnp.sum(
                    acc[h, k], axis=0, keepdims=True
                )


def partial_kernel(own, sibling, w_own, w_sibling, picked, mine, *others):
    total = dot_nt(w_own[...], own[...]) + dot_nt(w_sibling[...], sibling[...])
    rows = picked.shape[1]
    seqs, _, piece, frames = mine.shape
    mine[...] = (
        (total[:rows] + picked[0].astype(F32)).astype(BF16).reshape(seqs, 1, piece, frames)
    )
    for d, other in enumerate(others):
        other[...] = (
            total[(d + 1) * rows : (d + 2) * rows].astype(BF16).reshape(seqs, 1, piece, frames)
        )


def join_kernel(half, *refs):
    i = pl.program_id(0)

    @pl.when(i < half)
    def _():
        add_kernel(*refs[:-2], refs[-1])

    @pl.when(i >= half)
    def _():
        refs[-1][...] = refs[-2][...]


def add_kernel(*refs):
    total = refs[0][...].astype(F32)
    for other in refs[1:-1]:
        total = total + other[...].astype(F32)
    refs[-1][...] = total.astype(BF16)


def first_outer_kernel(grads, swished, out, acc):
    r = pl.program_id(0)
    add = dot_tn(swished[0], grads[0])
    acc[...] = add + jnp.where(r == 0, 0.0, acc[...])

    @pl.when(r == pl.num_programs(0) - 1)
    def _():
        seqs, _, piece, frames = out.shape
        shard = acc.shape[1] // seqs
        for s in range(seqs):
            for q in range(frames // shard):
                out[s, 0, :, q * shard : (q + 1) * shard] = acc[
                    q * piece : (q + 1) * piece, s * shard : (s + 1) * shard
                ].astype(BF16)


def outer_kernel(groups, parity, x, *refs):
    lefts, taps = refs[: len(groups)], refs[len(groups) : 2 * len(groups)]
    keep, send, acc = refs[2 * len(groups) :]
    records = groups[-1][0] + groups[-1][1]
    width = acc.shape[0] // 2
    shard = keep.shape[2]
    r = pl.program_id(0)
    for (first, size), left in zip(groups, lefts):

        @pl.when((r >= first) & (r < first + size))
        def _(left=left):
            add = dot_tn(left[...], x[0])
            acc[...] = add + jnp.where(r == 0, 0.0, acc[...])

    @pl.when(r == records - 1)
    def _():
        tap_sums = taps[0][...]
        for part in taps[1:]:
            tap_sums = tap_sums + part[...]

        def write(place, odd):
            for j in range(place.shape[0]):
                at = (2 * j + odd) * shard
                place[j, : 2 * width, :] = acc[:, at : at + shard].astype(BF16)
                for q in range(width // shard):
                    row = 2 * width + 16 * q
                    place[j, row : row + 16, :] = tap_sums[:, q * shard : (q + 1) * shard].astype(
                        BF16
                    )

        @pl.when(parity[0, 0] == 0)
        def _():
            write(keep, 0)
            write(send, 1)

        @pl.when(parity[0, 0] != 0)
        def _():
            write(keep, 1)
            write(send, 0)


def fold_kernel(parity, own, other, keep, send):
    def write(place, odd):
        for j in range(place.shape[0]):
            total = own[2 * j + odd].astype(F32) + other[2 * j + odd].astype(F32)
            place[j] = total.astype(BF16)

    @pl.when(parity[0, 0] == 0)
    def _():
        write(keep, 0)
        write(send, 1)

    @pl.when(parity[0, 0] != 0)
    def _():
        write(keep, 1)
        write(send, 0)


def finish_kernel(kernel, own, other, pieces, value, gate, out, taps):
    width = value.shape[1]
    shard = value.shape[0]

    def total(row, size):
        return own[0, row : row + size, :].astype(F32) + other[0, row : row + size, :].astype(F32)

    value[...] = total(0, width).T
    gate[...] = total(width, width).T
    ready = pieces[0, 0].astype(F32)
    for s in range(1, pieces.shape[0]):
        ready = ready + pieces[s, 0].astype(F32)
    blocks = [ready[:, q * shard : (q + 1) * shard] for q in range(ready.shape[1] // shard)]
    out[...] = jnp.concatenate(blocks, axis=0).T
    for q in range(width // shard):
        taps[:, q * shard : (q + 1) * shard] = total(2 * width + 16 * q, 16)[:kernel]


def place_kernel(moved, *refs):
    out = refs[-1]
    frames = moved.shape[3]
    for s in range(moved.shape[0]):
        out[0, :, s * frames : (s + 1) * frames] = moved[s, 0]


def exchange(copies, axis):
    return lax.all_to_all(copies, axis, 0, 0, tiled=True)


def per_device(
    normed,
    grad_out,
    value_weight,
    gate_weight,
    depth_taps,
    norm_gain,
    norm_shift,
    out_weight,
    lengths,
):
    recs, frames, model = normed.shape
    kernel = depth_taps.shape[0]
    width = value_weight.shape[1]
    seqs = lax.axis_size("seq")
    tps = lax.axis_size("tp")
    chips = tps // 2
    piece = model // (seqs * tps)
    rows = seqs * piece
    shard = model // seqs
    span = frames + 2 * EDGE
    seq_at = lax.axis_index("seq")
    tp_at = lax.axis_index("tp")
    chip_at, core_at = tp_at // 2, tp_at % 2
    count = jnp.sum(lengths).astype(F32)
    first = (seq_at * frames).astype(jnp.int32)
    meta = jnp.stack([lengths - first, jnp.full((recs,), 0, jnp.int32) - first])
    halves = width // LANES
    counts = count.reshape(1, 1)
    parity = (seq_at % 2).astype(jnp.int32).reshape(1, 1)
    sds = jax.ShapeDtypeStruct

    low_edge = jnp.concatenate([normed[:, -EDGE:], grad_out[:, -EDGE:]], axis=2)
    high_edge = jnp.concatenate([normed[:, :EDGE], grad_out[:, :EDGE]], axis=2)
    up = [(i, i + 1) for i in range(seqs - 1)]
    down = [(j, i) for i, j in up]
    halo = jnp.concatenate(
        [lax.ppermute(low_edge, "seq", up), lax.ppermute(high_edge, "seq", down)], axis=1
    )
    halo_x, halo_g = halo[:, :, :model], halo[:, :, model:]

    channel = (
        jnp.arange(seqs, dtype=jnp.int32)[:, None] * (tps * piece)
        + tp_at * piece
        + jnp.arange(piece, dtype=jnp.int32)[None, :]
    ).reshape(rows, 1)
    select = (channel == jnp.arange(model, dtype=jnp.int32)[None, :]).astype(BF16)
    array_bytes = recs * frames * width * 4
    input_bytes = recs * frames * model * 2
    matmul = 2 * recs * frames * model * width

    vl, sg, conv, stats = call(
        gate_kernel,
        "gate_conv",
        (recs,),
        [
            smem(),
            per_record((frames, model)),
            per_record((2 * EDGE, model)),
            whole((model, width)),
            whole((model, width)),
            whole((kernel, width)),
        ],
        [
            per_record((frames, width)),
            per_record((frames, width)),
            per_record((span, width)),
            whole((seqs, 2, width)),
        ],
        [
            sds((recs, frames, width), F32),
            sds((recs, frames, width), F32),
            sds((recs, span, width), F32),
            sds((seqs, 2, width), F32),
        ],
        [pltpu.VMEM((halves, frames + 4 * EDGE, LANES), F32), pltpu.VMEM((2, width), F32)],
        2 * matmul,
        input_bytes + 3 * array_bytes,
    )(meta, normed, halo_x, value_weight, gate_weight, depth_taps)
    both = jnp.concatenate([after(value_weight, stats), gate_weight], axis=1).reshape(seqs, tps, piece, 2 * width)

    def chosen(core):
        picks = [
            lax.dynamic_index_in_dim(both, ((chip_at + d) % chips) * 2 + core, 1, keepdims=False)
            for d in range(chips)
        ]
        return jnp.stack(picks).reshape(chips * rows, 2 * width)

    swap = [(i, i ^ 1) for i in range(tps)]
    w_own = chosen(core_at)
    w_sibling = lax.ppermute(chosen(1 - core_at), "tp", swap)

    stats = exchange(stats, "seq")

    chunk = block_rows(frames, 256)
    half_rows = block_rows(frames, 512)
    swished, gn, picked, sums = call(
        norm_kernel,
        "swish_norm",
        (recs,),
        [
            smem(),
            smem(),
            whole((seqs, 2, width)),
            whole((2, width)),
            whole((rows, model)),
            per_record((frames, model)),
            per_record((2 * EDGE, model)),
            whole((model, width)),
            per_record((span, width)),
        ],
        [
            per_record((frames, width)),
            per_record((span, width)),
            per_record((rows, frames)),
            whole((seqs, 2, width)),
        ],
        [
            sds((recs, frames, width), BF16),
            sds((recs, span, width), F32),
            sds((recs, rows, frames), BF16),
            sds((seqs, 2, width), F32),
        ],
        [
            pltpu.VMEM((2, width), F32),
            pltpu.VMEM((block_rows(frames, 512), width), F32),
            pltpu.VMEM((block_rows(frames, 512), width), F32),
        ],
        2 * matmul,
        input_bytes + 3 * array_bytes,
    )(
        meta,
        counts,
        stats,
        jnp.stack([norm_gain, norm_shift]),
        after(select, w_own, w_sibling),
        grad_out,
        halo_g,
        out_weight,
        conv,
    )
    w_out = call(
        first_outer_kernel,
        "outer_w_out",
        (recs,),
        [per_record((frames, model)), per_record((frames, width))],
        whole((seqs, 1, piece, frames)),
        sds((seqs, 1, piece, frames), BF16),
        [pltpu.VMEM((width, model), F32)],
        matmul,
        input_bytes,
    )(grad_out, swished)
    sums = exchange(sums, "seq")
    grad_shift, grad_gain = jnp.sum(sums, axis=0)

    blocks = frames // chunk
    parts_in = frames // half_rows

    def back(first, size, *earlier):
        def window(i):
            return (first + i // blocks, pl.multiple_of(i % blocks * chunk, chunk), 0)

        def block(i):
            return (first + i // blocks, i % blocks, 0)

        return call(
            functools.partial(back_kernel, first, blocks),
            "back_conv",
            (size * blocks,),
            [
                smem(),
                smem(),
                whole((seqs, 2, width)),
                whole((seqs, 2, width)),
                whole((1, width)),
                pl.BlockSpec((pl.Element(1), pl.Element(chunk + 2 * EDGE), pl.Element(width)), window),
                pl.BlockSpec((pl.Element(1), pl.Element(chunk + 2 * EDGE), pl.Element(width)), window),
                pl.BlockSpec((1, chunk, width), block),
                pl.BlockSpec((1, chunk, width), block),
                whole((kernel, width)),
            ],
            [pl.BlockSpec((chunk, 2 * width), lambda i: (i, 0)), whole((16, width))],
            [sds((size * frames, 2 * width), BF16), sds((16, width), F32)],
            [
                pltpu.VMEM((halves, chunk + 2 * EDGE, LANES), F32),
                pltpu.VMEM((halves, kernel, 8, LANES), F32),
            ],
            0,
            1024,
        )(meta, counts, stats, sums, norm_gain[None], gn, conv, vl, sg, after(depth_taps, *earlier))

    def partials(first, size, mine, *earlier):
        sibling = lax.ppermute(mine, "tp", swap)
        out = sds((seqs, size, piece, frames), BF16)
        return call(
            partial_kernel,
            "partial_in",
            (size * parts_in,),
            [
                pl.BlockSpec((half_rows, 2 * width), lambda i: (i, 0)),
                pl.BlockSpec((half_rows, 2 * width), lambda i: (i, 0)),
                whole((chips * rows, 2 * width)),
                whole((chips * rows, 2 * width)),
                pl.BlockSpec(
                    (1, rows, half_rows), lambda i: (first + i // parts_in, 0, i % parts_in)
                ),
            ],
            [
                pl.BlockSpec(
                    (seqs, 1, piece, half_rows), lambda i: (0, i // parts_in, 0, i % parts_in)
                )
            ]
            * chips,
            [out] * chips,
            [],
            0,
            1024,
        )(mine, sibling, after(w_own, *earlier), w_sibling, picked)

    def deliver(part, weight, *earlier, extra=None):
        arrived = []
        for d in range(1, chips):
            send = [(i, ((i // 2 + d) % chips) * 2 + i % 2) for i in range(tps)]
            arrived.append(lax.ppermute(part[d], "tp", send))
        size = part[0].shape[1]
        block = pl.BlockSpec(
            (seqs, 1, piece, half_rows), lambda i: (0, i // parts_in, 0, i % parts_in)
        )
        if extra is None:
            return call(
                add_kernel,
                "add",
                (size * parts_in,),
                [block] * chips,
                block,
                sds(part[0].shape, BF16),
                [],
                weight,
                1024,
            )(after(part[0], *earlier), *arrived)
        one = pl.BlockSpec((seqs, 1, piece, half_rows), lambda i: (0, 0, 0, i % parts_in))
        return call(
            functools.partial(join_kernel, parts_in),
            "add_join",
            (2 * parts_in,),
            [one] * (chips + 1),
            block,
            sds((seqs, 2, piece, frames), BF16),
            [],
            weight,
            1024,
        )(after(part[0], *earlier), *arrived, extra)

    groups = ((0, 1), (1, 1), (2, recs - 2))
    grads = [None] * 3
    taps = [None] * 3
    parts = [None] * 3
    owns = [None] * 3
    moved = [None] * 3
    grads[0], taps[0] = back(*groups[0], w_out)
    grads[1], taps[1] = back(*groups[1], grads[0])
    parts[0] = partials(*groups[0], grads[0], grads[1])
    grads[2], taps[2] = back(*groups[2], *parts[0])
    parts[1] = partials(*groups[1], grads[1], grads[2])
    owns[0] = deliver(parts[0], LONG, *parts[1], extra=w_out)
    moved[0] = exchange(owns[0], "seq")
    parts[2] = partials(*groups[2], grads[2], owns[0])

    slots = 2 * width + 16 * (width // shard)
    half = sds((seqs // 2, slots, shard), BF16)
    keep, send = call(
        functools.partial(outer_kernel, groups),
        "outer_w_in",
        (recs,),
        [smem(), per_record((frames, model))]
        + [
            pl.BlockSpec(
                (frames, 2 * width),
                lambda r, first=first, size=size: (jnp.clip(r - first, 0, size - 1), 0),
            )
            for first, size in groups
        ]
        + [whole((16, width))] * len(groups),
        [whole(half.shape)] * 2,
        [half] * 2,
        [pltpu.VMEM((2 * width, model), F32)],
        LONG,
        1024,
    )(parity, after(normed, *parts[2]), *grads, *taps)
    owns[1] = deliver(parts[1], LONG, keep)
    moved[1] = exchange(after(owns[1], moved[0]), "seq")
    owns[2] = deliver(parts[2], 0, owns[1])
    bit = 1
    while True:
        others = lax.ppermute(send, "seq", [(i, i ^ bit) for i in range(seqs)])
        if bit == 1:
            moved[2] = exchange(after(owns[2], moved[1], others), "seq")
        bit *= 2
        if bit == seqs:
            break
        if bit == 2:
            keep = after(keep, owns[2])
        shape = (keep.shape[0] // 2,) + keep.shape[1:]
        side = ((seq_at // bit) % 2).astype(jnp.int32).reshape(1, 1)
        keep, send = call(
            fold_kernel,
            "fold",
            (1,),
            [smem()] + [whole(keep.shape)] * 2,
            [whole(shape)] * 2,
            [sds(shape, BF16)] * 2,
            [],
            0,
            1024,
            vmem=20,
        )(side, keep, others)
    w_value, w_gate, w_out, grad_taps = call(
        functools.partial(finish_kernel, kernel),
        "finish",
        (1,),
        [whole(keep.shape)] * 2
        + [pl.BlockSpec((seqs, 1, piece, frames), lambda i: (0, 1, 0, 0))],
        [whole((shard, width))] * 3 + [whole((kernel, width))],
        [sds((shard, width), F32)] * 3 + [sds((kernel, width), F32)],
        [],
        0,
        1024,
        vmem=20,
    )(keep, others, moved[0])
    grad_in = ()
    for (first, size), part in zip(groups, moved):
        grad_in = (
            call(
                place_kernel,
                "place",
                (size,),
                [pl.BlockSpec((seqs, 1, piece, frames), lambda i: (0, i, 0, 0))]
                + [anywhere()] * len(grad_in),
                pl.BlockSpec((1, piece, seqs * frames), lambda i, first=first: (first + i, 0, 0)),
                sds((recs, piece, seqs * frames), BF16),
                [],
                0,
                4 * size * piece * seqs * frames,
                {1: 0} if grad_in else None,
                vmem=20,
            )(part, *grad_in),
        )
    (grad_in,) = grad_in
    return (grad_in, w_value, w_gate, w_out, grad_taps, grad_gain, grad_shift)


def solution(mesh):
    placed = (
        P(None, "seq", None),
        P(None, "seq", None),
        P(None, "tp"),
        P(None, "tp"),
        P(None, "tp"),
        P("tp"),
        P("tp"),
        P(None, "tp"),
        P(),
    )
    return jax.shard_map(
        per_device,
        mesh=mesh,
        in_specs=placed,
        out_specs=(
            P(None, ("seq", "tp"), None),
            P("seq", "tp"),
            P("seq", "tp"),
            P("seq", "tp"),
            P(None, "tp"),
            P("tp"),
            P("tp"),
        ),
        check_vma=False,
    )
```

```python
import functools

import jax
import jax.numpy as jnp
from jax import lax
from jax.experimental import pallas as pl
from jax.experimental.pallas import tpu as pltpu
from jax.sharding import PartitionSpec as P

EPSILON = 1e-05
EDGE = 8
LANES = 128
LONG = 50_000_000_000
F32 = jnp.float32
BF16 = jnp.bfloat16


def sigmoid(x):
    return 0.5 * jnp.tanh(0.5 * x) + 0.5


def dot(a, b):
    return jnp.dot(a, b, preferred_element_type=F32)


def dot_nt(a, b):
    return lax.dot_general(a, b, (((1,), (1,)), ((), ())), preferred_element_type=F32)


def dot_tn(a, b):
    return lax.dot_general(a, b, (((0,), (0,)), ((), ())), preferred_element_type=F32)


def rows_of(count, first):
    return first + lax.broadcasted_iota(jnp.int32, (count, 1), 0)


def fold_rows(x):
    return jnp.sum(x.reshape(x.shape[0] // 8, 8, x.shape[1]), axis=0)


def block_rows(total, most):
    return max(b for b in range(8, most + 1, 8) if total % b == 0)


def whole(shape):
    return pl.BlockSpec(shape, lambda *i: (0,) * len(shape))


def per_record(shape):
    return pl.BlockSpec((1,) + shape, lambda r: (r,) + (0,) * len(shape))


def smem():
    return pl.BlockSpec(memory_space=pltpu.SMEM)


def anywhere():
    return pl.BlockSpec(memory_space=pl.ANY)


def after(x, *earlier):
    return lax.optimization_barrier((x,) + earlier)[0]


def spread_sums(out, sums):
    for s in range(out.shape[0]):
        out[s] = sums


def call(
    kernel, name, grid, in_specs, out_specs, out_shape, scratch, flops, moved, aliases=None, vmem=63
):
    return pl.pallas_call(
        kernel,
        name=name,
        grid=grid,
        in_specs=in_specs,
        out_specs=out_specs,
        out_shape=out_shape,
        scratch_shapes=scratch,
        input_output_aliases=aliases or {},
        cost_estimate=pl.CostEstimate(flops=int(flops), bytes_accessed=int(moved), transcendentals=0),
        compiler_params=pltpu.CompilerParams(vmem_limit_bytes=vmem * 1024 * 1024),
    )


def gate_kernel(meta, x, halo, wv, wg, taps, vl_o, sg_o, conv_o, st_o, gp, st):
    r = pl.program_id(0)
    hi = meta[0, r]
    lo = meta[1, r]
    frames = x.shape[1]
    width = wv.shape[1]
    halves = width // LANES

    def put(row, value):
        for h in range(halves):
            gp[h, pl.ds(row, value.shape[0]), :] = value[:, h * LANES : (h + 1) * LANES]

    edge_v = dot(halo[0], wv[...])
    edge_g = dot(halo[0], wg[...])
    row = rows_of(2 * EDGE, 0)
    pos = jnp.where(row < EDGE, row - EDGE, row - EDGE + frames)
    edge = jnp.where((pos >= lo) & (pos < hi), edge_v * sigmoid(edge_g), 0.0)
    zero = jnp.zeros((EDGE, width), F32)
    put(0, zero)
    put(EDGE, edge[:EDGE])
    put(2 * EDGE + frames, edge[EDGE:])
    put(3 * EDGE + frames, zero)
    step = block_rows(frames, 512)
    small = block_rows(step, 64)
    for base in range(0, frames, step):
        xb = x[0, base : base + step, :]
        vl_o[0, base : base + step, :] = dot(xb, wv[...])
        sg_o[0, base : base + step, :] = dot(xb, wg[...])

    def gating(i, carry):
        base = pl.multiple_of(i * small, small)
        v = vl_o[0, pl.ds(base, small), :]
        s = sigmoid(sg_o[0, pl.ds(base, small), :])
        sg_o[0, pl.ds(base, small), :] = s
        put(2 * EDGE + base, jnp.where(rows_of(small, base) < hi, v * s, 0.0))
        return carry

    lax.fori_loop(0, frames // small, gating, 0)
    span = frames + 2 * EDGE
    cb = block_rows(span, 104)
    kernel = taps.shape[0]
    margin = (kernel - 1) // 2
    for h in range(halves):
        cols = slice(h * LANES, (h + 1) * LANES)

        def convolve(i, carry):
            s1, s2 = carry
            base = pl.multiple_of(i * cb, 8)
            acc = jnp.zeros((cb, LANES), F32)
            for k in range(kernel):
                acc = acc + taps[k : k + 1, cols] * gp[h, pl.ds(base + EDGE - margin + k, cb), :]
            conv_o[0, pl.ds(base, cb), cols] = acc
            pos = rows_of(cb, base - EDGE)
            kept = jnp.where((pos >= 0) & (pos < jnp.minimum(hi, frames)), acc, 0.0)
            return s1 + fold_rows(kept), s2 + fold_rows(kept * kept)

        none = jnp.zeros((8, LANES), F32)
        s1, s2 = lax.fori_loop(0, span // cb, convolve, (none, none))
        add = jnp.concatenate(
            [jnp.sum(s1, axis=0, keepdims=True), jnp.sum(s2, axis=0, keepdims=True)], axis=0
        )
        st[:, cols] = jnp.where(r == 0, 0.0, st[:, cols]) + add

    @pl.when(r == pl.num_programs(0) - 1)
    def _():
        spread_sums(st_o, st[...])


def batch_norm(stats, count):
    sums = jnp.sum(stats[...], axis=0)
    centre = sums[0:1] / count
    spread = sums[1:2] / count - centre * centre
    return centre, lax.rsqrt(spread + EPSILON)


def norm_kernel(
    meta, count, stats, affine, select, grads, halo, wo, conv,
    swished_o, gn_o, picked_o, st_o, st, ping, pong
):
    r = pl.program_id(0)
    hi = meta[0, r]
    lo = meta[1, r]
    frames = grads.shape[1]
    centre, inv = batch_norm(stats, count[0, 0])
    gain, shift = affine[0:1, :], affine[1:2, :]

    def part(row, swish_grad):
        size = swish_grad.shape[0]
        unit = (conv[0, pl.ds(row, size), :] - centre) * inv
        normalized = unit * gain + shift
        s = sigmoid(normalized)
        pos = rows_of(size, row - EDGE)
        keep = (pos >= lo) & (pos < hi)
        swished = jnp.where(keep, normalized * s, 0.0)
        gn = jnp.where(keep, swish_grad, 0.0) * (s + normalized * (s - s * s))
        gn_o[0, pl.ds(row, size), :] = gn
        return unit, swished, gn

    edge = dot(halo[0], wo[...])
    part(0, edge[:EDGE])
    part(frames + EDGE, edge[EDGE:])
    step = block_rows(frames, 512)
    small = block_rows(step, 32)
    s1 = jnp.zeros((8, conv.shape[2]), F32)
    s2 = s1
    held = (ping, pong)
    ping[...] = dot(grads[0, :step, :], wo[...])
    for i in range(frames // step):
        now = held[i % 2]
        if (i + 1) * step < frames:
            held[(i + 1) % 2][...] = dot(grads[0, (i + 1) * step : (i + 2) * step, :], wo[...])
        picked_o[0, :, i * step : (i + 1) * step] = dot_nt(
            select[...], grads[0, i * step : (i + 1) * step, :]
        ).astype(BF16)
        for j in range(step // small):
            base = i * step + j * small
            unit, swished, gn = part(base + EDGE, now[j * small : (j + 1) * small, :])
            swished_o[0, base : base + small, :] = swished.astype(BF16)
            s1 = s1 + fold_rows(gn)
            s2 = s2 + fold_rows(gn * unit)
    add = jnp.concatenate(
        [jnp.sum(s1, axis=0, keepdims=True), jnp.sum(s2, axis=0, keepdims=True)], axis=0
    )
    st[...] = jnp.where(r == 0, 0.0, st[...]) + add

    @pl.when(r == pl.num_programs(0) - 1)
    def _():
        spread_sums(st_o, st[...])


def back_kernel(
    record, blocks, meta, count, stats, sums, gain, gn, conv, vl, sg, taps, out, taps_o, gc, acc
):
    i = pl.program_id(0)
    frames, width = vl.shape[1:]
    hi = meta[0, record + i // blocks]
    lo = meta[1, record + i // blocks]
    halves = width // LANES
    span = frames + 2 * EDGE
    kernel = taps.shape[0]
    margin = (kernel - 1) // 2
    cb = block_rows(span, 144)
    step = block_rows(frames, 32)
    total_frames = count[0, 0]
    centre, inv = batch_norm(stats, total_frames)
    grad_sums = jnp.sum(sums[...], axis=0)
    scale = gain[...] * inv
    offset = scale * grad_sums[0:1] / total_frames
    slope = scale * inv * grad_sums[1:2] / total_frames
    first = i % blocks * frames

    @pl.when(i == 0)
    def _():
        acc[...] = jnp.zeros_like(acc)

    for h in range(halves):
        cols = slice(h * LANES, (h + 1) * LANES)
        for base in range(0, span, cb):
            pos = rows_of(cb, first + (base - EDGE))
            mean = offset[:, cols] + (conv[0, base : base + cb, cols] - centre[:, cols]) * slope[:, cols]
            gc[h, base : base + cb, :] = scale[:, cols] * gn[0, base : base + cb, cols] - jnp.where(
                (pos >= lo) & (pos < hi), mean, 0.0
            )
        sums_k = [acc[h, k] for k in range(kernel)]
        for base in range(0, frames, step):
            v = vl[0, base : base + step, cols]
            s = sg[0, base : base + step, cols]
            keep = rows_of(step, first + base) < hi
            vs = v * s
            gated = jnp.where(keep, vs, 0.0)
            total = jnp.zeros((step, LANES), F32)
            for k in range(kernel):
                window = gc[h, base + EDGE + margin - k : base + EDGE + margin - k + step, :]
                total = total + taps[k : k + 1, cols] * window
                sums_k[k] = sums_k[k] + fold_rows(window * gated)
            total = jnp.where(keep, total, 0.0)
            out[base : base + step, cols] = (total * s).astype(BF16)
            out[base : base + step, width + h * LANES : width + (h + 1) * LANES] = (
                total * (vs - vs * s)
            ).astype(BF16)
        for k in range(kernel):
            acc[h, k] = sums_k[k]

    @pl.when(i == pl.num_programs(0) - 1)
    def _():
        taps_o[...] = jnp.zeros_like(taps_o)
        for h in range(halves):
            for k in range(kernel):
                taps_o[k : k + 1, h * LANES : (h + 1) * LANES] = jnp.sum(
                    acc[h, k], axis=0, keepdims=True
                )


def partial_kernel(own, sibling, w_own, w_sibling, picked, mine, *others):
    total = dot_nt(w_own[...], own[...]) + dot_nt(w_sibling[...], sibling[...])
    rows = picked.shape[1]
    seqs, _, piece, frames = mine.shape
    mine[...] = (
        (total[:rows] + picked[0].astype(F32)).astype(BF16).reshape(seqs, 1, piece, frames)
    )
    for d, other in enumerate(others):
        other[...] = (
            total[(d + 1) * rows : (d + 2) * rows].astype(BF16).reshape(seqs, 1, piece, frames)
        )


def join_kernel(half, *refs):
    i = pl.program_id(0)

    @pl.when(i < half)
    def _():
        add_kernel(*refs[:-2], refs[-1])

    @pl.when(i >= half)
    def _():
        refs[-1][...] = refs[-2][...]


def add_kernel(*refs):
    total = refs[0][...].astype(F32)
    for other in refs[1:-1]:
        total = total + other[...].astype(F32)
    refs[-1][...] = total.astype(BF16)


def first_outer_kernel(grads, swished, out, acc):
    r = pl.program_id(0)
    add = dot_tn(swished[0], grads[0])
    acc[...] = add + jnp.where(r == 0, 0.0, acc[...])

    @pl.when(r == pl.num_programs(0) - 1)
    def _():
        seqs, _, piece, frames = out.shape
        shard = acc.shape[1] // seqs
        for s in range(seqs):
            for q in range(frames // shard):
                out[s, 0, :, q * shard : (q + 1) * shard] = acc[
                    q * piece : (q + 1) * piece, s * shard : (s + 1) * shard
                ].astype(BF16)


def outer_kernel(groups, parity, x, *refs):
    lefts, taps = refs[: len(groups)], refs[len(groups) : 2 * len(groups)]
    keep, send, acc = refs[2 * len(groups) :]
    records = groups[-1][0] + groups[-1][1]
    width = acc.shape[0] // 2
    shard = keep.shape[2]
    r = pl.program_id(0)
    for (first, size), left in zip(groups, lefts):

        @pl.when((r >= first) & (r < first + size))
        def _(left=left):
            add = dot_tn(left[...], x[0])
            acc[...] = add + jnp.where(r == 0, 0.0, acc[...])

    @pl.when(r == records - 1)
    def _():
        tap_sums = taps[0][...]
        for part in taps[1:]:
            tap_sums = tap_sums + part[...]

        def write(place, odd):
            for j in range(place.shape[0]):
                at = (2 * j + odd) * shard
                place[j, : 2 * width, :] = acc[:, at : at + shard].astype(BF16)
                for q in range(width // shard):
                    row = 2 * width + 16 * q
                    place[j, row : row + 16, :] = tap_sums[:, q * shard : (q + 1) * shard].astype(
                        BF16
                    )

        @pl.when(parity[0, 0] == 0)
        def _():
            write(keep, 0)
            write(send, 1)

        @pl.when(parity[0, 0] != 0)
        def _():
            write(keep, 1)
            write(send, 0)


def fold_kernel(parity, own, other, keep, send):
    def write(place, odd):
        for j in range(place.shape[0]):
            total = own[2 * j + odd].astype(F32) + other[2 * j + odd].astype(F32)
            place[j] = total.astype(BF16)

    @pl.when(parity[0, 0] == 0)
    def _():
        write(keep, 0)
        write(send, 1)

    @pl.when(parity[0, 0] != 0)
    def _():
        write(keep, 1)
        write(send, 0)


def finish_kernel(kernel, own, other, pieces, value, gate, out, taps):
    width = value.shape[1]
    shard = value.shape[0]

    def total(row, size):
        return own[0, row : row + size, :].astype(F32) + other[0, row : row + size, :].astype(F32)

    value[...] = total(0, width).T
    gate[...] = total(width, width).T
    ready = pieces[0, 0].astype(F32)
    for s in range(1, pieces.shape[0]):
        ready = ready + pieces[s, 0].astype(F32)
    blocks = [ready[:, q * shard : (q + 1) * shard] for q in range(ready.shape[1] // shard)]
    out[...] = jnp.concatenate(blocks, axis=0).T
    for q in range(width // shard):
        taps[:, q * shard : (q + 1) * shard] = total(2 * width + 16 * q, 16)[:kernel]


def place_kernel(moved, *refs):
    out = refs[-1]
    frames = moved.shape[3]
    for s in range(moved.shape[0]):
        out[0, :, s * frames : (s + 1) * frames] = moved[s, 0]


def exchange(copies, axis):
    return lax.all_to_all(copies, axis, 0, 0, tiled=True)


def per_device(
    normed,
    grad_out,
    value_weight,
    gate_weight,
    depth_taps,
    norm_gain,
    norm_shift,
    out_weight,
    lengths,
):
    recs, frames, model = normed.shape
    kernel = depth_taps.shape[0]
    width = value_weight.shape[1]
    seqs = lax.axis_size("seq")
    tps = lax.axis_size("tp")
    chips = tps // 2
    piece = model // (seqs * tps)
    rows = seqs * piece
    shard = model // seqs
    span = frames + 2 * EDGE
    seq_at = lax.axis_index("seq")
    tp_at = lax.axis_index("tp")
    chip_at, core_at = tp_at // 2, tp_at % 2
    count = jnp.sum(lengths).astype(F32)
    first = (seq_at * frames).astype(jnp.int32)
    meta = jnp.stack([lengths - first, jnp.full((recs,), 0, jnp.int32) - first])
    halves = width // LANES
    counts = count.reshape(1, 1)
    parity = (seq_at % 2).astype(jnp.int32).reshape(1, 1)
    sds = jax.ShapeDtypeStruct

    low_edge = jnp.concatenate([normed[:, -EDGE:], grad_out[:, -EDGE:]], axis=2)
    high_edge = jnp.concatenate([normed[:, :EDGE], grad_out[:, :EDGE]], axis=2)
    up = [(i, i + 1) for i in range(seqs - 1)]
    down = [(j, i) for i, j in up]
    halo = jnp.concatenate(
        [lax.ppermute(low_edge, "seq", up), lax.ppermute(high_edge, "seq", down)], axis=1
    )
    halo_x, halo_g = halo[:, :, :model], halo[:, :, model:]

    channel = (
        jnp.arange(seqs, dtype=jnp.int32)[:, None] * (tps * piece)
        + tp_at * piece
        + jnp.arange(piece, dtype=jnp.int32)[None, :]
    ).reshape(rows, 1)
    select = (channel == jnp.arange(model, dtype=jnp.int32)[None, :]).astype(BF16)
    array_bytes = recs * frames * width * 4
    input_bytes = recs * frames * model * 2
    matmul = 2 * recs * frames * model * width

    vl, sg, conv, stats = call(
        gate_kernel,
        "gate_conv",
        (recs,),
        [
            smem(),
            per_record((frames, model)),
            per_record((2 * EDGE, model)),
            whole((model, width)),
            whole((model, width)),
            whole((kernel, width)),
        ],
        [
            per_record((frames, width)),
            per_record((frames, width)),
            per_record((span, width)),
            whole((seqs, 2, width)),
        ],
        [
            sds((recs, frames, width), F32),
            sds((recs, frames, width), F32),
            sds((recs, span, width), F32),
            sds((seqs, 2, width), F32),
        ],
        [pltpu.VMEM((halves, frames + 4 * EDGE, LANES), F32), pltpu.VMEM((2, width), F32)],
        2 * matmul,
        input_bytes + 3 * array_bytes,
    )(meta, normed, halo_x, value_weight, gate_weight, depth_taps)
    both = jnp.concatenate([after(value_weight, stats), gate_weight], axis=1).reshape(seqs, tps, piece, 2 * width)

    def chosen(core):
        picks = [
            lax.dynamic_index_in_dim(both, ((chip_at + d) % chips) * 2 + core, 1, keepdims=False)
            for d in range(chips)
        ]
        return jnp.stack(picks).reshape(chips * rows, 2 * width)

    swap = [(i, i ^ 1) for i in range(tps)]
    w_own = chosen(core_at)
    w_sibling = lax.ppermute(chosen(1 - core_at), "tp", swap)

    stats = exchange(stats, "seq")

    chunk = block_rows(frames, 256)
    half_rows = block_rows(frames, 512)
    swished, gn, picked, sums = call(
        norm_kernel,
        "swish_norm",
        (recs,),
        [
            smem(),
            smem(),
            whole((seqs, 2, width)),
            whole((2, width)),
            whole((rows, model)),
            per_record((frames, model)),
            per_record((2 * EDGE, model)),
            whole((model, width)),
            per_record((span, width)),
        ],
        [
            per_record((frames, width)),
            per_record((span, width)),
            per_record((rows, frames)),
            whole((seqs, 2, width)),
        ],
        [
            sds((recs, frames, width), BF16),
            sds((recs, span, width), F32),
            sds((recs, rows, frames), BF16),
            sds((seqs, 2, width), F32),
        ],
        [
            pltpu.VMEM((2, width), F32),
            pltpu.VMEM((block_rows(frames, 512), width), F32),
            pltpu.VMEM((block_rows(frames, 512), width), F32),
        ],
        2 * matmul,
        input_bytes + 3 * array_bytes,
    )(
        meta,
        counts,
        stats,
        jnp.stack([norm_gain, norm_shift]),
        after(select, w_own, w_sibling),
        grad_out,
        halo_g,
        out_weight,
        conv,
    )
    w_out = call(
        first_outer_kernel,
        "outer_w_out",
        (recs,),
        [per_record((frames, model)), per_record((frames, width))],
        whole((seqs, 1, piece, frames)),
        sds((seqs, 1, piece, frames), BF16),
        [pltpu.VMEM((width, model), F32)],
        matmul,
        input_bytes,
    )(grad_out, swished)
    sums = exchange(sums, "seq")
    grad_shift, grad_gain = jnp.sum(sums, axis=0)

    blocks = frames // chunk
    parts_in = frames // half_rows

    def back(first, size, *earlier):
        def window(i):
            return (first + i // blocks, pl.multiple_of(i % blocks * chunk, chunk), 0)

        def block(i):
            return (first + i // blocks, i % blocks, 0)

        return call(
            functools.partial(back_kernel, first, blocks),
            "back_conv",
            (size * blocks,),
            [
                smem(),
                smem(),
                whole((seqs, 2, width)),
                whole((seqs, 2, width)),
                whole((1, width)),
                pl.BlockSpec((pl.Element(1), pl.Element(chunk + 2 * EDGE), pl.Element(width)), window),
                pl.BlockSpec((pl.Element(1), pl.Element(chunk + 2 * EDGE), pl.Element(width)), window),
                pl.BlockSpec((1, chunk, width), block),
                pl.BlockSpec((1, chunk, width), block),
                whole((kernel, width)),
            ],
            [pl.BlockSpec((chunk, 2 * width), lambda i: (i, 0)), whole((16, width))],
            [sds((size * frames, 2 * width), BF16), sds((16, width), F32)],
            [
                pltpu.VMEM((halves, chunk + 2 * EDGE, LANES), F32),
                pltpu.VMEM((halves, kernel, 8, LANES), F32),
            ],
            0,
            1024,
        )(meta, counts, stats, sums, norm_gain[None], gn, conv, vl, sg, after(depth_taps, *earlier))

    def partials(first, size, mine, *earlier):
        sibling = lax.ppermute(mine, "tp", swap)
        out = sds((seqs, size, piece, frames), BF16)
        return call(
            partial_kernel,
            "partial_in",
            (size * parts_in,),
            [
                pl.BlockSpec((half_rows, 2 * width), lambda i: (i, 0)),
                pl.BlockSpec((half_rows, 2 * width), lambda i: (i, 0)),
                whole((chips * rows, 2 * width)),
                whole((chips * rows, 2 * width)),
                pl.BlockSpec(
                    (1, rows, half_rows), lambda i: (first + i // parts_in, 0, i % parts_in)
                ),
            ],
            [
                pl.BlockSpec(
                    (seqs, 1, piece, half_rows), lambda i: (0, i // parts_in, 0, i % parts_in)
                )
            ]
            * chips,
            [out] * chips,
            [],
            0,
            1024,
        )(mine, sibling, after(w_own, *earlier), w_sibling, picked)

    def deliver(part, weight, *earlier, extra=None):
        arrived = []
        for d in range(1, chips):
            send = [(i, ((i // 2 + d) % chips) * 2 + i % 2) for i in range(tps)]
            arrived.append(lax.ppermute(part[d], "tp", send))
        size = part[0].shape[1]
        block = pl.BlockSpec(
            (seqs, 1, piece, half_rows), lambda i: (0, i // parts_in, 0, i % parts_in)
        )
        if extra is None:
            return call(
                add_kernel,
                "add",
                (size * parts_in,),
                [block] * chips,
                block,
                sds(part[0].shape, BF16),
                [],
                weight,
                1024,
            )(after(part[0], *earlier), *arrived)
        one = pl.BlockSpec((seqs, 1, piece, half_rows), lambda i: (0, 0, 0, i % parts_in))
        return call(
            functools.partial(join_kernel, parts_in),
            "add_join",
            (2 * parts_in,),
            [one] * (chips + 1),
            block,
            sds((seqs, 2, piece, frames), BF16),
            [],
            weight,
            1024,
        )(after(part[0], *earlier), *arrived, extra)

    groups = ((0, 1), (1, 1), (2, recs - 2))
    grads = [None] * 3
    taps = [None] * 3
    parts = [None] * 3
    owns = [None] * 3
    moved = [None] * 3
    grads[0], taps[0] = back(*groups[0], w_out)
    grads[1], taps[1] = back(*groups[1], grads[0])
    parts[0] = partials(*groups[0], grads[0], grads[1])
    grads[2], taps[2] = back(*groups[2], *parts[0])
    parts[1] = partials(*groups[1], grads[1], grads[2])
    owns[0] = deliver(parts[0], LONG, *parts[1], extra=w_out)
    moved[0] = exchange(owns[0], "seq")
    parts[2] = partials(*groups[2], grads[2], owns[0])

    slots = 2 * width + 16 * (width // shard)
    half = sds((seqs // 2, slots, shard), BF16)
    keep, send = call(
        functools.partial(outer_kernel, groups),
        "outer_w_in",
        (recs,),
        [smem(), per_record((frames, model))]
        + [
            pl.BlockSpec(
                (frames, 2 * width),
                lambda r, first=first, size=size: (jnp.clip(r - first, 0, size - 1), 0),
            )
            for first, size in groups
        ]
        + [whole((16, width))] * len(groups),
        [whole(half.shape)] * 2,
        [half] * 2,
        [pltpu.VMEM((2 * width, model), F32)],
        LONG,
        1024,
    )(parity, after(normed, *parts[2]), *grads, *taps)
    owns[1] = deliver(parts[1], LONG, keep)
    moved[1] = exchange(after(owns[1], moved[0]), "seq")
    bit = 1
    while True:
        others = lax.ppermute(send, "seq", [(i, i ^ bit) for i in range(seqs)])
        bit *= 2
        if bit == seqs:
            break
        if bit == 2:
            keep = after(keep, owns[1])
        shape = (keep.shape[0] // 2,) + keep.shape[1:]
        side = ((seq_at // bit) % 2).astype(jnp.int32).reshape(1, 1)
        keep, send = call(
            fold_kernel,
            "fold",
            (1,),
            [smem()] + [whole(keep.shape)] * 2,
            [whole(shape)] * 2,
            [sds(shape, BF16)] * 2,
            [],
            0,
            1024,
            vmem=20,
        )(side, keep, others)
        if bit == 2:
            owns[2] = deliver(parts[2], 0, keep)
        if bit == min(4, seqs // 2):
            moved[2] = exchange(after(owns[2], moved[1], keep), "seq")
    w_value, w_gate, w_out, grad_taps = call(
        functools.partial(finish_kernel, kernel),
        "finish",
        (1,),
        [whole(keep.shape)] * 2
        + [pl.BlockSpec((seqs, 1, piece, frames), lambda i: (0, 1, 0, 0))],
        [whole((shard, width))] * 3 + [whole((kernel, width))],
        [sds((shard, width), F32)] * 3 + [sds((kernel, width), F32)],
        [],
        0,
        1024,
        vmem=20,
    )(keep, others, moved[0])
    grad_in = ()
    for (first, size), part in zip(groups, moved):
        grad_in = (
            call(
                place_kernel,
                "place",
                (size,),
                [pl.BlockSpec((seqs, 1, piece, frames), lambda i: (0, i, 0, 0))]
                + [anywhere()] * len(grad_in),
                pl.BlockSpec((1, piece, seqs * frames), lambda i, first=first: (first + i, 0, 0)),
                sds((recs, piece, seqs * frames), BF16),
                [],
                0,
                4 * size * piece * seqs * frames,
                {1: 0} if grad_in else None,
                vmem=20,
            )(part, *grad_in),
        )
    (grad_in,) = grad_in
    return (grad_in, w_value, w_gate, w_out, grad_taps, grad_gain, grad_shift)


def solution(mesh):
    placed = (
        P(None, "seq", None),
        P(None, "seq", None),
        P(None, "tp"),
        P(None, "tp"),
        P(None, "tp"),
        P("tp"),
        P("tp"),
        P(None, "tp"),
        P(),
    )
    return jax.shard_map(
        per_device,
        mesh=mesh,
        in_specs=placed,
        out_specs=(
            P(None, ("seq", "tp"), None),
            P("seq", "tp"),
            P("seq", "tp"),
            P("seq", "tp"),
            P(None, "tp"),
            P("tp"),
            P("tp"),
        ),
        check_vma=False,
    )
```

```python
import functools

import jax
import jax.numpy as jnp
from jax import lax
from jax.experimental import pallas as pl
from jax.experimental.pallas import tpu as pltpu
from jax.sharding import PartitionSpec as P

EPSILON = 1e-05
EDGE = 8
LANES = 128
LONG = 50_000_000_000
F32 = jnp.float32
BF16 = jnp.bfloat16


def sigmoid(x):
    return 0.5 * jnp.tanh(0.5 * x) + 0.5


def dot(a, b):
    return jnp.dot(a, b, preferred_element_type=F32)


def dot_nt(a, b):
    return lax.dot_general(a, b, (((1,), (1,)), ((), ())), preferred_element_type=F32)


def dot_tn(a, b):
    return lax.dot_general(a, b, (((0,), (0,)), ((), ())), preferred_element_type=F32)


def rows_of(count, first):
    return first + lax.broadcasted_iota(jnp.int32, (count, 1), 0)


def fold_rows(x):
    return jnp.sum(x.reshape(x.shape[0] // 8, 8, x.shape[1]), axis=0)


def block_rows(total, most):
    return max(b for b in range(8, most + 1, 8) if total % b == 0)


def whole(shape):
    return pl.BlockSpec(shape, lambda *i: (0,) * len(shape))


def per_record(shape):
    return pl.BlockSpec((1,) + shape, lambda r: (r,) + (0,) * len(shape))


def smem():
    return pl.BlockSpec(memory_space=pltpu.SMEM)


def anywhere():
    return pl.BlockSpec(memory_space=pl.ANY)


def after(x, *earlier):
    return lax.optimization_barrier((x,) + earlier)[0]


def spread_sums(out, sums):
    for s in range(out.shape[0]):
        out[s] = sums


def call(
    kernel, name, grid, in_specs, out_specs, out_shape, scratch, flops, moved, aliases=None, vmem=63
):
    return pl.pallas_call(
        kernel,
        name=name,
        grid=grid,
        in_specs=in_specs,
        out_specs=out_specs,
        out_shape=out_shape,
        scratch_shapes=scratch,
        input_output_aliases=aliases or {},
        cost_estimate=pl.CostEstimate(flops=int(flops), bytes_accessed=int(moved), transcendentals=0),
        compiler_params=pltpu.CompilerParams(vmem_limit_bytes=vmem * 1024 * 1024),
    )


def gate_kernel(meta, x, halo, wv, wg, taps, vl_o, sg_o, conv_o, st_o, gp, st):
    r = pl.program_id(0)
    hi = meta[0, r]
    lo = meta[1, r]
    frames = x.shape[1]
    width = wv.shape[1]
    halves = width // LANES

    def put(row, value):
        for h in range(halves):
            gp[h, pl.ds(row, value.shape[0]), :] = value[:, h * LANES : (h + 1) * LANES]

    edge_v = dot(halo[0], wv[...])
    edge_g = dot(halo[0], wg[...])
    row = rows_of(2 * EDGE, 0)
    pos = jnp.where(row < EDGE, row - EDGE, row - EDGE + frames)
    edge = jnp.where((pos >= lo) & (pos < hi), edge_v * sigmoid(edge_g), 0.0)
    zero = jnp.zeros((EDGE, width), F32)
    put(0, zero)
    put(EDGE, edge[:EDGE])
    put(2 * EDGE + frames, edge[EDGE:])
    put(3 * EDGE + frames, zero)
    step = block_rows(frames, 512)
    small = block_rows(step, 64)
    for base in range(0, frames, step):
        xb = x[0, base : base + step, :]
        vl_o[0, base : base + step, :] = dot(xb, wv[...])
        sg_o[0, base : base + step, :] = dot(xb, wg[...])

    def gating(i, carry):
        base = pl.multiple_of(i * small, small)
        v = vl_o[0, pl.ds(base, small), :]
        s = sigmoid(sg_o[0, pl.ds(base, small), :])
        sg_o[0, pl.ds(base, small), :] = s
        put(2 * EDGE + base, jnp.where(rows_of(small, base) < hi, v * s, 0.0))
        return carry

    lax.fori_loop(0, frames // small, gating, 0)
    span = frames + 2 * EDGE
    cb = block_rows(span, 104)
    kernel = taps.shape[0]
    margin = (kernel - 1) // 2
    for h in range(halves):
        cols = slice(h * LANES, (h + 1) * LANES)

        def convolve(i, carry):
            s1, s2 = carry
            base = pl.multiple_of(i * cb, 8)
            acc = jnp.zeros((cb, LANES), F32)
            for k in range(kernel):
                acc = acc + taps[k : k + 1, cols] * gp[h, pl.ds(base + EDGE - margin + k, cb), :]
            conv_o[0, pl.ds(base, cb), cols] = acc
            pos = rows_of(cb, base - EDGE)
            kept = jnp.where((pos >= 0) & (pos < jnp.minimum(hi, frames)), acc, 0.0)
            return s1 + fold_rows(kept), s2 + fold_rows(kept * kept)

        none = jnp.zeros((8, LANES), F32)
        s1, s2 = lax.fori_loop(0, span // cb, convolve, (none, none))
        add = jnp.concatenate(
            [jnp.sum(s1, axis=0, keepdims=True), jnp.sum(s2, axis=0, keepdims=True)], axis=0
        )
        st[:, cols] = jnp.where(r == 0, 0.0, st[:, cols]) + add

    @pl.when(r == pl.num_programs(0) - 1)
    def _():
        spread_sums(st_o, st[...])


def batch_norm(stats, count):
    sums = jnp.sum(stats[...], axis=0)
    centre = sums[0:1] / count
    spread = sums[1:2] / count - centre * centre
    return centre, lax.rsqrt(spread + EPSILON)


def norm_kernel(
    meta, count, stats, affine, select, grads, halo, wo, conv,
    swished_o, gn_o, picked_o, st_o, st, ping, pong
):
    r = pl.program_id(0)
    hi = meta[0, r]
    lo = meta[1, r]
    frames = grads.shape[1]
    centre, inv = batch_norm(stats, count[0, 0])
    gain, shift = affine[0:1, :], affine[1:2, :]

    def part(row, swish_grad):
        size = swish_grad.shape[0]
        unit = (conv[0, pl.ds(row, size), :] - centre) * inv
        normalized = unit * gain + shift
        s = sigmoid(normalized)
        pos = rows_of(size, row - EDGE)
        keep = (pos >= lo) & (pos < hi)
        swished = jnp.where(keep, normalized * s, 0.0)
        gn = jnp.where(keep, swish_grad, 0.0) * (s + normalized * (s - s * s))
        gn_o[0, pl.ds(row, size), :] = gn
        return unit, swished, gn

    edge = dot(halo[0], wo[...])
    part(0, edge[:EDGE])
    part(frames + EDGE, edge[EDGE:])
    step = block_rows(frames, 512)
    small = block_rows(step, 32)
    s1 = jnp.zeros((8, conv.shape[2]), F32)
    s2 = s1
    held = (ping, pong)
    ping[...] = dot(grads[0, :step, :], wo[...])
    for i in range(frames // step):
        now = held[i % 2]
        if (i + 1) * step < frames:
            held[(i + 1) % 2][...] = dot(grads[0, (i + 1) * step : (i + 2) * step, :], wo[...])
        picked_o[0, :, i * step : (i + 1) * step] = dot_nt(
            select[...], grads[0, i * step : (i + 1) * step, :]
        ).astype(BF16)
        for j in range(step // small):
            base = i * step + j * small
            unit, swished, gn = part(base + EDGE, now[j * small : (j + 1) * small, :])
            swished_o[0, base : base + small, :] = swished.astype(BF16)
            s1 = s1 + fold_rows(gn)
            s2 = s2 + fold_rows(gn * unit)
    add = jnp.concatenate(
        [jnp.sum(s1, axis=0, keepdims=True), jnp.sum(s2, axis=0, keepdims=True)], axis=0
    )
    st[...] = jnp.where(r == 0, 0.0, st[...]) + add

    @pl.when(r == pl.num_programs(0) - 1)
    def _():
        spread_sums(st_o, st[...])


def back_kernel(
    record, blocks, meta, count, stats, sums, gain, gn, conv, vl, sg, taps, out, taps_o, gc, acc
):
    i = pl.program_id(0)
    frames, width = vl.shape[1:]
    hi = meta[0, record + i // blocks]
    lo = meta[1, record + i // blocks]
    halves = width // LANES
    span = frames + 2 * EDGE
    kernel = taps.shape[0]
    margin = (kernel - 1) // 2
    cb = block_rows(span, 144)
    step = block_rows(frames, 32)
    total_frames = count[0, 0]
    centre, inv = batch_norm(stats, total_frames)
    grad_sums = jnp.sum(sums[...], axis=0)
    scale = gain[...] * inv
    offset = scale * grad_sums[0:1] / total_frames
    slope = scale * inv * grad_sums[1:2] / total_frames
    first = i % blocks * frames

    @pl.when(i == 0)
    def _():
        acc[...] = jnp.zeros_like(acc)

    for h in range(halves):
        cols = slice(h * LANES, (h + 1) * LANES)
        for base in range(0, span, cb):
            pos = rows_of(cb, first + (base - EDGE))
            mean = offset[:, cols] + (conv[0, base : base + cb, cols] - centre[:, cols]) * slope[:, cols]
            gc[h, base : base + cb, :] = scale[:, cols] * gn[0, base : base + cb, cols] - jnp.where(
                (pos >= lo) & (pos < hi), mean, 0.0
            )
        sums_k = [acc[h, k] for k in range(kernel)]
        for base in range(0, frames, step):
            v = vl[0, base : base + step, cols]
            s = sg[0, base : base + step, cols]
            keep = rows_of(step, first + base) < hi
            vs = v * s
            gated = jnp.where(keep, vs, 0.0)
            total = jnp.zeros((step, LANES), F32)
            for k in range(kernel):
                window = gc[h, base + EDGE + margin - k : base + EDGE + margin - k + step, :]
                total = total + taps[k : k + 1, cols] * window
                sums_k[k] = sums_k[k] + fold_rows(window * gated)
            total = jnp.where(keep, total, 0.0)
            out[base : base + step, cols] = (total * s).astype(BF16)
            out[base : base + step, width + h * LANES : width + (h + 1) * LANES] = (
                total * (vs - vs * s)
            ).astype(BF16)
        for k in range(kernel):
            acc[h, k] = sums_k[k]

    @pl.when(i == pl.num_programs(0) - 1)
    def _():
        taps_o[...] = jnp.zeros_like(taps_o)
        for h in range(halves):
            for k in range(kernel):
                taps_o[k : k + 1, h * LANES : (h + 1) * LANES] = jnp.sum(
                    acc[h, k], axis=0, keepdims=True
                )


def partial_kernel(own, sibling, w_own, w_sibling, picked, mine, *others):
    total = dot_nt(w_own[...], own[...]) + dot_nt(w_sibling[...], sibling[...])
    rows = picked.shape[1]
    seqs, _, piece, frames = mine.shape
    mine[...] = (
        (total[:rows] + picked[0].astype(F32)).astype(BF16).reshape(seqs, 1, piece, frames)
    )
    for d, other in enumerate(others):
        other[...] = (
            total[(d + 1) * rows : (d + 2) * rows].astype(BF16).reshape(seqs, 1, piece, frames)
        )


def join_kernel(half, *refs):
    i = pl.program_id(0)

    @pl.when(i < half)
    def _():
        add_kernel(*refs[:-2], refs[-1])

    @pl.when(i >= half)
    def _():
        refs[-1][...] = refs[-2][...]


def add_kernel(*refs):
    total = refs[0][...].astype(F32)
    for other in refs[1:-1]:
        total = total + other[...].astype(F32)
    refs[-1][...] = total.astype(BF16)


def first_outer_kernel(grads, swished, out, acc):
    r = pl.program_id(0)
    add = dot_tn(swished[0], grads[0])
    acc[...] = add + jnp.where(r == 0, 0.0, acc[...])

    @pl.when(r == pl.num_programs(0) - 1)
    def _():
        seqs, _, piece, frames = out.shape
        shard = acc.shape[1] // seqs
        for s in range(seqs):
            for q in range(frames // shard):
                out[s, 0, :, q * shard : (q + 1) * shard] = acc[
                    q * piece : (q + 1) * piece, s * shard : (s + 1) * shard
                ].astype(BF16)


def outer_kernel(groups, parity, x, *refs):
    lefts, taps = refs[: len(groups)], refs[len(groups) : 2 * len(groups)]
    keep, send, acc = refs[2 * len(groups) :]
    records = groups[-1][0] + groups[-1][1]
    width = acc.shape[0] // 2
    shard = keep.shape[2]
    r = pl.program_id(0)
    for (first, size), left in zip(groups, lefts):

        @pl.when((r >= first) & (r < first + size))
        def _(left=left):
            add = dot_tn(left[...], x[0])
            acc[...] = add + jnp.where(r == 0, 0.0, acc[...])

    @pl.when(r == records - 1)
    def _():
        tap_sums = taps[0][...]
        for part in taps[1:]:
            tap_sums = tap_sums + part[...]

        def write(place, odd):
            for j in range(place.shape[0]):
                at = (2 * j + odd) * shard
                place[j, : 2 * width, :] = acc[:, at : at + shard].astype(BF16)
                for q in range(width // shard):
                    row = 2 * width + 16 * q
                    place[j, row : row + 16, :] = tap_sums[:, q * shard : (q + 1) * shard].astype(
                        BF16
                    )

        @pl.when(parity[0, 0] == 0)
        def _():
            write(keep, 0)
            write(send, 1)

        @pl.when(parity[0, 0] != 0)
        def _():
            write(keep, 1)
            write(send, 0)


def fold_kernel(parity, own, other, keep, send):
    def write(place, odd):
        for j in range(place.shape[0]):
            total = own[2 * j + odd].astype(F32) + other[2 * j + odd].astype(F32)
            place[j] = total.astype(BF16)

    @pl.when(parity[0, 0] == 0)
    def _():
        write(keep, 0)
        write(send, 1)

    @pl.when(parity[0, 0] != 0)
    def _():
        write(keep, 1)
        write(send, 0)


def finish_kernel(kernel, own, other, pieces, value, gate, out, taps):
    width = value.shape[1]
    shard = value.shape[0]

    def total(row, size):
        return own[0, row : row + size, :].astype(F32) + other[0, row : row + size, :].astype(F32)

    value[...] = total(0, width).T
    gate[...] = total(width, width).T
    ready = pieces[0, 0].astype(F32)
    for s in range(1, pieces.shape[0]):
        ready = ready + pieces[s, 0].astype(F32)
    blocks = [ready[:, q * shard : (q + 1) * shard] for q in range(ready.shape[1] // shard)]
    out[...] = jnp.concatenate(blocks, axis=0).T
    for q in range(width // shard):
        taps[:, q * shard : (q + 1) * shard] = total(2 * width + 16 * q, 16)[:kernel]


def place_kernel(moved, *refs):
    out = refs[-1]
    frames = moved.shape[3]
    for s in range(moved.shape[0]):
        out[0, :, s * frames : (s + 1) * frames] = moved[s, 0]


def exchange(copies, axis):
    return lax.all_to_all(copies, axis, 0, 0, tiled=True)


def per_device(
    normed,
    grad_out,
    value_weight,
    gate_weight,
    depth_taps,
    norm_gain,
    norm_shift,
    out_weight,
    lengths,
):
    recs, frames, model = normed.shape
    kernel = depth_taps.shape[0]
    width = value_weight.shape[1]
    seqs = lax.axis_size("seq")
    tps = lax.axis_size("tp")
    chips = tps // 2
    piece = model // (seqs * tps)
    rows = seqs * piece
    shard = model // seqs
    span = frames + 2 * EDGE
    seq_at = lax.axis_index("seq")
    tp_at = lax.axis_index("tp")
    chip_at, core_at = tp_at // 2, tp_at % 2
    count = jnp.sum(lengths).astype(F32)
    first = (seq_at * frames).astype(jnp.int32)
    meta = jnp.stack([lengths - first, jnp.full((recs,), 0, jnp.int32) - first])
    halves = width // LANES
    counts = count.reshape(1, 1)
    parity = (seq_at % 2).astype(jnp.int32).reshape(1, 1)
    sds = jax.ShapeDtypeStruct

    low_edge = jnp.concatenate([normed[:, -EDGE:], grad_out[:, -EDGE:]], axis=2)
    high_edge = jnp.concatenate([normed[:, :EDGE], grad_out[:, :EDGE]], axis=2)
    up = [(i, i + 1) for i in range(seqs - 1)]
    down = [(j, i) for i, j in up]
    halo = jnp.concatenate(
        [lax.ppermute(low_edge, "seq", up), lax.ppermute(high_edge, "seq", down)], axis=1
    )
    halo_x, halo_g = halo[:, :, :model], halo[:, :, model:]

    channel = (
        jnp.arange(seqs, dtype=jnp.int32)[:, None] * (tps * piece)
        + tp_at * piece
        + jnp.arange(piece, dtype=jnp.int32)[None, :]
    ).reshape(rows, 1)
    select = (channel == jnp.arange(model, dtype=jnp.int32)[None, :]).astype(BF16)
    array_bytes = recs * frames * width * 4
    input_bytes = recs * frames * model * 2
    matmul = 2 * recs * frames * model * width

    vl, sg, conv, stats = call(
        gate_kernel,
        "gate_conv",
        (recs,),
        [
            smem(),
            per_record((frames, model)),
            per_record((2 * EDGE, model)),
            whole((model, width)),
            whole((model, width)),
            whole((kernel, width)),
        ],
        [
            per_record((frames, width)),
            per_record((frames, width)),
            per_record((span, width)),
            whole((seqs, 2, width)),
        ],
        [
            sds((recs, frames, width), F32),
            sds((recs, frames, width), F32),
            sds((recs, span, width), F32),
            sds((seqs, 2, width), F32),
        ],
        [pltpu.VMEM((halves, frames + 4 * EDGE, LANES), F32), pltpu.VMEM((2, width), F32)],
        2 * matmul,
        input_bytes + 3 * array_bytes,
    )(meta, normed, halo_x, value_weight, gate_weight, depth_taps)
    both = jnp.concatenate([after(value_weight, stats), gate_weight], axis=1).reshape(seqs, tps, piece, 2 * width)

    def chosen(core):
        picks = [
            lax.dynamic_index_in_dim(both, ((chip_at + d) % chips) * 2 + core, 1, keepdims=False)
            for d in range(chips)
        ]
        return jnp.stack(picks).reshape(chips * rows, 2 * width)

    swap = [(i, i ^ 1) for i in range(tps)]
    w_own = chosen(core_at)
    w_sibling = lax.ppermute(chosen(1 - core_at), "tp", swap)

    stats = exchange(stats, "seq")

    chunk = block_rows(frames, 256)
    half_rows = block_rows(frames, 512)
    swished, gn, picked, sums = call(
        norm_kernel,
        "swish_norm",
        (recs,),
        [
            smem(),
            smem(),
            whole((seqs, 2, width)),
            whole((2, width)),
            whole((rows, model)),
            per_record((frames, model)),
            per_record((2 * EDGE, model)),
            whole((model, width)),
            per_record((span, width)),
        ],
        [
            per_record((frames, width)),
            per_record((span, width)),
            per_record((rows, frames)),
            whole((seqs, 2, width)),
        ],
        [
            sds((recs, frames, width), BF16),
            sds((recs, span, width), F32),
            sds((recs, rows, frames), BF16),
            sds((seqs, 2, width), F32),
        ],
        [
            pltpu.VMEM((2, width), F32),
            pltpu.VMEM((block_rows(frames, 512), width), F32),
            pltpu.VMEM((block_rows(frames, 512), width), F32),
        ],
        2 * matmul,
        input_bytes + 3 * array_bytes,
    )(
        meta,
        counts,
        stats,
        jnp.stack([norm_gain, norm_shift]),
        after(select, w_own, w_sibling),
        grad_out,
        halo_g,
        out_weight,
        conv,
    )
    w_out = call(
        first_outer_kernel,
        "outer_w_out",
        (recs,),
        [per_record((frames, model)), per_record((frames, width))],
        whole((seqs, 1, piece, frames)),
        sds((seqs, 1, piece, frames), BF16),
        [pltpu.VMEM((width, model), F32)],
        matmul,
        input_bytes,
    )(grad_out, swished)
    sums = exchange(sums, "seq")
    grad_shift, grad_gain = jnp.sum(sums, axis=0)

    blocks = frames // chunk
    parts_in = frames // half_rows

    def back(first, size, *earlier):
        def window(i):
            return (first + i // blocks, pl.multiple_of(i % blocks * chunk, chunk), 0)

        def block(i):
            return (first + i // blocks, i % blocks, 0)

        return call(
            functools.partial(back_kernel, first, blocks),
            "back_conv",
            (size * blocks,),
            [
                smem(),
                smem(),
                whole((seqs, 2, width)),
                whole((seqs, 2, width)),
                whole((1, width)),
                pl.BlockSpec((pl.Element(1), pl.Element(chunk + 2 * EDGE), pl.Element(width)), window),
                pl.BlockSpec((pl.Element(1), pl.Element(chunk + 2 * EDGE), pl.Element(width)), window),
                pl.BlockSpec((1, chunk, width), block),
                pl.BlockSpec((1, chunk, width), block),
                whole((kernel, width)),
            ],
            [pl.BlockSpec((chunk, 2 * width), lambda i: (i, 0)), whole((16, width))],
            [sds((size * frames, 2 * width), BF16), sds((16, width), F32)],
            [
                pltpu.VMEM((halves, chunk + 2 * EDGE, LANES), F32),
                pltpu.VMEM((halves, kernel, 8, LANES), F32),
            ],
            0,
            1024,
        )(meta, counts, stats, sums, norm_gain[None], gn, conv, vl, sg, after(depth_taps, *earlier))

    def partials(first, size, mine, *earlier):
        sibling = lax.ppermute(mine, "tp", swap)
        out = sds((seqs, size, piece, frames), BF16)
        return call(
            partial_kernel,
            "partial_in",
            (size * parts_in,),
            [
                pl.BlockSpec((half_rows, 2 * width), lambda i: (i, 0)),
                pl.BlockSpec((half_rows, 2 * width), lambda i: (i, 0)),
                whole((chips * rows, 2 * width)),
                whole((chips * rows, 2 * width)),
                pl.BlockSpec(
                    (1, rows, half_rows), lambda i: (first + i // parts_in, 0, i % parts_in)
                ),
            ],
            [
                pl.BlockSpec(
                    (seqs, 1, piece, half_rows), lambda i: (0, i // parts_in, 0, i % parts_in)
                )
            ]
            * chips,
            [out] * chips,
            [],
            0,
            1024,
        )(mine, sibling, after(w_own, *earlier), w_sibling, picked)

    def deliver(part, weight, *earlier, extra=None):
        arrived = []
        for d in range(1, chips):
            send = [(i, ((i // 2 + d) % chips) * 2 + i % 2) for i in range(tps)]
            arrived.append(lax.ppermute(part[d], "tp", send))
        size = part[0].shape[1]
        block = pl.BlockSpec(
            (seqs, 1, piece, half_rows), lambda i: (0, i // parts_in, 0, i % parts_in)
        )
        if extra is None:
            return call(
                add_kernel,
                "add",
                (size * parts_in,),
                [block] * chips,
                block,
                sds(part[0].shape, BF16),
                [],
                weight,
                1024,
            )(after(part[0], *earlier), *arrived)
        one = pl.BlockSpec((seqs, 1, piece, half_rows), lambda i: (0, 0, 0, i % parts_in))
        return call(
            functools.partial(join_kernel, parts_in),
            "add_join",
            (2 * parts_in,),
            [one] * (chips + 1),
            block,
            sds((seqs, 2, piece, frames), BF16),
            [],
            weight,
            1024,
        )(after(part[0], *earlier), *arrived, extra)

    groups = ((0, 1), (1, 1), (2, recs - 2))
    grads = [None] * 3
    taps = [None] * 3
    parts = [None] * 3
    owns = [None] * 3
    moved = [None] * 3
    grads[0], taps[0] = back(*groups[0], w_out)
    grads[1], taps[1] = back(*groups[1], grads[0])
    parts[0] = partials(*groups[0], grads[0], grads[1])
    grads[2], taps[2] = back(*groups[2], *parts[0])
    parts[1] = partials(*groups[1], grads[1], grads[2])
    owns[0] = deliver(parts[0], LONG, *parts[1], extra=w_out)
    moved[0] = exchange(owns[0], "seq")
    parts[2] = partials(*groups[2], grads[2], owns[0])

    slots = 2 * width + 16 * (width // shard)
    half = sds((seqs // 2, slots, shard), BF16)
    keep, send = call(
        functools.partial(outer_kernel, groups),
        "outer_w_in",
        (recs,),
        [smem(), per_record((frames, model))]
        + [
            pl.BlockSpec(
                (frames, 2 * width),
                lambda r, first=first, size=size: (jnp.clip(r - first, 0, size - 1), 0),
            )
            for first, size in groups
        ]
        + [whole((16, width))] * len(groups),
        [whole(half.shape)] * 2,
        [half] * 2,
        [pltpu.VMEM((2 * width, model), F32)],
        LONG,
        1024,
    )(parity, after(normed, *parts[2]), *grads, *taps)
    owns[1] = deliver(parts[1], LONG, keep)
    moved[1] = exchange(after(owns[1], moved[0]), "seq")
    bit = 1
    while True:
        others = lax.ppermute(send, "seq", [(i, i ^ bit) for i in range(seqs)])
        if bit == 1:
            owns[2] = deliver(parts[2], LONG, others, owns[1])
            moved[2] = exchange(after(owns[2], moved[1]), "seq")
        bit *= 2
        if bit == seqs:
            break
        if bit == 2:
            keep = after(keep, owns[2])
        shape = (keep.shape[0] // 2,) + keep.shape[1:]
        side = ((seq_at // bit) % 2).astype(jnp.int32).reshape(1, 1)
        keep, send = call(
            fold_kernel,
            "fold",
            (1,),
            [smem()] + [whole(keep.shape)] * 2,
            [whole(shape)] * 2,
            [sds(shape, BF16)] * 2,
            [],
            0,
            1024,
            vmem=20,
        )(side, keep, others)
    w_value, w_gate, w_out, grad_taps = call(
        functools.partial(finish_kernel, kernel),
        "finish",
        (1,),
        [whole(keep.shape)] * 2
        + [pl.BlockSpec((seqs, 1, piece, frames), lambda i: (0, 1, 0, 0))],
        [whole((shard, width))] * 3 + [whole((kernel, width))],
        [sds((shard, width), F32)] * 3 + [sds((kernel, width), F32)],
        [],
        0,
        1024,
        vmem=20,
    )(keep, others, moved[0])
    grad_in = ()
    for (first, size), part in zip(groups, moved):
        grad_in = (
            call(
                place_kernel,
                "place",
                (size,),
                [pl.BlockSpec((seqs, 1, piece, frames), lambda i: (0, i, 0, 0))]
                + [anywhere()] * len(grad_in),
                pl.BlockSpec((1, piece, seqs * frames), lambda i, first=first: (first + i, 0, 0)),
                sds((recs, piece, seqs * frames), BF16),
                [],
                0,
                4 * size * piece * seqs * frames,
                {1: 0} if grad_in else None,
                vmem=20,
            )(part, *grad_in),
        )
    (grad_in,) = grad_in
    return (grad_in, w_value, w_gate, w_out, grad_taps, grad_gain, grad_shift)


def solution(mesh):
    placed = (
        P(None, "seq", None),
        P(None, "seq", None),
        P(None, "tp"),
        P(None, "tp"),
        P(None, "tp"),
        P("tp"),
        P("tp"),
        P(None, "tp"),
        P(),
    )
    return jax.shard_map(
        per_device,
        mesh=mesh,
        in_specs=placed,
        out_specs=(
            P(None, ("seq", "tp"), None),
            P("seq", "tp"),
            P("seq", "tp"),
            P("seq", "tp"),
            P(None, "tp"),
            P("tp"),
            P("tp"),
        ),
        check_vma=False,
    )
```

```python
import functools

import jax
import jax.numpy as jnp
from jax import lax
from jax.experimental import pallas as pl
from jax.experimental.pallas import tpu as pltpu
from jax.sharding import PartitionSpec as P

EPSILON = 1e-05
EDGE = 8
LANES = 128
LONG = 50_000_000_000
F32 = jnp.float32
BF16 = jnp.bfloat16


def sigmoid(x):
    return 0.5 * jnp.tanh(0.5 * x) + 0.5


def dot(a, b):
    return jnp.dot(a, b, preferred_element_type=F32)


def dot_nt(a, b):
    return lax.dot_general(a, b, (((1,), (1,)), ((), ())), preferred_element_type=F32)


def dot_tn(a, b):
    return lax.dot_general(a, b, (((0,), (0,)), ((), ())), preferred_element_type=F32)


def rows_of(count, first):
    return first + lax.broadcasted_iota(jnp.int32, (count, 1), 0)


def fold_rows(x):
    return jnp.sum(x.reshape(x.shape[0] // 8, 8, x.shape[1]), axis=0)


def block_rows(total, most):
    return max(b for b in range(8, most + 1, 8) if total % b == 0)


def whole(shape):
    return pl.BlockSpec(shape, lambda *i: (0,) * len(shape))


def per_record(shape):
    return pl.BlockSpec((1,) + shape, lambda r: (r,) + (0,) * len(shape))


def smem():
    return pl.BlockSpec(memory_space=pltpu.SMEM)


def anywhere():
    return pl.BlockSpec(memory_space=pl.ANY)


def after(x, *earlier):
    return lax.optimization_barrier((x,) + earlier)[0]


def spread_sums(out, sums):
    for s in range(out.shape[0]):
        out[s] = sums


def call(
    kernel, name, grid, in_specs, out_specs, out_shape, scratch, flops, moved, aliases=None, vmem=63
):
    return pl.pallas_call(
        kernel,
        name=name,
        grid=grid,
        in_specs=in_specs,
        out_specs=out_specs,
        out_shape=out_shape,
        scratch_shapes=scratch,
        input_output_aliases=aliases or {},
        cost_estimate=pl.CostEstimate(flops=int(flops), bytes_accessed=int(moved), transcendentals=0),
        compiler_params=pltpu.CompilerParams(vmem_limit_bytes=vmem * 1024 * 1024),
    )


def gate_kernel(meta, x, halo, wv, wg, taps, vl_o, sg_o, conv_o, st_o, gp, st):
    r = pl.program_id(0)
    hi = meta[0, r]
    lo = meta[1, r]
    frames = x.shape[1]
    width = wv.shape[1]
    halves = width // LANES

    def put(row, value):
        for h in range(halves):
            gp[h, pl.ds(row, value.shape[0]), :] = value[:, h * LANES : (h + 1) * LANES]

    edge_v = dot(halo[0], wv[...])
    edge_g = dot(halo[0], wg[...])
    row = rows_of(2 * EDGE, 0)
    pos = jnp.where(row < EDGE, row - EDGE, row - EDGE + frames)
    edge = jnp.where((pos >= lo) & (pos < hi), edge_v * sigmoid(edge_g), 0.0)
    zero = jnp.zeros((EDGE, width), F32)
    put(0, zero)
    put(EDGE, edge[:EDGE])
    put(2 * EDGE + frames, edge[EDGE:])
    put(3 * EDGE + frames, zero)
    step = block_rows(frames, 512)
    small = block_rows(step, 64)
    for base in range(0, frames, step):
        xb = x[0, base : base + step, :]
        vl_o[0, base : base + step, :] = dot(xb, wv[...])
        sg_o[0, base : base + step, :] = dot(xb, wg[...])

    def gating(i, carry):
        base = pl.multiple_of(i * small, small)
        v = vl_o[0, pl.ds(base, small), :]
        s = sigmoid(sg_o[0, pl.ds(base, small), :])
        sg_o[0, pl.ds(base, small), :] = s
        put(2 * EDGE + base, jnp.where(rows_of(small, base) < hi, v * s, 0.0))
        return carry

    lax.fori_loop(0, frames // small, gating, 0)
    span = frames + 2 * EDGE
    cb = block_rows(span, 104)
    kernel = taps.shape[0]
    margin = (kernel - 1) // 2
    for h in range(halves):
        cols = slice(h * LANES, (h + 1) * LANES)

        def convolve(i, carry):
            s1, s2 = carry
            base = pl.multiple_of(i * cb, 8)
            acc = jnp.zeros((cb, LANES), F32)
            for k in range(kernel):
                acc = acc + taps[k : k + 1, cols] * gp[h, pl.ds(base + EDGE - margin + k, cb), :]
            conv_o[0, pl.ds(base, cb), cols] = acc
            pos = rows_of(cb, base - EDGE)
            kept = jnp.where((pos >= 0) & (pos < jnp.minimum(hi, frames)), acc, 0.0)
            return s1 + fold_rows(kept), s2 + fold_rows(kept * kept)

        none = jnp.zeros((8, LANES), F32)
        s1, s2 = lax.fori_loop(0, span // cb, convolve, (none, none))
        add = jnp.concatenate(
            [jnp.sum(s1, axis=0, keepdims=True), jnp.sum(s2, axis=0, keepdims=True)], axis=0
        )
        st[:, cols] = jnp.where(r == 0, 0.0, st[:, cols]) + add

    @pl.when(r == pl.num_programs(0) - 1)
    def _():
        spread_sums(st_o, st[...])


def batch_norm(stats, count):
    sums = jnp.sum(stats[...], axis=0)
    centre = sums[0:1] / count
    spread = sums[1:2] / count - centre * centre
    return centre, lax.rsqrt(spread + EPSILON)


def norm_kernel(
    meta, count, stats, affine, select, grads, halo, wo, conv,
    swished_o, gn_o, picked_o, st_o, st, ping, pong
):
    r = pl.program_id(0)
    hi = meta[0, r]
    lo = meta[1, r]
    frames = grads.shape[1]
    centre, inv = batch_norm(stats, count[0, 0])
    gain, shift = affine[0:1, :], affine[1:2, :]

    def part(row, swish_grad):
        size = swish_grad.shape[0]
        unit = (conv[0, pl.ds(row, size), :] - centre) * inv
        normalized = unit * gain + shift
        s = sigmoid(normalized)
        pos = rows_of(size, row - EDGE)
        keep = (pos >= lo) & (pos < hi)
        swished = jnp.where(keep, normalized * s, 0.0)
        gn = jnp.where(keep, swish_grad, 0.0) * (s + normalized * (s - s * s))
        gn_o[0, pl.ds(row, size), :] = gn
        return unit, swished, gn

    edge = dot(halo[0], wo[...])
    part(0, edge[:EDGE])
    part(frames + EDGE, edge[EDGE:])
    step = block_rows(frames, 512)
    small = block_rows(step, 32)
    s1 = jnp.zeros((8, conv.shape[2]), F32)
    s2 = s1
    held = (ping, pong)
    ping[...] = dot(grads[0, :step, :], wo[...])
    for i in range(frames // step):
        now = held[i % 2]
        if (i + 1) * step < frames:
            held[(i + 1) % 2][...] = dot(grads[0, (i + 1) * step : (i + 2) * step, :], wo[...])
        picked_o[0, :, i * step : (i + 1) * step] = dot_nt(
            select[...], grads[0, i * step : (i + 1) * step, :]
        ).astype(BF16)
        for j in range(step // small):
            base = i * step + j * small
            unit, swished, gn = part(base + EDGE, now[j * small : (j + 1) * small, :])
            swished_o[0, base : base + small, :] = swished.astype(BF16)
            s1 = s1 + fold_rows(gn)
            s2 = s2 + fold_rows(gn * unit)
    add = jnp.concatenate(
        [jnp.sum(s1, axis=0, keepdims=True), jnp.sum(s2, axis=0, keepdims=True)], axis=0
    )
    st[...] = jnp.where(r == 0, 0.0, st[...]) + add

    @pl.when(r == pl.num_programs(0) - 1)
    def _():
        spread_sums(st_o, st[...])


def back_kernel(
    record, blocks, meta, count, stats, sums, gain, gn, conv, vl, sg, taps, out, taps_o, gc, acc
):
    i = pl.program_id(0)
    frames, width = vl.shape[1:]
    hi = meta[0, record + i // blocks]
    lo = meta[1, record + i // blocks]
    halves = width // LANES
    span = frames + 2 * EDGE
    kernel = taps.shape[0]
    margin = (kernel - 1) // 2
    cb = block_rows(span, 144)
    step = block_rows(frames, 32)
    total_frames = count[0, 0]
    centre, inv = batch_norm(stats, total_frames)
    grad_sums = jnp.sum(sums[...], axis=0)
    scale = gain[...] * inv
    offset = scale * grad_sums[0:1] / total_frames
    slope = scale * inv * grad_sums[1:2] / total_frames
    first = i % blocks * frames

    @pl.when(i == 0)
    def _():
        acc[...] = jnp.zeros_like(acc)

    for h in range(halves):
        cols = slice(h * LANES, (h + 1) * LANES)
        for base in range(0, span, cb):
            pos = rows_of(cb, first + (base - EDGE))
            mean = offset[:, cols] + (conv[0, base : base + cb, cols] - centre[:, cols]) * slope[:, cols]
            gc[h, base : base + cb, :] = scale[:, cols] * gn[0, base : base + cb, cols] - jnp.where(
                (pos >= lo) & (pos < hi), mean, 0.0
            )
        sums_k = [acc[h, k] for k in range(kernel)]
        for base in range(0, frames, step):
            v = vl[0, base : base + step, cols]
            s = sg[0, base : base + step, cols]
            keep = rows_of(step, first + base) < hi
            vs = v * s
            gated = jnp.where(keep, vs, 0.0)
            total = jnp.zeros((step, LANES), F32)
            for k in range(kernel):
                window = gc[h, base + EDGE + margin - k : base + EDGE + margin - k + step, :]
                total = total + taps[k : k + 1, cols] * window
                sums_k[k] = sums_k[k] + fold_rows(window * gated)
            total = jnp.where(keep, total, 0.0)
            out[base : base + step, cols] = (total * s).astype(BF16)
            out[base : base + step, width + h * LANES : width + (h + 1) * LANES] = (
                total * (vs - vs * s)
            ).astype(BF16)
        for k in range(kernel):
            acc[h, k] = sums_k[k]

    @pl.when(i == pl.num_programs(0) - 1)
    def _():
        taps_o[...] = jnp.zeros_like(taps_o)
        for h in range(halves):
            for k in range(kernel):
                taps_o[k : k + 1, h * LANES : (h + 1) * LANES] = jnp.sum(
                    acc[h, k], axis=0, keepdims=True
                )


def partial_kernel(own, sibling, w_own, w_sibling, picked, mine, *others):
    total = dot_nt(w_own[...], own[...]) + dot_nt(w_sibling[...], sibling[...])
    rows = picked.shape[1]
    seqs, _, piece, frames = mine.shape
    mine[...] = (
        (total[:rows] + picked[0].astype(F32)).astype(BF16).reshape(seqs, 1, piece, frames)
    )
    for d, other in enumerate(others):
        other[...] = (
            total[(d + 1) * rows : (d + 2) * rows].astype(BF16).reshape(seqs, 1, piece, frames)
        )


def join_kernel(half, *refs):
    i = pl.program_id(0)

    @pl.when(i < half)
    def _():
        add_kernel(*refs[:-2], refs[-1])

    @pl.when(i >= half)
    def _():
        refs[-1][...] = refs[-2][...]


def add_kernel(*refs):
    total = refs[0][...].astype(F32)
    for other in refs[1:-1]:
        total = total + other[...].astype(F32)
    refs[-1][...] = total.astype(BF16)


def first_outer_kernel(grads, swished, out, acc):
    r = pl.program_id(0)
    add = dot_tn(swished[0], grads[0])
    acc[...] = add + jnp.where(r == 0, 0.0, acc[...])

    @pl.when(r == pl.num_programs(0) - 1)
    def _():
        seqs, _, piece, frames = out.shape
        shard = acc.shape[1] // seqs
        for s in range(seqs):
            for q in range(frames // shard):
                out[s, 0, :, q * shard : (q + 1) * shard] = acc[
                    q * piece : (q + 1) * piece, s * shard : (s + 1) * shard
                ].astype(BF16)


def outer_kernel(groups, parity, x, *refs):
    lefts, taps = refs[: len(groups)], refs[len(groups) : 2 * len(groups)]
    keep, send, acc = refs[2 * len(groups) :]
    records = groups[-1][0] + groups[-1][1]
    width = acc.shape[0] // 2
    shard = keep.shape[2]
    r = pl.program_id(0)
    for (first, size), left in zip(groups, lefts):

        @pl.when((r >= first) & (r < first + size))
        def _(left=left):
            add = dot_tn(left[...], x[0])
            acc[...] = add + jnp.where(r == 0, 0.0, acc[...])

    @pl.when(r == records - 1)
    def _():
        tap_sums = taps[0][...]
        for part in taps[1:]:
            tap_sums = tap_sums + part[...]

        def write(place, odd):
            for j in range(place.shape[0]):
                at = (2 * j + odd) * shard
                place[j, : 2 * width, :] = acc[:, at : at + shard].astype(BF16)
                for q in range(width // shard):
                    row = 2 * width + 16 * q
                    place[j, row : row + 16, :] = tap_sums[:, q * shard : (q + 1) * shard].astype(
                        BF16
                    )

        @pl.when(parity[0, 0] == 0)
        def _():
            write(keep, 0)
            write(send, 1)

        @pl.when(parity[0, 0] != 0)
        def _():
            write(keep, 1)
            write(send, 0)


def fold_kernel(parity, own, other, keep, send):
    def write(place, odd):
        for j in range(place.shape[0]):
            total = own[2 * j + odd].astype(F32) + other[2 * j + odd].astype(F32)
            place[j] = total.astype(BF16)

    @pl.when(parity[0, 0] == 0)
    def _():
        write(keep, 0)
        write(send, 1)

    @pl.when(parity[0, 0] != 0)
    def _():
        write(keep, 1)
        write(send, 0)


def finish_kernel(kernel, own, other, value, gate, taps):
    width = value.shape[1]
    shard = value.shape[0]

    def total(row, size):
        return own[0, row : row + size, :].astype(F32) + other[0, row : row + size, :].astype(F32)

    value[...] = total(0, width).T
    gate[...] = total(width, width).T
    for q in range(width // shard):
        taps[:, q * shard : (q + 1) * shard] = total(2 * width + 16 * q, 16)[:kernel]


def finish_out_kernel(pieces, out):
    shard = out.shape[0]
    ready = pieces[0, 0].astype(F32)
    for s in range(1, pieces.shape[0]):
        ready = ready + pieces[s, 0].astype(F32)
    blocks = [ready[:, q * shard : (q + 1) * shard] for q in range(ready.shape[1] // shard)]
    out[...] = jnp.concatenate(blocks, axis=0).T


def place_kernel(moved, *refs):
    out = refs[-1]
    frames = moved.shape[3]
    for s in range(moved.shape[0]):
        out[0, :, s * frames : (s + 1) * frames] = moved[s, 0]


def exchange(copies, axis):
    return lax.all_to_all(copies, axis, 0, 0, tiled=True)


def per_device(
    normed,
    grad_out,
    value_weight,
    gate_weight,
    depth_taps,
    norm_gain,
    norm_shift,
    out_weight,
    lengths,
):
    recs, frames, model = normed.shape
    kernel = depth_taps.shape[0]
    width = value_weight.shape[1]
    seqs = lax.axis_size("seq")
    tps = lax.axis_size("tp")
    chips = tps // 2
    piece = model // (seqs * tps)
    rows = seqs * piece
    shard = model // seqs
    span = frames + 2 * EDGE
    seq_at = lax.axis_index("seq")
    tp_at = lax.axis_index("tp")
    chip_at, core_at = tp_at // 2, tp_at % 2
    count = jnp.sum(lengths).astype(F32)
    first = (seq_at * frames).astype(jnp.int32)
    meta = jnp.stack([lengths - first, jnp.full((recs,), 0, jnp.int32) - first])
    halves = width // LANES
    counts = count.reshape(1, 1)
    parity = (seq_at % 2).astype(jnp.int32).reshape(1, 1)
    sds = jax.ShapeDtypeStruct

    low_edge = jnp.concatenate([normed[:, -EDGE:], grad_out[:, -EDGE:]], axis=2)
    high_edge = jnp.concatenate([normed[:, :EDGE], grad_out[:, :EDGE]], axis=2)
    up = [(i, i + 1) for i in range(seqs - 1)]
    down = [(j, i) for i, j in up]
    halo = jnp.concatenate(
        [lax.ppermute(low_edge, "seq", up), lax.ppermute(high_edge, "seq", down)], axis=1
    )
    halo_x, halo_g = halo[:, :, :model], halo[:, :, model:]

    channel = (
        jnp.arange(seqs, dtype=jnp.int32)[:, None] * (tps * piece)
        + tp_at * piece
        + jnp.arange(piece, dtype=jnp.int32)[None, :]
    ).reshape(rows, 1)
    select = (channel == jnp.arange(model, dtype=jnp.int32)[None, :]).astype(BF16)
    array_bytes = recs * frames * width * 4
    input_bytes = recs * frames * model * 2
    matmul = 2 * recs * frames * model * width

    vl, sg, conv, stats = call(
        gate_kernel,
        "gate_conv",
        (recs,),
        [
            smem(),
            per_record((frames, model)),
            per_record((2 * EDGE, model)),
            whole((model, width)),
            whole((model, width)),
            whole((kernel, width)),
        ],
        [
            per_record((frames, width)),
            per_record((frames, width)),
            per_record((span, width)),
            whole((seqs, 2, width)),
        ],
        [
            sds((recs, frames, width), F32),
            sds((recs, frames, width), F32),
            sds((recs, span, width), F32),
            sds((seqs, 2, width), F32),
        ],
        [pltpu.VMEM((halves, frames + 4 * EDGE, LANES), F32), pltpu.VMEM((2, width), F32)],
        2 * matmul,
        input_bytes + 3 * array_bytes,
    )(meta, normed, halo_x, value_weight, gate_weight, depth_taps)
    both = jnp.concatenate([after(value_weight, stats), gate_weight], axis=1).reshape(seqs, tps, piece, 2 * width)

    def chosen(core):
        picks = [
            lax.dynamic_index_in_dim(both, ((chip_at + d) % chips) * 2 + core, 1, keepdims=False)
            for d in range(chips)
        ]
        return jnp.stack(picks).reshape(chips * rows, 2 * width)

    swap = [(i, i ^ 1) for i in range(tps)]
    w_own = chosen(core_at)
    w_sibling = lax.ppermute(chosen(1 - core_at), "tp", swap)

    stats = exchange(stats, "seq")

    chunk = block_rows(frames, 256)
    half_rows = block_rows(frames, 512)
    swished, gn, picked, sums = call(
        norm_kernel,
        "swish_norm",
        (recs,),
        [
            smem(),
            smem(),
            whole((seqs, 2, width)),
            whole((2, width)),
            whole((rows, model)),
            per_record((frames, model)),
            per_record((2 * EDGE, model)),
            whole((model, width)),
            per_record((span, width)),
        ],
        [
            per_record((frames, width)),
            per_record((span, width)),
            per_record((rows, frames)),
            whole((seqs, 2, width)),
        ],
        [
            sds((recs, frames, width), BF16),
            sds((recs, span, width), F32),
            sds((recs, rows, frames), BF16),
            sds((seqs, 2, width), F32),
        ],
        [
            pltpu.VMEM((2, width), F32),
            pltpu.VMEM((block_rows(frames, 512), width), F32),
            pltpu.VMEM((block_rows(frames, 512), width), F32),
        ],
        2 * matmul,
        input_bytes + 3 * array_bytes,
    )(
        meta,
        counts,
        stats,
        jnp.stack([norm_gain, norm_shift]),
        after(select, w_own, w_sibling),
        grad_out,
        halo_g,
        out_weight,
        conv,
    )
    w_out = call(
        first_outer_kernel,
        "outer_w_out",
        (recs,),
        [per_record((frames, model)), per_record((frames, width))],
        whole((seqs, 1, piece, frames)),
        sds((seqs, 1, piece, frames), BF16),
        [pltpu.VMEM((width, model), F32)],
        matmul,
        input_bytes,
    )(grad_out, swished)
    sums = exchange(sums, "seq")
    grad_shift, grad_gain = jnp.sum(sums, axis=0)

    blocks = frames // chunk
    parts_in = frames // half_rows

    def back(first, size, *earlier):
        def window(i):
            return (first + i // blocks, pl.multiple_of(i % blocks * chunk, chunk), 0)

        def block(i):
            return (first + i // blocks, i % blocks, 0)

        return call(
            functools.partial(back_kernel, first, blocks),
            "back_conv",
            (size * blocks,),
            [
                smem(),
                smem(),
                whole((seqs, 2, width)),
                whole((seqs, 2, width)),
                whole((1, width)),
                pl.BlockSpec((pl.Element(1), pl.Element(chunk + 2 * EDGE), pl.Element(width)), window),
                pl.BlockSpec((pl.Element(1), pl.Element(chunk + 2 * EDGE), pl.Element(width)), window),
                pl.BlockSpec((1, chunk, width), block),
                pl.BlockSpec((1, chunk, width), block),
                whole((kernel, width)),
            ],
            [pl.BlockSpec((chunk, 2 * width), lambda i: (i, 0)), whole((16, width))],
            [sds((size * frames, 2 * width), BF16), sds((16, width), F32)],
            [
                pltpu.VMEM((halves, chunk + 2 * EDGE, LANES), F32),
                pltpu.VMEM((halves, kernel, 8, LANES), F32),
            ],
            0,
            1024,
        )(meta, counts, stats, sums, norm_gain[None], gn, conv, vl, sg, after(depth_taps, *earlier))

    def partials(first, size, mine, *earlier):
        sibling = lax.ppermute(mine, "tp", swap)
        out = sds((seqs, size, piece, frames), BF16)
        return call(
            partial_kernel,
            "partial_in",
            (size * parts_in,),
            [
                pl.BlockSpec((half_rows, 2 * width), lambda i: (i, 0)),
                pl.BlockSpec((half_rows, 2 * width), lambda i: (i, 0)),
                whole((chips * rows, 2 * width)),
                whole((chips * rows, 2 * width)),
                pl.BlockSpec(
                    (1, rows, half_rows), lambda i: (first + i // parts_in, 0, i % parts_in)
                ),
            ],
            [
                pl.BlockSpec(
                    (seqs, 1, piece, half_rows), lambda i: (0, i // parts_in, 0, i % parts_in)
                )
            ]
            * chips,
            [out] * chips,
            [],
            0,
            1024,
        )(mine, sibling, after(w_own, *earlier), w_sibling, picked)

    def deliver(part, weight, *earlier, extra=None):
        arrived = []
        for d in range(1, chips):
            send = [(i, ((i // 2 + d) % chips) * 2 + i % 2) for i in range(tps)]
            arrived.append(lax.ppermute(part[d], "tp", send))
        size = part[0].shape[1]
        block = pl.BlockSpec(
            (seqs, 1, piece, half_rows), lambda i: (0, i // parts_in, 0, i % parts_in)
        )
        if extra is None:
            return call(
                add_kernel,
                "add",
                (size * parts_in,),
                [block] * chips,
                block,
                sds(part[0].shape, BF16),
                [],
                weight,
                1024,
            )(after(part[0], *earlier), *arrived)
        one = pl.BlockSpec((seqs, 1, piece, half_rows), lambda i: (0, 0, 0, i % parts_in))
        return call(
            functools.partial(join_kernel, parts_in),
            "add_join",
            (2 * parts_in,),
            [one] * (chips + 1),
            block,
            sds((seqs, 2, piece, frames), BF16),
            [],
            weight,
            1024,
        )(after(part[0], *earlier), *arrived, extra)

    groups = ((0, 1), (1, 1), (2, recs - 2))
    grads = [None] * 3
    taps = [None] * 3
    parts = [None] * 3
    owns = [None] * 3
    moved = [None] * 3
    grads[0], taps[0] = back(*groups[0], w_out)
    grads[1], taps[1] = back(*groups[1], grads[0])
    parts[0] = partials(*groups[0], grads[0], grads[1])
    grads[2], taps[2] = back(*groups[2], *parts[0])
    parts[1] = partials(*groups[1], grads[1], grads[2])
    owns[0] = deliver(parts[0], LONG, *parts[1], extra=w_out)
    moved[0] = exchange(owns[0], "seq")
    parts[2] = partials(*groups[2], grads[2], owns[0])

    slots = 2 * width + 16 * (width // shard)
    half = sds((seqs // 2, slots, shard), BF16)
    keep, send = call(
        functools.partial(outer_kernel, groups),
        "outer_w_in",
        (recs,),
        [smem(), per_record((frames, model))]
        + [
            pl.BlockSpec(
                (frames, 2 * width),
                lambda r, first=first, size=size: (jnp.clip(r - first, 0, size - 1), 0),
            )
            for first, size in groups
        ]
        + [whole((16, width))] * len(groups),
        [whole(half.shape)] * 2,
        [half] * 2,
        [pltpu.VMEM((2 * width, model), F32)],
        LONG,
        1024,
    )(parity, after(normed, *parts[2]), *grads, *taps)
    owns[1] = deliver(parts[1], LONG, keep)
    moved[1] = exchange(after(owns[1], moved[0]), "seq")
    bit = 1
    while True:
        others = lax.ppermute(send, "seq", [(i, i ^ bit) for i in range(seqs)])
        if bit == 1:
            owns[2] = deliver(parts[2], LONG, others, owns[1])
            moved[2] = exchange(after(owns[2], moved[1]), "seq")
        bit *= 2
        if bit == seqs:
            break
        if bit == 2:
            keep = after(keep, owns[2])
        shape = (keep.shape[0] // 2,) + keep.shape[1:]
        side = ((seq_at // bit) % 2).astype(jnp.int32).reshape(1, 1)
        keep, send = call(
            fold_kernel,
            "fold",
            (1,),
            [smem()] + [whole(keep.shape)] * 2,
            [whole(shape)] * 2,
            [sds(shape, BF16)] * 2,
            [],
            2 * LONG if bit == 4 else 0,
            1024,
            vmem=20,
        )(side, keep, others)
    w_out = call(
        finish_out_kernel,
        "finish_w_out",
        (1,),
        [pl.BlockSpec((seqs, 1, piece, frames), lambda i: (0, 1, 0, 0))],
        whole((shard, width)),
        sds((shard, width), F32),
        [],
        0,
        1024,
        vmem=20,
    )(moved[0])
    w_value, w_gate, grad_taps = call(
        functools.partial(finish_kernel, kernel),
        "finish",
        (1,),
        [whole(keep.shape)] * 2,
        [whole((shard, width))] * 2 + [whole((kernel, width))],
        [sds((shard, width), F32)] * 2 + [sds((kernel, width), F32)],
        [],
        0,
        1024,
        vmem=20,
    )(keep, others)
    grad_in = ()
    for (first, size), part in zip(groups, moved):
        grad_in = (
            call(
                place_kernel,
                "place",
                (size,),
                [pl.BlockSpec((seqs, 1, piece, frames), lambda i: (0, i, 0, 0))]
                + [anywhere()] * len(grad_in),
                pl.BlockSpec((1, piece, seqs * frames), lambda i, first=first: (first + i, 0, 0)),
                sds((recs, piece, seqs * frames), BF16),
                [],
                0,
                4 * size * piece * seqs * frames,
                {1: 0} if grad_in else None,
                vmem=20,
            )(part, *grad_in),
        )
    (grad_in,) = grad_in
    return (grad_in, w_value, w_gate, w_out, grad_taps, grad_gain, grad_shift)


def solution(mesh):
    placed = (
        P(None, "seq", None),
        P(None, "seq", None),
        P(None, "tp"),
        P(None, "tp"),
        P(None, "tp"),
        P("tp"),
        P("tp"),
        P(None, "tp"),
        P(),
    )
    return jax.shard_map(
        per_device,
        mesh=mesh,
        in_specs=placed,
        out_specs=(
            P(None, ("seq", "tp"), None),
            P("seq", "tp"),
            P("seq", "tp"),
            P("seq", "tp"),
            P(None, "tp"),
            P("tp"),
            P("tp"),
        ),
        check_vma=False,
    )
```

```python
import functools

import jax
import jax.numpy as jnp
from jax import lax
from jax.experimental import pallas as pl
from jax.experimental.pallas import tpu as pltpu
from jax.sharding import PartitionSpec as P

EPSILON = 1e-05
EDGE = 8
LANES = 128
LONG = 50_000_000_000
F32 = jnp.float32
BF16 = jnp.bfloat16


def sigmoid(x):
    return 0.5 * jnp.tanh(0.5 * x) + 0.5


def dot(a, b):
    return jnp.dot(a, b, preferred_element_type=F32)


def dot_nt(a, b):
    return lax.dot_general(a, b, (((1,), (1,)), ((), ())), preferred_element_type=F32)


def dot_tn(a, b):
    return lax.dot_general(a, b, (((0,), (0,)), ((), ())), preferred_element_type=F32)


def rows_of(count, first):
    return first + lax.broadcasted_iota(jnp.int32, (count, 1), 0)


def fold_rows(x):
    return jnp.sum(x.reshape(x.shape[0] // 8, 8, x.shape[1]), axis=0)


def block_rows(total, most):
    return max(b for b in range(8, most + 1, 8) if total % b == 0)


def whole(shape):
    return pl.BlockSpec(shape, lambda *i: (0,) * len(shape))


def per_record(shape):
    return pl.BlockSpec((1,) + shape, lambda r: (r,) + (0,) * len(shape))


def smem():
    return pl.BlockSpec(memory_space=pltpu.SMEM)


def anywhere():
    return pl.BlockSpec(memory_space=pl.ANY)


def after(x, *earlier):
    return lax.optimization_barrier((x,) + earlier)[0]


def spread_sums(out, sums):
    for s in range(out.shape[0]):
        out[s] = sums


def call(
    kernel, name, grid, in_specs, out_specs, out_shape, scratch, flops, moved, aliases=None, vmem=63
):
    return pl.pallas_call(
        kernel,
        name=name,
        grid=grid,
        in_specs=in_specs,
        out_specs=out_specs,
        out_shape=out_shape,
        scratch_shapes=scratch,
        input_output_aliases=aliases or {},
        cost_estimate=pl.CostEstimate(flops=int(flops), bytes_accessed=int(moved), transcendentals=0),
        compiler_params=pltpu.CompilerParams(vmem_limit_bytes=vmem * 1024 * 1024),
    )


def gate_kernel(meta, x, halo, wv, wg, taps, vl_o, sg_o, conv_o, st_o, gp, st):
    r = pl.program_id(0)
    hi = meta[0, r]
    lo = meta[1, r]
    frames = x.shape[1]
    width = wv.shape[1]
    halves = width // LANES

    def put(row, value):
        for h in range(halves):
            gp[h, pl.ds(row, value.shape[0]), :] = value[:, h * LANES : (h + 1) * LANES]

    edge_v = dot(halo[0], wv[...])
    edge_g = dot(halo[0], wg[...])
    row = rows_of(2 * EDGE, 0)
    pos = jnp.where(row < EDGE, row - EDGE, row - EDGE + frames)
    edge = jnp.where((pos >= lo) & (pos < hi), edge_v * sigmoid(edge_g), 0.0)
    zero = jnp.zeros((EDGE, width), F32)
    put(0, zero)
    put(EDGE, edge[:EDGE])
    put(2 * EDGE + frames, edge[EDGE:])
    put(3 * EDGE + frames, zero)
    step = block_rows(frames, 512)
    small = block_rows(step, 32)
    for base in range(0, frames, step):
        xb = x[0, base : base + step, :]
        vl_o[0, base : base + step, :] = dot(xb, wv[...])
        sg_o[0, base : base + step, :] = dot(xb, wg[...])

    def gating(i, carry):
        base = pl.multiple_of(i * small, small)
        v = vl_o[0, pl.ds(base, small), :]
        s = sigmoid(sg_o[0, pl.ds(base, small), :])
        sg_o[0, pl.ds(base, small), :] = s
        put(2 * EDGE + base, jnp.where(rows_of(small, base) < hi, v * s, 0.0))
        return carry

    lax.fori_loop(0, frames // small, gating, 0)
    span = frames + 2 * EDGE
    cb = block_rows(span, 104)
    kernel = taps.shape[0]
    margin = (kernel - 1) // 2
    for h in range(halves):
        cols = slice(h * LANES, (h + 1) * LANES)

        def convolve(i, carry):
            s1, s2 = carry
            base = pl.multiple_of(i * cb, 8)
            acc = jnp.zeros((cb, LANES), F32)
            for k in range(kernel):
                acc = acc + taps[k : k + 1, cols] * gp[h, pl.ds(base + EDGE - margin + k, cb), :]
            conv_o[0, pl.ds(base, cb), cols] = acc
            pos = rows_of(cb, base - EDGE)
            kept = jnp.where((pos >= 0) & (pos < jnp.minimum(hi, frames)), acc, 0.0)
            return s1 + fold_rows(kept), s2 + fold_rows(kept * kept)

        none = jnp.zeros((8, LANES), F32)
        s1, s2 = lax.fori_loop(0, span // cb, convolve, (none, none))
        add = jnp.concatenate(
            [jnp.sum(s1, axis=0, keepdims=True), jnp.sum(s2, axis=0, keepdims=True)], axis=0
        )
        st[:, cols] = jnp.where(r == 0, 0.0, st[:, cols]) + add

    @pl.when(r == pl.num_programs(0) - 1)
    def _():
        spread_sums(st_o, st[...])


def batch_norm(stats, count):
    sums = jnp.sum(stats[...], axis=0)
    centre = sums[0:1] / count
    spread = sums[1:2] / count - centre * centre
    return centre, lax.rsqrt(spread + EPSILON)


def norm_kernel(
    meta, count, stats, affine, select, grads, halo, wo, conv,
    swished_o, gn_o, picked_o, st_o, st, ping, pong
):
    r = pl.program_id(0)
    hi = meta[0, r]
    lo = meta[1, r]
    frames = grads.shape[1]
    centre, inv = batch_norm(stats, count[0, 0])
    gain, shift = affine[0:1, :], affine[1:2, :]

    def part(row, swish_grad):
        size = swish_grad.shape[0]
        unit = (conv[0, pl.ds(row, size), :] - centre) * inv
        normalized = unit * gain + shift
        s = sigmoid(normalized)
        pos = rows_of(size, row - EDGE)
        keep = (pos >= lo) & (pos < hi)
        swished = jnp.where(keep, normalized * s, 0.0)
        gn = jnp.where(keep, swish_grad, 0.0) * (s + normalized * (s - s * s))
        gn_o[0, pl.ds(row, size), :] = gn
        return unit, swished, gn

    edge = dot(halo[0], wo[...])
    part(0, edge[:EDGE])
    part(frames + EDGE, edge[EDGE:])
    step = block_rows(frames, 512)
    small = block_rows(step, 16)
    s1 = jnp.zeros((8, conv.shape[2]), F32)
    s2 = s1
    held = (ping, pong)
    ping[...] = dot(grads[0, :step, :], wo[...])
    for i in range(frames // step):
        now = held[i % 2]
        if (i + 1) * step < frames:
            held[(i + 1) % 2][...] = dot(grads[0, (i + 1) * step : (i + 2) * step, :], wo[...])
        picked_o[0, :, i * step : (i + 1) * step] = dot_nt(
            select[...], grads[0, i * step : (i + 1) * step, :]
        ).astype(BF16)
        for j in range(step // small):
            base = i * step + j * small
            unit, swished, gn = part(base + EDGE, now[j * small : (j + 1) * small, :])
            swished_o[0, base : base + small, :] = swished.astype(BF16)
            s1 = s1 + fold_rows(gn)
            s2 = s2 + fold_rows(gn * unit)
    add = jnp.concatenate(
        [jnp.sum(s1, axis=0, keepdims=True), jnp.sum(s2, axis=0, keepdims=True)], axis=0
    )
    st[...] = jnp.where(r == 0, 0.0, st[...]) + add

    @pl.when(r == pl.num_programs(0) - 1)
    def _():
        spread_sums(st_o, st[...])


def back_kernel(
    record, blocks, meta, count, stats, sums, gain, gn, conv, vl, sg, taps, out, taps_o, gc, acc
):
    i = pl.program_id(0)
    frames, width = vl.shape[1:]
    hi = meta[0, record + i // blocks]
    lo = meta[1, record + i // blocks]
    halves = width // LANES
    span = frames + 2 * EDGE
    kernel = taps.shape[0]
    margin = (kernel - 1) // 2
    cb = block_rows(span, 144)
    step = block_rows(frames, 32)
    total_frames = count[0, 0]
    centre, inv = batch_norm(stats, total_frames)
    grad_sums = jnp.sum(sums[...], axis=0)
    scale = gain[...] * inv
    offset = scale * grad_sums[0:1] / total_frames
    slope = scale * inv * grad_sums[1:2] / total_frames
    first = i % blocks * frames

    @pl.when(i == 0)
    def _():
        acc[...] = jnp.zeros_like(acc)

    for h in range(halves):
        cols = slice(h * LANES, (h + 1) * LANES)
        for base in range(0, span, cb):
            pos = rows_of(cb, first + (base - EDGE))
            mean = offset[:, cols] + (conv[0, base : base + cb, cols] - centre[:, cols]) * slope[:, cols]
            gc[h, base : base + cb, :] = scale[:, cols] * gn[0, base : base + cb, cols] - jnp.where(
                (pos >= lo) & (pos < hi), mean, 0.0
            )
        sums_k = [acc[h, k] for k in range(kernel)]
        for base in range(0, frames, step):
            v = vl[0, base : base + step, cols]
            s = sg[0, base : base + step, cols]
            keep = rows_of(step, first + base) < hi
            vs = v * s
            gated = jnp.where(keep, vs, 0.0)
            total = jnp.zeros((step, LANES), F32)
            for k in range(kernel):
                window = gc[h, base + EDGE + margin - k : base + EDGE + margin - k + step, :]
                total = total + taps[k : k + 1, cols] * window
                sums_k[k] = sums_k[k] + fold_rows(window * gated)
            total = jnp.where(keep, total, 0.0)
            out[base : base + step, cols] = (total * s).astype(BF16)
            out[base : base + step, width + h * LANES : width + (h + 1) * LANES] = (
                total * (vs - vs * s)
            ).astype(BF16)
        for k in range(kernel):
            acc[h, k] = sums_k[k]

    @pl.when(i == pl.num_programs(0) - 1)
    def _():
        taps_o[...] = jnp.zeros_like(taps_o)
        for h in range(halves):
            for k in range(kernel):
                taps_o[k : k + 1, h * LANES : (h + 1) * LANES] = jnp.sum(
                    acc[h, k], axis=0, keepdims=True
                )


def partial_kernel(own, sibling, w_own, w_sibling, picked, mine, *others):
    total = dot_nt(w_own[...], own[...]) + dot_nt(w_sibling[...], sibling[...])
    rows = picked.shape[1]
    seqs, _, piece, frames = mine.shape
    mine[...] = (
        (total[:rows] + picked[0].astype(F32)).astype(BF16).reshape(seqs, 1, piece, frames)
    )
    for d, other in enumerate(others):
        other[...] = (
            total[(d + 1) * rows : (d + 2) * rows].astype(BF16).reshape(seqs, 1, piece, frames)
        )


def join_kernel(half, *refs):
    i = pl.program_id(0)

    @pl.when(i < half)
    def _():
        add_kernel(*refs[:-2], refs[-1])

    @pl.when(i >= half)
    def _():
        refs[-1][...] = refs[-2][...]


def add_kernel(*refs):
    total = refs[0][...].astype(F32)
    for other in refs[1:-1]:
        total = total + other[...].astype(F32)
    refs[-1][...] = total.astype(BF16)


def first_outer_kernel(grads, swished, out, acc):
    r = pl.program_id(0)
    add = dot_tn(swished[0], grads[0])
    acc[...] = add + jnp.where(r == 0, 0.0, acc[...])

    @pl.when(r == pl.num_programs(0) - 1)
    def _():
        seqs, _, piece, frames = out.shape
        shard = acc.shape[1] // seqs
        for s in range(seqs):
            for q in range(frames // shard):
                out[s, 0, :, q * shard : (q + 1) * shard] = acc[
                    q * piece : (q + 1) * piece, s * shard : (s + 1) * shard
                ].astype(BF16)


def outer_kernel(groups, parity, x, *refs):
    lefts, taps = refs[: len(groups)], refs[len(groups) : 2 * len(groups)]
    keep, send, acc = refs[2 * len(groups) :]
    records = groups[-1][0] + groups[-1][1]
    width = acc.shape[0] // 2
    shard = keep.shape[2]
    r = pl.program_id(0)
    for (first, size), left in zip(groups, lefts):

        @pl.when((r >= first) & (r < first + size))
        def _(left=left):
            add = dot_tn(left[...], x[0])
            acc[...] = add + jnp.where(r == 0, 0.0, acc[...])

    @pl.when(r == records - 1)
    def _():
        tap_sums = taps[0][...]
        for part in taps[1:]:
            tap_sums = tap_sums + part[...]

        def write(place, odd):
            for j in range(place.shape[0]):
                at = (2 * j + odd) * shard
                place[j, : 2 * width, :] = acc[:, at : at + shard].astype(BF16)
                for q in range(width // shard):
                    row = 2 * width + 16 * q
                    place[j, row : row + 16, :] = tap_sums[:, q * shard : (q + 1) * shard].astype(
                        BF16
                    )

        @pl.when(parity[0, 0] == 0)
        def _():
            write(keep, 0)
            write(send, 1)

        @pl.when(parity[0, 0] != 0)
        def _():
            write(keep, 1)
            write(send, 0)


def fold_kernel(parity, own, other, keep, send):
    def write(place, odd):
        for j in range(place.shape[0]):
            total = own[2 * j + odd].astype(F32) + other[2 * j + odd].astype(F32)
            place[j] = total.astype(BF16)

    @pl.when(parity[0, 0] == 0)
    def _():
        write(keep, 0)
        write(send, 1)

    @pl.when(parity[0, 0] != 0)
    def _():
        write(keep, 1)
        write(send, 0)


def finish_kernel(kernel, own, other, value, gate, taps):
    width = value.shape[1]
    shard = value.shape[0]

    def total(row, size):
        return own[0, row : row + size, :].astype(F32) + other[0, row : row + size, :].astype(F32)

    value[...] = total(0, width).T
    gate[...] = total(width, width).T
    for q in range(width // shard):
        taps[:, q * shard : (q + 1) * shard] = total(2 * width + 16 * q, 16)[:kernel]


def finish_out_kernel(pieces, out):
    shard = out.shape[0]
    ready = pieces[0, 0].astype(F32)
    for s in range(1, pieces.shape[0]):
        ready = ready + pieces[s, 0].astype(F32)
    blocks = [ready[:, q * shard : (q + 1) * shard] for q in range(ready.shape[1] // shard)]
    out[...] = jnp.concatenate(blocks, axis=0).T


def place_kernel(moved, *refs):
    out = refs[-1]
    frames = moved.shape[3]
    for s in range(moved.shape[0]):
        out[0, :, s * frames : (s + 1) * frames] = moved[s, 0]


def exchange(copies, axis):
    return lax.all_to_all(copies, axis, 0, 0, tiled=True)


def per_device(
    normed,
    grad_out,
    value_weight,
    gate_weight,
    depth_taps,
    norm_gain,
    norm_shift,
    out_weight,
    lengths,
):
    recs, frames, model = normed.shape
    kernel = depth_taps.shape[0]
    width = value_weight.shape[1]
    seqs = lax.axis_size("seq")
    tps = lax.axis_size("tp")
    chips = tps // 2
    piece = model // (seqs * tps)
    rows = seqs * piece
    shard = model // seqs
    span = frames + 2 * EDGE
    seq_at = lax.axis_index("seq")
    tp_at = lax.axis_index("tp")
    chip_at, core_at = tp_at // 2, tp_at % 2
    count = jnp.sum(lengths).astype(F32)
    first = (seq_at * frames).astype(jnp.int32)
    meta = jnp.stack([lengths - first, jnp.full((recs,), 0, jnp.int32) - first])
    halves = width // LANES
    counts = count.reshape(1, 1)
    parity = (seq_at % 2).astype(jnp.int32).reshape(1, 1)
    sds = jax.ShapeDtypeStruct

    low_edge = jnp.concatenate([normed[:, -EDGE:], grad_out[:, -EDGE:]], axis=2)
    high_edge = jnp.concatenate([normed[:, :EDGE], grad_out[:, :EDGE]], axis=2)
    up = [(i, i + 1) for i in range(seqs - 1)]
    down = [(j, i) for i, j in up]
    halo = jnp.concatenate(
        [lax.ppermute(low_edge, "seq", up), lax.ppermute(high_edge, "seq", down)], axis=1
    )
    halo_x, halo_g = halo[:, :, :model], halo[:, :, model:]

    channel = (
        jnp.arange(seqs, dtype=jnp.int32)[:, None] * (tps * piece)
        + tp_at * piece
        + jnp.arange(piece, dtype=jnp.int32)[None, :]
    ).reshape(rows, 1)
    select = (channel == jnp.arange(model, dtype=jnp.int32)[None, :]).astype(BF16)
    array_bytes = recs * frames * width * 4
    input_bytes = recs * frames * model * 2
    matmul = 2 * recs * frames * model * width

    vl, sg, conv, stats = call(
        gate_kernel,
        "gate_conv",
        (recs,),
        [
            smem(),
            per_record((frames, model)),
            per_record((2 * EDGE, model)),
            whole((model, width)),
            whole((model, width)),
            whole((kernel, width)),
        ],
        [
            per_record((frames, width)),
            per_record((frames, width)),
            per_record((span, width)),
            whole((seqs, 2, width)),
        ],
        [
            sds((recs, frames, width), F32),
            sds((recs, frames, width), F32),
            sds((recs, span, width), F32),
            sds((seqs, 2, width), F32),
        ],
        [pltpu.VMEM((halves, frames + 4 * EDGE, LANES), F32), pltpu.VMEM((2, width), F32)],
        2 * matmul,
        input_bytes + 3 * array_bytes,
    )(meta, normed, halo_x, value_weight, gate_weight, depth_taps)
    both = jnp.concatenate([after(value_weight, stats), gate_weight], axis=1).reshape(seqs, tps, piece, 2 * width)

    def chosen(core):
        picks = [
            lax.dynamic_index_in_dim(both, ((chip_at + d) % chips) * 2 + core, 1, keepdims=False)
            for d in range(chips)
        ]
        return jnp.stack(picks).reshape(chips * rows, 2 * width)

    swap = [(i, i ^ 1) for i in range(tps)]
    w_own = chosen(core_at)
    w_sibling = lax.ppermute(chosen(1 - core_at), "tp", swap)

    stats = exchange(stats, "seq")

    chunk = block_rows(frames, 256)
    half_rows = block_rows(frames, 512)
    swished, gn, picked, sums = call(
        norm_kernel,
        "swish_norm",
        (recs,),
        [
            smem(),
            smem(),
            whole((seqs, 2, width)),
            whole((2, width)),
            whole((rows, model)),
            per_record((frames, model)),
            per_record((2 * EDGE, model)),
            whole((model, width)),
            per_record((span, width)),
        ],
        [
            per_record((frames, width)),
            per_record((span, width)),
            per_record((rows, frames)),
            whole((seqs, 2, width)),
        ],
        [
            sds((recs, frames, width), BF16),
            sds((recs, span, width), F32),
            sds((recs, rows, frames), BF16),
            sds((seqs, 2, width), F32),
        ],
        [
            pltpu.VMEM((2, width), F32),
            pltpu.VMEM((block_rows(frames, 512), width), F32),
            pltpu.VMEM((block_rows(frames, 512), width), F32),
        ],
        2 * matmul,
        input_bytes + 3 * array_bytes,
    )(
        meta,
        counts,
        stats,
        jnp.stack([norm_gain, norm_shift]),
        after(select, w_own, w_sibling),
        grad_out,
        halo_g,
        out_weight,
        conv,
    )
    w_out = call(
        first_outer_kernel,
        "outer_w_out",
        (recs,),
        [per_record((frames, model)), per_record((frames, width))],
        whole((seqs, 1, piece, frames)),
        sds((seqs, 1, piece, frames), BF16),
        [pltpu.VMEM((width, model), F32)],
        matmul,
        input_bytes,
    )(grad_out, swished)
    sums = exchange(sums, "seq")
    grad_shift, grad_gain = jnp.sum(sums, axis=0)

    blocks = frames // chunk
    parts_in = frames // half_rows

    def back(first, size, *earlier):
        def window(i):
            return (first + i // blocks, pl.multiple_of(i % blocks * chunk, chunk), 0)

        def block(i):
            return (first + i // blocks, i % blocks, 0)

        return call(
            functools.partial(back_kernel, first, blocks),
            "back_conv",
            (size * blocks,),
            [
                smem(),
                smem(),
                whole((seqs, 2, width)),
                whole((seqs, 2, width)),
                whole((1, width)),
                pl.BlockSpec((pl.Element(1), pl.Element(chunk + 2 * EDGE), pl.Element(width)), window),
                pl.BlockSpec((pl.Element(1), pl.Element(chunk + 2 * EDGE), pl.Element(width)), window),
                pl.BlockSpec((1, chunk, width), block),
                pl.BlockSpec((1, chunk, width), block),
                whole((kernel, width)),
            ],
            [pl.BlockSpec((chunk, 2 * width), lambda i: (i, 0)), whole((16, width))],
            [sds((size * frames, 2 * width), BF16), sds((16, width), F32)],
            [
                pltpu.VMEM((halves, chunk + 2 * EDGE, LANES), F32),
                pltpu.VMEM((halves, kernel, 8, LANES), F32),
            ],
            0,
            1024,
        )(meta, counts, stats, sums, norm_gain[None], gn, conv, vl, sg, after(depth_taps, *earlier))

    def partials(first, size, mine, *earlier):
        sibling = lax.ppermute(mine, "tp", swap)
        out = sds((seqs, size, piece, frames), BF16)
        return call(
            partial_kernel,
            "partial_in",
            (size * parts_in,),
            [
                pl.BlockSpec((half_rows, 2 * width), lambda i: (i, 0)),
                pl.BlockSpec((half_rows, 2 * width), lambda i: (i, 0)),
                whole((chips * rows, 2 * width)),
                whole((chips * rows, 2 * width)),
                pl.BlockSpec(
                    (1, rows, half_rows), lambda i: (first + i // parts_in, 0, i % parts_in)
                ),
            ],
            [
                pl.BlockSpec(
                    (seqs, 1, piece, half_rows), lambda i: (0, i // parts_in, 0, i % parts_in)
                )
            ]
            * chips,
            [out] * chips,
            [],
            0,
            1024,
        )(mine, sibling, after(w_own, *earlier), w_sibling, picked)

    def deliver(part, weight, *earlier, extra=None):
        arrived = []
        for d in range(1, chips):
            send = [(i, ((i // 2 + d) % chips) * 2 + i % 2) for i in range(tps)]
            arrived.append(lax.ppermute(part[d], "tp", send))
        size = part[0].shape[1]
        block = pl.BlockSpec(
            (seqs, 1, piece, half_rows), lambda i: (0, i // parts_in, 0, i % parts_in)
        )
        if extra is None:
            return call(
                add_kernel,
                "add",
                (size * parts_in,),
                [block] * chips,
                block,
                sds(part[0].shape, BF16),
                [],
                weight,
                1024,
            )(after(part[0], *earlier), *arrived)
        one = pl.BlockSpec((seqs, 1, piece, half_rows), lambda i: (0, 0, 0, i % parts_in))
        return call(
            functools.partial(join_kernel, parts_in),
            "add_join",
            (2 * parts_in,),
            [one] * (chips + 1),
            block,
            sds((seqs, 2, piece, frames), BF16),
            [],
            weight,
            1024,
        )(after(part[0], *earlier), *arrived, extra)

    groups = ((0, 1), (1, 1), (2, recs - 2))
    grads = [None] * 3
    taps = [None] * 3
    parts = [None] * 3
    owns = [None] * 3
    moved = [None] * 3
    grads[0], taps[0] = back(*groups[0], w_out)
    grads[1], taps[1] = back(*groups[1], grads[0])
    parts[0] = partials(*groups[0], grads[0], grads[1])
    grads[2], taps[2] = back(*groups[2], *parts[0])
    parts[1] = partials(*groups[1], grads[1], grads[2])
    owns[0] = deliver(parts[0], LONG, *parts[1], extra=w_out)
    moved[0] = exchange(owns[0], "seq")
    parts[2] = partials(*groups[2], grads[2], owns[0])

    slots = 2 * width + 16 * (width // shard)
    half = sds((seqs // 2, slots, shard), BF16)
    keep, send = call(
        functools.partial(outer_kernel, groups),
        "outer_w_in",
        (recs,),
        [smem(), per_record((frames, model))]
        + [
            pl.BlockSpec(
                (frames, 2 * width),
                lambda r, first=first, size=size: (jnp.clip(r - first, 0, size - 1), 0),
            )
            for first, size in groups
        ]
        + [whole((16, width))] * len(groups),
        [whole(half.shape)] * 2,
        [half] * 2,
        [pltpu.VMEM((2 * width, model), F32)],
        LONG,
        1024,
    )(parity, after(normed, *parts[2]), *grads, *taps)
    owns[1] = deliver(parts[1], LONG, keep)
    moved[1] = exchange(after(owns[1], moved[0]), "seq")
    bit = 1
    while True:
        others = lax.ppermute(send, "seq", [(i, i ^ bit) for i in range(seqs)])
        if bit == 1:
            owns[2] = deliver(parts[2], LONG, others, owns[1])
            moved[2] = exchange(after(owns[2], moved[1]), "seq")
        bit *= 2
        if bit == seqs:
            break
        if bit == 2:
            keep = after(keep, owns[2])
        shape = (keep.shape[0] // 2,) + keep.shape[1:]
        side = ((seq_at // bit) % 2).astype(jnp.int32).reshape(1, 1)
        keep, send = call(
            fold_kernel,
            "fold",
            (1,),
            [smem()] + [whole(keep.shape)] * 2,
            [whole(shape)] * 2,
            [sds(shape, BF16)] * 2,
            [],
            2 * LONG if bit == 4 else 0,
            1024,
            vmem=20,
        )(side, keep, others)
    w_out = call(
        finish_out_kernel,
        "finish_w_out",
        (1,),
        [pl.BlockSpec((seqs, 1, piece, frames), lambda i: (0, 1, 0, 0))],
        whole((shard, width)),
        sds((shard, width), F32),
        [],
        0,
        1024,
        vmem=20,
    )(moved[0])
    w_value, w_gate, grad_taps = call(
        functools.partial(finish_kernel, kernel),
        "finish",
        (1,),
        [whole(keep.shape)] * 2,
        [whole((shard, width))] * 2 + [whole((kernel, width))],
        [sds((shard, width), F32)] * 2 + [sds((kernel, width), F32)],
        [],
        0,
        1024,
        vmem=20,
    )(keep, others)
    grad_in = ()
    for (first, size), part in zip(groups, moved):
        grad_in = (
            call(
                place_kernel,
                "place",
                (size,),
                [pl.BlockSpec((seqs, 1, piece, frames), lambda i: (0, i, 0, 0))]
                + [anywhere()] * len(grad_in),
                pl.BlockSpec((1, piece, seqs * frames), lambda i, first=first: (first + i, 0, 0)),
                sds((recs, piece, seqs * frames), BF16),
                [],
                0,
                4 * size * piece * seqs * frames,
                {1: 0} if grad_in else None,
                vmem=20,
            )(part, *grad_in),
        )
    (grad_in,) = grad_in
    return (grad_in, w_value, w_gate, w_out, grad_taps, grad_gain, grad_shift)


def solution(mesh):
    placed = (
        P(None, "seq", None),
        P(None, "seq", None),
        P(None, "tp"),
        P(None, "tp"),
        P(None, "tp"),
        P("tp"),
        P("tp"),
        P(None, "tp"),
        P(),
    )
    return jax.shard_map(
        per_device,
        mesh=mesh,
        in_specs=placed,
        out_specs=(
            P(None, ("seq", "tp"), None),
            P("seq", "tp"),
            P("seq", "tp"),
            P("seq", "tp"),
            P(None, "tp"),
            P("tp"),
            P("tp"),
        ),
        check_vma=False,
    )
```
